32 devices in a mesh: grp: 4 (over x, core), seq: 8 (over z, y).
Axes of the slice: x: 2, y: 2, z: 4, core: 2. Of those that a mesh axis runs over, the one named last changes fastest.
Arguments:
- hidden: bfloat16 [4096, 1536], P(('grp', 'seq')), may hold values from -6 to 6
- latent_shape: int32 [4, 3, 2], P('grp'), may hold values from 2 to 64, as said below
- cond_r: float32 [12, 64], P('grp'), may hold values from -6 to 6
- clip: bfloat16 [12, 77, 1280], P('grp'), may hold values from -6 to 6
- cotangent: bfloat16 [4096, 1536], P(('grp', 'seq')), may hold values from -6 to 6
- conv_weight: bfloat16 [9, 1536], P(None, 'seq'), may hold values from -2 to 2
- conv_bias: bfloat16 [1536], P('seq'), may hold values from -3 to 3
- fc1_weight: bfloat16 [1536, 6144], P(None, 'seq'), may hold values from -0.15625 to 0.15625
- fc1_bias: bfloat16 [6144], P('seq'), may hold values from -2 to 2
- grn_gamma: bfloat16 [6144], P('seq'), may hold values from -3 to 3
- grn_beta: bfloat16 [6144], P('seq'), may hold values from -2 to 2
- fc2_weight: bfloat16 [6144, 1536], P(None, 'seq'), may hold values from -0.078125 to 0.078125
- fc2_bias: bfloat16 [1536], P('seq'), may hold values from -2 to 2
- time_weight: bfloat16 [64, 3072], P(None, 'seq'), may hold values from -0.25 to 0.25
- time_bias: bfloat16 [3072], P('seq'), may hold values from -1.5 to 1.5
- map_weight: bfloat16 [1280, 1536], P(None, 'seq'), may hold values from -0.15625 to 0.15625
- map_bias: bfloat16 [1536], P('seq'), may hold values from -2 to 2
- query_weight: bfloat16 [1536, 1536], P(None, 'seq'), may hold values from -0.15625 to 0.15625
- query_bias: bfloat16 [1536], P('seq'), may hold values from -2 to 2
- key_weight: bfloat16 [1536, 1536], P(None, 'seq'), may hold values from -0.15625 to 0.15625
- value_weight: bfloat16 [1536, 1536], P(None, 'seq'), may hold values from -0.15625 to 0.15625
- value_bias: bfloat16 [1536], P('seq'), may hold values from -2 to 2
- out_weight: bfloat16 [1536, 1536], P(None, 'seq'), may hold values from -3 to 3
- out_bias: bfloat16 [1536], P('seq'), may hold values from -2 to 2
Outputs:
- activations: bfloat16 [4096, 1536], P(('grp', 'seq'))
- input_grad: float32 [4096, 1536], P(('grp', 'seq'))
- conv_weight_grad: float32 [9, 1536], P(None, 'seq')
- conv_bias_grad: float32 [1536], P('seq')
- fc1_weight_grad: float32 [1536, 6144], P(None, 'seq')
- fc1_bias_grad: float32 [6144], P('seq')
- grn_gamma_grad: float32 [6144], P('seq')
- grn_beta_grad: float32 [6144], P('seq')
- fc2_weight_grad: float32 [6144, 1536], P(None, 'seq')
- fc2_bias_grad: float32 [1536], P('seq')
- time_weight_grad: float32 [64, 3072], P(None, 'seq')
- time_bias_grad: float32 [3072], P('seq')
- map_weight_grad: float32 [1280, 1536], P(None, 'seq')
- map_bias_grad: float32 [1536], P('seq')
- query_weight_grad: float32 [1536, 1536], P(None, 'seq')
- query_bias_grad: float32 [1536], P('seq')
- key_weight_grad: float32 [1536, 1536], P(None, 'seq')
- value_weight_grad: float32 [1536, 1536], P(None, 'seq')
- value_bias_grad: float32 [1536], P('seq')
- out_weight_grad: float32 [1536, 1536], P(None, 'seq')
- out_bias_grad: float32 [1536], P('seq')
The draws below stay inside these ranges and needn't reach their ends.
Inputs may be any that keep to these rules, and one draw needn't show every extreme that they name: `latent_shape`: each group packs its three latents without gaps into its 1024 pixels, all 64 pixels wide; the middle latent has 10 rows, the first and last latents share the remaining rows, each with 2 rows or more; in some group the first latent has exactly that many.
All inputs are finite; a program needn't handle non-finite values.
Results may differ from the reference program's by a relative error of at most 0.018.
Values may be sent and summed in bfloat16 or wider, within the bound.
A program may use at most 384 MiB of HBM per device.

```python
import jax
import jax.numpy as jnp
from jax import lax

C = 1536
HEADS = 24
HEAD_DIM = 64
FF = 6144
CLIP = 1280
NCTX = 77
RDIM = 64
NLAT = 3
WMAX = 64
GROUP_TOK = 1024
GROUPS = 4
TOKENS = 4096


def draw_latent_shape(key, part):
    key = jax.random.fold_in(key, 11)
    pick_key, upper_key = jax.random.split(key, 2)
    rows_all = GROUP_TOK // WMAX
    middle_height = rows_all // 2 + rows_all // 8
    lowest = max(1, rows_all // 8)
    highest = rows_all - middle_height - lowest
    group_ids = jnp.arange(GROUPS, dtype=jnp.int32)
    upper_rows = jax.random.randint(upper_key, (GROUPS,), lowest, highest + 1).astype(jnp.int32)
    anchor = jax.random.randint(pick_key, (), 0, GROUPS)
    upper_rows = jnp.where(group_ids == anchor, lowest, upper_rows).astype(jnp.int32)
    lower_rows = (rows_all - middle_height - upper_rows).astype(jnp.int32)
    middle_rows = jnp.full((GROUPS,), middle_height, jnp.int32)
    heights = jnp.stack([upper_rows, middle_rows, lower_rows], axis=1)
    widths = jnp.full((GROUPS, NLAT), WMAX, jnp.int32)
    return jnp.stack([heights, widths], axis=-1).astype(jnp.int32)


def steps_of(key, extent, shards, smallest, top_value):
    def one(dim, shards_of):
        steps = jax.random.uniform(jax.random.fold_in(jax.random.fold_in(key, 6), dim), (shards_of,), jnp.float32, smallest / len(shards), top_value / len(shards))
        return jnp.repeat(jnp.exp(steps), extent[dim] // shards_of).reshape((-1,) + (1,) * (len(extent) - dim - 1))

    level = one(*shards[0])
    for cut in shards[1:]:
        level = level * one(*cut)
    return level


def gaussian(rng, shape, spread, limit, cuts=(), kind=jnp.bfloat16):
    level = steps_of(rng, shape, cuts, -0.22, 0.18) if cuts else 1.0
    drawn = jax.random.normal(rng, shape, jnp.float32) * spread * level
    return jnp.minimum(jnp.maximum(drawn, -limit), limit).astype(kind)


def setup_inputs(seed: int = 0) -> dict:
    seeds = jax.random.split(jax.random.key(seed), 25)
    hidden = gaussian(seeds[0], (TOKENS, C), 1.0, 6.0, ((0, 32),))
    latent_shape = draw_latent_shape(jax.random.fold_in(seeds[24], 71), 0)
    cond_r = gaussian(seeds[2], (GROUPS * NLAT, RDIM), 1.0, 6.0, ((0, 4),), jnp.float32)
    clip = gaussian(seeds[3], (GROUPS * NLAT, NCTX, CLIP), 1.0, 6.0, ((0, 4),))
    cotangent = gaussian(seeds[4], (TOKENS, C), 1.0, 6.0, ((0, 32),))
    conv_weight = gaussian(seeds[5], (9, C), 9 ** -0.5, 2.0, ((1, 8),))
    conv_bias = gaussian(seeds[6], (C,), 0.5, 3.0, ((0, 8),))
    fc1_weight = gaussian(seeds[7], (C, FF), C ** -0.5, 0.15625, ((1, 8),))
    fc1_bias = gaussian(seeds[8], (FF,), 0.3, 2.0, ((0, 8),))
    grn_gamma = gaussian(seeds[9], (FF,), 0.5, 3.0, ((0, 8),))
    grn_beta = gaussian(seeds[10], (FF,), 0.3, 2.0, ((0, 8),))
    fc2_weight = gaussian(seeds[11], (FF, C), FF ** -0.5, 0.078125, ((1, 8),))
    fc2_bias = gaussian(seeds[12], (C,), 0.3, 2.0, ((0, 8),))
    time_weight = gaussian(seeds[13], (RDIM, 2 * C), (9 * RDIM) ** -0.5, 0.25, ((1, 8),))
    time_bias = gaussian(seeds[14], (2 * C,), 0.2, 1.5, ((0, 8),))
    map_weight = gaussian(seeds[15], (CLIP, C), CLIP ** -0.5, 0.15625, ((1, 8),))
    map_bias = gaussian(seeds[16], (C,), 0.3, 2.0, ((0, 8),))
    query_weight = gaussian(seeds[17], (C, C), C ** -0.5, 0.15625, ((1, 8),))
    query_bias = gaussian(seeds[18], (C,), 0.3, 2.0, ((0, 8),))
    key_weight = gaussian(seeds[19], (C, C), C ** -0.5, 0.15625, ((1, 8),))
    value_weight = gaussian(seeds[20], (C, C), C ** -0.5, 0.15625, ((1, 8),))
    value_bias = gaussian(seeds[21], (C,), 0.3, 2.0, ((0, 8),))
    out_weight = gaussian(seeds[22], (C, C), (max(1, 3 * C // GROUP_TOK)) ** -0.5, 3.0, ((1, 8),))
    out_bias = gaussian(seeds[23], (C,), 0.3, 2.0, ((0, 8),))
    return {"hidden": hidden, "latent_shape": latent_shape, "cond_r": cond_r, "clip": clip, "cotangent": cotangent, "conv_weight": conv_weight, "conv_bias": conv_bias, "fc1_weight": fc1_weight, "fc1_bias": fc1_bias, "grn_gamma": grn_gamma, "grn_beta": grn_beta, "fc2_weight": fc2_weight, "fc2_bias": fc2_bias, "time_weight": time_weight, "time_bias": time_bias, "map_weight": map_weight, "map_bias": map_bias, "query_weight": query_weight, "query_bias": query_bias, "key_weight": key_weight, "value_weight": value_weight, "value_bias": value_bias, "out_weight": out_weight, "out_bias": out_bias}


@jax.custom_vjp
def low(v):
    return lax.optimization_barrier(v.astype(jnp.bfloat16)).astype(jnp.float32)

@jax.custom_vjp
def low_back(v):
    return v

def low_keep(v):
    return (low(v), None)

def low_pass(kept, grad):
    return (grad,)

def back_keep(v):
    return (v, None)

def back_low(kept, grad):
    return (low(grad),)
low.defvjp(low_keep, low_pass)
low_back.defvjp(back_keep, back_low)
EPS_NORM = 1e-06
SCORE_SCALE = 0.125
MASKED = -1e+30
HIGHEST_PRECISION = lax.Precision.HIGHEST

def mat(left, right):
    return jnp.dot(left, right, precision=HIGHEST_PRECISION, preferred_element_type=jnp.float32)

def layer_norm(values_in):
    average = lax.optimization_barrier(jnp.mean(values_in, axis=-1, keepdims=True))
    centred = values_in - average
    variance = lax.optimization_barrier(jnp.mean(centred * centred, axis=-1, keepdims=True))
    return centred * lax.rsqrt(variance + EPS_NORM)

def latent_grid(positions, shape_row):
    latent_count = shape_row.shape[0]
    heights = shape_row[:, 0].astype(jnp.int32)
    latent_width = shape_row[0, 1].astype(jnp.int32)
    pixel_counts = heights * latent_width
    end_points = jnp.cumsum(pixel_counts).astype(jnp.int32)
    start_points = (end_points - pixel_counts).astype(jnp.int32)
    segment = lax.optimization_barrier(jnp.sum((positions[:, None] >= end_points[None, :]).astype(jnp.int32), axis=1)).astype(jnp.int32)
    segment = jnp.minimum(segment, latent_count - 1)
    picked = (segment[:, None] == jnp.arange(latent_count, dtype=jnp.int32)[None, :]).astype(jnp.int32)
    first_pixel = lax.optimization_barrier(jnp.sum(picked * start_points[None, :], axis=1)).astype(jnp.int32)
    height = lax.optimization_barrier(jnp.sum(picked * heights[None, :], axis=1)).astype(jnp.int32)
    offset_in = positions - first_pixel
    row_index = jnp.floor_divide(offset_in, latent_width)
    column = offset_in - row_index * latent_width
    return (segment, row_index, column, height, latent_width)

def valid_tap(row_index, column, height, latent_width, down_step, side_step):
    upright = (row_index + down_step >= 0) & (row_index + down_step < height)
    across = (column + side_step >= 0) & (column + side_step < latent_width)
    return (upright & across).astype(jnp.float32)

def softmax_rows(scores):
    shifted = scores - lax.optimization_barrier(jnp.max(scores, axis=-1, keepdims=True))
    expo = jnp.exp(shifted)
    return expo / lax.optimization_barrier(jnp.sum(expo, axis=-1, keepdims=True))

def forward_group(hidden_rows, cond_rows, clip_rows, shape_row, params):
    kernel, kernel_bias, expand, expand_bias, gamma, beta, shrink, shrink_bias, time_map, time_bias, mapper, mapper_bias, query_map, query_bias, key_map, value_map, value_bias, output_map, output_bias = params
    group_rows = hidden_rows.shape[0]
    positions = jnp.arange(group_rows, dtype=jnp.int32)
    segment, row_index, column, height, latent_width = latent_grid(positions, shape_row)
    margin = WMAX + 1
    padded = jnp.pad(hidden_rows, ((margin, margin), (0, 0)))
    conv_out = jnp.broadcast_to(kernel_bias[None, :], hidden_rows.shape)
    for down_step in (-1, 0, 1):
        for side_step in (-1, 0, 1):
            tap_number = 3 * (down_step + 1) + (side_step + 1)
            valid = valid_tap(row_index, column, height, latent_width, down_step, side_step)
            offset_rows = (down_step * latent_width + side_step).astype(jnp.int32)
            nearby = lax.dynamic_slice_in_dim(padded, margin + offset_rows, group_rows, 0)
            conv_out = conv_out + kernel[tap_number][None, :] * nearby * valid[:, None]
    conv_out = low_back(conv_out)
    normed = low(layer_norm(conv_out))
    pre_act = low_back(mat(normed, expand) + expand_bias)
    activated = jax.nn.gelu(pre_act, approximate=False)
    picked = (segment[:, None] == jnp.arange(NLAT, dtype=jnp.int32)[None, :]).astype(jnp.float32)
    energy = mat(picked.T, activated * activated)
    root = jnp.sqrt(energy + 1.0)
    ratio = root / (lax.optimization_barrier(jnp.mean(root, axis=-1, keepdims=True)) + EPS_NORM)
    ratio_rows = mat(picked, ratio)
    response = low(gamma * (activated * ratio_rows) + beta + activated)
    first_sum = hidden_rows + low_back(mat(response, shrink) + shrink_bias)
    modulation = mat(cond_rows, time_map) + time_bias
    mod_rows = mat(picked, modulation)
    second_sum = first_sum * (1.0 + mod_rows[:, :C]) + mod_rows[:, C:]
    attn_in = low(layer_norm(second_sum))
    context_in = low(jax.nn.silu(clip_rows.reshape(NLAT * NCTX, CLIP)))
    context = low(mat(context_in, mapper) + mapper_bias)
    queries = low(low_back(mat(attn_in, query_map) + query_bias))
    keys_all = low(low_back(mat(attn_in, key_map)))
    values_all = low(low_back(mat(attn_in, value_map) + value_bias))
    context_keys = low(mat(context, key_map))
    context_values = low(mat(context, value_map) + value_bias)
    key_heads = jnp.concatenate([keys_all, context_keys], axis=0).reshape(-1, HEADS, HEAD_DIM)
    value_heads = jnp.concatenate([values_all, context_values], axis=0).reshape(-1, HEADS, HEAD_DIM)
    context_segment = (jnp.arange(NLAT * NCTX, dtype=jnp.int32) // NCTX).astype(jnp.int32)
    key_segment = jnp.concatenate([segment, context_segment], axis=0)
    block_rows = 512 if group_rows % 512 == 0 else group_rows
    query_stack = queries.reshape(group_rows // block_rows, block_rows, HEADS, HEAD_DIM)
    segment_stack = segment.reshape(group_rows // block_rows, block_rows)

    def attend_block(element):
        query_block, segment_block = element
        scores = jnp.einsum('qhd,khd->hqk', query_block, key_heads, precision=HIGHEST_PRECISION) * SCORE_SCALE
        admitted = segment_block[:, None] == key_segment[None, :]
        scores = low_back(jnp.where(admitted[None], scores, MASKED))
        weights = low(softmax_rows(scores))
        return jnp.einsum('hqk,khd->qhd', weights, value_heads, precision=HIGHEST_PRECISION)
    mixed = lax.map(jax.checkpoint(attend_block), (query_stack, segment_stack)).reshape(group_rows, C)
    mixed = low(low_back(mixed))
    return second_sum + low_back(mat(mixed, output_map) + output_bias)

def reference(hidden, latent_shape, cond_r, clip, cotangent, conv_weight, conv_bias, fc1_weight, fc1_bias, grn_gamma, grn_beta, fc2_weight, fc2_bias, time_weight, time_bias, map_weight, map_bias, query_weight, query_bias, key_weight, value_weight, value_bias, out_weight, out_bias):
    params = tuple((item.astype(jnp.float32) for item in (conv_weight, conv_bias, fc1_weight, fc1_bias, grn_gamma, grn_beta, fc2_weight, fc2_bias, time_weight, time_bias, map_weight, map_bias, query_weight, query_bias, key_weight, value_weight, value_bias, out_weight, out_bias)))
    totals = tuple((jnp.zeros_like(item) for item in params))
    outputs = []
    input_grads = []
    for group_index in range(GROUPS):
        lower_row = group_index * GROUP_TOK
        group_hidden = hidden[lower_row:lower_row + GROUP_TOK].astype(jnp.float32)
        group_cot = cotangent[lower_row:lower_row + GROUP_TOK].astype(jnp.float32)
        group_cond = cond_r[group_index * NLAT:(group_index + 1) * NLAT].astype(jnp.float32)
        group_clip = clip[group_index * NLAT:(group_index + 1) * NLAT].astype(jnp.float32)
        group_shape = latent_shape[group_index]

        def apply_group(values_in, weights_in):
            return forward_group(values_in, group_cond, group_clip, group_shape, weights_in)
        result, pullback = jax.vjp(apply_group, group_hidden, params)
        hidden_grad, weight_grads = pullback(group_cot)
        outputs.append(result.astype(jnp.bfloat16))
        input_grads.append(hidden_grad)
        totals = tuple((total + part for total, part in zip(totals, weight_grads)))
    activations = jnp.concatenate(outputs, axis=0)
    input_grad = jnp.concatenate(input_grads, axis=0)
    return (activations, input_grad, totals[0], totals[1], totals[2], totals[3], totals[4], totals[5], totals[6], totals[7], totals[8], totals[9], totals[10], totals[11], totals[12], totals[13], totals[14], totals[15], totals[16], totals[17], totals[18])
```

```python
import math

import jax
import jax.numpy as jnp
from jax import lax
from jax.sharding import PartitionSpec as P

C = 1536
HEADS = 24
HEAD_DIM = 64
FF = 6144
CLIP = 1280
NCTX = 77
NLAT = 3
WMAX = 64


EPS_NORM = 1e-06
SCORE_SCALE = 0.125
MASKED = -1e30
HIGHEST_PRECISION = lax.Precision.HIGHEST


def padded_2(block, sides, width):
    for axis, dim in sides:
        count = lax.axis_size(axis)
        forward = [(i, i + 1) for i in range(count - 1)]
        backward = [(target, source) for source, target in forward]
        low = lax.ppermute(
            lax.slice_in_dim(block, block.shape[dim] - width, None, axis=dim), axis, forward
        )
        high = lax.ppermute(lax.slice_in_dim(block, 0, width, axis=dim), axis, backward)
        block = jnp.concatenate([low, block, high], axis=dim)
    return block


def latent_grid(positions, shape_row):
    latent_count = shape_row.shape[0]
    heights = shape_row[:, 0]
    latent_width = shape_row[0, 1]
    pixel_counts = heights * latent_width
    end_points = jnp.cumsum(pixel_counts)
    start_points = end_points - pixel_counts
    segment = jnp.sum((positions[:, None] >= end_points[None, :]).astype(jnp.int32), axis=1)
    segment = jnp.minimum(segment, latent_count - 1)
    picked = (segment[:, None] == jnp.arange(latent_count, dtype=jnp.int32)[None, :]).astype(
        jnp.int32
    )
    first_pixel = jnp.sum(picked * start_points[None, :], axis=1)
    height = jnp.sum(picked * heights[None, :], axis=1)
    offset_in = positions - first_pixel
    row_index = jnp.floor_divide(offset_in, latent_width)
    column = offset_in - row_index * latent_width
    return (segment, row_index, column, height, latent_width)


def valid_tap(row_index, column, height, latent_width, down_step, side_step):
    upright = (row_index + down_step >= 0) & (row_index + down_step < height)
    across = (column + side_step >= 0) & (column + side_step < latent_width)
    return (upright & across).astype(jnp.float32)


def layer_stats(values_in):
    average = jnp.mean(values_in, axis=-1, keepdims=True)
    centred = values_in - average
    variance = jnp.mean(centred * centred, axis=-1, keepdims=True)
    inverse = lax.rsqrt(variance + EPS_NORM)
    return (centred * inverse, inverse)


def layer_back(gradient, normed, inverse):
    mean_grad = jnp.mean(gradient, axis=-1, keepdims=True)
    mean_mixed = jnp.mean(gradient * normed, axis=-1, keepdims=True)
    return inverse * (gradient - mean_grad - normed * mean_mixed)


def against(values_low, weight_low):
    return lax.dot_general(
        values_low, weight_low, (((1,), (1,)), ((), ())), preferred_element_type=jnp.float32
    )


def against_exact(values_in, weight_in):
    return lax.dot_general(
        values_in,
        weight_in,
        (((1,), (1,)), ((), ())),
        precision=HIGHEST_PRECISION,
        preferred_element_type=jnp.float32,
    )


def outer_sum(left_low, right_low):
    return lax.dot_general(
        left_low, right_low, (((0,), (0,)), ((), ())), preferred_element_type=jnp.float32
    )


def column_sum(picked, values_in):
    return lax.dot_general(
        picked,
        values_in,
        (((0,), (0,)), ((), ())),
        precision=HIGHEST_PRECISION,
        preferred_element_type=jnp.float32,
    )


def exact_gelu(values_in):
    return jax.nn.gelu(values_in, approximate=False)


def block_size(row_count, shard_rows):
    shard_total = row_count // shard_rows
    return math.gcd(shard_total, max(1, 1024 // shard_rows)) * shard_rows


def on_device(
    hidden,
    latent_shape,
    cond_r,
    clip,
    cotangent,
    conv_weight,
    conv_bias,
    fc1_weight,
    fc1_bias,
    grn_gamma,
    grn_beta,
    fc2_weight,
    fc2_bias,
    time_weight,
    time_bias,
    map_weight,
    map_bias,
    query_weight,
    query_bias,
    key_weight,
    value_weight,
    value_bias,
    out_weight,
    out_bias,
):
    tok_rows = hidden.shape[0]
    positions = lax.axis_index("seq") * tok_rows + jnp.arange(tok_rows, dtype=jnp.int32)
    shape_row = latent_shape[0]
    segment, row_index, column, height, latent_width = latent_grid(positions, shape_row)
    margin = WMAX + 1
    gathered = (
        lax.all_gather(conv_weight, "seq", axis=1, tiled=True),
        lax.all_gather(conv_bias, "seq", axis=0, tiled=True),
        lax.all_gather(fc1_weight, "seq", axis=1, tiled=True),
        lax.all_gather(fc1_bias, "seq", axis=0, tiled=True),
        lax.all_gather(grn_gamma, "seq", axis=0, tiled=True),
        lax.all_gather(grn_beta, "seq", axis=0, tiled=True),
        lax.all_gather(fc2_weight, "seq", axis=1, tiled=True),
        lax.all_gather(fc2_bias, "seq", axis=0, tiled=True),
        lax.all_gather(time_weight, "seq", axis=1, tiled=True),
        lax.all_gather(time_bias, "seq", axis=0, tiled=True),
        lax.all_gather(map_weight, "seq", axis=1, tiled=True),
        lax.all_gather(map_bias, "seq", axis=0, tiled=True),
        lax.all_gather(query_weight, "seq", axis=1, tiled=True),
        lax.all_gather(query_bias, "seq", axis=0, tiled=True),
        lax.all_gather(key_weight, "seq", axis=1, tiled=True),
        lax.all_gather(value_weight, "seq", axis=1, tiled=True),
        lax.all_gather(value_bias, "seq", axis=0, tiled=True),
        lax.all_gather(out_weight, "seq", axis=1, tiled=True),
        lax.all_gather(out_bias, "seq", axis=0, tiled=True),
    )
    (
        kernel_full,
        kernel_bias,
        expand_full,
        expand_bias,
        gamma_full,
        beta_full,
        shrink_full,
        shrink_bias,
        time_full,
        time_bias_full,
        mapper_full,
        mapper_bias,
        query_full,
        query_bias_full,
        key_full,
        value_full,
        value_bias_full,
        output_full,
        output_bias_full,
    ) = gathered
    padded = padded_2(hidden, (("seq", 0),), margin)
    conv_out = jnp.broadcast_to(kernel_bias.astype(jnp.float32)[None, :], (tok_rows, C))
    tap_list = []
    for down_step in (-1, 0, 1):
        for side_step in (-1, 0, 1):
            tap_number = 3 * (down_step + 1) + (side_step + 1)
            valid = valid_tap(row_index, column, height, latent_width, down_step, side_step)
            offset_rows = down_step * latent_width + side_step
            nearby = lax.dynamic_slice_in_dim(padded, margin + offset_rows, tok_rows, 0).astype(
                jnp.float32
            )
            conv_out = (
                conv_out
                + kernel_full[tap_number].astype(jnp.float32)[None, :] * nearby * valid[:, None]
            )
            tap_list.append((tap_number, down_step, side_step, offset_rows, valid))
    normed_one, inverse_one = layer_stats(conv_out)
    normed_low = normed_one.astype(jnp.bfloat16)
    pre_act = jnp.dot(
        normed_low, expand_full, preferred_element_type=jnp.float32
    ) + expand_bias.astype(jnp.float32)
    activated, gelu_pull = jax.vjp(exact_gelu, pre_act)
    picked = (segment[:, None] == jnp.arange(NLAT, dtype=jnp.int32)[None, :]).astype(jnp.float32)
    energy = lax.psum(column_sum(picked, activated * activated), "seq")
    root = jnp.sqrt(energy + 1.0)
    denom = jnp.mean(root, axis=-1, keepdims=True) + EPS_NORM
    ratio = root / denom
    ratio_rows = jnp.dot(picked, ratio, precision=HIGHEST_PRECISION)
    gamma_value = gamma_full.astype(jnp.float32)
    response = gamma_value * (activated * ratio_rows) + beta_full.astype(jnp.float32) + activated
    response_low = response.astype(jnp.bfloat16)
    branch = jnp.dot(
        response_low, shrink_full, preferred_element_type=jnp.float32
    ) + shrink_bias.astype(jnp.float32)
    first_sum = hidden.astype(jnp.float32) + branch
    modulation = jnp.dot(
        cond_r, time_full.astype(jnp.float32), precision=HIGHEST_PRECISION
    ) + time_bias_full.astype(jnp.float32)
    mod_rows = jnp.dot(picked, modulation, precision=HIGHEST_PRECISION)
    scale_rows = 1.0 + mod_rows[:, :C]
    second_sum = first_sum * scale_rows + mod_rows[:, C:]
    normed_two, inverse_two = layer_stats(second_sum)
    attn_in = normed_two.astype(jnp.bfloat16)
    context_in = jax.nn.silu(clip.reshape(NLAT * NCTX, CLIP).astype(jnp.float32)).astype(
        jnp.bfloat16
    )
    context = (
        jnp.dot(context_in, mapper_full, preferred_element_type=jnp.float32)
        + mapper_bias.astype(jnp.float32)
    ).astype(jnp.bfloat16)
    queries = (
        jnp.dot(attn_in, query_full, preferred_element_type=jnp.float32)
        + query_bias_full.astype(jnp.float32)
    ).astype(jnp.bfloat16)
    keys_low = jnp.dot(attn_in, key_full, preferred_element_type=jnp.float32).astype(jnp.bfloat16)
    values_low = (
        jnp.dot(attn_in, value_full, preferred_element_type=jnp.float32)
        + value_bias_full.astype(jnp.float32)
    ).astype(jnp.bfloat16)
    context_keys = jnp.dot(context, key_full, preferred_element_type=jnp.float32).astype(
        jnp.bfloat16
    )
    context_values = (
        jnp.dot(context, value_full, preferred_element_type=jnp.float32)
        + value_bias_full.astype(jnp.float32)
    ).astype(jnp.bfloat16)
    query_heads = queries.reshape(tok_rows, HEADS, HEAD_DIM)
    key_heads = keys_low.reshape(tok_rows, HEADS, HEAD_DIM)
    value_heads = values_low.reshape(tok_rows, HEADS, HEAD_DIM)
    ctx_key_heads = context_keys.reshape(NLAT * NCTX, HEADS, HEAD_DIM)
    ctx_value_heads = context_values.reshape(NLAT * NCTX, HEADS, HEAD_DIM)
    context_segment = jnp.arange(NLAT * NCTX, dtype=jnp.int32) // NCTX
    ctx_admit = segment[:, None] == context_segment[None, :]

    def segments_at(first_row, length):
        return latent_grid(first_row + jnp.arange(length, dtype=jnp.int32), shape_row)[0]

    ctx_scores = (
        jnp.einsum("qhd,khd->hqk", query_heads, ctx_key_heads, preferred_element_type=jnp.float32)
        * SCORE_SCALE
    )
    ctx_scores = jnp.where(ctx_admit[None], ctx_scores, MASKED)
    start_max = jnp.max(ctx_scores, axis=-1)
    ctx_expo = jnp.exp(ctx_scores - start_max[..., None])
    start_total = jnp.sum(ctx_expo, axis=-1)
    start_accum = jnp.einsum(
        "hqk,khd->qhd",
        ctx_expo.astype(jnp.bfloat16),
        ctx_value_heads,
        preferred_element_type=jnp.float32,
    )
    key_part = lax.all_gather(keys_low, "seq", axis=0, tiled=True)
    value_part = lax.all_gather(values_low, "seq", axis=0, tiled=True)
    block_rows = block_size(key_part.shape[0], tok_rows)
    block_count = key_part.shape[0] // block_rows
    key_stack = key_part.reshape(block_count, block_rows, HEADS, HEAD_DIM)
    value_stack = value_part.reshape(block_count, block_rows, HEADS, HEAD_DIM)

    def attend_visit(state_now, element):
        key_block, value_block, block_index = element
        key_segment = segments_at(block_index * block_rows, block_rows)
        admitted = segment[:, None] == key_segment[None, :]
        scores = (
            jnp.einsum("qhd,khd->hqk", query_heads, key_block, preferred_element_type=jnp.float32)
            * SCORE_SCALE
        )
        scores = jnp.where(admitted[None], scores, MASKED)
        old_max, old_total, old_accum = state_now
        new_max = jnp.maximum(old_max, jnp.max(scores, axis=-1))
        factor = jnp.exp(old_max - new_max)
        expo_block = jnp.exp(scores - new_max[..., None])
        new_total = old_total * factor + jnp.sum(expo_block, axis=-1)
        new_accum = old_accum * factor.T[:, :, None] + jnp.einsum(
            "hqk,khd->qhd",
            expo_block.astype(jnp.bfloat16),
            value_block,
            preferred_element_type=jnp.float32,
        )
        return ((new_max, new_total, new_accum), None)

    state_end, ignored = lax.scan(
        attend_visit,
        (start_max, start_total, start_accum),
        (key_stack, value_stack, jnp.arange(block_count, dtype=jnp.int32)),
    )
    run_max, run_total, accum = state_end
    mixed = accum / run_total.T[:, :, None]
    log_total = run_max + jnp.log(run_total)
    mixed_low = mixed.reshape(tok_rows, C).astype(jnp.bfloat16)
    activations = (
        second_sum
        + jnp.dot(mixed_low, output_full, preferred_element_type=jnp.float32)
        + output_bias_full.astype(jnp.float32)
    ).astype(jnp.bfloat16)
    cot_value = cotangent.astype(jnp.float32)
    grad_out_w = outer_sum(mixed_low, cotangent)
    grad_out_b = jnp.sum(cot_value, axis=0)
    d_mixed_low = against(cotangent, output_full).astype(jnp.bfloat16)
    dmix_heads = d_mixed_low.reshape(tok_rows, HEADS, HEAD_DIM)
    delta = jnp.sum(dmix_heads.astype(jnp.float32) * mixed, axis=-1).T
    ctx_probs = jnp.exp(ctx_scores - log_total[..., None])
    ctx_dprob = jnp.einsum(
        "qhd,khd->hqk", dmix_heads, ctx_value_heads, preferred_element_type=jnp.float32
    )
    ctx_dscore = (ctx_probs * (ctx_dprob - delta[..., None])).astype(jnp.bfloat16)
    dquery_start = (
        jnp.einsum("hqk,khd->qhd", ctx_dscore, ctx_key_heads, preferred_element_type=jnp.float32)
        * SCORE_SCALE
    )
    ctx_dkey_part = (
        jnp.einsum("hqk,qhd->khd", ctx_dscore, query_heads, preferred_element_type=jnp.float32)
        * SCORE_SCALE
    )
    ctx_dvalue_part = jnp.einsum(
        "hqk,qhd->khd",
        ctx_probs.astype(jnp.bfloat16),
        dmix_heads,
        preferred_element_type=jnp.float32,
    )
    key_part = lax.all_gather(keys_low, "seq", axis=0, tiled=True)
    value_part = lax.all_gather(values_low, "seq", axis=0, tiled=True)
    query_block_rows = block_size(key_part.shape[0], tok_rows)
    block_count = key_part.shape[0] // query_block_rows
    key_stack = key_part.reshape(block_count, query_block_rows, HEADS, HEAD_DIM)
    value_stack = value_part.reshape(block_count, query_block_rows, HEADS, HEAD_DIM)

    def query_visit(state_now, element):
        key_block, value_block, block_index = element
        key_segment = segments_at(block_index * query_block_rows, query_block_rows)
        admitted = segment[:, None] == key_segment[None, :]
        scores = (
            jnp.einsum("qhd,khd->hqk", query_heads, key_block, preferred_element_type=jnp.float32)
            * SCORE_SCALE
        )
        scores = jnp.where(admitted[None], scores, MASKED)
        probs = jnp.exp(scores - log_total[..., None])
        dprob = jnp.einsum(
            "qhd,khd->hqk", dmix_heads, value_block, preferred_element_type=jnp.float32
        )
        dscore = (probs * (dprob - delta[..., None])).astype(jnp.bfloat16)
        added = (
            jnp.einsum("hqk,khd->qhd", dscore, key_block, preferred_element_type=jnp.float32)
            * SCORE_SCALE
        )
        return (state_now + added, None)

    state_end, ignored = lax.scan(
        query_visit,
        dquery_start,
        (key_stack, value_stack, jnp.arange(block_count, dtype=jnp.int32)),
    )
    dquery = state_end
    lse_all, delta_all = (
        lax.all_gather(log_total.T, "seq", axis=0, tiled=True),
        lax.all_gather(delta.T, "seq", axis=0, tiled=True),
    )
    zero_heads = jnp.zeros((tok_rows, HEADS, HEAD_DIM), jnp.float32)
    query_part = lax.all_gather(queries, "seq", axis=0, tiled=True)
    dmix_part = lax.all_gather(d_mixed_low, "seq", axis=0, tiled=True)
    row_count = query_part.shape[0]
    key_block_rows = block_size(row_count, tok_rows)
    block_count = row_count // key_block_rows
    query_stack = query_part.reshape(block_count, key_block_rows, HEADS, HEAD_DIM)
    dmix_stack = dmix_part.reshape(block_count, key_block_rows, HEADS, HEAD_DIM)
    lse_stack = lse_all.reshape(block_count, key_block_rows, HEADS)
    delta_stack = delta_all.reshape(block_count, key_block_rows, HEADS)

    def key_visit(state_now, element):
        query_block, dmix_block, lse_block, delta_block, block_index = element
        query_segment = segments_at(block_index * key_block_rows, key_block_rows)
        admitted = segment[:, None] == query_segment[None, :]
        scores = (
            jnp.einsum("khd,qhd->hkq", key_heads, query_block, preferred_element_type=jnp.float32)
            * SCORE_SCALE
        )
        scores = jnp.where(admitted[None], scores, MASKED)
        probs = jnp.exp(scores - lse_block.T[:, None, :])
        dkey_now, dvalue_now = state_now
        dvalue_now = dvalue_now + jnp.einsum(
            "hkq,qhd->khd",
            probs.astype(jnp.bfloat16),
            dmix_block,
            preferred_element_type=jnp.float32,
        )
        dprob = jnp.einsum(
            "khd,qhd->hkq", value_heads, dmix_block, preferred_element_type=jnp.float32
        )
        dscore = (probs * (dprob - delta_block.T[:, None, :])).astype(jnp.bfloat16)
        dkey_now = (
            dkey_now
            + jnp.einsum("hkq,qhd->khd", dscore, query_block, preferred_element_type=jnp.float32)
            * SCORE_SCALE
        )
        return ((dkey_now, dvalue_now), None)

    state_end, ignored = lax.scan(
        key_visit,
        (zero_heads, zero_heads),
        (query_stack, dmix_stack, lse_stack, delta_stack, jnp.arange(block_count, dtype=jnp.int32)),
    )
    dkey, dvalue = state_end
    dquery_low = dquery.reshape(tok_rows, C).astype(jnp.bfloat16)
    dkey_low = dkey.reshape(tok_rows, C).astype(jnp.bfloat16)
    dvalue_low = dvalue.reshape(tok_rows, C).astype(jnp.bfloat16)
    ctx_dkey_flat = ctx_dkey_part.reshape(NLAT * NCTX, C)
    ctx_dvalue_flat = ctx_dvalue_part.reshape(NLAT * NCTX, C)
    context_value = context.astype(jnp.float32)
    d_attn_in = (
        against(dquery_low, query_full)
        + against(dkey_low, key_full)
        + against(dvalue_low, value_full)
    )
    grad_query_w = outer_sum(attn_in, dquery_low)
    grad_query_b = jnp.sum(dquery_low.astype(jnp.float32), axis=0)
    grad_key_w = outer_sum(attn_in, dkey_low) + column_sum(context_value, ctx_dkey_flat)
    grad_value_w = outer_sum(attn_in, dvalue_low) + column_sum(context_value, ctx_dvalue_flat)
    grad_value_b = jnp.sum(dvalue_low.astype(jnp.float32), axis=0) + jnp.sum(
        ctx_dvalue_flat, axis=0
    )
    d_context = against_exact(ctx_dkey_flat, key_full.astype(jnp.float32)) + against_exact(
        ctx_dvalue_flat, value_full.astype(jnp.float32)
    )
    grad_map_w = column_sum(context_in.astype(jnp.float32), d_context)
    grad_map_b = jnp.sum(d_context, axis=0)
    d_second = cot_value + layer_back(d_attn_in, normed_two, inverse_two)
    d_first = d_second * scale_rows
    d_mod_rows = jnp.concatenate([d_second * first_sum, d_second], axis=1)
    d_modulation = column_sum(picked, d_mod_rows)
    grad_time_w = lax.dot_general(
        cond_r,
        d_modulation,
        (((0,), (0,)), ((), ())),
        precision=HIGHEST_PRECISION,
        preferred_element_type=jnp.float32,
    )
    grad_time_b = jnp.sum(d_modulation, axis=0)
    d_branch_low = d_first.astype(jnp.bfloat16)
    grad_shrink_w = outer_sum(response_low, d_branch_low)
    grad_shrink_b = jnp.sum(d_branch_low.astype(jnp.float32), axis=0)
    d_response = against(d_branch_low, shrink_full)
    grad_gamma = jnp.sum(d_response * activated * ratio_rows, axis=0)
    grad_beta = jnp.sum(d_response, axis=0)
    d_ratio = lax.psum(column_sum(picked, d_response * gamma_value * activated), "seq")
    d_root = d_ratio / denom - jnp.sum(d_ratio * root, axis=-1, keepdims=True) / (
        FF * denom * denom
    )
    d_act = d_response * (gamma_value * ratio_rows + 1.0) + activated * jnp.dot(
        picked, d_root / root, precision=HIGHEST_PRECISION
    )
    d_pre_low = gelu_pull(d_act)[0].astype(jnp.bfloat16)
    grad_expand_w = outer_sum(normed_low, d_pre_low)
    grad_expand_b = jnp.sum(d_pre_low.astype(jnp.float32), axis=0)
    d_normed = against(d_pre_low, expand_full)
    d_conv_low = layer_back(d_normed, normed_one, inverse_one).astype(jnp.bfloat16)
    d_conv = d_conv_low.astype(jnp.float32)
    grad_kernel_b = jnp.sum(d_conv, axis=0)
    d_padded = padded_2(d_conv_low, (("seq", 0),), margin)
    kernel_rows = []
    input_grad = d_first
    for tap_number, down_step, side_step, offset_rows, valid in tap_list:
        nearby = lax.dynamic_slice_in_dim(padded, margin + offset_rows, tok_rows, 0).astype(
            jnp.float32
        )
        kernel_rows.append(jnp.sum(d_conv * nearby * valid[:, None], axis=0))
        source = positions - offset_rows
        src_segment, src_row, src_column, src_height, src_width = latent_grid(source, shape_row)
        src_valid = valid_tap(src_row, src_column, src_height, src_width, down_step, side_step)
        behind = lax.dynamic_slice_in_dim(d_padded, margin - offset_rows, tok_rows, 0).astype(
            jnp.float32
        )
        input_grad = (
            input_grad
            + kernel_full[tap_number].astype(jnp.float32)[None, :] * behind * src_valid[:, None]
        )
    grad_kernel_w = jnp.stack(kernel_rows, axis=0)
    gradients = (
        grad_kernel_w,
        grad_kernel_b,
        grad_expand_w,
        grad_expand_b,
        grad_gamma,
        grad_beta,
        grad_shrink_w,
        grad_shrink_b,
        grad_time_w,
        grad_time_b,
        grad_map_w,
        grad_map_b,
        grad_query_w,
        grad_query_b,
        grad_key_w,
        grad_value_w,
        grad_value_b,
        grad_out_w,
        grad_out_b,
    )
    shares = (
        lax.psum_scatter(gradients[0], "seq", scatter_dimension=1, tiled=True),
        lax.psum_scatter(gradients[1], "seq", scatter_dimension=0, tiled=True),
        lax.psum_scatter(gradients[2], "seq", scatter_dimension=1, tiled=True),
        lax.psum_scatter(gradients[3], "seq", scatter_dimension=0, tiled=True),
        lax.psum_scatter(gradients[4], "seq", scatter_dimension=0, tiled=True),
        lax.psum_scatter(gradients[5], "seq", scatter_dimension=0, tiled=True),
        lax.psum_scatter(gradients[6], "seq", scatter_dimension=1, tiled=True),
        lax.psum_scatter(gradients[7], "seq", scatter_dimension=0, tiled=True),
        lax.psum_scatter(gradients[8], "seq", scatter_dimension=1, tiled=True),
        lax.psum_scatter(gradients[9], "seq", scatter_dimension=0, tiled=True),
        lax.psum_scatter(gradients[10], "seq", scatter_dimension=1, tiled=True),
        lax.psum_scatter(gradients[11], "seq", scatter_dimension=0, tiled=True),
        lax.psum_scatter(gradients[12], "seq", scatter_dimension=1, tiled=True),
        lax.psum_scatter(gradients[13], "seq", scatter_dimension=0, tiled=True),
        lax.psum_scatter(gradients[14], "seq", scatter_dimension=1, tiled=True),
        lax.psum_scatter(gradients[15], "seq", scatter_dimension=1, tiled=True),
        lax.psum_scatter(gradients[16], "seq", scatter_dimension=0, tiled=True),
        lax.psum_scatter(gradients[17], "seq", scatter_dimension=1, tiled=True),
        lax.psum_scatter(gradients[18], "seq", scatter_dimension=0, tiled=True),
    )
    summed = (
        lax.psum(shares[0].astype(jnp.bfloat16), "grp").astype(jnp.float32),
        lax.psum(shares[1].astype(jnp.bfloat16), "grp").astype(jnp.float32),
        lax.psum(shares[2].astype(jnp.bfloat16), "grp").astype(jnp.float32),
        lax.psum(shares[3].astype(jnp.bfloat16), "grp").astype(jnp.float32),
        lax.psum(shares[4].astype(jnp.bfloat16), "grp").astype(jnp.float32),
        lax.psum(shares[5].astype(jnp.bfloat16), "grp").astype(jnp.float32),
        lax.psum(shares[6].astype(jnp.bfloat16), "grp").astype(jnp.float32),
        lax.psum(shares[7].astype(jnp.bfloat16), "grp").astype(jnp.float32),
        lax.psum(shares[8].astype(jnp.bfloat16), "grp").astype(jnp.float32),
        lax.psum(shares[9].astype(jnp.bfloat16), "grp").astype(jnp.float32),
        lax.psum(shares[10].astype(jnp.bfloat16), "grp").astype(jnp.float32),
        lax.psum(shares[11].astype(jnp.bfloat16), "grp").astype(jnp.float32),
        lax.psum(shares[12].astype(jnp.bfloat16), "grp").astype(jnp.float32),
        lax.psum(shares[13].astype(jnp.bfloat16), "grp").astype(jnp.float32),
        lax.psum(shares[14].astype(jnp.bfloat16), "grp").astype(jnp.float32),
        lax.psum(shares[15].astype(jnp.bfloat16), "grp").astype(jnp.float32),
        lax.psum(shares[16].astype(jnp.bfloat16), "grp").astype(jnp.float32),
        lax.psum(shares[17].astype(jnp.bfloat16), "grp").astype(jnp.float32),
        lax.psum(shares[18].astype(jnp.bfloat16), "grp").astype(jnp.float32),
    )
    return (
        activations,
        input_grad,
        summed[0],
        summed[1],
        summed[2],
        summed[3],
        summed[4],
        summed[5],
        summed[6],
        summed[7],
        summed[8],
        summed[9],
        summed[10],
        summed[11],
        summed[12],
        summed[13],
        summed[14],
        summed[15],
        summed[16],
        summed[17],
        summed[18],
    )


def gather_rows(block):
    return lax.all_gather(block, "seq", axis=0, tiled=True)


def scatter_rows(partial):
    return lax.psum_scatter(
        partial.astype(jnp.bfloat16), "seq", scatter_dimension=0, tiled=True
    ).astype(jnp.float32)


def mm(left, right):
    return jnp.dot(left, right, preferred_element_type=jnp.float32)


def on_device_heads(
    hidden,
    latent_shape,
    cond_r,
    clip,
    cotangent,
    conv_weight,
    conv_bias,
    fc1_weight,
    fc1_bias,
    grn_gamma,
    grn_beta,
    fc2_weight,
    fc2_bias,
    time_weight,
    time_bias,
    map_weight,
    map_bias,
    query_weight,
    query_bias,
    key_weight,
    value_weight,
    value_bias,
    out_weight,
    out_bias,
):
    f32, bf16 = jnp.float32, jnp.bfloat16
    shards = lax.axis_size("seq")
    me = lax.axis_index("seq")
    rows = hidden.shape[0]
    total = rows * shards
    cols = C // shards
    local_heads = HEADS // shards
    margin = WMAX + 1
    shape_row = latent_shape[0]
    positions = me * rows + jnp.arange(rows, dtype=jnp.int32)
    segment, row_index, column, height, latent_width = latent_grid(positions, shape_row)
    all_segment = latent_grid(jnp.arange(total, dtype=jnp.int32), shape_row)[0]
    latents = jnp.arange(NLAT, dtype=jnp.int32)
    picked = (segment[:, None] == latents[None, :]).astype(f32)
    all_picked = (all_segment[:, None] == latents[None, :]).astype(f32)

    mod_cols = jnp.dot(
        cond_r, time_weight.astype(f32), precision=HIGHEST_PRECISION
    ) + time_bias.astype(f32)
    pack = jnp.concatenate(
        [
            conv_weight.astype(f32),
            conv_bias.astype(f32)[None],
            fc2_bias.astype(f32)[None],
            mod_cols.reshape(NLAT * 2, cols),
        ],
        axis=0,
    )
    packed = lax.all_gather(pack, "seq", axis=0)
    kernel_full = packed[:, :9].transpose(1, 0, 2).reshape(9, C)
    kernel_bias = packed[:, 9].reshape(C)
    shrink_bias = packed[:, 10].reshape(C)
    modulation = (
        packed[:, 11:].reshape(shards, NLAT, 2 * cols).transpose(1, 0, 2).reshape(NLAT, 2 * C)
    )
    mod_rows = jnp.dot(picked, modulation, precision=HIGHEST_PRECISION)
    scale_rows = 1.0 + mod_rows[:, :C]

    shrink_rows = lax.all_to_all(fc2_weight, "seq", 0, 1, tiled=True)
    output_rows = lax.all_to_all(out_weight, "seq", 0, 1, tiled=True)
    cot_full = gather_rows(cotangent)

    padded = padded_2(hidden, (("seq", 0),), margin)
    conv_out = jnp.broadcast_to(kernel_bias[None, :], (rows, C))
    tap_list = []
    for down_step in (-1, 0, 1):
        for side_step in (-1, 0, 1):
            tap_number = 3 * (down_step + 1) + (side_step + 1)
            valid = valid_tap(row_index, column, height, latent_width, down_step, side_step)
            offset = down_step * WMAX + side_step
            nearby = padded[margin + offset : margin + offset + rows].astype(f32)
            conv_out = conv_out + kernel_full[tap_number][None, :] * nearby * valid[:, None]
            tap_list.append((tap_number, down_step, side_step, offset, valid))
    normed_one, inverse_one = layer_stats(conv_out)
    normed_full = gather_rows(normed_one.astype(bf16))

    pre_act = mm(normed_full, fc1_weight) + fc1_bias.astype(f32)
    phi = 0.5 * (1.0 + lax.erf(pre_act * math.sqrt(0.5)))
    activated = pre_act * phi
    energy = column_sum(all_picked, activated * activated)
    root = jnp.sqrt(energy + 1.0)
    denom = lax.psum(jnp.sum(root, axis=-1, keepdims=True), "seq") / FF + EPS_NORM
    ratio = root / denom
    ratio_rows = jnp.dot(all_picked, ratio, precision=HIGHEST_PRECISION)
    gamma = grn_gamma.astype(f32)
    response = gamma * (activated * ratio_rows) + grn_beta.astype(f32) + activated
    response_low = response.astype(bf16)
    branch = scatter_rows(mm(response_low, shrink_rows)) + shrink_bias
    first_sum = hidden.astype(f32) + branch
    second_sum = first_sum * scale_rows + mod_rows[:, C:]
    normed_two, inverse_two = layer_stats(second_sum)
    attn_full = gather_rows(normed_two.astype(bf16))

    context_in = jax.nn.silu(clip.reshape(NLAT * NCTX, CLIP).astype(f32)).astype(bf16)
    context_cols = (mm(context_in, map_weight) + map_bias.astype(f32)).astype(bf16)
    context = lax.all_gather(context_cols, "seq", axis=1, tiled=True)

    heads = lambda values: values.reshape(values.shape[0], local_heads, HEAD_DIM)
    value_shift = value_bias.astype(f32)
    queries = (mm(attn_full, query_weight) + query_bias.astype(f32)).astype(bf16)
    inputs = jnp.concatenate([attn_full, context], axis=0)
    keys = mm(inputs, key_weight).astype(bf16)
    values = (mm(inputs, value_weight) + value_shift).astype(bf16)
    key_segment = jnp.concatenate(
        [all_segment, jnp.arange(NLAT * NCTX, dtype=jnp.int32) // NCTX], axis=0
    )
    admitted = all_segment[:, None] == key_segment[None, :]
    scores = (
        jnp.einsum("qhd,khd->hqk", heads(queries), heads(keys), preferred_element_type=f32)
        * SCORE_SCALE
    )
    scores = jnp.where(admitted[None], scores, MASKED)
    top = jnp.max(scores, axis=-1, keepdims=True)
    expo = jnp.exp(scores - top)
    probs = expo / jnp.sum(expo, axis=-1, keepdims=True)
    probs_low = probs.astype(bf16)
    mixed = jnp.einsum("hqk,khd->qhd", probs_low, heads(values), preferred_element_type=f32)
    mixed_low = mixed.reshape(total, cols).astype(bf16)
    mixed_full = lax.all_gather(mixed_low, "seq", axis=1, tiled=True)
    out_cols = (mm(mixed_full, out_weight) + out_bias.astype(f32)).astype(bf16)
    activations = (
        second_sum + lax.all_to_all(out_cols, "seq", 0, 1, tiled=True).astype(f32)
    ).astype(bf16)

    cot_cols = lax.dynamic_slice_in_dim(cot_full, me * cols, cols, 1)
    grad_out_w = outer_sum(mixed_full, cot_cols)
    grad_out_b = jnp.sum(cot_cols.astype(f32), axis=0)
    d_mixed_low = against(cot_full, output_rows).astype(bf16)
    d_mixed = heads(d_mixed_low)
    delta = jnp.sum(d_mixed.astype(f32) * mixed, axis=-1).T
    d_probs = jnp.einsum("qhd,khd->hqk", d_mixed, heads(values), preferred_element_type=f32)
    d_scores = (probs * (d_probs - delta[..., None])).astype(bf16)
    d_queries = (
        jnp.einsum("hqk,khd->qhd", d_scores, heads(keys), preferred_element_type=f32) * SCORE_SCALE
    ).reshape(total, cols)
    d_keys = (
        jnp.einsum("hqk,qhd->khd", d_scores, heads(queries), preferred_element_type=f32)
        * SCORE_SCALE
    ).reshape(-1, cols)
    d_values = jnp.einsum("hqk,qhd->khd", probs_low, d_mixed, preferred_element_type=f32).reshape(
        -1, cols
    )
    d_queries_low = d_queries.astype(bf16)
    d_keys_low = d_keys.astype(bf16)
    d_values_low = d_values.astype(bf16)
    grad_query_w = outer_sum(attn_full, d_queries_low)
    grad_query_b = jnp.sum(d_queries_low.astype(f32), axis=0)
    grad_key_w = outer_sum(inputs, d_keys_low)
    grad_value_w = outer_sum(inputs, d_values_low)
    grad_value_b = jnp.sum(d_values_low.astype(f32), axis=0)
    ctx_part = against(d_keys_low[total:], key_weight) + against(d_values_low[total:], value_weight)
    d_context = lax.psum_scatter(ctx_part, "seq", scatter_dimension=1, tiled=True)
    grad_map_w = outer_sum(context_in, d_context.astype(bf16))
    grad_map_b = jnp.sum(d_context, axis=0)
    d_attn = scatter_rows(
        against(d_queries_low, query_weight)
        + against(d_keys_low[:total], key_weight)
        + against(d_values_low[:total], value_weight)
    )
    d_second = cotangent.astype(f32) + layer_back(d_attn, normed_two, inverse_two)
    d_first = d_second * scale_rows
    d_mod = column_sum(picked, jnp.concatenate([d_second * first_sum, d_second], axis=1))
    d_branch_low = d_first.astype(bf16)
    branch_full = gather_rows(d_branch_low)
    grad_shrink_rows = outer_sum(response_low, branch_full).astype(bf16)
    grad_shrink_w = lax.all_to_all(grad_shrink_rows, "seq", 1, 0, tiled=True)
    grad_shrink_b = jnp.sum(
        lax.dynamic_slice_in_dim(branch_full, me * cols, cols, 1).astype(f32), axis=0
    )
    d_response = against(branch_full, shrink_rows)
    d_scaled = d_response * activated
    grad_gamma = jnp.sum(d_scaled * ratio_rows, axis=0)
    grad_beta = jnp.sum(d_response, axis=0)
    d_ratio = column_sum(all_picked, d_scaled * gamma)
    pulled = lax.psum(jnp.sum(d_ratio * root, axis=-1, keepdims=True), "seq")
    d_root = d_ratio / denom - pulled / (FF * denom * denom)
    d_act = d_response * (gamma * ratio_rows + 1.0) + activated * jnp.dot(
        all_picked, d_root / root, precision=HIGHEST_PRECISION
    )
    density = jnp.exp(-0.5 * pre_act * pre_act) * (1.0 / math.sqrt(2.0 * math.pi))
    d_pre_low = (d_act * (phi + pre_act * density)).astype(bf16)
    grad_expand_w = outer_sum(normed_full, d_pre_low)
    grad_expand_b = jnp.sum(d_pre_low.astype(f32), axis=0)
    d_normed = scatter_rows(against(d_pre_low, fc1_weight))
    d_conv_low = layer_back(d_normed, normed_one, inverse_one).astype(bf16)
    d_conv = d_conv_low.astype(f32)
    d_padded = padded_2(d_conv_low, (("seq", 0),), margin)
    small_rows = []
    input_grad = d_first
    for tap_number, down_step, side_step, offset, valid in tap_list:
        nearby = padded[margin + offset : margin + offset + rows].astype(f32)
        small_rows.append(jnp.sum(d_conv * nearby * valid[:, None], axis=0))
        src_grid = latent_grid(positions - offset, shape_row)
        src_valid = valid_tap(*src_grid[1:], down_step, side_step)
        behind = d_padded[margin - offset : margin - offset + rows].astype(f32)
        input_grad = input_grad + kernel_full[tap_number][None, :] * behind * src_valid[:, None]
    small_rows.append(jnp.sum(d_conv, axis=0))
    small = jnp.concatenate([jnp.stack(small_rows), d_mod.reshape(NLAT * 2, C)], axis=0)
    conv_small = lax.psum_scatter(small[:10], "seq", scatter_dimension=1, tiled=True)
    d_modulation = lax.psum_scatter(d_mod, "seq", scatter_dimension=1, tiled=True)
    grad_time_w = lax.dot_general(
        cond_r,
        d_modulation,
        (((0,), (0,)), ((), ())),
        precision=HIGHEST_PRECISION,
        preferred_element_type=f32,
    )
    grad_time_b = jnp.sum(d_modulation, axis=0)
    gradients = (
        conv_small[:9],
        conv_small[9],
        grad_expand_w,
        grad_expand_b,
        grad_gamma,
        grad_beta,
        grad_shrink_w,
        grad_shrink_b,
        grad_time_w,
        grad_time_b,
        grad_map_w,
        grad_map_b,
        grad_query_w,
        grad_query_b,
        grad_key_w,
        grad_value_w,
        grad_value_b,
        grad_out_w,
        grad_out_b,
    )
    summed = tuple(lax.psum(item.astype(bf16), "grp").astype(f32) for item in gradients)
    return (activations, input_grad) + summed


def solution(mesh):
    in_specs = (
        P(("grp", "seq"), None),
        P("grp", None, None),
        P("grp", None),
        P("grp", None, None),
        P(("grp", "seq"), None),
        P(None, "seq"),
        P("seq"),
        P(None, "seq"),
        P("seq"),
        P("seq"),
        P("seq"),
        P(None, "seq"),
        P("seq"),
        P(None, "seq"),
        P("seq"),
        P(None, "seq"),
        P("seq"),
        P(None, "seq"),
        P("seq"),
        P(None, "seq"),
        P(None, "seq"),
        P("seq"),
        P(None, "seq"),
        P("seq"),
    )
    out_specs = (
        P(("grp", "seq"), None),
        P(("grp", "seq"), None),
        P(None, "seq"),
        P("seq"),
        P(None, "seq"),
        P("seq"),
        P("seq"),
        P("seq"),
        P(None, "seq"),
        P("seq"),
        P(None, "seq"),
        P("seq"),
        P(None, "seq"),
        P("seq"),
        P(None, "seq"),
        P("seq"),
        P(None, "seq"),
        P(None, "seq"),
        P("seq"),
        P(None, "seq"),
        P("seq"),
    )
    by_heads = HEADS % mesh.shape["seq"] == 0 and FF % mesh.shape["seq"] == 0
    return jax.shard_map(
        on_device_heads if by_heads else on_device, mesh=mesh, in_specs=in_specs, out_specs=out_specs, check_vma=False
    )
```

```python
import functools
import math

import jax
import jax.numpy as jnp
from jax import lax
from jax.experimental import pallas as pl
from jax.experimental.pallas import tpu as pltpu
from jax.sharding import PartitionSpec as P

C = 1536
HEADS = 24
HEAD_DIM = 64
FF = 6144
CLIP = 1280
NCTX = 77
NLAT = 3
WMAX = 64


EPS_NORM = 1e-06
SCORE_SCALE = 0.125
MASKED = -1e30
HIGHEST_PRECISION = lax.Precision.HIGHEST


def padded_2(block, sides, width):
    for axis, dim in sides:
        count = lax.axis_size(axis)
        forward = [(i, i + 1) for i in range(count - 1)]
        backward = [(target, source) for source, target in forward]
        low = lax.ppermute(
            lax.slice_in_dim(block, block.shape[dim] - width, None, axis=dim), axis, forward
        )
        high = lax.ppermute(lax.slice_in_dim(block, 0, width, axis=dim), axis, backward)
        block = jnp.concatenate([low, block, high], axis=dim)
    return block


def latent_grid(positions, shape_row):
    latent_count = shape_row.shape[0]
    heights = shape_row[:, 0]
    latent_width = shape_row[0, 1]
    pixel_counts = heights * latent_width
    end_points = jnp.cumsum(pixel_counts)
    start_points = end_points - pixel_counts
    segment = jnp.sum((positions[:, None] >= end_points[None, :]).astype(jnp.int32), axis=1)
    segment = jnp.minimum(segment, latent_count - 1)
    picked = (segment[:, None] == jnp.arange(latent_count, dtype=jnp.int32)[None, :]).astype(
        jnp.int32
    )
    first_pixel = jnp.sum(picked * start_points[None, :], axis=1)
    height = jnp.sum(picked * heights[None, :], axis=1)
    offset_in = positions - first_pixel
    row_index = jnp.floor_divide(offset_in, latent_width)
    column = offset_in - row_index * latent_width
    return (segment, row_index, column, height, latent_width)


def valid_tap(row_index, column, height, latent_width, down_step, side_step):
    upright = (row_index + down_step >= 0) & (row_index + down_step < height)
    across = (column + side_step >= 0) & (column + side_step < latent_width)
    return (upright & across).astype(jnp.float32)


def layer_stats(values_in):
    average = jnp.mean(values_in, axis=-1, keepdims=True)
    centred = values_in - average
    variance = jnp.mean(centred * centred, axis=-1, keepdims=True)
    inverse = lax.rsqrt(variance + EPS_NORM)
    return (centred * inverse, inverse)


def layer_back(gradient, normed, inverse):
    mean_grad = jnp.mean(gradient, axis=-1, keepdims=True)
    mean_mixed = jnp.mean(gradient * normed, axis=-1, keepdims=True)
    return inverse * (gradient - mean_grad - normed * mean_mixed)


def against(values_low, weight_low):
    return lax.dot_general(
        values_low, weight_low, (((1,), (1,)), ((), ())), preferred_element_type=jnp.float32
    )


def against_exact(values_in, weight_in):
    return lax.dot_general(
        values_in,
        weight_in,
        (((1,), (1,)), ((), ())),
        precision=HIGHEST_PRECISION,
        preferred_element_type=jnp.float32,
    )


def outer_sum(left_low, right_low):
    return lax.dot_general(
        left_low, right_low, (((0,), (0,)), ((), ())), preferred_element_type=jnp.float32
    )


def column_sum(picked, values_in):
    return lax.dot_general(
        picked,
        values_in,
        (((0,), (0,)), ((), ())),
        precision=HIGHEST_PRECISION,
        preferred_element_type=jnp.float32,
    )


def exact_gelu(values_in):
    return jax.nn.gelu(values_in, approximate=False)


def block_size(row_count, shard_rows):
    shard_total = row_count // shard_rows
    return math.gcd(shard_total, max(1, 1024 // shard_rows)) * shard_rows


def on_device(
    hidden,
    latent_shape,
    cond_r,
    clip,
    cotangent,
    conv_weight,
    conv_bias,
    fc1_weight,
    fc1_bias,
    grn_gamma,
    grn_beta,
    fc2_weight,
    fc2_bias,
    time_weight,
    time_bias,
    map_weight,
    map_bias,
    query_weight,
    query_bias,
    key_weight,
    value_weight,
    value_bias,
    out_weight,
    out_bias,
):
    tok_rows = hidden.shape[0]
    positions = lax.axis_index("seq") * tok_rows + jnp.arange(tok_rows, dtype=jnp.int32)
    shape_row = latent_shape[0]
    segment, row_index, column, height, latent_width = latent_grid(positions, shape_row)
    margin = WMAX + 1
    gathered = (
        lax.all_gather(conv_weight, "seq", axis=1, tiled=True),
        lax.all_gather(conv_bias, "seq", axis=0, tiled=True),
        lax.all_gather(fc1_weight, "seq", axis=1, tiled=True),
        lax.all_gather(fc1_bias, "seq", axis=0, tiled=True),
        lax.all_gather(grn_gamma, "seq", axis=0, tiled=True),
        lax.all_gather(grn_beta, "seq", axis=0, tiled=True),
        lax.all_gather(fc2_weight, "seq", axis=1, tiled=True),
        lax.all_gather(fc2_bias, "seq", axis=0, tiled=True),
        lax.all_gather(time_weight, "seq", axis=1, tiled=True),
        lax.all_gather(time_bias, "seq", axis=0, tiled=True),
        lax.all_gather(map_weight, "seq", axis=1, tiled=True),
        lax.all_gather(map_bias, "seq", axis=0, tiled=True),
        lax.all_gather(query_weight, "seq", axis=1, tiled=True),
        lax.all_gather(query_bias, "seq", axis=0, tiled=True),
        lax.all_gather(key_weight, "seq", axis=1, tiled=True),
        lax.all_gather(value_weight, "seq", axis=1, tiled=True),
        lax.all_gather(value_bias, "seq", axis=0, tiled=True),
        lax.all_gather(out_weight, "seq", axis=1, tiled=True),
        lax.all_gather(out_bias, "seq", axis=0, tiled=True),
    )
    (
        kernel_full,
        kernel_bias,
        expand_full,
        expand_bias,
        gamma_full,
        beta_full,
        shrink_full,
        shrink_bias,
        time_full,
        time_bias_full,
        mapper_full,
        mapper_bias,
        query_full,
        query_bias_full,
        key_full,
        value_full,
        value_bias_full,
        output_full,
        output_bias_full,
    ) = gathered
    padded = padded_2(hidden, (("seq", 0),), margin)
    conv_out = jnp.broadcast_to(kernel_bias.astype(jnp.float32)[None, :], (tok_rows, C))
    tap_list = []
    for down_step in (-1, 0, 1):
        for side_step in (-1, 0, 1):
            tap_number = 3 * (down_step + 1) + (side_step + 1)
            valid = valid_tap(row_index, column, height, latent_width, down_step, side_step)
            offset_rows = down_step * latent_width + side_step
            nearby = lax.dynamic_slice_in_dim(padded, margin + offset_rows, tok_rows, 0).astype(
                jnp.float32
            )
            conv_out = (
                conv_out
                + kernel_full[tap_number].astype(jnp.float32)[None, :] * nearby * valid[:, None]
            )
            tap_list.append((tap_number, down_step, side_step, offset_rows, valid))
    normed_one, inverse_one = layer_stats(conv_out)
    normed_low = normed_one.astype(jnp.bfloat16)
    pre_act = jnp.dot(
        normed_low, expand_full, preferred_element_type=jnp.float32
    ) + expand_bias.astype(jnp.float32)
    activated, gelu_pull = jax.vjp(exact_gelu, pre_act)
    picked = (segment[:, None] == jnp.arange(NLAT, dtype=jnp.int32)[None, :]).astype(jnp.float32)
    energy = lax.psum(column_sum(picked, activated * activated), "seq")
    root = jnp.sqrt(energy + 1.0)
    denom = jnp.mean(root, axis=-1, keepdims=True) + EPS_NORM
    ratio = root / denom
    ratio_rows = jnp.dot(picked, ratio, precision=HIGHEST_PRECISION)
    gamma_value = gamma_full.astype(jnp.float32)
    response = gamma_value * (activated * ratio_rows) + beta_full.astype(jnp.float32) + activated
    response_low = response.astype(jnp.bfloat16)
    branch = jnp.dot(
        response_low, shrink_full, preferred_element_type=jnp.float32
    ) + shrink_bias.astype(jnp.float32)
    first_sum = hidden.astype(jnp.float32) + branch
    modulation = jnp.dot(
        cond_r, time_full.astype(jnp.float32), precision=HIGHEST_PRECISION
    ) + time_bias_full.astype(jnp.float32)
    mod_rows = jnp.dot(picked, modulation, precision=HIGHEST_PRECISION)
    scale_rows = 1.0 + mod_rows[:, :C]
    second_sum = first_sum * scale_rows + mod_rows[:, C:]
    normed_two, inverse_two = layer_stats(second_sum)
    attn_in = normed_two.astype(jnp.bfloat16)
    context_in = jax.nn.silu(clip.reshape(NLAT * NCTX, CLIP).astype(jnp.float32)).astype(
        jnp.bfloat16
    )
    context = (
        jnp.dot(context_in, mapper_full, preferred_element_type=jnp.float32)
        + mapper_bias.astype(jnp.float32)
    ).astype(jnp.bfloat16)
    queries = (
        jnp.dot(attn_in, query_full, preferred_element_type=jnp.float32)
        + query_bias_full.astype(jnp.float32)
    ).astype(jnp.bfloat16)
    keys_low = jnp.dot(attn_in, key_full, preferred_element_type=jnp.float32).astype(jnp.bfloat16)
    values_low = (
        jnp.dot(attn_in, value_full, preferred_element_type=jnp.float32)
        + value_bias_full.astype(jnp.float32)
    ).astype(jnp.bfloat16)
    context_keys = jnp.dot(context, key_full, preferred_element_type=jnp.float32).astype(
        jnp.bfloat16
    )
    context_values = (
        jnp.dot(context, value_full, preferred_element_type=jnp.float32)
        + value_bias_full.astype(jnp.float32)
    ).astype(jnp.bfloat16)
    query_heads = queries.reshape(tok_rows, HEADS, HEAD_DIM)
    key_heads = keys_low.reshape(tok_rows, HEADS, HEAD_DIM)
    value_heads = values_low.reshape(tok_rows, HEADS, HEAD_DIM)
    ctx_key_heads = context_keys.reshape(NLAT * NCTX, HEADS, HEAD_DIM)
    ctx_value_heads = context_values.reshape(NLAT * NCTX, HEADS, HEAD_DIM)
    context_segment = jnp.arange(NLAT * NCTX, dtype=jnp.int32) // NCTX
    ctx_admit = segment[:, None] == context_segment[None, :]

    def segments_at(first_row, length):
        return latent_grid(first_row + jnp.arange(length, dtype=jnp.int32), shape_row)[0]

    ctx_scores = (
        jnp.einsum("qhd,khd->hqk", query_heads, ctx_key_heads, preferred_element_type=jnp.float32)
        * SCORE_SCALE
    )
    ctx_scores = jnp.where(ctx_admit[None], ctx_scores, MASKED)
    start_max = jnp.max(ctx_scores, axis=-1)
    ctx_expo = jnp.exp(ctx_scores - start_max[..., None])
    start_total = jnp.sum(ctx_expo, axis=-1)
    start_accum = jnp.einsum(
        "hqk,khd->qhd",
        ctx_expo.astype(jnp.bfloat16),
        ctx_value_heads,
        preferred_element_type=jnp.float32,
    )
    key_part = lax.all_gather(keys_low, "seq", axis=0, tiled=True)
    value_part = lax.all_gather(values_low, "seq", axis=0, tiled=True)
    block_rows = block_size(key_part.shape[0], tok_rows)
    block_count = key_part.shape[0] // block_rows
    key_stack = key_part.reshape(block_count, block_rows, HEADS, HEAD_DIM)
    value_stack = value_part.reshape(block_count, block_rows, HEADS, HEAD_DIM)

    def attend_visit(state_now, element):
        key_block, value_block, block_index = element
        key_segment = segments_at(block_index * block_rows, block_rows)
        admitted = segment[:, None] == key_segment[None, :]
        scores = (
            jnp.einsum("qhd,khd->hqk", query_heads, key_block, preferred_element_type=jnp.float32)
            * SCORE_SCALE
        )
        scores = jnp.where(admitted[None], scores, MASKED)
        old_max, old_total, old_accum = state_now
        new_max = jnp.maximum(old_max, jnp.max(scores, axis=-1))
        factor = jnp.exp(old_max - new_max)
        expo_block = jnp.exp(scores - new_max[..., None])
        new_total = old_total * factor + jnp.sum(expo_block, axis=-1)
        new_accum = old_accum * factor.T[:, :, None] + jnp.einsum(
            "hqk,khd->qhd",
            expo_block.astype(jnp.bfloat16),
            value_block,
            preferred_element_type=jnp.float32,
        )
        return ((new_max, new_total, new_accum), None)

    state_end, ignored = lax.scan(
        attend_visit,
        (start_max, start_total, start_accum),
        (key_stack, value_stack, jnp.arange(block_count, dtype=jnp.int32)),
    )
    run_max, run_total, accum = state_end
    mixed = accum / run_total.T[:, :, None]
    log_total = run_max + jnp.log(run_total)
    mixed_low = mixed.reshape(tok_rows, C).astype(jnp.bfloat16)
    activations = (
        second_sum
        + jnp.dot(mixed_low, output_full, preferred_element_type=jnp.float32)
        + output_bias_full.astype(jnp.float32)
    ).astype(jnp.bfloat16)
    cot_value = cotangent.astype(jnp.float32)
    grad_out_w = outer_sum(mixed_low, cotangent)
    grad_out_b = jnp.sum(cot_value, axis=0)
    d_mixed_low = against(cotangent, output_full).astype(jnp.bfloat16)
    dmix_heads = d_mixed_low.reshape(tok_rows, HEADS, HEAD_DIM)
    delta = jnp.sum(dmix_heads.astype(jnp.float32) * mixed, axis=-1).T
    ctx_probs = jnp.exp(ctx_scores - log_total[..., None])
    ctx_dprob = jnp.einsum(
        "qhd,khd->hqk", dmix_heads, ctx_value_heads, preferred_element_type=jnp.float32
    )
    ctx_dscore = (ctx_probs * (ctx_dprob - delta[..., None])).astype(jnp.bfloat16)
    dquery_start = (
        jnp.einsum("hqk,khd->qhd", ctx_dscore, ctx_key_heads, preferred_element_type=jnp.float32)
        * SCORE_SCALE
    )
    ctx_dkey_part = (
        jnp.einsum("hqk,qhd->khd", ctx_dscore, query_heads, preferred_element_type=jnp.float32)
        * SCORE_SCALE
    )
    ctx_dvalue_part = jnp.einsum(
        "hqk,qhd->khd",
        ctx_probs.astype(jnp.bfloat16),
        dmix_heads,
        preferred_element_type=jnp.float32,
    )
    key_part = lax.all_gather(keys_low, "seq", axis=0, tiled=True)
    value_part = lax.all_gather(values_low, "seq", axis=0, tiled=True)
    query_block_rows = block_size(key_part.shape[0], tok_rows)
    block_count = key_part.shape[0] // query_block_rows
    key_stack = key_part.reshape(block_count, query_block_rows, HEADS, HEAD_DIM)
    value_stack = value_part.reshape(block_count, query_block_rows, HEADS, HEAD_DIM)

    def query_visit(state_now, element):
        key_block, value_block, block_index = element
        key_segment = segments_at(block_index * query_block_rows, query_block_rows)
        admitted = segment[:, None] == key_segment[None, :]
        scores = (
            jnp.einsum("qhd,khd->hqk", query_heads, key_block, preferred_element_type=jnp.float32)
            * SCORE_SCALE
        )
        scores = jnp.where(admitted[None], scores, MASKED)
        probs = jnp.exp(scores - log_total[..., None])
        dprob = jnp.einsum(
            "qhd,khd->hqk", dmix_heads, value_block, preferred_element_type=jnp.float32
        )
        dscore = (probs * (dprob - delta[..., None])).astype(jnp.bfloat16)
        added = (
            jnp.einsum("hqk,khd->qhd", dscore, key_block, preferred_element_type=jnp.float32)
            * SCORE_SCALE
        )
        return (state_now + added, None)

    state_end, ignored = lax.scan(
        query_visit,
        dquery_start,
        (key_stack, value_stack, jnp.arange(block_count, dtype=jnp.int32)),
    )
    dquery = state_end
    lse_all, delta_all = (
        lax.all_gather(log_total.T, "seq", axis=0, tiled=True),
        lax.all_gather(delta.T, "seq", axis=0, tiled=True),
    )
    zero_heads = jnp.zeros((tok_rows, HEADS, HEAD_DIM), jnp.float32)
    query_part = lax.all_gather(queries, "seq", axis=0, tiled=True)
    dmix_part = lax.all_gather(d_mixed_low, "seq", axis=0, tiled=True)
    row_count = query_part.shape[0]
    key_block_rows = block_size(row_count, tok_rows)
    block_count = row_count // key_block_rows
    query_stack = query_part.reshape(block_count, key_block_rows, HEADS, HEAD_DIM)
    dmix_stack = dmix_part.reshape(block_count, key_block_rows, HEADS, HEAD_DIM)
    lse_stack = lse_all.reshape(block_count, key_block_rows, HEADS)
    delta_stack = delta_all.reshape(block_count, key_block_rows, HEADS)

    def key_visit(state_now, element):
        query_block, dmix_block, lse_block, delta_block, block_index = element
        query_segment = segments_at(block_index * key_block_rows, key_block_rows)
        admitted = segment[:, None] == query_segment[None, :]
        scores = (
            jnp.einsum("khd,qhd->hkq", key_heads, query_block, preferred_element_type=jnp.float32)
            * SCORE_SCALE
        )
        scores = jnp.where(admitted[None], scores, MASKED)
        probs = jnp.exp(scores - lse_block.T[:, None, :])
        dkey_now, dvalue_now = state_now
        dvalue_now = dvalue_now + jnp.einsum(
            "hkq,qhd->khd",
            probs.astype(jnp.bfloat16),
            dmix_block,
            preferred_element_type=jnp.float32,
        )
        dprob = jnp.einsum(
            "khd,qhd->hkq", value_heads, dmix_block, preferred_element_type=jnp.float32
        )
        dscore = (probs * (dprob - delta_block.T[:, None, :])).astype(jnp.bfloat16)
        dkey_now = (
            dkey_now
            + jnp.einsum("hkq,qhd->khd", dscore, query_block, preferred_element_type=jnp.float32)
            * SCORE_SCALE
        )
        return ((dkey_now, dvalue_now), None)

    state_end, ignored = lax.scan(
        key_visit,
        (zero_heads, zero_heads),
        (query_stack, dmix_stack, lse_stack, delta_stack, jnp.arange(block_count, dtype=jnp.int32)),
    )
    dkey, dvalue = state_end
    dquery_low = dquery.reshape(tok_rows, C).astype(jnp.bfloat16)
    dkey_low = dkey.reshape(tok_rows, C).astype(jnp.bfloat16)
    dvalue_low = dvalue.reshape(tok_rows, C).astype(jnp.bfloat16)
    ctx_dkey_flat = ctx_dkey_part.reshape(NLAT * NCTX, C)
    ctx_dvalue_flat = ctx_dvalue_part.reshape(NLAT * NCTX, C)
    context_value = context.astype(jnp.float32)
    d_attn_in = (
        against(dquery_low, query_full)
        + against(dkey_low, key_full)
        + against(dvalue_low, value_full)
    )
    grad_query_w = outer_sum(attn_in, dquery_low)
    grad_query_b = jnp.sum(dquery_low.astype(jnp.float32), axis=0)
    grad_key_w = outer_sum(attn_in, dkey_low) + column_sum(context_value, ctx_dkey_flat)
    grad_value_w = outer_sum(attn_in, dvalue_low) + column_sum(context_value, ctx_dvalue_flat)
    grad_value_b = jnp.sum(dvalue_low.astype(jnp.float32), axis=0) + jnp.sum(
        ctx_dvalue_flat, axis=0
    )
    d_context = against_exact(ctx_dkey_flat, key_full.astype(jnp.float32)) + against_exact(
        ctx_dvalue_flat, value_full.astype(jnp.float32)
    )
    grad_map_w = column_sum(context_in.astype(jnp.float32), d_context)
    grad_map_b = jnp.sum(d_context, axis=0)
    d_second = cot_value + layer_back(d_attn_in, normed_two, inverse_two)
    d_first = d_second * scale_rows
    d_mod_rows = jnp.concatenate([d_second * first_sum, d_second], axis=1)
    d_modulation = column_sum(picked, d_mod_rows)
    grad_time_w = lax.dot_general(
        cond_r,
        d_modulation,
        (((0,), (0,)), ((), ())),
        precision=HIGHEST_PRECISION,
        preferred_element_type=jnp.float32,
    )
    grad_time_b = jnp.sum(d_modulation, axis=0)
    d_branch_low = d_first.astype(jnp.bfloat16)
    grad_shrink_w = outer_sum(response_low, d_branch_low)
    grad_shrink_b = jnp.sum(d_branch_low.astype(jnp.float32), axis=0)
    d_response = against(d_branch_low, shrink_full)
    grad_gamma = jnp.sum(d_response * activated * ratio_rows, axis=0)
    grad_beta = jnp.sum(d_response, axis=0)
    d_ratio = lax.psum(column_sum(picked, d_response * gamma_value * activated), "seq")
    d_root = d_ratio / denom - jnp.sum(d_ratio * root, axis=-1, keepdims=True) / (
        FF * denom * denom
    )
    d_act = d_response * (gamma_value * ratio_rows + 1.0) + activated * jnp.dot(
        picked, d_root / root, precision=HIGHEST_PRECISION
    )
    d_pre_low = gelu_pull(d_act)[0].astype(jnp.bfloat16)
    grad_expand_w = outer_sum(normed_low, d_pre_low)
    grad_expand_b = jnp.sum(d_pre_low.astype(jnp.float32), axis=0)
    d_normed = against(d_pre_low, expand_full)
    d_conv_low = layer_back(d_normed, normed_one, inverse_one).astype(jnp.bfloat16)
    d_conv = d_conv_low.astype(jnp.float32)
    grad_kernel_b = jnp.sum(d_conv, axis=0)
    d_padded = padded_2(d_conv_low, (("seq", 0),), margin)
    kernel_rows = []
    input_grad = d_first
    for tap_number, down_step, side_step, offset_rows, valid in tap_list:
        nearby = lax.dynamic_slice_in_dim(padded, margin + offset_rows, tok_rows, 0).astype(
            jnp.float32
        )
        kernel_rows.append(jnp.sum(d_conv * nearby * valid[:, None], axis=0))
        source = positions - offset_rows
        src_segment, src_row, src_column, src_height, src_width = latent_grid(source, shape_row)
        src_valid = valid_tap(src_row, src_column, src_height, src_width, down_step, side_step)
        behind = lax.dynamic_slice_in_dim(d_padded, margin - offset_rows, tok_rows, 0).astype(
            jnp.float32
        )
        input_grad = (
            input_grad
            + kernel_full[tap_number].astype(jnp.float32)[None, :] * behind * src_valid[:, None]
        )
    grad_kernel_w = jnp.stack(kernel_rows, axis=0)
    gradients = (
        grad_kernel_w,
        grad_kernel_b,
        grad_expand_w,
        grad_expand_b,
        grad_gamma,
        grad_beta,
        grad_shrink_w,
        grad_shrink_b,
        grad_time_w,
        grad_time_b,
        grad_map_w,
        grad_map_b,
        grad_query_w,
        grad_query_b,
        grad_key_w,
        grad_value_w,
        grad_value_b,
        grad_out_w,
        grad_out_b,
    )
    shares = (
        lax.psum_scatter(gradients[0], "seq", scatter_dimension=1, tiled=True),
        lax.psum_scatter(gradients[1], "seq", scatter_dimension=0, tiled=True),
        lax.psum_scatter(gradients[2], "seq", scatter_dimension=1, tiled=True),
        lax.psum_scatter(gradients[3], "seq", scatter_dimension=0, tiled=True),
        lax.psum_scatter(gradients[4], "seq", scatter_dimension=0, tiled=True),
        lax.psum_scatter(gradients[5], "seq", scatter_dimension=0, tiled=True),
        lax.psum_scatter(gradients[6], "seq", scatter_dimension=1, tiled=True),
        lax.psum_scatter(gradients[7], "seq", scatter_dimension=0, tiled=True),
        lax.psum_scatter(gradients[8], "seq", scatter_dimension=1, tiled=True),
        lax.psum_scatter(gradients[9], "seq", scatter_dimension=0, tiled=True),
        lax.psum_scatter(gradients[10], "seq", scatter_dimension=1, tiled=True),
        lax.psum_scatter(gradients[11], "seq", scatter_dimension=0, tiled=True),
        lax.psum_scatter(gradients[12], "seq", scatter_dimension=1, tiled=True),
        lax.psum_scatter(gradients[13], "seq", scatter_dimension=0, tiled=True),
        lax.psum_scatter(gradients[14], "seq", scatter_dimension=1, tiled=True),
        lax.psum_scatter(gradients[15], "seq", scatter_dimension=1, tiled=True),
        lax.psum_scatter(gradients[16], "seq", scatter_dimension=0, tiled=True),
        lax.psum_scatter(gradients[17], "seq", scatter_dimension=1, tiled=True),
        lax.psum_scatter(gradients[18], "seq", scatter_dimension=0, tiled=True),
    )
    summed = (
        lax.psum(shares[0].astype(jnp.bfloat16), "grp").astype(jnp.float32),
        lax.psum(shares[1].astype(jnp.bfloat16), "grp").astype(jnp.float32),
        lax.psum(shares[2].astype(jnp.bfloat16), "grp").astype(jnp.float32),
        lax.psum(shares[3].astype(jnp.bfloat16), "grp").astype(jnp.float32),
        lax.psum(shares[4].astype(jnp.bfloat16), "grp").astype(jnp.float32),
        lax.psum(shares[5].astype(jnp.bfloat16), "grp").astype(jnp.float32),
        lax.psum(shares[6].astype(jnp.bfloat16), "grp").astype(jnp.float32),
        lax.psum(shares[7].astype(jnp.bfloat16), "grp").astype(jnp.float32),
        lax.psum(shares[8].astype(jnp.bfloat16), "grp").astype(jnp.float32),
        lax.psum(shares[9].astype(jnp.bfloat16), "grp").astype(jnp.float32),
        lax.psum(shares[10].astype(jnp.bfloat16), "grp").astype(jnp.float32),
        lax.psum(shares[11].astype(jnp.bfloat16), "grp").astype(jnp.float32),
        lax.psum(shares[12].astype(jnp.bfloat16), "grp").astype(jnp.float32),
        lax.psum(shares[13].astype(jnp.bfloat16), "grp").astype(jnp.float32),
        lax.psum(shares[14].astype(jnp.bfloat16), "grp").astype(jnp.float32),
        lax.psum(shares[15].astype(jnp.bfloat16), "grp").astype(jnp.float32),
        lax.psum(shares[16].astype(jnp.bfloat16), "grp").astype(jnp.float32),
        lax.psum(shares[17].astype(jnp.bfloat16), "grp").astype(jnp.float32),
        lax.psum(shares[18].astype(jnp.bfloat16), "grp").astype(jnp.float32),
    )
    return (
        activations,
        input_grad,
        summed[0],
        summed[1],
        summed[2],
        summed[3],
        summed[4],
        summed[5],
        summed[6],
        summed[7],
        summed[8],
        summed[9],
        summed[10],
        summed[11],
        summed[12],
        summed[13],
        summed[14],
        summed[15],
        summed[16],
        summed[17],
        summed[18],
    )


def mm(left, right):
    return jnp.dot(left, right, preferred_element_type=jnp.float32)


MESH_ID = pl.DeviceIdType.MESH


def dot_nt(left, right):
    return lax.dot_general(
        left, right, (((1,), (1,)), ((), ())), preferred_element_type=jnp.float32
    )


def place():
    me = lax.axis_index("seq")
    z, y = me // 2, lax.rem(me, 2)
    return me, z, y, me + 1 - 2 * y


def seq_copy(src, dst, send, recv, target):
    return pltpu.make_async_remote_copy(
        src_ref=src,
        dst_ref=dst,
        send_sem=send,
        recv_sem=recv,
        device_id={"seq": target},
        device_id_type=MESH_ID,
    )


def dot_tn(left, right):
    return lax.dot_general(
        left, right, (((0,), (0,)), ((), ())), preferred_element_type=jnp.float32
    )


def grp_copy(src, dst, send, recv, target):
    return pltpu.make_async_remote_copy(
        src_ref=src,
        dst_ref=dst,
        send_sem=send,
        recv_sem=recv,
        device_id={"grp": target},
        device_id_type=MESH_ID,
    )


def group_place():
    group = lax.axis_index("grp")
    core = lax.rem(group, 2)
    return group // 2, core, group + 1 - 2 * core, lax.rem(group + 2, 4)


def meet_all(shards, groups=0):
    me = lax.axis_index("seq")
    barrier = pltpu.get_barrier_semaphore()
    for step in range(1, groups):
        pl.semaphore_signal(
            barrier,
            inc=1,
            device_id={"grp": lax.rem(lax.axis_index("grp") + step, groups)},
            device_id_type=MESH_ID,
        )
    for step in range(1, shards):
        pl.semaphore_signal(
            barrier,
            inc=1,
            device_id={"seq": lax.rem(me + step, shards)},
            device_id_type=MESH_ID,
        )
    pl.semaphore_wait(barrier, shards - 1 + max(groups - 1, 0))


def tile_loop(count, body):
    def step(index, carry):
        body(index)
        return carry

    lax.fori_loop(0, count, step, 0)


def add_rows(target, target_row, left, left_row, right, count):
    def tile(index):
        low = index * 32
        here = pl.ds(pl.multiple_of(target_row + low, 32), 32)
        there = pl.ds(pl.multiple_of(left_row + low, 32), 32)
        value = left[there, :].astype(jnp.float32) + right[
            pl.ds(pl.multiple_of(low, 32), 32), :
        ].astype(jnp.float32)
        target[here, :] = value.astype(target.dtype)

    tile_loop(count // 32, tile)


class PairSum:
    def __init__(self, own, got, other, out, sems):
        x, core, self.core_peer, self.x_peer = group_place()
        self.half = own.shape[0] // 2
        self.own, self.got, self.other, self.out = own, got, other, out
        self.low = pl.multiple_of(core * self.half, self.half)
        mine = pl.ds(self.low, self.half)
        theirs = pl.ds(pl.multiple_of((1 - core) * self.half, self.half), self.half)
        pair = lambda k: (sems.at[0, k], sems.at[1, k])
        self.copies = (
            grp_copy(own.at[theirs], got, *pair(0), self.core_peer),
            grp_copy(own.at[mine], other, *pair(1), self.x_peer),
            grp_copy(out.at[mine], out.at[mine], *pair(2), self.core_peer),
        )

    def begin(self):
        self.copies[0].start()

    def across(self):
        self.copies[0].wait_recv()
        add_rows(self.own, self.low, self.own, self.low, self.got, self.half)
        self.copies[1].start()

    def share(self):
        self.copies[1].wait_recv()
        add_rows(self.out, self.low, self.own, self.low, self.other, self.half)
        self.copies[2].start()

    def finish(self):
        self.copies[2].wait_recv()
        for copy in self.copies:
            copy.wait_send()


class QuarterSum:
    def __init__(self, shards, own, got, other, out, sems):
        x, core, core_peer, x_peer = group_place()
        me = lax.axis_index("seq")
        units, width = own.shape[2], own.shape[3]
        self.own, self.got, self.other, self.out = own, got, other, out
        self.core, self.shards = core, shards
        self.mine = x * 2 + core
        pair = lambda k: (sems.at[0, k], sems.at[1, k])

        def rows(quarter):
            return pl.ds(pl.multiple_of(quarter * units, units), units)

        self.block = (rows(self.mine), pl.ds(pl.multiple_of(me * width, 128), width))
        self.me = me
        self.first = [
            grp_copy(own.at[:, side * 2 + 1 - core], got.at[side], *pair(side), core_peer)
            for side in (0, 1)
        ]
        self.second = grp_copy(own.at[:, (1 - x) * 2 + core], other, *pair(2), x_peer)
        self.third = []
        for step in range(1, shards):
            goal = lax.rem(me + step, shards)
            self.third.append(
                seq_copy(own.at[goal, self.mine], out.at[self.block], *pair(2 + step), goal)
            )
        base = 2 + shards
        whole = out.at[rows(self.mine)]
        self.fourth = grp_copy(whole, whole, *pair(base), x_peer)
        self.fifth = []
        for side in (0, 1):
            whole = out.at[rows(side * 2 + core)]
            self.fifth.append(grp_copy(whole, whole, *pair(base + 1 + side), core_peer))

    def add(self, quarter, right):
        def tile(index):
            self.own[index, quarter] = (
                self.own[index, quarter].astype(jnp.float32) + right(index).astype(jnp.float32)
            ).astype(self.own.dtype)

        tile_loop(self.shards, tile)

    def begin(self):
        for copy in self.first:
            copy.start()

    def across(self):
        for copy in self.first:
            copy.wait_recv()
        for side in (0, 1):
            self.add(side * 2 + self.core, lambda index, side=side: self.got[side, index])
        self.second.start()

    def spread(self):
        self.second.wait_recv()
        self.add(self.mine, lambda index: self.other[index])
        for copy in self.third:
            copy.start()
        self.out[self.block] = self.own[self.me, self.mine]

    def share(self):
        for copy in self.third:
            copy.wait_recv()
        self.fourth.start()

    def share_core(self):
        self.fourth.wait_recv()
        for copy in self.fifth:
            copy.start()

    def finish(self):
        for copy in self.fifth:
            copy.wait_recv()
        for copy in (*self.first, self.second, *self.third, self.fourth, *self.fifth):
            copy.wait_send()


def in_line(direction, z, hops, depth):
    return z >= hops if direction == 0 else z + hops < depth


class Gather:
    def __init__(self, full, sems, depth):
        self.full, self.depth = full, depth
        self.sems = [sems.at[k] for k in range(4)]
        self.me, self.z, self.y, self.other = place()

    def origin(self, direction, hops, far):
        column = 1 - self.y if far else self.y
        return (self.z - hops if direction == 0 else self.z + hops) * 2 + column

    def z_copy(self, direction, hops):
        block = self.full.at[self.origin(direction, hops, False)]
        send, recv = self.sems[0], self.sems[1]
        target = self.me + 2 if direction == 0 else self.me - 2
        return seq_copy(
            block, block, send.at[direction, hops], recv.at[direction, hops + 1], target
        )

    def z_arrival(self, direction, hops):
        block = self.full.at[self.origin(direction, hops, False)]
        send, recv = self.sems[0], self.sems[1]
        return seq_copy(
            block, block, send.at[direction, hops], recv.at[direction, hops], self.other
        )

    def y_copy(self, direction, hops, arrival=False):
        block = self.full.at[self.origin(direction, hops, arrival)]
        send, recv = self.sems[2], self.sems[3]
        return seq_copy(
            block, block, send.at[direction, hops], recv.at[direction, hops], self.other
        )

    def here(self, direction, hops):
        return in_line(direction, self.z, hops, self.depth)

    def onward(self, direction):
        return self.z < self.depth - 1 if direction == 0 else self.z > 0

    def start(self):
        for direction in (0, 1):

            @pl.when(self.onward(direction))
            def _():
                self.z_copy(direction, 0).start()

        self.y_copy(0, 0).start()

    def hop(self, hops):
        for direction in (0, 1):

            @pl.when((hops < self.depth) & self.here(direction, hops))
            def _():
                self.z_arrival(direction, hops).wait_recv()

                @pl.when(self.onward(direction))
                def _():
                    self.z_copy(direction, hops).start()

                self.y_copy(direction, hops).start()

    def near(self, hops, visit):
        for direction in (0, 1):

            @pl.when((hops < self.depth) & self.here(direction, hops))
            def _():
                visit(self.origin(direction, hops, False))

    def far(self, hops, visit):
        for direction in (0, 1):
            here = self.here(direction, hops)
            if direction == 1:
                here = here & (hops > 0)

            @pl.when(here)
            def _():
                self.y_copy(direction, hops, True).wait_recv()
                visit(self.origin(direction, hops, True))

    def drain(self):
        def step(hops, carry):
            for direction in (0, 1):
                here = self.here(direction, hops)

                @pl.when(here & self.onward(direction))
                def _():
                    self.z_copy(direction, hops).wait_send()

                if direction == 1:
                    here = here & (hops > 0)

                @pl.when(here)
                def _():
                    self.y_copy(direction, hops).wait_send()

            return carry

        lax.fori_loop(0, self.depth, step, 0)

    def finish(self):
        tile_loop(self.depth, lambda hops: self.far(hops, lambda block: None))
        self.drain()

    def run(self, visit, hook=None):
        self.start()
        visit(self.me)

        def step(hops, carry):
            self.hop(hops)
            self.near(hops, visit)
            self.far(hops - 1, visit)
            if hook is not None:
                hook(hops)
            return carry

        lax.fori_loop(1, self.depth + 1, step, 0)
        self.drain()


class Reshard:
    def __init__(self, shards, part, out, local_sem, sems):
        x, core, core_peer, x_peer = group_place()
        me = lax.axis_index("seq")
        mine = x * 2 + core
        pair = lambda k: (sems.at[0, k], sems.at[1, k])
        self.local = pltpu.make_async_copy(part(me, mine), out.at[me, mine], local_sem)
        self.first = []
        for step in range(1, shards):
            goal = lax.rem(me + step, shards)
            self.first.append(seq_copy(part(goal, mine), out.at[me, mine], *pair(step - 1), goal))
        self.second = grp_copy(out.at[:, mine], out.at[:, mine], *pair(shards - 1), x_peer)
        self.third = []
        for side in (0, 1):
            whole = out.at[:, side * 2 + core]
            self.third.append(grp_copy(whole, whole, *pair(shards + side), core_peer))

    def begin(self):
        self.local.start()
        for copy in self.first:
            copy.start()

    def share(self):
        self.local.wait()
        for copy in self.first:
            copy.wait_recv()
        self.second.start()

    def share_core(self):
        self.second.wait_recv()
        for copy in self.third:
            copy.start()

    def finish(self):
        for copy in self.third:
            copy.wait_recv()
        for copy in (*self.first, self.second, *self.third):
            copy.wait_send()


def side_by_side(target, row, parts, count):
    for pair in range(count // 2):
        value = jnp.concatenate([parts(2 * pair), parts(2 * pair + 1)], axis=1)
        rows, cols = value.shape
        target[row : row + rows, pair * cols : (pair + 1) * cols] = value


def scatter_blocks(
    partial, to_y, from_y, to_z, from_z, acc, y_sems, z_sems, depth, between=None, hook=None
):
    me, z, y, other = place()
    low = to_y.dtype

    def y_copy(goal):
        return seq_copy(
            to_y.at[goal], from_y.at[goal], y_sems.at[0, goal], y_sems.at[1, goal], other
        )

    def z_copy(direction, goal):
        return seq_copy(
            to_z.at[goal],
            from_z.at[direction, goal],
            z_sems.at[0, direction, goal],
            z_sems.at[1, direction, goal],
            me + 2 if direction == 0 else me - 2,
        )

    def z_arrival(direction, goal):
        return seq_copy(
            to_z.at[goal],
            from_z.at[direction, goal],
            z_sems.at[0, direction, goal],
            z_sems.at[1, direction, goal],
            other,
        )

    def ahead(direction, hops):
        return in_line(1 - direction, z, hops, depth)

    def goal_of(direction, hops):
        return z + hops if direction == 0 else z - hops

    def over_y(step, carry):
        hops = depth - 1 - step
        for direction in (0, 1):
            here = ahead(direction, hops)
            if direction == 1:
                here = here & (hops > 0)

            @pl.when(here)
            def _():
                goal = goal_of(direction, hops)
                to_y[goal] = partial(goal * 2 + other - z * 2).astype(low)
                y_copy(goal).start()

        return carry

    lax.fori_loop(0, depth, over_y, 0)
    if between is not None:
        between()

    def along_z(step, carry):
        hops = depth - 1 - step
        for direction in (0, 1):

            @pl.when(ahead(direction, hops))
            def _():
                goal = goal_of(direction, hops)
                acc[...] = partial(goal * 2 + y)
                y_copy(goal).wait_recv()
                acc[...] += from_y[goal].astype(jnp.float32)

                @pl.when(in_line(direction, z, 1, depth))
                def _():
                    z_arrival(direction, goal).wait_recv()
                    acc[...] += from_z[direction, goal].astype(jnp.float32)

                to_z[goal] = acc[...].astype(low)
                z_copy(direction, goal).start()

        if hook is not None:
            hook(step)
        return carry

    lax.fori_loop(0, depth - 1, along_z, 0)
    acc[...] = partial(me)
    y_copy(z).wait_recv()
    acc[...] += from_y[z].astype(jnp.float32)
    for direction in (0, 1):

        @pl.when(in_line(direction, z, 1, depth))
        def _():
            z_arrival(direction, z).wait_recv()
            acc[...] += from_z[direction, z].astype(jnp.float32)

    def drain(goal, carry):
        y_copy(goal).wait_send()
        for direction in (0, 1):
            sent = goal > z if direction == 0 else goal < z

            @pl.when(sent)
            def _():
                z_copy(direction, goal).wait_send()

        return carry

    lax.fori_loop(0, depth, drain, 0)


def peer_total(mine, theirs, sems, shards, meanwhile=None):
    me = lax.axis_index("seq")
    copies = [
        seq_copy(
            mine,
            theirs.at[step - 1],
            sems.at[0, step - 1],
            sems.at[1, step - 1],
            lax.rem(me + step, shards),
        )
        for step in range(1, shards)
    ]
    for copy in copies:
        copy.start()
    if meanwhile is not None:
        meanwhile()
    for copy in copies:
        copy.wait()
    total = mine[...]
    for step in range(1, shards):
        total = total + theirs[step - 1]
    return total


EDGE = 80
VMEM_BYTES = 56 * 1024 * 1024
ROOT_HALF = math.sqrt(0.5)
DENSITY = 1.0 / math.sqrt(2.0 * math.pi)


def exchange_edges(held, sems, rows, shards):
    me = lax.axis_index("seq")

    def copy(kind):
        if kind == 0:
            source, target = pl.ds(EDGE + rows - WMAX, WMAX), pl.ds(EDGE - WMAX, WMAX)
        else:
            source, target = pl.ds(EDGE, WMAX), pl.ds(EDGE + rows, WMAX)
        return seq_copy(
            held.at[source],
            held.at[target],
            sems.at[0, kind],
            sems.at[1, kind],
            me + 1 if kind == 0 else me - 1,
        )

    first, last = me == 0, me == shards - 1
    zeros = jnp.zeros((EDGE, held.shape[1]), held.dtype)

    held[pl.ds(0, EDGE - WMAX), :] = zeros[: EDGE - WMAX]
    held[pl.ds(EDGE + rows + WMAX, EDGE - WMAX), :] = zeros[: EDGE - WMAX]

    @pl.when(first)
    def _():
        held[pl.ds(EDGE - WMAX, WMAX), :] = zeros[:WMAX]

    @pl.when(last)
    def _():
        held[pl.ds(EDGE + rows, WMAX), :] = zeros[:WMAX]

    @pl.when(jnp.logical_not(last))
    def _():
        copy(0).start()

    @pl.when(jnp.logical_not(first))
    def _():
        copy(1).start()

    def finish():
        @pl.when(jnp.logical_not(last))
        def _():
            copy(0).wait_send()
            copy(1).wait_recv()

        @pl.when(jnp.logical_not(first))
        def _():
            copy(1).wait_send()
            copy(0).wait_recv()

    return finish


VEC_STEP = 256
VEC_TAIL = 8 * VEC_STEP


def column_of(row):
    return jnp.broadcast_to(row, (8, row.shape[1])).T[:, 0:1]


def stats_of(values_in):
    average = jnp.mean(values_in, axis=-1, keepdims=True)
    centred = values_in - average
    variance = jnp.mean(centred * centred, axis=-1, keepdims=True)
    inverse = lax.rsqrt(variance + EPS_NORM)
    return centred * inverse, inverse


class Latents:
    def __init__(self, shape, total):
        self.ends = []
        low = 0
        for latent in range(NLAT - 1):
            low = low + shape[latent, 0] * WMAX
            self.ends.append(low)
        self.total = total

    def segment(self, positions):
        out = jnp.zeros_like(positions)
        for end in self.ends:
            out = out + (positions >= end).astype(jnp.int32)
        return out

    def picks(self, start, count):
        segment = self.segment(start + lax.broadcasted_iota(jnp.int32, (count, 1), 0))
        return [(segment == latent).astype(jnp.float32) for latent in range(NLAT)]

    def valid(self, positions, down_step, side_step):
        segment = self.segment(positions)
        low, high = jnp.zeros_like(positions), jnp.full_like(positions, self.total)
        for latent, end in enumerate(self.ends):
            low = jnp.where(segment > latent, end, low)
            high = jnp.where(segment == latent, end, high)
        moved = positions + down_step * WMAX
        column = (positions & (WMAX - 1)) + side_step
        good = (moved >= low) & (moved < high) & (column >= 0) & (column < WMAX)
        return good.astype(jnp.float32)


def rows_of(picks, table):
    out = picks[0] * table[0:1]
    for latent in range(1, NLAT):
        out = out + picks[latent] * table[latent : latent + 1]
    return out


WIDE_SCALE, WIDE_SHIFT = 16, 24
SMALL_FC1, SMALL_GAMMA, SMALL_BETA, SMALL_TIME = 64, 66, 68, 70
SMALL_QUERY, SMALL_VALUE, SMALL_OUT, SMALL_MAP, SMALL_ROWS = 71, 72, 73, 74, 80


def mixer_kernel(
    shards,
    shape,
    hidden,
    cond,
    time_weight,
    conv_weight,
    vec,
    fc1,
    ctx_cols,
    cot,
    fc2,
    out_weight,
    full,
    held,
    wide,
    normed,
    inverse,
    pre,
    root_out,
    ratio_out,
    denom_out,
    response,
    ctx_full,
    cot_full,
    fc2_rows,
    out_rows,
    pack,
    packed,
    floats,
    conv,
    act,
    energy,
    mine,
    theirs,
    edge_sems,
    pack_sems,
    gather_sems,
    total_sems,
    ctx_sems,
    cot_sems,
    out_parts,
    local_sems,
    fc2_sems,
    out_sems,
):
    f32 = jnp.float32
    rows = hidden.shape[0]
    depth = shards // 2
    me = lax.axis_index("seq")
    meet_all(shards, lax.axis_size("grp"))
    units, width = fc2_rows.shape[2:]
    out_units = out_parts.shape[2]

    def fc2_part(goal, quarter):
        here = pl.ds(pl.multiple_of(quarter * units, units), units)
        return fc2.at[here, pl.ds(pl.multiple_of(goal * width, 128), width)]

    def out_part(goal, quarter):
        low = (goal * 4 + quarter) * out_units
        return out_weight.at[pl.ds(pl.multiple_of(low, out_units), out_units)]

    fc2_shard = Reshard(shards, fc2_part, fc2_rows, local_sems.at[0], fc2_sems)
    out_shard = Reshard(shards, out_part, out_parts, local_sems.at[1], out_sems)
    ctx_gather = Gather(ctx_full, ctx_sems, depth)
    cot_gather = Gather(cot_full, cot_sems, depth)
    ctx_full[me] = ctx_cols[...]
    cot_full[me] = cot[...]
    latents = Latents(shape, shards * rows)
    cols = pack.shape[1]
    width_one = fc1.shape[1]
    fc1_bias, gamma, beta = (vec[:, n * width_one : (n + 1) * width_one] for n in range(3))
    vec_at = lambda n: vec[:, 3 * width_one + n * VEC_STEP : 3 * width_one + n * VEC_STEP + cols]
    time_bias = vec[:, 3 * width_one + 6 * VEC_STEP : 3 * width_one + 6 * VEC_STEP + 2 * cols]
    mod = (
        jnp.dot(
            cond[...],
            time_weight[...].astype(f32),
            precision=HIGHEST_PRECISION,
            preferred_element_type=f32,
        )
        + time_bias
    )
    pack[...] = jnp.zeros_like(pack)
    pack[0:9, :] = conv_weight[...].astype(f32)
    pack[9:10, :] = vec_at(0)
    pack[10:11, :] = vec_at(1)
    pack[11 : 11 + NLAT, :] = mod[:, :cols]
    pack[11 + NLAT : 11 + 2 * NLAT, :] = mod[:, cols:]
    packed[me] = pack[...]
    pack_copies = [
        seq_copy(
            pack,
            packed.at[me],
            pack_sems.at[0, step - 1],
            pack_sems.at[1, step - 1],
            lax.rem(me + step, shards),
        )
        for step in range(1, shards)
    ]
    held[pl.ds(EDGE, rows), :] = hidden[...]
    finish = exchange_edges(held, edge_sems, rows, shards)
    for copy in pack_copies:
        copy.start()
    finish()
    fc2_shard.begin()
    out_shard.begin()
    ctx_gather.start()
    cot_gather.start()
    tile_loop(
        floats.shape[0] // 32,
        lambda i: floats.__setitem__(
            (pl.ds(i * 32, 32), slice(None)), held[pl.ds(i * 32, 32), :].astype(f32)
        ),
    )
    for copy in pack_copies:
        copy.wait()
    wide[...] = jnp.zeros_like(wide)
    wide[0:16, :] = jnp.concatenate([packed[j, 0:16, :] for j in range(shards)], axis=1)
    for low, device in ((WIDE_SCALE, 0), (WIDE_SHIFT, shards // 2)):
        parts = []
        for j in range(device, device + shards // 2):
            parts.append(packed[j, 11 : 11 + NLAT, :])
            parts.append(packed[j, 11 + NLAT : 11 + 2 * NLAT, :])
        wide[low : low + NLAT, :] = jnp.concatenate(parts, axis=1)
    positions = me * rows + lax.broadcasted_iota(jnp.int32, (rows, 1), 0)
    masks = [latents.valid(positions, tap // 3 - 1, tap % 3 - 1) for tap in range(9)]

    def conv_tile(index):
        cols = pl.ds(pl.multiple_of(index * 256, 256), 256)
        total = jnp.broadcast_to(wide[9:10, cols], (rows, 256))
        for tap in range(9):
            offset = EDGE + (tap // 3 - 1) * WMAX + tap % 3 - 1
            total = total + (
                floats[offset : offset + rows, cols] * wide[tap : tap + 1, cols]
            ) * masks[tap]
        conv[:, cols] = total

    tile_loop(C // 256, conv_tile)

    def norm_tile(index):
        here = pl.ds(pl.multiple_of(index * 16, 16), 16)
        values, factor = stats_of(conv[here, :])
        normed[here, :] = values
        inverse[here, :] = factor
        full[me, here, :] = values.astype(full.dtype)

    tile_loop(rows // 16, norm_tile)
    energy[...] = jnp.zeros_like(energy)

    def visit(block):
        pre[block] = (
            jnp.dot(full[block], fc1[...], preferred_element_type=f32) + fc1_bias
        )

        def tile(index):
            here = pl.ds(pl.multiple_of(index * 32, 32), 32)
            value = pre[block, here, :]
            value = value * (0.5 * (1.0 + lax.erf(value * ROOT_HALF)))
            act[block, here, :] = value
            square = value * value
            pick = latents.picks(block * rows + index * 32, 32)
            for latent in range(NLAT):
                energy[latent : latent + 1, :] += jnp.sum(
                    square * pick[latent], axis=0, keepdims=True
                )

        tile_loop(rows // 32, tile)

    def hook(hops):
        @pl.when(hops == 1)
        def _():
            ctx_gather.hop(1)

        @pl.when(hops == 2)
        def _():
            fc2_shard.share()
            out_shard.share()
            ctx_gather.hop(2)
            cot_gather.hop(1)

        @pl.when(hops == 3)
        def _():
            ctx_gather.hop(3)

    Gather(full, gather_sems, depth).run(visit, hook)
    cot_gather.hop(2)
    fc2_shard.share_core()
    out_shard.share_core()
    root = jnp.sqrt(energy[...] + 1.0)
    mine[...] = jnp.broadcast_to(jnp.sum(root, axis=1, keepdims=True), mine.shape)
    denom = peer_total(mine, theirs, total_sems, shards) / FF + EPS_NORM
    ratio = root / denom[:, 0:1]
    cot_gather.hop(3)
    root_out[...] = root
    denom_out[...] = denom
    ratio_out[...] = ratio
    scaled = ratio * gamma + 1.0

    def respond(index):
        block = index // (rows // 32)
        here = pl.ds(pl.multiple_of(lax.rem(index, rows // 32) * 32, 32), 32)
        response[block, here, :] = (
            act[block, here, :] * rows_of(latents.picks(index * 32, 32), scaled) + beta
        ).astype(response.dtype)

    tile_loop(shards * rows // 32, respond)
    ctx_gather.finish()
    fc2_shard.finish()
    out_shard.finish()
    for quarter in range(4):
        side_by_side(
            out_rows, quarter * out_units, lambda j, quarter=quarter: out_parts[j, quarter], shards
        )
    cot_gather.finish()


def mixed_in_kernel(
    shards,
    shape,
    response,
    fc2,
    hidden,
    wide,
    w_qkv,
    vec,
    context,
    full,
    first,
    second,
    normed,
    inverse,
    queries,
    keys,
    values,
    acc,
    to_y,
    from_y,
    to_z,
    from_z,
    y_sems,
    z_sems,
    gather_sems,
):
    f32 = jnp.float32
    rows = hidden.shape[0]
    depth = shards // 2
    me = lax.axis_index("seq")
    meet_all(shards)
    latents = Latents(shape, shards * rows)
    cols = keys.shape[0]
    base = vec.shape[1] - VEC_TAIL
    q_bias = vec[:, base + 2 * VEC_STEP : base + 2 * VEC_STEP + cols]
    v_bias = column_of(vec[:, base + 3 * VEC_STEP : base + 4 * VEC_STEP])[:cols]
    bias = wide[10:11, :]
    scale, shift = wide[WIDE_SCALE : WIDE_SCALE + 8, :], wide[WIDE_SHIFT : WIDE_SHIFT + 8, :]

    def partial(block):
        return dot_nt(response[block], fc2[...])

    scatter_blocks(partial, to_y, from_y, to_z, from_z, acc, y_sems, z_sems, depth)

    def norm_tile(index):
        here = pl.ds(pl.multiple_of(index * 16, 16), 16)
        one = hidden[here, :].astype(f32) + acc[here, :] + bias
        pick = latents.picks(me * rows + index * 16, 16)
        two = one * (1.0 + rows_of(pick, scale)) + rows_of(pick, shift)
        first[here, :] = one
        second[here, :] = two
        value, factor = stats_of(two)
        normed[here, :] = value
        inverse[here, :] = factor
        full[me, here, :] = value.astype(full.dtype)

    tile_loop(rows // 16, norm_tile)

    side = jnp.dot(w_qkv[cols:, :], context[...], preferred_element_type=f32)
    keys[:, shards * rows :] = side[:cols].astype(keys.dtype)
    values[:, shards * rows :] = (side[cols:] + v_bias).astype(values.dtype)

    def visit(block):
        value = full[block]
        query = dot_nt(value, w_qkv[:cols, :]) + q_bias
        queries[block] = query.astype(queries.dtype)
        here = pl.ds(pl.multiple_of(block * rows, 128), rows)
        side = dot_nt(w_qkv[cols:, :], value)
        keys[:, here] = side[:cols].astype(keys.dtype)
        values[:, here] = (side[cols:] + v_bias).astype(values.dtype)

    Gather(full, gather_sems, depth).run(visit)


def attend_kernel(
    shards,
    shape,
    queries,
    keys,
    values,
    cot,
    out_rows,
    d_qkv,
    mixed,
    cot_cols,
    dk_sum,
    dv_sum,
    probs_at,
    sems,
):
    f32, bf16 = jnp.float32, jnp.bfloat16
    cols = keys.shape[0]
    heads = cols // HEAD_DIM
    tiles, tile_rows = mixed.shape[0], mixed.shape[3]
    span = tile_rows // queries.shape[1]
    depth = shards // 2
    me = lax.axis_index("seq")
    meet_all(shards)
    latents = Latents(shape, tiles * tile_rows)
    place_at = lax.broadcasted_iota(jnp.int32, (1, keys.shape[1]), 1)
    token = place_at - tiles * tile_rows
    of_token = jnp.full_like(token, -1)
    for latent in range(NLAT):
        inside = (token >= latent * NCTX) & (token < (latent + 1) * NCTX)
        of_token = jnp.where(inside, latent, of_token)
    k_segment = jnp.where(token < 0, latents.segment(place_at), of_token)
    dk_sum[...] = jnp.zeros_like(dk_sum)
    dv_sum[...] = jnp.zeros_like(dv_sum)

    def gather_of(tile):
        return Gather(mixed.at[tile], sems.at[tile], depth)

    def step(tile, carry):
        blocks = pl.ds(tile * span, span)
        here = pl.ds(pl.multiple_of(tile * tile_rows, 128), tile_rows)
        query = queries[blocks].reshape(tile_rows, cols) * SCORE_SCALE
        cot_tile = cot[blocks].reshape(tile_rows, C)
        for j in range(shards):

            @pl.when(me == j)
            def _():
                cot_cols[:, here] = cot_tile[:, j * cols : (j + 1) * cols].T

        d_mixed = dot_nt(cot_tile, out_rows[...]).astype(bf16)
        q_segment = latents.segment(
            tile * tile_rows + lax.broadcasted_iota(jnp.int32, (tile_rows, 1), 0)
        )
        bias = jnp.where(q_segment == k_segment, 0.0, MASKED)
        mixed_parts, d_query_parts = [], []
        for head in range(heads):
            own = slice(head * HEAD_DIM, (head + 1) * HEAD_DIM)
            scores = jnp.dot(query[:, own], keys[own, :], preferred_element_type=f32) + bias
            expo = jnp.exp(scores - jnp.max(scores, axis=-1, keepdims=True))
            probs_at[head] = expo * (1.0 / jnp.sum(expo, axis=-1, keepdims=True))
            mixed_parts.append(dot_nt(probs_at[head].astype(bf16), values[own, :]))
        mixed[tile, me] = jnp.concatenate(mixed_parts, axis=1).T.astype(bf16)
        gather_of(tile).start()
        for hops in range(1, depth):

            @pl.when(tile >= hops)
            def _():
                gather_of(tile - hops).hop(hops)

        for head in range(heads):
            own = slice(head * HEAD_DIM, (head + 1) * HEAD_DIM)
            dm_head = d_mixed[:, own]
            delta = jnp.sum(dm_head.astype(f32) * mixed_parts[head], axis=-1, keepdims=True)
            d_probs = jnp.dot(dm_head, values[own, :], preferred_element_type=f32)
            d_scores = (probs_at[head] * (d_probs - delta)).astype(bf16)
            d_query_parts.append(dot_nt(d_scores, keys[own, :]) * SCORE_SCALE)
            dk_sum[own, :] += dot_tn(query[:, own], d_scores)
            dv_sum[own, :] += dot_tn(dm_head, probs_at[head].astype(bf16))
        d_qkv[:cols, here] = jnp.concatenate(d_query_parts, axis=1).T.astype(bf16)
        return carry

    lax.fori_loop(0, tiles, step, 0)
    for late in range(1, depth):
        for hops in range(late, depth):
            gather_of(tiles - 1 + late - hops).hop(hops)
    d_qkv[:cols, tiles * tile_rows :] = jnp.zeros(
        (cols, d_qkv.shape[1] - tiles * tile_rows), bf16
    )
    d_qkv[cols : 2 * cols, :] = dk_sum[...].astype(bf16)
    d_qkv[2 * cols :, :] = dv_sum[...].astype(bf16)

    def close(tile, carry):
        gather_of(tile).finish()
        return carry

    lax.fori_loop(0, tiles, close, 0)


def norm_back(gradient, normed, inverse):
    mean_grad = jnp.mean(gradient, axis=-1, keepdims=True)
    mean_mixed = jnp.mean(gradient * normed, axis=-1, keepdims=True)
    return inverse * (gradient - mean_grad - normed * mean_mixed)


def attn_back_kernel(
    shards,
    shape,
    cond,
    d_qkv,
    w_qkv,
    attn,
    context,
    mixed,
    cot_cols,
    out_weight,
    vec,
    second,
    cot,
    normed,
    inverse,
    first,
    wide,
    context_in,
    fc2,
    pre,
    root,
    ratio,
    denom,
    full,
    d_first,
    d_pre,
    small,
    map_grad,
    weight_grads,
    activations,
    d_mod,
    acc,
    d_resp,
    act,
    slope,
    sums,
    mine,
    theirs,
    to_y,
    from_y,
    to_z,
    from_z,
    y_sems,
    z_sems,
    gather_sems,
    total_sems,
    g_own,
    g_got,
    g_other,
    g_sems,
    ctx_out,
    ctx_in,
    ctx_sems,
    mod_in,
    mod_sems,
    act_out,
    act_in,
    act_sems,
):
    f32 = jnp.float32
    rows = cot.shape[0]
    depth = shards // 2
    me = lax.axis_index("seq")
    meet_all(shards, lax.axis_size("grp"))
    cols = ctx_out.shape[1]
    total = shards * rows
    latents = Latents(shape, total)
    base = vec.shape[1] - VEC_TAIL
    width_one = base // 3
    gamma = vec[:, width_one : 2 * width_one]
    out_bias = column_of(vec[:, base + 4 * VEC_STEP : base + 5 * VEC_STEP])[:cols]
    scale = wide[WIDE_SCALE : WIDE_SCALE + 8, :]
    weight_sum = PairSum(g_own, g_got, g_other, weight_grads, g_sems)
    peers = [lax.rem(me + step, shards) for step in range(1, shards)]
    ctx_copies = [
        seq_copy(ctx_out.at[peer], ctx_in.at[me], ctx_sems.at[0, k], ctx_sems.at[1, k], peer)
        for k, peer in enumerate(peers)
    ]

    act_copies = [
        seq_copy(
            act_out.at[:, pl.ds(pl.multiple_of(peer * rows, 128), rows)],
            act_in.at[me],
            act_sems.at[0, k],
            act_sems.at[1, k],
            peer,
        )
        for k, peer in enumerate(peers)
    ]

    def partial(block):
        here = pl.ds(pl.multiple_of(block * rows, 128), rows)
        return dot_tn(d_qkv[:, here], w_qkv[...])

    def between():
        low_type = ctx_out.dtype
        for device in range(shards):
            ctx_out[device] = dot_tn(
                w_qkv[:, device * cols : (device + 1) * cols], d_qkv[:, total:]
            ).astype(low_type)
        ctx_in[me] = ctx_out[me]
        g_own[: 3 * cols, :] = (
            jnp.dot(d_qkv[:, :total], attn[...].reshape(total, C), preferred_element_type=f32)
            + dot_nt(d_qkv[:, total:], context[...])
        ).astype(low_type)
        grad = None
        for tile in range(mixed.shape[0]):
            here = slice(tile * mixed.shape[3], (tile + 1) * mixed.shape[3])
            block = mixed[tile].reshape(C, mixed.shape[3])
            act_out[:, here] = (
                jnp.dot(out_weight[...], block, preferred_element_type=f32) + out_bias
            ).astype(low_type)
            part = dot_nt(cot_cols[:, here], block)
            grad = part if grad is None else grad + part
        g_own[3 * cols :, :] = grad.astype(low_type)
        weight_sum.begin()
        act_in[me] = act_out[:, pl.ds(pl.multiple_of(me * rows, 128), rows)]

    def scatter_hook(step):
        @pl.when(step == 1)
        def _():
            weight_sum.across()

    scatter_blocks(
        partial, to_y, from_y, to_z, from_z, acc, y_sems, z_sems, depth, between, scatter_hook
    )
    d_mod[...] = jnp.zeros_like(d_mod)

    def norm_tile(index):
        here = pl.ds(pl.multiple_of(index * 16, 16), 16)
        d_second = cot[here, :].astype(f32) + norm_back(
            acc[here, :], normed[here, :], inverse[here, :]
        )
        pick = latents.picks(me * rows + index * 16, 16)
        value = d_second * (1.0 + rows_of(pick, scale))
        d_first[here, :] = value
        full[me, here, :] = value.astype(full.dtype)
        scaled = d_second * first[here, :]
        for latent in range(NLAT):
            chosen = pick[latent]
            d_mod[2 * latent : 2 * latent + 1, :] += jnp.sum(scaled * chosen, axis=0, keepdims=True)
            d_mod[2 * latent + 1 : 2 * latent + 2, :] += jnp.sum(
                d_second * chosen, axis=0, keepdims=True
            )

    tile_loop(rows // 16, norm_tile)
    sums[...] = jnp.zeros_like(sums)
    wide_mod = 2 * cols
    half = shards // 2

    def mod_part(device):
        low = pl.multiple_of(lax.rem(device, half) * wide_mod, 128)
        return d_mod.at[:, pl.ds(low, wide_mod)]

    mod_in[me] = mod_part(me)[...]
    mod_copies = [
        seq_copy(mod_part(peer), mod_in.at[me], mod_sems.at[0, k], mod_sems.at[1, k], peer)
        for k, peer in enumerate(peers)
    ]
    for copy in mod_copies:
        copy.start()

    def gather_hook(hops):
        @pl.when(hops == 2)
        def _():
            weight_sum.share()

    def visit(block):
        d_resp[block] = jnp.dot(full[block], fc2[...], preferred_element_type=f32)

        def tile(index):
            here = pl.ds(pl.multiple_of(index * 32, 32), 32)
            value = pre[block, here, :]
            phi = 0.5 * (1.0 + lax.erf(value * ROOT_HALF))
            slope[block, here, :] = phi + value * (DENSITY * jnp.exp(-0.5 * value * value))
            value = value * phi
            act[block, here, :] = value
            pull = d_resp[block, here, :]
            sums[NLAT : NLAT + 1, :] += jnp.sum(pull, axis=0, keepdims=True)
            pull = pull * value
            pick = latents.picks(block * rows + index * 32, 32)
            for latent in range(NLAT):
                sums[latent : latent + 1, :] += jnp.sum(
                    pull * pick[latent], axis=0, keepdims=True
                )

        tile_loop(rows // 32, tile)

    Gather(full, gather_sems, depth).run(visit, gather_hook)
    small[...] = jnp.zeros_like(small)
    wide_row = 2 * cols

    def keep(row, value):
        for part in range(value.shape[1] // wide_row):
            small[row + part : row + part + 1, :] = value[
                :, part * wide_row : (part + 1) * wide_row
            ]

    keep(SMALL_BETA, sums[NLAT : NLAT + 1, :])
    pulls = sums[...]
    keep(SMALL_GAMMA, jnp.sum(pulls[:NLAT] * ratio[:NLAT, :], axis=0, keepdims=True))
    d_ratio = pulls * gamma
    mine[...] = jnp.broadcast_to(jnp.sum(d_ratio * root[...], axis=1, keepdims=True), mine.shape)

    def meanwhile():
        for copy in (*ctx_copies, *act_copies):
            copy.start()

    pulled = peer_total(mine, theirs, total_sems, shards, meanwhile)[:, 0:1]
    below = denom[:, 0:1]
    d_root = d_ratio / below - pulled / (FF * below * below)
    back = d_root / root[...]
    scaled = ratio[...] * gamma + 1.0
    sums[0:1, :] = jnp.zeros((1, width_one), f32)

    def respond(index):
        block = index // (rows // 32)
        here = pl.ds(pl.multiple_of(lax.rem(index, rows // 32) * 32, 32), 32)
        pick = latents.picks(index * 32, 32)
        d_act = d_resp[block, here, :] * rows_of(pick, scaled) + act[block, here, :] * rows_of(
            pick, back
        )
        value = (d_act * slope[block, here, :]).astype(d_pre.dtype)
        d_pre[block, here, :] = value
        sums[0:1, :] += jnp.sum(value.astype(f32), axis=0, keepdims=True)

    tile_loop(shards * rows // 32, respond)
    for copy in (*ctx_copies, *mod_copies, *act_copies):
        copy.wait()
    activations[...] = (second[...] + act_in[...].reshape(C, rows).astype(f32).T).astype(
        activations.dtype
    )
    context_sum = ctx_in[0].astype(f32)
    mod_sum = mod_in[0]
    for device in range(1, shards):
        context_sum = context_sum + ctx_in[device].astype(f32)
        mod_sum = mod_sum + mod_in[device]
    keep(SMALL_FC1, sums[0:1, :])
    at = lax.broadcasted_iota(jnp.int32, (1, context.shape[1]), 1)
    context_sum = jnp.where(at < NLAT * NCTX, context_sum, 0.0)
    map_grad[...] = jnp.dot(
        context_sum.astype(map_grad.dtype), context_in[...], preferred_element_type=f32
    ).astype(map_grad.dtype)
    chosen = [
        jnp.where(me < half, mod_sum[2 * n : 2 * n + 1], mod_sum[2 * n + 1 : 2 * n + 2])
        for n in range(NLAT)
    ]
    chosen = jnp.concatenate(chosen, axis=0)
    small[0:SMALL_FC1, :] = lax.dot_general(
        cond[...],
        chosen,
        (((0,), (0,)), ((), ())),
        precision=HIGHEST_PRECISION,
        preferred_element_type=f32,
    )
    keep(SMALL_TIME, jnp.sum(chosen, axis=0, keepdims=True))
    ones = lambda values: jnp.ones((8, values.shape[1]), values.dtype)
    for row, value in (
        (SMALL_QUERY, d_qkv[:cols, :]),
        (SMALL_VALUE, d_qkv[2 * cols :, :]),
        (SMALL_OUT, cot_cols[...]),
    ):
        small[row : row + 1, :cols] = dot_nt(ones(value), value)[0:1]
    small[SMALL_MAP : SMALL_MAP + 1, :cols] = lax.dot_general(
        ones(context_sum),
        context_sum,
        (((1,), (1,)), ((), ())),
        precision=HIGHEST_PRECISION,
        preferred_element_type=f32,
    )[0:1]
    weight_sum.finish()


def conv_back_kernel(
    shards,
    shape,
    d_pre,
    fc1,
    normed,
    inverse,
    d_first,
    hidden,
    wide,
    normed_full,
    response,
    branch,
    map_grad,
    small,
    input_grad,
    fc1_sum,
    fc2_sum,
    map_sum,
    small_sum,
    conv_sum,
    held,
    floats,
    acc,
    to_y,
    from_y,
    to_z,
    from_z,
    y_sems,
    z_sems,
    edge_sems,
    d_conv_params,
    fc1_own,
    fc1_got,
    fc1_other,
    fc2_own,
    fc2_got,
    fc2_other,
    map_own,
    map_got,
    map_other,
    pair_sems,
    fc2_sems,
    small_in,
    small_sems,
    conv_out,
    conv_in,
    conv_part,
    conv_group,
    conv_sems,
):
    f32 = jnp.float32
    rows = normed.shape[0]
    depth = shards // 2
    groups = lax.axis_size("grp")
    me = lax.axis_index("seq")
    meet_all(shards, groups)
    cols = conv_part.shape[1]
    units, width = fc2_own.shape[2:]
    total = shards * rows
    latents = Latents(shape, total)
    positions = me * rows + lax.broadcasted_iota(jnp.int32, (rows, 1), 0)
    fc1_pair = PairSum(fc1_own, fc1_got, fc1_other, fc1_sum, pair_sems.at[0])
    map_pair = PairSum(map_own, map_got, map_other, map_sum, pair_sems.at[1])
    fc2_quarter = QuarterSum(shards, fc2_own, fc2_got, fc2_other, fc2_sum, fc2_sems)
    group = lax.axis_index("grp")
    small_copies = [
        grp_copy(
            small,
            small_in.at[step - 1],
            small_sems.at[0, step - 1],
            small_sems.at[1, step - 1],
            lax.rem(group + step, groups),
        )
        for step in range(1, groups)
    ]

    def partial(block):
        return dot_nt(d_pre[block], fc1[...])

    def between():
        map_own[...] = map_grad[...]
        map_pair.begin()
        for copy in small_copies:
            copy.start()
        right = response[...].reshape(total, width)
        for goal in range(0, shards, 4):
            here = slice(goal * 4 * units, (goal + 4) * 4 * units)
            part = dot_tn(branch[:, :, here].reshape(total, 16 * units), right)
            fc2_own[goal : goal + 4] = part.reshape(4, 4, units, width).astype(fc2_own.dtype)
        fc2_quarter.begin()

        def tile(index):
            here = pl.ds(pl.multiple_of(index * 256, 256), 256)
            fc1_own[here, :] = dot_tn(
                normed_full[:, :, here].reshape(total, 256),
                d_pre[...].reshape(total, width),
            ).astype(fc1_own.dtype)

        tile_loop(C // 256, tile)
        fc1_pair.begin()

    def scatter_hook(step):
        @pl.when(step == 0)
        def _():
            fc2_quarter.across()
            fc1_pair.across()

        @pl.when(step == 2)
        def _():
            fc2_quarter.spread()
            map_pair.across()

    scatter_blocks(
        partial, to_y, from_y, to_z, from_z, acc, y_sems, z_sems, depth, between, scatter_hook
    )

    def norm_tile(index):
        start = pl.multiple_of(index * 16, 16)
        here = pl.ds(start, 16)
        held[pl.ds(EDGE + start, 16), :] = norm_back(
            acc[here, :], normed[here, :], inverse[here, :]
        ).astype(held.dtype)

    tile_loop(rows // 16, norm_tile)
    finish = exchange_edges(held, edge_sems, rows, shards)
    tile_loop(
        floats.shape[0] // 32,
        lambda i: floats.__setitem__(
            (pl.ds(i * 32, 32), slice(None)), hidden[pl.ds(i * 32, 32), :].astype(f32)
        ),
    )
    d_conv_params[...] = jnp.zeros_like(d_conv_params)
    masks = [latents.valid(positions, tap // 3 - 1, tap % 3 - 1) for tap in range(9)]

    def grad_tile(index):
        cols = pl.ds(pl.multiple_of(index * 256, 256), 256)
        d_conv = held[pl.ds(EDGE, rows), cols].astype(f32)
        d_conv_params[9:10, cols] = jnp.sum(d_conv, axis=0, keepdims=True)
        d_conv_params[10:11, cols] = jnp.sum(branch[me, :, cols].astype(f32), axis=0, keepdims=True)
        for tap in range(9):
            offset = EDGE + (tap // 3 - 1) * WMAX + tap % 3 - 1
            d_conv_params[tap : tap + 1, cols] = jnp.sum(
                d_conv * floats[offset : offset + rows, cols] * masks[tap],
                axis=0,
                keepdims=True,
            )

    tile_loop(C // 256, grad_tile)
    for goal in range(shards):
        conv_out[goal] = d_conv_params[:, goal * cols : (goal + 1) * cols]
    conv_in[me] = conv_out[me]
    conv_copies = []
    for step in range(1, shards):
        goal = lax.rem(me + step, shards)
        conv_copies.append(
            seq_copy(
                conv_out.at[goal],
                conv_in.at[me],
                conv_sems.at[0, step - 1],
                conv_sems.at[1, step - 1],
                goal,
            )
        )
        conv_copies[-1].start()
    finish()
    fc2_quarter.share()
    tile_loop(
        floats.shape[0] // 32,
        lambda i: floats.__setitem__(
            (pl.ds(i * 32, 32), slice(None)), held[pl.ds(i * 32, 32), :].astype(f32)
        ),
    )

    back_masks = []
    for tap in range(9):
        down_step, side_step = tap // 3 - 1, tap % 3 - 1
        back_masks.append(
            latents.valid(positions - down_step * WMAX - side_step, down_step, side_step)
        )

    def input_tile(index):
        cols = pl.ds(pl.multiple_of(index * 256, 256), 256)
        total = d_first[:, cols]
        for tap in range(9):
            offset = EDGE - (tap // 3 - 1) * WMAX - tap % 3 + 1
            total = total + (
                floats[offset : offset + rows, cols] * wide[tap : tap + 1, cols]
            ) * back_masks[tap]
        input_grad[:, cols] = total

    for copy in conv_copies:
        copy.wait()
    conv_total = conv_in[0]
    for device in range(1, shards):
        conv_total = conv_total + conv_in[device]
    conv_part[...] = conv_total
    group_copies = []
    for step in range(1, groups):
        k = shards - 2 + step
        group_copies.append(
            grp_copy(
                conv_part,
                conv_group.at[step - 1],
                conv_sems.at[0, k],
                conv_sems.at[1, k],
                lax.rem(group + step, groups),
            )
        )
        group_copies[-1].start()
    tile_loop(C // 256, input_tile)
    fc1_pair.share()
    map_pair.share()
    fc2_quarter.share_core()
    for copy in (*small_copies, *group_copies):
        copy.wait()
    small_sum[...] = small[...] + small_in[0] + small_in[1] + small_in[2]
    conv_sum[...] = conv_part[...] + conv_group[0] + conv_group[1] + conv_group[2]
    fc1_pair.finish()
    map_pair.finish()
    fc2_quarter.finish()


def kernel_call(body, name, number, outs, scratch, operands, flops=0, far=(), scalars=()):
    vmem, anywhere, smem = (
        pl.BlockSpec(memory_space=space) for space in (pltpu.VMEM, pl.ANY, pltpu.SMEM)
    )
    space_of = lambda k: anywhere if k in far else smem if k in scalars else vmem
    shapes = [jax.ShapeDtypeStruct(shape, dtype) for shape, dtype in outs]
    moved = sum(math.prod(s.shape) * s.dtype.itemsize for s in shapes) + sum(
        x.size * x.dtype.itemsize for x in operands
    )
    return pl.pallas_call(
        body,
        out_shape=shapes,
        in_specs=[space_of(k) for k in range(len(operands))],
        out_specs=[vmem] * len(shapes),
        scratch_shapes=scratch,
        name=name,
        cost_estimate=pl.CostEstimate(flops=flops, bytes_accessed=moved, transcendentals=0),
        compiler_params=pltpu.CompilerParams(
            collective_id=number, has_side_effects=True, vmem_limit_bytes=VMEM_BYTES
        ),
    )(*operands)


def scatter_scratch(rows, depth):
    bf16 = jnp.bfloat16
    return [
        pltpu.VMEM((depth, rows, C), bf16),
        pltpu.VMEM((depth, rows, C), bf16),
        pltpu.VMEM((depth, rows, C), bf16),
        pltpu.VMEM((2, depth, rows, C), bf16),
        pltpu.SemaphoreType.DMA((2, depth)),
        pltpu.SemaphoreType.DMA((2, 2, depth)),
    ]


def gather_scratch(depth):
    return pltpu.SemaphoreType.DMA((4, 2, depth + 1))


def total_scratch(shards):
    return [
        pltpu.VMEM((8, 128), jnp.float32),
        pltpu.VMEM((shards - 1, 8, 128), jnp.float32),
    ], pltpu.SemaphoreType.DMA((2, shards - 1))


def on_device_heads(
    hidden,
    latent_shape,
    cond_r,
    clip,
    cotangent,
    conv_weight,
    conv_bias,
    fc1_weight,
    fc1_bias,
    grn_gamma,
    grn_beta,
    fc2_weight,
    fc2_bias,
    time_weight,
    time_bias,
    map_weight,
    map_bias,
    query_weight,
    query_bias,
    key_weight,
    value_weight,
    value_bias,
    out_weight,
    out_bias,
):
    f32, bf16 = jnp.float32, jnp.bfloat16
    shards = lax.axis_size("seq")
    rows = hidden.shape[0]
    total = rows * shards
    cols = C // shards
    depth = shards // 2
    hidden_cols = FF // shards
    shape = latent_shape[0]
    slot = lambda item: jnp.pad(item, (0, VEC_STEP - item.shape[0]))
    vec = jnp.concatenate(
        [
            fc1_bias,
            grn_gamma,
            grn_beta,
            *(slot(item) for item in (conv_bias, fc2_bias, query_bias, value_bias, out_bias)),
            slot(map_bias),
            jnp.pad(time_bias, (0, 2 * VEC_STEP - time_bias.shape[0])),
        ]
    ).astype(f32)[None]
    w_qkv = jnp.concatenate([query_weight.T, key_weight.T, value_weight.T], axis=0)
    ctx_rows = 256
    context_in = jax.nn.silu(clip.reshape(NLAT * NCTX, CLIP).astype(f32)).astype(bf16)
    context_in = jnp.pad(context_in, ((0, ctx_rows - NLAT * NCTX), (0, 0)))
    ctx_cols = (against(map_weight.T, context_in) + map_bias.astype(f32)[:, None]).astype(bf16)
    units = cols // 4
    vmem = pltpu.VMEM
    total_vmem, total_sems = total_scratch(shards)
    (
        normed_full,
        held,
        wide,
        normed_one,
        inverse_one,
        pre_act,
        root,
        ratio,
        denom,
        response,
        context,
        cot_full,
        shrink_parts,
        output_rows,
    ) = kernel_call(
        functools.partial(mixer_kernel, shards),
        "mixer",
        1,
        [
            ((shards, rows, C), bf16),
            ((rows + 2 * EDGE, C), bf16),
            ((32, C), f32),
            ((rows, C), f32),
            ((rows, 1), f32),
            ((shards, rows, hidden_cols), f32),
            ((8, hidden_cols), f32),
            ((8, hidden_cols), f32),
            ((8, 128), f32),
            ((shards, rows, hidden_cols), bf16),
            ((shards, cols, ctx_rows), bf16),
            ((shards, rows, C), bf16),
            ((shards, 4, units, hidden_cols), bf16),
            ((cols, C), bf16),
        ],
        [
            vmem((24, cols), f32),
            vmem((shards, 24, cols), f32),
            vmem((rows + 2 * EDGE, C), f32),
            vmem((rows, C), f32),
            vmem((shards, rows, hidden_cols), f32),
            vmem((8, hidden_cols), f32),
            *total_vmem,
            pltpu.SemaphoreType.DMA((2, 2)),
            pltpu.SemaphoreType.DMA((2, shards - 1)),
            gather_scratch(depth),
            total_sems,
            gather_scratch(depth),
            gather_scratch(depth),
            vmem((shards, 4, units, cols), bf16),
            pltpu.SemaphoreType.DMA((2,)),
            pltpu.SemaphoreType.DMA((2, shards + 2)),
            pltpu.SemaphoreType.DMA((2, shards + 2)),
        ],
        (
            shape,
            hidden,
            cond_r,
            time_weight,
            conv_weight,
            vec,
            fc1_weight,
            ctx_cols,
            cotangent,
            fc2_weight.T,
            out_weight,
        ),
        flops=2 * total * C * hidden_cols,
        far=(9, 10),
        scalars=(0,),
    )
    context = context.reshape(C, ctx_rows)
    shrink_rows = shrink_parts.reshape(C, hidden_cols)
    keys_all = total + ctx_rows
    (
        attn_blocks,
        first_sum,
        second_sum,
        normed_two,
        inverse_two,
        queries,
        keys,
        values,
    ) = kernel_call(
        functools.partial(mixed_in_kernel, shards),
        "mixed_in",
        2,
        [
            ((shards, rows, C), bf16),
            ((rows, C), f32),
            ((rows, C), f32),
            ((rows, C), f32),
            ((rows, 1), f32),
            ((shards, rows, cols), bf16),
            ((cols, keys_all), bf16),
            ((cols, keys_all), bf16),
        ],
        [pltpu.VMEM((rows, C), f32), *scatter_scratch(rows, depth), gather_scratch(depth)],
        (
            shape,
            response,
            shrink_rows,
            hidden,
            wide,
            w_qkv,
            vec,
            context,
        ),
        flops=2 * total * C * (hidden_cols + 3 * cols),
        scalars=(0,),
    )

    tiles, tile_rows = 4, total // 4
    d_qkv, mixed_full, cot_cols = kernel_call(
        functools.partial(attend_kernel, shards),
        "attend",
        5,
        [
            ((3 * cols, keys_all), bf16),
            ((tiles, shards, cols, tile_rows), bf16),
            ((cols, total), bf16),
        ],
        [
            vmem((cols, keys_all), f32),
            vmem((cols, keys_all), f32),
            vmem((cols // HEAD_DIM, tile_rows, keys_all), f32),
            pltpu.SemaphoreType.DMA((tiles, 4, 2, depth + 1)),
        ],
        (
            shape,
            queries,
            keys,
            values,
            cot_full,
            output_rows,
        ),
        flops=12 * total * keys_all * 3 * 256,
        scalars=(0,),
    )
    (
        branch_blocks,
        d_first,
        d_pre,
        small,
        grad_map_w,
        weight_sums,
        activations,
    ) = kernel_call(
        functools.partial(attn_back_kernel, shards),
        "attn_back",
        3,
        [
            ((shards, rows, C), bf16),
            ((rows, C), f32),
            ((shards, rows, hidden_cols), bf16),
            ((SMALL_ROWS, 2 * cols), f32),
            ((cols, CLIP), bf16),
            ((4 * cols, C), bf16),
            ((rows, C), bf16),
        ],
        [
            vmem((8, C), f32),
            pltpu.VMEM((rows, C), f32),
            pltpu.VMEM((shards, rows, hidden_cols), f32),
            pltpu.VMEM((shards, rows, hidden_cols), f32),
            pltpu.VMEM((shards, rows, hidden_cols), f32),
            pltpu.VMEM((8, hidden_cols), f32),
            *total_vmem,
            *scatter_scratch(rows, depth),
            gather_scratch(depth),
            total_sems,
            vmem((4 * cols, C), bf16),
            vmem((2 * cols, C), bf16),
            vmem((2 * cols, C), bf16),
            pltpu.SemaphoreType.DMA((2, 3)),
            vmem((shards, cols, ctx_rows), bf16),
            vmem((shards, cols, ctx_rows), bf16),
            pltpu.SemaphoreType.DMA((2, shards - 1)),
            vmem((shards, 8, 2 * cols), f32),
            pltpu.SemaphoreType.DMA((2, shards - 1)),
            vmem((cols, total), bf16),
            vmem((shards, cols, rows), bf16),
            pltpu.SemaphoreType.DMA((2, shards - 1)),
        ],
        (
            shape,
            cond_r,
            d_qkv,
            w_qkv,
            attn_blocks,
            context,
            mixed_full,
            cot_cols,
            out_weight.T,
            vec,
            second_sum,
            cotangent,
            normed_two,
            inverse_two,
            first_sum,
            wide,
            context_in,
            shrink_rows,
            pre_act,
            root,
            ratio,
            denom,
        ),
        flops=2 * total * C * (hidden_cols + 6 * cols),
        scalars=(0,),
    )
    groups = lax.axis_size("grp")
    input_grad, fc1_sum, fc2_sum, map_sum, small, conv_small = kernel_call(
        functools.partial(conv_back_kernel, shards),
        "conv_back",
        4,
        [
            ((rows, C), f32),
            ((C, hidden_cols), bf16),
            ((cols, FF), bf16),
            ((cols, CLIP), bf16),
            ((SMALL_ROWS, 2 * cols), f32),
            ((16, cols), f32),
        ],
        [
            vmem((rows + 2 * EDGE, C), bf16),
            vmem((rows + 2 * EDGE, C), f32),
            vmem((rows, C), f32),
            *scatter_scratch(rows, depth),
            pltpu.SemaphoreType.DMA((2, 2)),
            vmem((16, C), f32),
            vmem((C, hidden_cols), bf16),
            vmem((C // 2, hidden_cols), bf16),
            vmem((C // 2, hidden_cols), bf16),
            vmem((shards, 4, units, hidden_cols), bf16),
            vmem((2, shards, units, hidden_cols), bf16),
            vmem((shards, units, hidden_cols), bf16),
            vmem((cols, CLIP), bf16),
            vmem((cols // 2, CLIP), bf16),
            vmem((cols // 2, CLIP), bf16),
            pltpu.SemaphoreType.DMA((2, 2, 3)),
            pltpu.SemaphoreType.DMA((2, 5 + shards)),
            vmem((groups - 1, SMALL_ROWS, 2 * cols), f32),
            pltpu.SemaphoreType.DMA((2, groups - 1)),
            vmem((shards, 16, cols), f32),
            vmem((shards, 16, cols), f32),
            vmem((16, cols), f32),
            vmem((groups - 1, 16, cols), f32),
            pltpu.SemaphoreType.DMA((2, shards + groups - 2)),
        ],
        (
            shape,
            d_pre,
            fc1_weight,
            normed_one,
            inverse_one,
            d_first,
            held,
            wide,
            normed_full,
            response,
            branch_blocks,
            grad_map_w,
            small,
        ),
        flops=6 * total * C * hidden_cols,
        scalars=(0,),
    )
    two = lambda row: small[row : row + 2].reshape(hidden_cols)
    one = lambda row: small[row, :cols]
    part = lambda k: weight_sums[k * cols : (k + 1) * cols].astype(f32).T
    return (
        activations,
        input_grad,
        conv_small[:9],
        conv_small[9],
        fc1_sum.astype(f32),
        two(SMALL_FC1),
        two(SMALL_GAMMA),
        two(SMALL_BETA),
        fc2_sum.astype(f32).T,
        conv_small[10],
        small[:SMALL_FC1],
        small[SMALL_TIME],
        map_sum.astype(f32).T,
        one(SMALL_MAP),
        part(0),
        one(SMALL_QUERY),
        part(1),
        part(2),
        one(SMALL_VALUE),
        part(3),
        one(SMALL_OUT),
    )


def solution(mesh):
    in_specs = (
        P(("grp", "seq"), None),
        P("grp", None, None),
        P("grp", None),
        P("grp", None, None),
        P(("grp", "seq"), None),
        P(None, "seq"),
        P("seq"),
        P(None, "seq"),
        P("seq"),
        P("seq"),
        P("seq"),
        P(None, "seq"),
        P("seq"),
        P(None, "seq"),
        P("seq"),
        P(None, "seq"),
        P("seq"),
        P(None, "seq"),
        P("seq"),
        P(None, "seq"),
        P(None, "seq"),
        P("seq"),
        P(None, "seq"),
        P("seq"),
    )
    out_specs = (
        P(("grp", "seq"), None),
        P(("grp", "seq"), None),
        P(None, "seq"),
        P("seq"),
        P(None, "seq"),
        P("seq"),
        P("seq"),
        P("seq"),
        P(None, "seq"),
        P("seq"),
        P(None, "seq"),
        P("seq"),
        P(None, "seq"),
        P("seq"),
        P(None, "seq"),
        P("seq"),
        P(None, "seq"),
        P(None, "seq"),
        P("seq"),
        P(None, "seq"),
        P("seq"),
    )
    by_heads = mesh.shape["seq"] == 8 and mesh.shape["grp"] == 4
    return jax.shard_map(
        on_device_heads if by_heads else on_device, mesh=mesh, in_specs=in_specs, out_specs=out_specs, check_vma=False
    )
```

```python
import functools
import math

import jax
import jax.numpy as jnp
from jax import lax
from jax.experimental import pallas as pl
from jax.experimental.pallas import tpu as pltpu
from jax.sharding import PartitionSpec as P

C = 1536
HEADS = 24
HEAD_DIM = 64
FF = 6144
CLIP = 1280
NCTX = 77
NLAT = 3
WMAX = 64


EPS_NORM = 1e-06
SCORE_SCALE = 0.125
MASKED = -1e30
HIGHEST_PRECISION = lax.Precision.HIGHEST


def padded_2(block, sides, width):
    for axis, dim in sides:
        count = lax.axis_size(axis)
        forward = [(i, i + 1) for i in range(count - 1)]
        backward = [(target, source) for source, target in forward]
        low = lax.ppermute(
            lax.slice_in_dim(block, block.shape[dim] - width, None, axis=dim), axis, forward
        )
        high = lax.ppermute(lax.slice_in_dim(block, 0, width, axis=dim), axis, backward)
        block = jnp.concatenate([low, block, high], axis=dim)
    return block


def latent_grid(positions, shape_row):
    latent_count = shape_row.shape[0]
    heights = shape_row[:, 0]
    latent_width = shape_row[0, 1]
    pixel_counts = heights * latent_width
    end_points = jnp.cumsum(pixel_counts)
    start_points = end_points - pixel_counts
    segment = jnp.sum((positions[:, None] >= end_points[None, :]).astype(jnp.int32), axis=1)
    segment = jnp.minimum(segment, latent_count - 1)
    picked = (segment[:, None] == jnp.arange(latent_count, dtype=jnp.int32)[None, :]).astype(
        jnp.int32
    )
    first_pixel = jnp.sum(picked * start_points[None, :], axis=1)
    height = jnp.sum(picked * heights[None, :], axis=1)
    offset_in = positions - first_pixel
    row_index = jnp.floor_divide(offset_in, latent_width)
    column = offset_in - row_index * latent_width
    return (segment, row_index, column, height, latent_width)


def valid_tap(row_index, column, height, latent_width, down_step, side_step):
    upright = (row_index + down_step >= 0) & (row_index + down_step < height)
    across = (column + side_step >= 0) & (column + side_step < latent_width)
    return (upright & across).astype(jnp.float32)


def layer_stats(values_in):
    average = jnp.mean(values_in, axis=-1, keepdims=True)
    centred = values_in - average
    variance = jnp.mean(centred * centred, axis=-1, keepdims=True)
    inverse = lax.rsqrt(variance + EPS_NORM)
    return (centred * inverse, inverse)


def layer_back(gradient, normed, inverse):
    mean_grad = jnp.mean(gradient, axis=-1, keepdims=True)
    mean_mixed = jnp.mean(gradient * normed, axis=-1, keepdims=True)
    return inverse * (gradient - mean_grad - normed * mean_mixed)


def against(values_low, weight_low):
    return lax.dot_general(
        values_low, weight_low, (((1,), (1,)), ((), ())), preferred_element_type=jnp.float32
    )


def against_exact(values_in, weight_in):
    return lax.dot_general(
        values_in,
        weight_in,
        (((1,), (1,)), ((), ())),
        precision=HIGHEST_PRECISION,
        preferred_element_type=jnp.float32,
    )


def outer_sum(left_low, right_low):
    return lax.dot_general(
        left_low, right_low, (((0,), (0,)), ((), ())), preferred_element_type=jnp.float32
    )


def column_sum(picked, values_in):
    return lax.dot_general(
        picked,
        values_in,
        (((0,), (0,)), ((), ())),
        precision=HIGHEST_PRECISION,
        preferred_element_type=jnp.float32,
    )


def exact_gelu(values_in):
    return jax.nn.gelu(values_in, approximate=False)


def block_size(row_count, shard_rows):
    shard_total = row_count // shard_rows
    return math.gcd(shard_total, max(1, 1024 // shard_rows)) * shard_rows


def on_device(
    hidden,
    latent_shape,
    cond_r,
    clip,
    cotangent,
    conv_weight,
    conv_bias,
    fc1_weight,
    fc1_bias,
    grn_gamma,
    grn_beta,
    fc2_weight,
    fc2_bias,
    time_weight,
    time_bias,
    map_weight,
    map_bias,
    query_weight,
    query_bias,
    key_weight,
    value_weight,
    value_bias,
    out_weight,
    out_bias,
):
    tok_rows = hidden.shape[0]
    positions = lax.axis_index("seq") * tok_rows + jnp.arange(tok_rows, dtype=jnp.int32)
    shape_row = latent_shape[0]
    segment, row_index, column, height, latent_width = latent_grid(positions, shape_row)
    margin = WMAX + 1
    gathered = (
        lax.all_gather(conv_weight, "seq", axis=1, tiled=True),
        lax.all_gather(conv_bias, "seq", axis=0, tiled=True),
        lax.all_gather(fc1_weight, "seq", axis=1, tiled=True),
        lax.all_gather(fc1_bias, "seq", axis=0, tiled=True),
        lax.all_gather(grn_gamma, "seq", axis=0, tiled=True),
        lax.all_gather(grn_beta, "seq", axis=0, tiled=True),
        lax.all_gather(fc2_weight, "seq", axis=1, tiled=True),
        lax.all_gather(fc2_bias, "seq", axis=0, tiled=True),
        lax.all_gather(time_weight, "seq", axis=1, tiled=True),
        lax.all_gather(time_bias, "seq", axis=0, tiled=True),
        lax.all_gather(map_weight, "seq", axis=1, tiled=True),
        lax.all_gather(map_bias, "seq", axis=0, tiled=True),
        lax.all_gather(query_weight, "seq", axis=1, tiled=True),
        lax.all_gather(query_bias, "seq", axis=0, tiled=True),
        lax.all_gather(key_weight, "seq", axis=1, tiled=True),
        lax.all_gather(value_weight, "seq", axis=1, tiled=True),
        lax.all_gather(value_bias, "seq", axis=0, tiled=True),
        lax.all_gather(out_weight, "seq", axis=1, tiled=True),
        lax.all_gather(out_bias, "seq", axis=0, tiled=True),
    )
    (
        kernel_full,
        kernel_bias,
        expand_full,
        expand_bias,
        gamma_full,
        beta_full,
        shrink_full,
        shrink_bias,
        time_full,
        time_bias_full,
        mapper_full,
        mapper_bias,
        query_full,
        query_bias_full,
        key_full,
        value_full,
        value_bias_full,
        output_full,
        output_bias_full,
    ) = gathered
    padded = padded_2(hidden, (("seq", 0),), margin)
    conv_out = jnp.broadcast_to(kernel_bias.astype(jnp.float32)[None, :], (tok_rows, C))
    tap_list = []
    for down_step in (-1, 0, 1):
        for side_step in (-1, 0, 1):
            tap_number = 3 * (down_step + 1) + (side_step + 1)
            valid = valid_tap(row_index, column, height, latent_width, down_step, side_step)
            offset_rows = down_step * latent_width + side_step
            nearby = lax.dynamic_slice_in_dim(padded, margin + offset_rows, tok_rows, 0).astype(
                jnp.float32
            )
            conv_out = (
                conv_out
                + kernel_full[tap_number].astype(jnp.float32)[None, :] * nearby * valid[:, None]
            )
            tap_list.append((tap_number, down_step, side_step, offset_rows, valid))
    normed_one, inverse_one = layer_stats(conv_out)
    normed_low = normed_one.astype(jnp.bfloat16)
    pre_act = jnp.dot(
        normed_low, expand_full, preferred_element_type=jnp.float32
    ) + expand_bias.astype(jnp.float32)
    activated, gelu_pull = jax.vjp(exact_gelu, pre_act)
    picked = (segment[:, None] == jnp.arange(NLAT, dtype=jnp.int32)[None, :]).astype(jnp.float32)
    energy = lax.psum(column_sum(picked, activated * activated), "seq")
    root = jnp.sqrt(energy + 1.0)
    denom = jnp.mean(root, axis=-1, keepdims=True) + EPS_NORM
    ratio = root / denom
    ratio_rows = jnp.dot(picked, ratio, precision=HIGHEST_PRECISION)
    gamma_value = gamma_full.astype(jnp.float32)
    response = gamma_value * (activated * ratio_rows) + beta_full.astype(jnp.float32) + activated
    response_low = response.astype(jnp.bfloat16)
    branch = jnp.dot(
        response_low, shrink_full, preferred_element_type=jnp.float32
    ) + shrink_bias.astype(jnp.float32)
    first_sum = hidden.astype(jnp.float32) + branch
    modulation = jnp.dot(
        cond_r, time_full.astype(jnp.float32), precision=HIGHEST_PRECISION
    ) + time_bias_full.astype(jnp.float32)
    mod_rows = jnp.dot(picked, modulation, precision=HIGHEST_PRECISION)
    scale_rows = 1.0 + mod_rows[:, :C]
    second_sum = first_sum * scale_rows + mod_rows[:, C:]
    normed_two, inverse_two = layer_stats(second_sum)
    attn_in = normed_two.astype(jnp.bfloat16)
    context_in = jax.nn.silu(clip.reshape(NLAT * NCTX, CLIP).astype(jnp.float32)).astype(
        jnp.bfloat16
    )
    context = (
        jnp.dot(context_in, mapper_full, preferred_element_type=jnp.float32)
        + mapper_bias.astype(jnp.float32)
    ).astype(jnp.bfloat16)
    queries = (
        jnp.dot(attn_in, query_full, preferred_element_type=jnp.float32)
        + query_bias_full.astype(jnp.float32)
    ).astype(jnp.bfloat16)
    keys_low = jnp.dot(attn_in, key_full, preferred_element_type=jnp.float32).astype(jnp.bfloat16)
    values_low = (
        jnp.dot(attn_in, value_full, preferred_element_type=jnp.float32)
        + value_bias_full.astype(jnp.float32)
    ).astype(jnp.bfloat16)
    context_keys = jnp.dot(context, key_full, preferred_element_type=jnp.float32).astype(
        jnp.bfloat16
    )
    context_values = (
        jnp.dot(context, value_full, preferred_element_type=jnp.float32)
        + value_bias_full.astype(jnp.float32)
    ).astype(jnp.bfloat16)
    query_heads = queries.reshape(tok_rows, HEADS, HEAD_DIM)
    key_heads = keys_low.reshape(tok_rows, HEADS, HEAD_DIM)
    value_heads = values_low.reshape(tok_rows, HEADS, HEAD_DIM)
    ctx_key_heads = context_keys.reshape(NLAT * NCTX, HEADS, HEAD_DIM)
    ctx_value_heads = context_values.reshape(NLAT * NCTX, HEADS, HEAD_DIM)
    context_segment = jnp.arange(NLAT * NCTX, dtype=jnp.int32) // NCTX
    ctx_admit = segment[:, None] == context_segment[None, :]

    def segments_at(first_row, length):
        return latent_grid(first_row + jnp.arange(length, dtype=jnp.int32), shape_row)[0]

    ctx_scores = (
        jnp.einsum("qhd,khd->hqk", query_heads, ctx_key_heads, preferred_element_type=jnp.float32)
        * SCORE_SCALE
    )
    ctx_scores = jnp.where(ctx_admit[None], ctx_scores, MASKED)
    start_max = jnp.max(ctx_scores, axis=-1)
    ctx_expo = jnp.exp(ctx_scores - start_max[..., None])
    start_total = jnp.sum(ctx_expo, axis=-1)
    start_accum = jnp.einsum(
        "hqk,khd->qhd",
        ctx_expo.astype(jnp.bfloat16),
        ctx_value_heads,
        preferred_element_type=jnp.float32,
    )
    key_part = lax.all_gather(keys_low, "seq", axis=0, tiled=True)
    value_part = lax.all_gather(values_low, "seq", axis=0, tiled=True)
    block_rows = block_size(key_part.shape[0], tok_rows)
    block_count = key_part.shape[0] // block_rows
    key_stack = key_part.reshape(block_count, block_rows, HEADS, HEAD_DIM)
    value_stack = value_part.reshape(block_count, block_rows, HEADS, HEAD_DIM)

    def attend_visit(state_now, element):
        key_block, value_block, block_index = element
        key_segment = segments_at(block_index * block_rows, block_rows)
        admitted = segment[:, None] == key_segment[None, :]
        scores = (
            jnp.einsum("qhd,khd->hqk", query_heads, key_block, preferred_element_type=jnp.float32)
            * SCORE_SCALE
        )
        scores = jnp.where(admitted[None], scores, MASKED)
        old_max, old_total, old_accum = state_now
        new_max = jnp.maximum(old_max, jnp.max(scores, axis=-1))
        factor = jnp.exp(old_max - new_max)
        expo_block = jnp.exp(scores - new_max[..., None])
        new_total = old_total * factor + jnp.sum(expo_block, axis=-1)
        new_accum = old_accum * factor.T[:, :, None] + jnp.einsum(
            "hqk,khd->qhd",
            expo_block.astype(jnp.bfloat16),
            value_block,
            preferred_element_type=jnp.float32,
        )
        return ((new_max, new_total, new_accum), None)

    state_end, ignored = lax.scan(
        attend_visit,
        (start_max, start_total, start_accum),
        (key_stack, value_stack, jnp.arange(block_count, dtype=jnp.int32)),
    )
    run_max, run_total, accum = state_end
    mixed = accum / run_total.T[:, :, None]
    log_total = run_max + jnp.log(run_total)
    mixed_low = mixed.reshape(tok_rows, C).astype(jnp.bfloat16)
    activations = (
        second_sum
        + jnp.dot(mixed_low, output_full, preferred_element_type=jnp.float32)
        + output_bias_full.astype(jnp.float32)
    ).astype(jnp.bfloat16)
    cot_value = cotangent.astype(jnp.float32)
    grad_out_w = outer_sum(mixed_low, cotangent)
    grad_out_b = jnp.sum(cot_value, axis=0)
    d_mixed_low = against(cotangent, output_full).astype(jnp.bfloat16)
    dmix_heads = d_mixed_low.reshape(tok_rows, HEADS, HEAD_DIM)
    delta = jnp.sum(dmix_heads.astype(jnp.float32) * mixed, axis=-1).T
    ctx_probs = jnp.exp(ctx_scores - log_total[..., None])
    ctx_dprob = jnp.einsum(
        "qhd,khd->hqk", dmix_heads, ctx_value_heads, preferred_element_type=jnp.float32
    )
    ctx_dscore = (ctx_probs * (ctx_dprob - delta[..., None])).astype(jnp.bfloat16)
    dquery_start = (
        jnp.einsum("hqk,khd->qhd", ctx_dscore, ctx_key_heads, preferred_element_type=jnp.float32)
        * SCORE_SCALE
    )
    ctx_dkey_part = (
        jnp.einsum("hqk,qhd->khd", ctx_dscore, query_heads, preferred_element_type=jnp.float32)
        * SCORE_SCALE
    )
    ctx_dvalue_part = jnp.einsum(
        "hqk,qhd->khd",
        ctx_probs.astype(jnp.bfloat16),
        dmix_heads,
        preferred_element_type=jnp.float32,
    )
    key_part = lax.all_gather(keys_low, "seq", axis=0, tiled=True)
    value_part = lax.all_gather(values_low, "seq", axis=0, tiled=True)
    query_block_rows = block_size(key_part.shape[0], tok_rows)
    block_count = key_part.shape[0] // query_block_rows
    key_stack = key_part.reshape(block_count, query_block_rows, HEADS, HEAD_DIM)
    value_stack = value_part.reshape(block_count, query_block_rows, HEADS, HEAD_DIM)

    def query_visit(state_now, element):
        key_block, value_block, block_index = element
        key_segment = segments_at(block_index * query_block_rows, query_block_rows)
        admitted = segment[:, None] == key_segment[None, :]
        scores = (
            jnp.einsum("qhd,khd->hqk", query_heads, key_block, preferred_element_type=jnp.float32)
            * SCORE_SCALE
        )
        scores = jnp.where(admitted[None], scores, MASKED)
        probs = jnp.exp(scores - log_total[..., None])
        dprob = jnp.einsum(
            "qhd,khd->hqk", dmix_heads, value_block, preferred_element_type=jnp.float32
        )
        dscore = (probs * (dprob - delta[..., None])).astype(jnp.bfloat16)
        added = (
            jnp.einsum("hqk,khd->qhd", dscore, key_block, preferred_element_type=jnp.float32)
            * SCORE_SCALE
        )
        return (state_now + added, None)

    state_end, ignored = lax.scan(
        query_visit,
        dquery_start,
        (key_stack, value_stack, jnp.arange(block_count, dtype=jnp.int32)),
    )
    dquery = state_end
    lse_all, delta_all = (
        lax.all_gather(log_total.T, "seq", axis=0, tiled=True),
        lax.all_gather(delta.T, "seq", axis=0, tiled=True),
    )
    zero_heads = jnp.zeros((tok_rows, HEADS, HEAD_DIM), jnp.float32)
    query_part = lax.all_gather(queries, "seq", axis=0, tiled=True)
    dmix_part = lax.all_gather(d_mixed_low, "seq", axis=0, tiled=True)
    row_count = query_part.shape[0]
    key_block_rows = block_size(row_count, tok_rows)
    block_count = row_count // key_block_rows
    query_stack = query_part.reshape(block_count, key_block_rows, HEADS, HEAD_DIM)
    dmix_stack = dmix_part.reshape(block_count, key_block_rows, HEADS, HEAD_DIM)
    lse_stack = lse_all.reshape(block_count, key_block_rows, HEADS)
    delta_stack = delta_all.reshape(block_count, key_block_rows, HEADS)

    def key_visit(state_now, element):
        query_block, dmix_block, lse_block, delta_block, block_index = element
        query_segment = segments_at(block_index * key_block_rows, key_block_rows)
        admitted = segment[:, None] == query_segment[None, :]
        scores = (
            jnp.einsum("khd,qhd->hkq", key_heads, query_block, preferred_element_type=jnp.float32)
            * SCORE_SCALE
        )
        scores = jnp.where(admitted[None], scores, MASKED)
        probs = jnp.exp(scores - lse_block.T[:, None, :])
        dkey_now, dvalue_now = state_now
        dvalue_now = dvalue_now + jnp.einsum(
            "hkq,qhd->khd",
            probs.astype(jnp.bfloat16),
            dmix_block,
            preferred_element_type=jnp.float32,
        )
        dprob = jnp.einsum(
            "khd,qhd->hkq", value_heads, dmix_block, preferred_element_type=jnp.float32
        )
        dscore = (probs * (dprob - delta_block.T[:, None, :])).astype(jnp.bfloat16)
        dkey_now = (
            dkey_now
            + jnp.einsum("hkq,qhd->khd", dscore, query_block, preferred_element_type=jnp.float32)
            * SCORE_SCALE
        )
        return ((dkey_now, dvalue_now), None)

    state_end, ignored = lax.scan(
        key_visit,
        (zero_heads, zero_heads),
        (query_stack, dmix_stack, lse_stack, delta_stack, jnp.arange(block_count, dtype=jnp.int32)),
    )
    dkey, dvalue = state_end
    dquery_low = dquery.reshape(tok_rows, C).astype(jnp.bfloat16)
    dkey_low = dkey.reshape(tok_rows, C).astype(jnp.bfloat16)
    dvalue_low = dvalue.reshape(tok_rows, C).astype(jnp.bfloat16)
    ctx_dkey_flat = ctx_dkey_part.reshape(NLAT * NCTX, C)
    ctx_dvalue_flat = ctx_dvalue_part.reshape(NLAT * NCTX, C)
    context_value = context.astype(jnp.float32)
    d_attn_in = (
        against(dquery_low, query_full)
        + against(dkey_low, key_full)
        + against(dvalue_low, value_full)
    )
    grad_query_w = outer_sum(attn_in, dquery_low)
    grad_query_b = jnp.sum(dquery_low.astype(jnp.float32), axis=0)
    grad_key_w = outer_sum(attn_in, dkey_low) + column_sum(context_value, ctx_dkey_flat)
    grad_value_w = outer_sum(attn_in, dvalue_low) + column_sum(context_value, ctx_dvalue_flat)
    grad_value_b = jnp.sum(dvalue_low.astype(jnp.float32), axis=0) + jnp.sum(
        ctx_dvalue_flat, axis=0
    )
    d_context = against_exact(ctx_dkey_flat, key_full.astype(jnp.float32)) + against_exact(
        ctx_dvalue_flat, value_full.astype(jnp.float32)
    )
    grad_map_w = column_sum(context_in.astype(jnp.float32), d_context)
    grad_map_b = jnp.sum(d_context, axis=0)
    d_second = cot_value + layer_back(d_attn_in, normed_two, inverse_two)
    d_first = d_second * scale_rows
    d_mod_rows = jnp.concatenate([d_second * first_sum, d_second], axis=1)
    d_modulation = column_sum(picked, d_mod_rows)
    grad_time_w = lax.dot_general(
        cond_r,
        d_modulation,
        (((0,), (0,)), ((), ())),
        precision=HIGHEST_PRECISION,
        preferred_element_type=jnp.float32,
    )
    grad_time_b = jnp.sum(d_modulation, axis=0)
    d_branch_low = d_first.astype(jnp.bfloat16)
    grad_shrink_w = outer_sum(response_low, d_branch_low)
    grad_shrink_b = jnp.sum(d_branch_low.astype(jnp.float32), axis=0)
    d_response = against(d_branch_low, shrink_full)
    grad_gamma = jnp.sum(d_response * activated * ratio_rows, axis=0)
    grad_beta = jnp.sum(d_response, axis=0)
    d_ratio = lax.psum(column_sum(picked, d_response * gamma_value * activated), "seq")
    d_root = d_ratio / denom - jnp.sum(d_ratio * root, axis=-1, keepdims=True) / (
        FF * denom * denom
    )
    d_act = d_response * (gamma_value * ratio_rows + 1.0) + activated * jnp.dot(
        picked, d_root / root, precision=HIGHEST_PRECISION
    )
    d_pre_low = gelu_pull(d_act)[0].astype(jnp.bfloat16)
    grad_expand_w = outer_sum(normed_low, d_pre_low)
    grad_expand_b = jnp.sum(d_pre_low.astype(jnp.float32), axis=0)
    d_normed = against(d_pre_low, expand_full)
    d_conv_low = layer_back(d_normed, normed_one, inverse_one).astype(jnp.bfloat16)
    d_conv = d_conv_low.astype(jnp.float32)
    grad_kernel_b = jnp.sum(d_conv, axis=0)
    d_padded = padded_2(d_conv_low, (("seq", 0),), margin)
    kernel_rows = []
    input_grad = d_first
    for tap_number, down_step, side_step, offset_rows, valid in tap_list:
        nearby = lax.dynamic_slice_in_dim(padded, margin + offset_rows, tok_rows, 0).astype(
            jnp.float32
        )
        kernel_rows.append(jnp.sum(d_conv * nearby * valid[:, None], axis=0))
        source = positions - offset_rows
        src_segment, src_row, src_column, src_height, src_width = latent_grid(source, shape_row)
        src_valid = valid_tap(src_row, src_column, src_height, src_width, down_step, side_step)
        behind = lax.dynamic_slice_in_dim(d_padded, margin - offset_rows, tok_rows, 0).astype(
            jnp.float32
        )
        input_grad = (
            input_grad
            + kernel_full[tap_number].astype(jnp.float32)[None, :] * behind * src_valid[:, None]
        )
    grad_kernel_w = jnp.stack(kernel_rows, axis=0)
    gradients = (
        grad_kernel_w,
        grad_kernel_b,
        grad_expand_w,
        grad_expand_b,
        grad_gamma,
        grad_beta,
        grad_shrink_w,
        grad_shrink_b,
        grad_time_w,
        grad_time_b,
        grad_map_w,
        grad_map_b,
        grad_query_w,
        grad_query_b,
        grad_key_w,
        grad_value_w,
        grad_value_b,
        grad_out_w,
        grad_out_b,
    )
    shares = (
        lax.psum_scatter(gradients[0], "seq", scatter_dimension=1, tiled=True),
        lax.psum_scatter(gradients[1], "seq", scatter_dimension=0, tiled=True),
        lax.psum_scatter(gradients[2], "seq", scatter_dimension=1, tiled=True),
        lax.psum_scatter(gradients[3], "seq", scatter_dimension=0, tiled=True),
        lax.psum_scatter(gradients[4], "seq", scatter_dimension=0, tiled=True),
        lax.psum_scatter(gradients[5], "seq", scatter_dimension=0, tiled=True),
        lax.psum_scatter(gradients[6], "seq", scatter_dimension=1, tiled=True),
        lax.psum_scatter(gradients[7], "seq", scatter_dimension=0, tiled=True),
        lax.psum_scatter(gradients[8], "seq", scatter_dimension=1, tiled=True),
        lax.psum_scatter(gradients[9], "seq", scatter_dimension=0, tiled=True),
        lax.psum_scatter(gradients[10], "seq", scatter_dimension=1, tiled=True),
        lax.psum_scatter(gradients[11], "seq", scatter_dimension=0, tiled=True),
        lax.psum_scatter(gradients[12], "seq", scatter_dimension=1, tiled=True),
        lax.psum_scatter(gradients[13], "seq", scatter_dimension=0, tiled=True),
        lax.psum_scatter(gradients[14], "seq", scatter_dimension=1, tiled=True),
        lax.psum_scatter(gradients[15], "seq", scatter_dimension=1, tiled=True),
        lax.psum_scatter(gradients[16], "seq", scatter_dimension=0, tiled=True),
        lax.psum_scatter(gradients[17], "seq", scatter_dimension=1, tiled=True),
        lax.psum_scatter(gradients[18], "seq", scatter_dimension=0, tiled=True),
    )
    summed = (
        lax.psum(shares[0].astype(jnp.bfloat16), "grp").astype(jnp.float32),
        lax.psum(shares[1].astype(jnp.bfloat16), "grp").astype(jnp.float32),
        lax.psum(shares[2].astype(jnp.bfloat16), "grp").astype(jnp.float32),
        lax.psum(shares[3].astype(jnp.bfloat16), "grp").astype(jnp.float32),
        lax.psum(shares[4].astype(jnp.bfloat16), "grp").astype(jnp.float32),
        lax.psum(shares[5].astype(jnp.bfloat16), "grp").astype(jnp.float32),
        lax.psum(shares[6].astype(jnp.bfloat16), "grp").astype(jnp.float32),
        lax.psum(shares[7].astype(jnp.bfloat16), "grp").astype(jnp.float32),
        lax.psum(shares[8].astype(jnp.bfloat16), "grp").astype(jnp.float32),
        lax.psum(shares[9].astype(jnp.bfloat16), "grp").astype(jnp.float32),
        lax.psum(shares[10].astype(jnp.bfloat16), "grp").astype(jnp.float32),
        lax.psum(shares[11].astype(jnp.bfloat16), "grp").astype(jnp.float32),
        lax.psum(shares[12].astype(jnp.bfloat16), "grp").astype(jnp.float32),
        lax.psum(shares[13].astype(jnp.bfloat16), "grp").astype(jnp.float32),
        lax.psum(shares[14].astype(jnp.bfloat16), "grp").astype(jnp.float32),
        lax.psum(shares[15].astype(jnp.bfloat16), "grp").astype(jnp.float32),
        lax.psum(shares[16].astype(jnp.bfloat16), "grp").astype(jnp.float32),
        lax.psum(shares[17].astype(jnp.bfloat16), "grp").astype(jnp.float32),
        lax.psum(shares[18].astype(jnp.bfloat16), "grp").astype(jnp.float32),
    )
    return (
        activations,
        input_grad,
        summed[0],
        summed[1],
        summed[2],
        summed[3],
        summed[4],
        summed[5],
        summed[6],
        summed[7],
        summed[8],
        summed[9],
        summed[10],
        summed[11],
        summed[12],
        summed[13],
        summed[14],
        summed[15],
        summed[16],
        summed[17],
        summed[18],
    )


def mm(left, right):
    return jnp.dot(left, right, preferred_element_type=jnp.float32)


MESH_ID = pl.DeviceIdType.MESH


def dot_nt(left, right):
    return lax.dot_general(
        left, right, (((1,), (1,)), ((), ())), preferred_element_type=jnp.float32
    )


def place():
    me = lax.axis_index("seq")
    z, y = me // 2, lax.rem(me, 2)
    return me, z, y, me + 1 - 2 * y


def seq_copy(src, dst, send, recv, target):
    return pltpu.make_async_remote_copy(
        src_ref=src,
        dst_ref=dst,
        send_sem=send,
        recv_sem=recv,
        device_id={"seq": target},
        device_id_type=MESH_ID,
    )


def dot_tn(left, right):
    return lax.dot_general(
        left, right, (((0,), (0,)), ((), ())), preferred_element_type=jnp.float32
    )


def grp_copy(src, dst, send, recv, target):
    return pltpu.make_async_remote_copy(
        src_ref=src,
        dst_ref=dst,
        send_sem=send,
        recv_sem=recv,
        device_id={"grp": target},
        device_id_type=MESH_ID,
    )


def group_place():
    group = lax.axis_index("grp")
    core = lax.rem(group, 2)
    return group // 2, core, group + 1 - 2 * core, lax.rem(group + 2, 4)


def meet_all(shards, groups=0):
    me = lax.axis_index("seq")
    barrier = pltpu.get_barrier_semaphore()
    for step in range(1, groups):
        pl.semaphore_signal(
            barrier,
            inc=1,
            device_id={"grp": lax.rem(lax.axis_index("grp") + step, groups)},
            device_id_type=MESH_ID,
        )
    for step in range(1, shards):
        pl.semaphore_signal(
            barrier,
            inc=1,
            device_id={"seq": lax.rem(me + step, shards)},
            device_id_type=MESH_ID,
        )
    pl.semaphore_wait(barrier, shards - 1 + max(groups - 1, 0))


def tile_loop(count, body):
    def step(index, carry):
        body(index)
        return carry

    lax.fori_loop(0, count, step, 0)


def add_rows(target, target_row, left, left_row, right, count):
    def tile(index):
        low = index * 32
        here = pl.ds(pl.multiple_of(target_row + low, 32), 32)
        there = pl.ds(pl.multiple_of(left_row + low, 32), 32)
        value = left[there, :].astype(jnp.float32) + right[
            pl.ds(pl.multiple_of(low, 32), 32), :
        ].astype(jnp.float32)
        target[here, :] = value.astype(target.dtype)

    tile_loop(count // 32, tile)


class PairSum:
    def __init__(self, own, got, other, out, sems):
        x, core, self.core_peer, self.x_peer = group_place()
        self.half = own.shape[0] // 2
        self.own, self.got, self.other, self.out = own, got, other, out
        self.low = pl.multiple_of(core * self.half, self.half)
        mine = pl.ds(self.low, self.half)
        theirs = pl.ds(pl.multiple_of((1 - core) * self.half, self.half), self.half)
        pair = lambda k: (sems.at[0, k], sems.at[1, k])
        self.copies = (
            grp_copy(own.at[theirs], got, *pair(0), self.core_peer),
            grp_copy(own.at[mine], other, *pair(1), self.x_peer),
            grp_copy(out.at[mine], out.at[mine], *pair(2), self.core_peer),
        )

    def begin(self):
        self.copies[0].start()

    def across(self):
        self.copies[0].wait_recv()
        add_rows(self.own, self.low, self.own, self.low, self.got, self.half)
        self.copies[1].start()

    def share(self):
        self.copies[1].wait_recv()
        add_rows(self.out, self.low, self.own, self.low, self.other, self.half)
        self.copies[2].start()

    def finish(self):
        self.copies[2].wait_recv()
        for copy in self.copies:
            copy.wait_send()


class CoreHalf:
    def __init__(self, own, got, half, sems):
        _, core, core_peer, _ = group_place()
        self.own, self.got, self.half, self.core = own, got, half, core
        self.copies = [
            grp_copy(
                own.at[:, side * 2 + 1 - core],
                got.at[side],
                sems.at[0, side],
                sems.at[1, side],
                core_peer,
            )
            for side in (0, 1)
        ]

    def begin(self):
        for copy in self.copies:
            copy.start()

    def finish(self):
        for side, copy in enumerate(self.copies):
            copy.wait_recv()

            def tile(index, side=side):
                self.half[index, side] = (
                    self.own[index, side * 2 + self.core].astype(jnp.float32)
                    + self.got[side, index].astype(jnp.float32)
                ).astype(self.half.dtype)

            tile_loop(self.own.shape[0], tile)
        for copy in self.copies:
            copy.wait_send()


class QuarterSum:
    def __init__(self, shards, half, other, part, out, sems):
        x, core, core_peer, x_peer = group_place()
        me = lax.axis_index("seq")
        units, width = half.shape[2], half.shape[3]
        self.half, self.other, self.part, self.out = half, other, part, out
        self.x, self.me, self.shards = x, me, shards
        mine = x * 2 + core
        pair = lambda k: (sems.at[0, k], sems.at[1, k])

        def rows(quarter):
            return pl.ds(pl.multiple_of(quarter * units, units), units)

        self.block = (rows(mine), pl.ds(pl.multiple_of(me * width, 128), width))
        self.second = grp_copy(half.at[:, 1 - x], other, *pair(0), x_peer)
        self.third = []
        for step in range(1, shards):
            goal = lax.rem(me + step, shards)
            self.third.append(seq_copy(part.at[goal], out.at[self.block], *pair(step), goal))
        whole = out.at[rows(mine)]
        self.fourth = grp_copy(whole, whole, *pair(shards), x_peer)
        self.fifth = []
        for side in (0, 1):
            whole = out.at[rows(side * 2 + core)]
            self.fifth.append(grp_copy(whole, whole, *pair(shards + 1 + side), core_peer))

    def begin(self):
        self.second.start()

    def spread(self):
        self.second.wait_recv()

        def tile(index):
            self.part[index] = (
                self.half[index, self.x].astype(jnp.float32)
                + self.other[index].astype(jnp.float32)
            ).astype(self.part.dtype)

        tile_loop(self.shards, tile)
        for copy in self.third:
            copy.start()
        self.out[self.block] = self.part[self.me]

    def share(self):
        for copy in self.third:
            copy.wait_recv()
        self.fourth.start()

    def share_core(self):
        self.fourth.wait_recv()
        for copy in self.fifth:
            copy.start()

    def finish(self):
        for copy in self.fifth:
            copy.wait_recv()
        for copy in (self.second, *self.third, self.fourth, *self.fifth):
            copy.wait_send()


def in_line(direction, z, hops, depth):
    return z >= hops if direction == 0 else z + hops < depth


class Gather:
    def __init__(self, full, sems, depth, extra=0):
        self.full, self.depth, self.extra = full, depth, extra
        self.sems = [sems.at[k] for k in range(6)]
        self.me, self.z, self.y, self.other = place()
        self.rows = full.shape[1]

    def origin(self, direction, hops, far):
        column = 1 - self.y if far else self.y
        return (self.z - hops if direction == 0 else self.z + hops) * 2 + column

    def block(self, direction, hops, far=False):
        origin = self.origin(direction, hops, far)
        if not self.extra:
            return self.full.at[origin]
        return self.full.at[origin, pl.ds(0, self.rows - self.extra)]

    def pair(self, direction, hops):
        low = self.origin(direction, hops, False) - self.y
        return self.full.at[pl.ds(low, 2), pl.ds(self.rows - self.extra, self.extra)]

    def z_move(self, block, kind, direction, hops, arrival):
        send, recv = self.sems[kind], self.sems[kind + 1]
        target = self.me + 2 if direction == 0 else self.me - 2
        return seq_copy(
            block,
            block,
            send.at[direction, hops],
            recv.at[direction, hops if arrival else hops + 1],
            self.other if arrival else target,
        )

    def z_copy(self, direction, hops, arrival=False):
        return self.z_move(self.block(direction, hops), 0, direction, hops, arrival)

    def pair_copy(self, direction, hops, arrival=False):
        return self.z_move(self.pair(direction, hops), 4, direction, hops, arrival)

    def y_copy(self, direction, hops, arrival=False, own=False):
        if own:
            block = self.full.at[self.origin(direction, hops, arrival)]
        else:
            block = self.block(direction, hops, arrival)
        send, recv = self.sems[2], self.sems[3]
        return seq_copy(
            block, block, send.at[direction, hops], recv.at[direction, hops], self.other
        )

    def here(self, direction, hops):
        return in_line(direction, self.z, hops, self.depth)

    def onward(self, direction):
        return self.z < self.depth - 1 if direction == 0 else self.z > 0

    def start(self):
        for direction in (0, 1):

            @pl.when(self.onward(direction))
            def _():
                self.z_copy(direction, 0).start()

        self.y_copy(0, 0, own=True).start()

    def cross(self):
        self.y_copy(0, 0, True, own=True).wait_recv()
        if self.extra:
            for direction in (0, 1):

                @pl.when(self.onward(direction))
                def _():
                    self.pair_copy(direction, 0).start()

    def hop(self, hops):
        for direction in (0, 1):

            @pl.when(self.here(direction, hops))
            def _():
                self.z_copy(direction, hops, True).wait_recv()

                @pl.when(self.onward(direction))
                def _():
                    self.z_copy(direction, hops).start()

                self.y_copy(direction, hops).start()

        if self.extra:
            for direction in (0, 1):

                @pl.when(self.here(direction, hops))
                def _():
                    self.pair_copy(direction, hops, True).wait_recv()

                    @pl.when(self.onward(direction))
                    def _():
                        self.pair_copy(direction, hops).start()

    def near(self, hops, visit):
        for direction in (0, 1):

            @pl.when(self.here(direction, hops))
            def _():
                visit(self.origin(direction, hops, False))

    def far(self, hops, visit=None):
        for direction in (0, 1):

            @pl.when(self.here(direction, hops))
            def _():
                self.y_copy(direction, hops, True).wait_recv()
                if visit is not None:
                    visit(self.origin(direction, hops, True))

    def drain(self):
        self.y_copy(0, 0, own=True).wait_send()

        def step(hops, carry):
            for direction in (0, 1):
                here = self.here(direction, hops)

                @pl.when(here & self.onward(direction))
                def _():
                    self.z_copy(direction, hops).wait_send()
                    if self.extra:
                        self.pair_copy(direction, hops).wait_send()

                @pl.when(here & (hops > 0))
                def _():
                    self.y_copy(direction, hops).wait_send()

            return carry

        lax.fori_loop(0, self.depth, step, 0)

    def finish(self):
        def step(hops, carry):
            self.far(hops)
            return carry

        lax.fori_loop(1, self.depth, step, 0)
        self.drain()

    def run(self, visit, hook=None):
        self.start()
        visit(self.me)
        self.cross()
        visit(self.other)

        def step(hops, carry):
            @pl.when(hops < self.depth)
            def _():
                self.hop(hops)
                self.near(hops, visit)

            @pl.when(hops > 1)
            def _():
                self.far(hops - 1, visit)

            if hook is not None:
                hook(hops)
            return carry

        lax.fori_loop(1, self.depth + 1, step, 0)
        self.drain()


class Reshard:
    def __init__(self, shards, part, out, local_sem, sems):
        x, core, core_peer, x_peer = group_place()
        me = lax.axis_index("seq")
        mine = x * 2 + core
        pair = lambda k: (sems.at[0, k], sems.at[1, k])
        self.local = pltpu.make_async_copy(part(me, mine), out.at[me, mine], local_sem)
        self.first = []
        for step in range(1, shards):
            goal = lax.rem(me + step, shards)
            self.first.append(seq_copy(part(goal, mine), out.at[me, mine], *pair(step - 1), goal))
        self.second = grp_copy(out.at[:, mine], out.at[:, mine], *pair(shards - 1), x_peer)
        self.third = []
        for side in (0, 1):
            whole = out.at[:, side * 2 + core]
            self.third.append(grp_copy(whole, whole, *pair(shards + side), core_peer))

    def begin(self):
        self.local.start()
        for copy in self.first:
            copy.start()

    def share(self):
        self.local.wait()
        for copy in self.first:
            copy.wait_recv()
        self.second.start()

    def share_core(self):
        self.second.wait_recv()
        for copy in self.third:
            copy.start()

    def finish(self):
        for copy in self.third:
            copy.wait_recv()
        for copy in (*self.first, self.second, *self.third):
            copy.wait_send()


def side_by_side(target, row, parts, count):
    for pair in range(count // 2):
        value = jnp.concatenate([parts(2 * pair), parts(2 * pair + 1)], axis=1)
        rows, cols = value.shape
        target[row : row + rows, pair * cols : (pair + 1) * cols] = value


def scatter_blocks(
    partial, to_y, from_y, to_z, from_z, acc, y_sems, z_sems, depth, between=None, hook=None, early=None
):
    me, z, y, other = place()
    low = to_y.dtype

    def y_copy(goal):
        return seq_copy(
            to_y.at[goal], from_y.at[goal], y_sems.at[0, goal], y_sems.at[1, goal], other
        )

    def slot(direction, goal, at):
        return goal if direction == 0 else jnp.where(goal == at, depth, goal)

    def z_copy(direction, goal):
        return seq_copy(
            to_z.at[goal],
            from_z.at[slot(direction, goal, z - 1)],
            z_sems.at[0, direction, goal],
            z_sems.at[1, direction, goal],
            me + 2 if direction == 0 else me - 2,
        )

    def z_arrival(direction, goal):
        return seq_copy(
            to_z.at[goal],
            from_z.at[slot(direction, goal, z)],
            z_sems.at[0, direction, goal],
            z_sems.at[1, direction, goal],
            other,
        )

    def ahead(direction, hops):
        return in_line(1 - direction, z, hops, depth)

    def goal_of(direction, hops):
        return z + hops if direction == 0 else z - hops

    def over_y(step, carry):
        hops = depth - 1 - step
        for direction in (0, 1):
            here = ahead(direction, hops)
            if direction == 1:
                here = here & (hops > 0)

            @pl.when(here)
            def _():
                goal = goal_of(direction, hops)
                to_y[goal] = partial(goal * 2 + other - z * 2).astype(low)
                y_copy(goal).start()

        if early is not None:
            early(step)
        return carry

    lax.fori_loop(0, depth, over_y, 0)
    if between is not None:
        between()

    def along_z(step, carry):
        hops = depth - 1 - step
        for direction in (0, 1):

            @pl.when(ahead(direction, hops))
            def _():
                goal = goal_of(direction, hops)
                acc[...] = partial(goal * 2 + y)
                y_copy(goal).wait_recv()
                acc[...] += from_y[goal].astype(jnp.float32)

                @pl.when(in_line(direction, z, 1, depth))
                def _():
                    z_arrival(direction, goal).wait_recv()
                    acc[...] += from_z[slot(direction, goal, z)].astype(jnp.float32)

                to_z[goal] = acc[...].astype(low)
                z_copy(direction, goal).start()

        if hook is not None:
            hook(step)
        return carry

    lax.fori_loop(0, depth - 1, along_z, 0)
    acc[...] = partial(me)
    y_copy(z).wait_recv()
    acc[...] += from_y[z].astype(jnp.float32)
    for direction in (0, 1):

        @pl.when(in_line(direction, z, 1, depth))
        def _():
            z_arrival(direction, z).wait_recv()
            acc[...] += from_z[slot(direction, z, z)].astype(jnp.float32)

    def drain(goal, carry):
        y_copy(goal).wait_send()
        for direction in (0, 1):
            sent = goal > z if direction == 0 else goal < z

            @pl.when(sent)
            def _():
                z_copy(direction, goal).wait_send()

        return carry

    lax.fori_loop(0, depth, drain, 0)


def peer_total(mine, theirs, sems, shards, meanwhile=None):
    me = lax.axis_index("seq")
    copies = [
        seq_copy(
            mine,
            theirs.at[step - 1],
            sems.at[0, step - 1],
            sems.at[1, step - 1],
            lax.rem(me + step, shards),
        )
        for step in range(1, shards)
    ]
    for copy in copies:
        copy.start()
    if meanwhile is not None:
        meanwhile()
    for copy in copies:
        copy.wait()
    total = mine[...]
    for step in range(1, shards):
        total = total + theirs[step - 1]
    return total


EDGE = 80
VMEM_BYTES = 58 * 1024 * 1024
ROOT_HALF = math.sqrt(0.5)
DENSITY = 1.0 / math.sqrt(2.0 * math.pi)


def exchange_edges(held, sems, rows, shards):
    me = lax.axis_index("seq")

    def copy(kind):
        if kind == 0:
            source, target = pl.ds(EDGE + rows - WMAX, WMAX), pl.ds(EDGE - WMAX, WMAX)
        else:
            source, target = pl.ds(EDGE, WMAX), pl.ds(EDGE + rows, WMAX)
        return seq_copy(
            held.at[source],
            held.at[target],
            sems.at[0, kind],
            sems.at[1, kind],
            me + 1 if kind == 0 else me - 1,
        )

    first, last = me == 0, me == shards - 1
    zeros = jnp.zeros((EDGE, held.shape[1]), held.dtype)

    held[pl.ds(0, EDGE - WMAX), :] = zeros[: EDGE - WMAX]
    held[pl.ds(EDGE + rows + WMAX, EDGE - WMAX), :] = zeros[: EDGE - WMAX]

    @pl.when(first)
    def _():
        held[pl.ds(EDGE - WMAX, WMAX), :] = zeros[:WMAX]

    @pl.when(last)
    def _():
        held[pl.ds(EDGE + rows, WMAX), :] = zeros[:WMAX]

    @pl.when(jnp.logical_not(last))
    def _():
        copy(0).start()

    @pl.when(jnp.logical_not(first))
    def _():
        copy(1).start()

    def finish():
        @pl.when(jnp.logical_not(last))
        def _():
            copy(0).wait_send()
            copy(1).wait_recv()

        @pl.when(jnp.logical_not(first))
        def _():
            copy(1).wait_send()
            copy(0).wait_recv()

    return finish


VEC_STEP = 256
VEC_TAIL = 8 * VEC_STEP


def column_of(row):
    return jnp.broadcast_to(row, (8, row.shape[1])).T[:, 0:1]


def stats_of(values_in):
    average = jnp.mean(values_in, axis=-1, keepdims=True)
    centred = values_in - average
    variance = jnp.mean(centred * centred, axis=-1, keepdims=True)
    inverse = lax.rsqrt(variance + EPS_NORM)
    return centred * inverse, inverse


class Latents:
    def __init__(self, shape, total):
        self.ends = []
        low = 0
        for latent in range(NLAT - 1):
            low = low + shape[latent, 0] * WMAX
            self.ends.append(low)
        self.total = total

    def segment(self, positions):
        out = jnp.zeros_like(positions)
        for end in self.ends:
            out = out + (positions >= end).astype(jnp.int32)
        return out

    def picks(self, start, count):
        segment = self.segment(start + lax.broadcasted_iota(jnp.int32, (count, 1), 0))
        return [(segment == latent).astype(jnp.float32) for latent in range(NLAT)]

    def valid(self, positions, down_step, side_step):
        segment = self.segment(positions)
        low, high = jnp.zeros_like(positions), jnp.full_like(positions, self.total)
        for latent, end in enumerate(self.ends):
            low = jnp.where(segment > latent, end, low)
            high = jnp.where(segment == latent, end, high)
        moved = positions + down_step * WMAX
        column = (positions & (WMAX - 1)) + side_step
        good = (moved >= low) & (moved < high) & (column >= 0) & (column < WMAX)
        return good.astype(jnp.float32)


def rows_of(picks, table):
    out = picks[0] * table[0:1]
    for latent in range(1, NLAT):
        out = out + picks[latent] * table[latent : latent + 1]
    return out


WIDE_SCALE, WIDE_SHIFT = 16, 24
SMALL_FC1, SMALL_GAMMA, SMALL_BETA, SMALL_TIME = 64, 66, 68, 70
SMALL_QUERY, SMALL_VALUE, SMALL_OUT, SMALL_MAP, SMALL_ROWS = 71, 72, 73, 74, 80


def mixer_kernel(
    shards,
    emit,
    shape,
    hidden,
    cond,
    time_weight,
    conv_weight,
    vec,
    fc1,
    ctx_cols,
    cot,
    fc2,
    out_weight,
    full,
    held,
    wide,
    normed,
    inverse,
    pre,
    root_out,
    ratio_out,
    denom_out,
    response,
    ctx_full,
    cot_full,
    fc2_rows,
    out_rows,
    pack,
    packed,
    floats,
    conv,
    act,
    energy,
    mine,
    theirs,
    edge_sems,
    pack_sems,
    gather_sems,
    total_sems,
    ctx_sems,
    cot_sems,
    out_parts,
    local_sems,
    fc2_sems,
    out_sems,
):
    f32 = jnp.float32
    rows = hidden.shape[0]
    depth = shards // 2
    me = lax.axis_index("seq")
    meet_all(shards, lax.axis_size("grp"))
    units, width = fc2_rows.shape[2:]
    out_units = out_parts.shape[2]

    def fc2_part(goal, quarter):
        here = pl.ds(pl.multiple_of(quarter * units, units), units)
        return fc2.at[here, pl.ds(pl.multiple_of(goal * width, 128), width)]

    def out_part(goal, quarter):
        low = (goal * 4 + quarter) * out_units
        return out_weight.at[pl.ds(pl.multiple_of(low, out_units), out_units)]

    fc2_shard = Reshard(shards, fc2_part, fc2_rows, local_sems.at[0], fc2_sems)
    out_shard = Reshard(shards, out_part, out_parts, local_sems.at[1], out_sems)
    ctx_gather = Gather(ctx_full, ctx_sems, depth)
    cot_gather = Gather(cot_full, cot_sems, depth, rows // 8)
    ctx_full[me] = ctx_cols[...]
    latents = Latents(shape, shards * rows)
    cols = pack.shape[1]
    width_one = response.shape[2]
    fc1_bias, gamma, beta = (vec[:, n * width_one : (n + 1) * width_one] for n in range(3))
    vec_at = lambda n: vec[:, 3 * width_one + n * VEC_STEP : 3 * width_one + n * VEC_STEP + cols]
    time_bias = vec[:, 3 * width_one + 6 * VEC_STEP : 3 * width_one + 6 * VEC_STEP + 2 * cols]
    mod = (
        jnp.dot(
            cond[...],
            time_weight[...].astype(f32),
            precision=HIGHEST_PRECISION,
            preferred_element_type=f32,
        )
        + time_bias
    )
    pack[...] = jnp.zeros_like(pack)
    pack[0:9, :] = conv_weight[...].astype(f32)
    pack[9:10, :] = vec_at(0)
    pack[10:11, :] = vec_at(1)
    pack[11 : 11 + NLAT, :] = mod[:, :cols]
    pack[11 + NLAT : 11 + 2 * NLAT, :] = mod[:, cols:]
    packed[me] = pack[...]
    pack_copies = [
        seq_copy(
            pack,
            packed.at[me],
            pack_sems.at[0, step - 1],
            pack_sems.at[1, step - 1],
            lax.rem(me + step, shards),
        )
        for step in range(1, shards)
    ]
    held[pl.ds(EDGE, rows), :] = hidden[...]
    finish = exchange_edges(held, edge_sems, rows, shards)
    for copy in pack_copies:
        copy.start()
    finish()
    fc2_shard.begin()
    out_shard.begin()
    ctx_gather.start()
    cot_full[me] = cot.wait()[...]
    cot_gather.start()
    emit(held)
    tile_loop(
        floats.shape[0] // 32,
        lambda i: floats.__setitem__(
            (pl.ds(i * 32, 32), slice(None)), held[pl.ds(i * 32, 32), :].astype(f32)
        ),
    )
    for copy in pack_copies:
        copy.wait()
    wide[...] = jnp.zeros_like(wide)
    wide[0:16, :] = jnp.concatenate([packed[j, 0:16, :] for j in range(shards)], axis=1)
    for low, device in ((WIDE_SCALE, 0), (WIDE_SHIFT, shards // 2)):
        parts = []
        for j in range(device, device + shards // 2):
            parts.append(packed[j, 11 : 11 + NLAT, :])
            parts.append(packed[j, 11 + NLAT : 11 + 2 * NLAT, :])
        wide[low : low + NLAT, :] = jnp.concatenate(parts, axis=1)
    positions = me * rows + lax.broadcasted_iota(jnp.int32, (rows, 1), 0)
    masks = [latents.valid(positions, tap // 3 - 1, tap % 3 - 1) for tap in range(9)]

    def conv_tile(index):
        cols = pl.ds(pl.multiple_of(index * 256, 256), 256)
        total = jnp.broadcast_to(wide[9:10, cols], (rows, 256))
        for tap in range(9):
            offset = EDGE + (tap // 3 - 1) * WMAX + tap % 3 - 1
            total = total + (
                floats[offset : offset + rows, cols] * wide[tap : tap + 1, cols]
            ) * masks[tap]
        conv[:, cols] = total

    tile_loop(C // 256, conv_tile)

    def norm_tile(index):
        here = pl.ds(pl.multiple_of(index * 16, 16), 16)
        values, factor = stats_of(conv[here, :])
        normed[here, :] = values
        inverse[here, :] = factor
        full[me, here, :] = values.astype(full.dtype)

    tile_loop(rows // 16, norm_tile)
    energy[...] = jnp.zeros_like(energy)
    fc1 = fc1.wait()
    emit(wide, normed)

    def visit(block):
        pre[block] = (
            jnp.dot(full[block], fc1[...], preferred_element_type=f32) + fc1_bias
        )

        def tile(index):
            here = pl.ds(pl.multiple_of(index * 32, 32), 32)
            value = pre[block, here, :]
            value = value * (0.5 * (1.0 + lax.erf(value * ROOT_HALF)))
            act[block, here, :] = value
            square = value * value
            pick = latents.picks(block * rows + index * 32, 32)
            for latent in range(NLAT):
                energy[latent : latent + 1, :] += jnp.sum(
                    square * pick[latent], axis=0, keepdims=True
                )

        tile_loop(rows // 32, tile)

    def hook(hops):
        @pl.when(hops == 1)
        def _():
            ctx_gather.cross()
            ctx_gather.hop(1)

        @pl.when(hops == 2)
        def _():
            fc2_shard.share()
            out_shard.share()
            ctx_gather.hop(2)
            cot_gather.cross()
            cot_gather.hop(1)

        @pl.when(hops == 3)
        def _():
            ctx_gather.hop(3)

    Gather(full, gather_sems, depth, rows // 8).run(visit, hook)
    emit(full, pre)
    cot_gather.hop(2)
    fc2_shard.share_core()
    out_shard.share_core()
    root = jnp.sqrt(energy[...] + 1.0)
    mine[...] = jnp.broadcast_to(jnp.sum(root, axis=1, keepdims=True), mine.shape)
    denom = peer_total(mine, theirs, total_sems, shards) / FF + EPS_NORM
    ratio = root / denom[:, 0:1]
    cot_gather.hop(3)
    root_out[...] = root
    denom_out[...] = denom
    ratio_out[...] = ratio
    scaled = ratio * gamma + 1.0

    def respond(index):
        block = index // (rows // 32)
        here = pl.ds(pl.multiple_of(lax.rem(index, rows // 32) * 32, 32), 32)
        response[block, here, :] = (
            act[block, here, :] * rows_of(latents.picks(index * 32, 32), scaled) + beta
        ).astype(response.dtype)

    tile_loop(shards * rows // 32, respond)
    emit(response)
    ctx_gather.finish()
    emit(ctx_full)
    fc2_shard.finish()
    emit(fc2_rows)
    out_shard.finish()
    for quarter in range(4):
        side_by_side(
            out_rows, quarter * out_units, lambda j, quarter=quarter: out_parts[j, quarter], shards
        )
    cot_gather.finish()


def mixed_in_kernel(
    shards,
    emit,
    shape,
    response,
    fc2,
    hidden,
    wide,
    w_qkv,
    vec,
    context,
    full,
    first,
    second,
    normed,
    inverse,
    queries,
    keys,
    values,
    acc,
    to_y,
    from_y,
    to_z,
    from_z,
    y_sems,
    z_sems,
    gather_sems,
):
    f32 = jnp.float32
    rows = acc.shape[0]
    depth = shards // 2
    me = lax.axis_index("seq")
    meet_all(shards)
    latents = Latents(shape, shards * rows)
    cols = keys.shape[0]
    base = vec.shape[1] - VEC_TAIL
    q_bias = vec[:, base + 2 * VEC_STEP : base + 2 * VEC_STEP + cols]
    v_bias = column_of(vec[:, base + 3 * VEC_STEP : base + 4 * VEC_STEP])[:cols]
    bias = wide[10:11, :]
    scale, shift = wide[WIDE_SCALE : WIDE_SCALE + 8, :], wide[WIDE_SHIFT : WIDE_SHIFT + 8, :]

    def partial(block):
        return dot_nt(response[block], fc2[...])

    scatter_blocks(partial, to_y, from_y, to_z, from_z, acc, y_sems, z_sems, depth)

    hidden = hidden.wait()

    def norm_tile(index):
        here = pl.ds(pl.multiple_of(index * 16, 16), 16)
        one = hidden[here, :].astype(f32) + acc[here, :] + bias
        pick = latents.picks(me * rows + index * 16, 16)
        two = one * (1.0 + rows_of(pick, scale)) + rows_of(pick, shift)
        first[here, :] = one
        second[here, :] = two
        value, factor = stats_of(two)
        normed[here, :] = value
        inverse[here, :] = factor
        full[me, here, :] = value.astype(full.dtype)

    tile_loop(rows // 16, norm_tile)
    emit(first, second, normed)
    w_qkv, context = w_qkv.wait(), context.wait()

    side = jnp.dot(w_qkv[cols:, :], context[...], preferred_element_type=f32)
    keys[:, shards * rows :] = side[:cols].astype(keys.dtype)
    values[:, shards * rows :] = (side[cols:] + v_bias).astype(values.dtype)

    def visit(block):
        value = full[block]
        query = dot_nt(value, w_qkv[:cols, :]) + q_bias
        queries[block] = query.astype(queries.dtype)
        here = pl.ds(pl.multiple_of(block * rows, 128), rows)
        side = dot_nt(w_qkv[cols:, :], value)
        keys[:, here] = side[:cols].astype(keys.dtype)
        values[:, here] = (side[cols:] + v_bias).astype(values.dtype)

    Gather(full, gather_sems, depth, rows // 8).run(visit)


def attend_kernel(
    shards,
    emit,
    shape,
    queries,
    keys,
    values,
    cot,
    out_rows,
    d_qkv,
    mixed,
    cot_cols,
    dk_sum,
    dv_sum,
    probs_at,
    sems,
):
    f32, bf16 = jnp.float32, jnp.bfloat16
    cols = keys.shape[0]
    heads = cols // HEAD_DIM
    tiles, tile_rows = mixed.shape[0], mixed.shape[3]
    span = tile_rows // queries.shape[1]
    depth = shards // 2
    me = lax.axis_index("seq")
    meet_all(shards)
    latents = Latents(shape, tiles * tile_rows)
    place_at = lax.broadcasted_iota(jnp.int32, (1, keys.shape[1]), 1)
    token = place_at - tiles * tile_rows
    of_token = jnp.full_like(token, -1)
    for latent in range(NLAT):
        inside = (token >= latent * NCTX) & (token < (latent + 1) * NCTX)
        of_token = jnp.where(inside, latent, of_token)
    k_segment = jnp.where(token < 0, latents.segment(place_at), of_token)
    dk_sum[...] = jnp.zeros_like(dk_sum)
    dv_sum[...] = jnp.zeros_like(dv_sum)

    def gather_of(tile):
        return Gather(mixed.at[tile], sems.at[tile], depth)

    def step(tile, carry):
        blocks = pl.ds(tile * span, span)
        here = pl.ds(pl.multiple_of(tile * tile_rows, 128), tile_rows)
        query = queries[blocks].reshape(tile_rows, cols) * SCORE_SCALE
        cot_tile = cot[blocks].reshape(tile_rows, C)
        for j in range(shards):

            @pl.when(me == j)
            def _():
                cot_cols[:, here] = cot_tile[:, j * cols : (j + 1) * cols].T

        d_mixed = dot_nt(cot_tile, out_rows[...]).astype(bf16)
        q_segment = latents.segment(
            tile * tile_rows + lax.broadcasted_iota(jnp.int32, (tile_rows, 1), 0)
        )
        bias = jnp.where(q_segment == k_segment, 0.0, MASKED)
        mixed_parts, d_query_parts = [], []
        for head in range(heads):
            own = slice(head * HEAD_DIM, (head + 1) * HEAD_DIM)
            scores = jnp.dot(query[:, own], keys[own, :], preferred_element_type=f32) + bias
            expo = jnp.exp(scores - jnp.max(scores, axis=-1, keepdims=True))
            probs_at[head] = expo * (1.0 / jnp.sum(expo, axis=-1, keepdims=True))
            mixed_parts.append(dot_nt(probs_at[head].astype(bf16), values[own, :]))
        mixed[tile, me] = jnp.concatenate(mixed_parts, axis=1).T.astype(bf16)
        gather_of(tile).start()
        for hops in range(1, depth):

            @pl.when(tile >= hops)
            def _():
                if hops == 1:
                    gather_of(tile - 1).cross()
                gather_of(tile - hops).hop(hops)

        for head in range(heads):
            own = slice(head * HEAD_DIM, (head + 1) * HEAD_DIM)
            dm_head = d_mixed[:, own]
            delta = jnp.sum(dm_head.astype(f32) * mixed_parts[head], axis=-1, keepdims=True)
            d_probs = jnp.dot(dm_head, values[own, :], preferred_element_type=f32)
            d_scores = (probs_at[head] * (d_probs - delta)).astype(bf16)
            d_query_parts.append(dot_nt(d_scores, keys[own, :]) * SCORE_SCALE)
            dk_sum[own, :] += dot_tn(query[:, own], d_scores)
            dv_sum[own, :] += dot_tn(dm_head, probs_at[head].astype(bf16))
        d_qkv[:cols, here] = jnp.concatenate(d_query_parts, axis=1).T.astype(bf16)
        return carry

    lax.fori_loop(0, tiles, step, 0)
    for late in range(1, depth):
        for hops in range(late, depth):
            if hops == 1:
                gather_of(tiles - 1).cross()
            gather_of(tiles - 1 + late - hops).hop(hops)
    d_qkv[:cols, tiles * tile_rows :] = jnp.zeros(
        (cols, d_qkv.shape[1] - tiles * tile_rows), bf16
    )
    d_qkv[cols : 2 * cols, :] = dk_sum[...].astype(bf16)
    d_qkv[2 * cols :, :] = dv_sum[...].astype(bf16)

    def close(tile, carry):
        gather_of(tile).finish()
        return carry

    lax.fori_loop(0, tiles, close, 0)


def norm_back(gradient, normed, inverse):
    mean_grad = jnp.mean(gradient, axis=-1, keepdims=True)
    mean_mixed = jnp.mean(gradient * normed, axis=-1, keepdims=True)
    return inverse * (gradient - mean_grad - normed * mean_mixed)


def attn_back_kernel(
    shards,
    emit,
    shape,
    cond,
    d_qkv,
    w_qkv,
    attn,
    context,
    mixed,
    cot_cols,
    out_weight,
    vec,
    cot,
    normed,
    inverse,
    first,
    wide,
    fc2,
    pre,
    root,
    ratio,
    denom,
    response,
    context_in,
    full,
    d_first,
    d_pre,
    small_out,
    weight_grads,
    map_grad,
    act_out,
    fc2_half,
    d_mod,
    small,
    acc,
    d_resp,
    act,
    sums,
    mine,
    theirs,
    to_y,
    from_y,
    to_z,
    from_z,
    y_sems,
    z_sems,
    gather_sems,
    total_sems,
    g_own,
    g_got,
    g_other,
    g_sems,
    mod_in,
    mod_sems,
    fc2_own,
    fc2_got,
    fc2_sems,
    ctx_out,
    ctx_in,
    ctx_sems,
):
    f32 = jnp.float32
    rows = acc.shape[0]
    depth = shards // 2
    me = lax.axis_index("seq")
    meet_all(shards, lax.axis_size("grp"))
    cols = ctx_out.shape[1]
    total = shards * rows
    latents = Latents(shape, total)
    base = vec.shape[1] - VEC_TAIL
    width_one = base // 3
    gamma = vec[:, width_one : 2 * width_one]
    out_bias = column_of(vec[:, base + 4 * VEC_STEP : base + 5 * VEC_STEP])[:cols]
    scale = wide[WIDE_SCALE : WIDE_SCALE + 8, :]
    later = (attn, context, mixed, cot_cols, out_weight)
    weight_sum = PairSum(g_own, g_got, g_other, weight_grads, g_sems)
    peers = [lax.rem(me + step, shards) for step in range(1, shards)]
    ctx_copies = [
        seq_copy(ctx_out.at[peer], ctx_in.at[me], ctx_sems.at[0, n], ctx_sems.at[1, n], peer)
        for n, peer in enumerate(peers)
    ]
    fc2_sum = CoreHalf(fc2_own, fc2_got, fc2_half, fc2_sems)

    def partial(block):
        here = pl.ds(pl.multiple_of(block * rows, 128), rows)
        return dot_tn(d_qkv[:, here], w_qkv[...])

    def between():
        low_type = ctx_out.dtype
        attn, context, mixed, cot_cols, out_weight = (item.wait() for item in later)
        for device in range(shards):
            ctx_out[device] = dot_tn(
                w_qkv[:, device * cols : (device + 1) * cols], d_qkv[:, total:]
            ).astype(low_type)
        g_own[: 3 * cols, :] = (
            jnp.dot(d_qkv[:, :total], attn[...].reshape(total, C), preferred_element_type=f32)
            + dot_nt(d_qkv[:, total:], context[...])
        ).astype(low_type)
        grad = None
        for tile in range(mixed.shape[0]):
            here = slice(tile * mixed.shape[3], (tile + 1) * mixed.shape[3])
            block = mixed[tile].reshape(C, mixed.shape[3])
            act_out[:, here] = (
                jnp.dot(out_weight[...], block, preferred_element_type=f32) + out_bias
            ).astype(low_type)
            part = dot_nt(cot_cols[:, here], block)
            grad = part if grad is None else grad + part
        g_own[3 * cols :, :] = grad.astype(low_type)
        weight_sum.begin()

    def scatter_hook(step):
        @pl.when(step == 1)
        def _():
            weight_sum.across()

    scatter_blocks(
        partial, to_y, from_y, to_z, from_z, acc, y_sems, z_sems, depth, between, scatter_hook
    )
    d_mod[...] = jnp.zeros_like(d_mod)
    cot, normed, first = cot.wait(), normed.wait(), first.wait()

    def norm_tile(index):
        here = pl.ds(pl.multiple_of(index * 16, 16), 16)
        d_second = cot[here, :].astype(f32) + norm_back(
            acc[here, :], normed[here, :], inverse[here, :]
        )
        pick = latents.picks(me * rows + index * 16, 16)
        value = d_second * (1.0 + rows_of(pick, scale))
        d_first[here, :] = value
        full[me, here, :] = value.astype(full.dtype)
        scaled = d_second * first[here, :]
        for latent in range(NLAT):
            chosen = pick[latent]
            d_mod[2 * latent : 2 * latent + 1, :] += jnp.sum(scaled * chosen, axis=0, keepdims=True)
            d_mod[2 * latent + 1 : 2 * latent + 2, :] += jnp.sum(
                d_second * chosen, axis=0, keepdims=True
            )

    tile_loop(rows // 16, norm_tile)
    sums[...] = jnp.zeros_like(sums)
    emit(d_first)
    fc2, pre = fc2.wait(), pre.wait()
    wide_mod = 2 * cols
    half = shards // 2

    def mod_part(device):
        low = pl.multiple_of(lax.rem(device, half) * wide_mod, 128)
        return d_mod.at[:, pl.ds(low, wide_mod)]

    mod_in[me] = mod_part(me)[...]
    mod_copies = [
        seq_copy(mod_part(peer), mod_in.at[me], mod_sems.at[0, k], mod_sems.at[1, k], peer)
        for k, peer in enumerate(peers)
    ]
    for copy in mod_copies:
        copy.start()

    def gather_hook(hops):
        @pl.when(hops == 2)
        def _():
            weight_sum.share()

    def visit(block):
        d_resp[block] = jnp.dot(full[block], fc2[...], preferred_element_type=f32)

        def tile(index):
            here = pl.ds(pl.multiple_of(index * 32, 32), 32)
            value = pre[block, here, :]
            phi = 0.5 * (1.0 + lax.erf(value * ROOT_HALF))
            pre[block, here, :] = phi + value * (DENSITY * jnp.exp(-0.5 * value * value))
            value = value * phi
            act[block, here, :] = value.astype(act.dtype)
            pull = d_resp[block, here, :]
            sums[NLAT : NLAT + 1, :] += jnp.sum(pull, axis=0, keepdims=True)
            pull = pull * value
            pick = latents.picks(block * rows + index * 32, 32)
            for latent in range(NLAT):
                sums[latent : latent + 1, :] += jnp.sum(
                    pull * pick[latent], axis=0, keepdims=True
                )

        tile_loop(rows // 32, tile)

    Gather(full, gather_sems, depth, rows // 8).run(visit, gather_hook)
    emit(full)
    small[...] = jnp.zeros_like(small)
    wide_row = 2 * cols

    def keep(row, value):
        for part in range(value.shape[1] // wide_row):
            small[row + part : row + part + 1, :] = value[
                :, part * wide_row : (part + 1) * wide_row
            ]

    keep(SMALL_BETA, sums[NLAT : NLAT + 1, :])
    pulls = sums[...]
    keep(SMALL_GAMMA, jnp.sum(pulls[:NLAT] * ratio[:NLAT, :], axis=0, keepdims=True))
    d_ratio = pulls * gamma
    mine[...] = jnp.broadcast_to(jnp.sum(d_ratio * root[...], axis=1, keepdims=True), mine.shape)

    def meanwhile():
        for copy in ctx_copies:
            copy.start()
        ctx_in[me] = ctx_out[me]
        right = response.wait()[...].reshape(total, width_one)
        units = fc2_own.shape[2]
        for goal in range(0, shards, 4):
            here = slice(goal * 4 * units, (goal + 4) * 4 * units)
            part = dot_tn(full[:, :, here].reshape(total, 16 * units), right)
            fc2_own[goal : goal + 4] = part.reshape(4, 4, units, width_one).astype(fc2_own.dtype)
        fc2_sum.begin()

    pulled = peer_total(mine, theirs, total_sems, shards, meanwhile)[:, 0:1]
    below = denom[:, 0:1]
    d_root = d_ratio / below - pulled / (FF * below * below)
    back = d_root / root[...]
    scaled = ratio[...] * gamma + 1.0
    sums[0:1, :] = jnp.zeros((1, width_one), f32)

    def respond(index):
        block = index // (rows // 32)
        here = pl.ds(pl.multiple_of(lax.rem(index, rows // 32) * 32, 32), 32)
        pick = latents.picks(index * 32, 32)
        d_act = d_resp[block, here, :] * rows_of(pick, scaled) + act[block, here, :].astype(f32) * rows_of(
            pick, back
        )
        value = (d_act * pre[block, here, :]).astype(d_pre.dtype)
        d_pre[block, here, :] = value
        sums[0:1, :] += jnp.sum(value.astype(f32), axis=0, keepdims=True)

    tile_loop(shards * rows // 32, respond)
    emit(d_pre)
    for copy in mod_copies:
        copy.wait()
    mod_sum = mod_in[0]
    for device in range(1, shards):
        mod_sum = mod_sum + mod_in[device]
    keep(SMALL_FC1, sums[0:1, :])
    fc2_sum.finish()
    emit(fc2_half)
    chosen = [
        jnp.where(me < half, mod_sum[2 * n : 2 * n + 1], mod_sum[2 * n + 1 : 2 * n + 2])
        for n in range(NLAT)
    ]
    chosen = jnp.concatenate(chosen, axis=0)
    small[0:SMALL_FC1, :] = lax.dot_general(
        cond[...],
        chosen,
        (((0,), (0,)), ((), ())),
        precision=HIGHEST_PRECISION,
        preferred_element_type=f32,
    )
    keep(SMALL_TIME, jnp.sum(chosen, axis=0, keepdims=True))
    ones = lambda values: jnp.ones((8, values.shape[1]), values.dtype)
    for row, value in (
        (SMALL_QUERY, d_qkv[:cols, :]),
        (SMALL_VALUE, d_qkv[2 * cols :, :]),
        (SMALL_OUT, later[3].buffer[...]),
    ):
        small[row : row + 1, :cols] = dot_nt(ones(value), value)[0:1]
    for copy in ctx_copies:
        copy.wait()
    context_sum = ctx_in[0].astype(f32)
    for device in range(1, shards):
        context_sum = context_sum + ctx_in[device].astype(f32)
    at = lax.broadcasted_iota(jnp.int32, (1, context_sum.shape[1]), 1)
    context_sum = jnp.where(at < NLAT * NCTX, context_sum, 0.0)
    map_grad[...] = jnp.dot(
        context_sum.astype(map_grad.dtype), context_in.wait()[...], preferred_element_type=f32
    ).astype(map_grad.dtype)
    small[SMALL_MAP : SMALL_MAP + 1, :cols] = lax.dot_general(
        ones(context_sum),
        context_sum,
        (((1,), (1,)), ((), ())),
        precision=HIGHEST_PRECISION,
        preferred_element_type=f32,
    )[0:1]
    small_out[...] = small[...].astype(small_out.dtype)
    weight_sum.finish()


def conv_back_kernel(
    shards,
    emit,
    shape,
    d_pre,
    fc1,
    normed,
    inverse,
    d_first,
    hidden,
    wide,
    normed_full,
    branch,
    map_grad,
    act_out,
    second,
    fc2_half,
    small,
    input_grad,
    fc1_sum,
    fc2_sum,
    map_sum,
    small_sum,
    conv_sum,
    activations,
    held,
    floats,
    acc,
    to_y,
    from_y,
    to_z,
    from_z,
    y_sems,
    z_sems,
    edge_sems,
    d_conv_params,
    fc1_own,
    fc1_got,
    fc1_other,
    fc2_other,
    fc2_part,
    map_own,
    map_got,
    map_other,
    pair_sems,
    fc2_sems,
    small_in,
    small_sems,
    conv_out,
    conv_in,
    conv_part,
    conv_group,
    conv_sems,
    act_in,
    act_sems,
):
    f32 = jnp.float32
    rows = acc.shape[0]
    depth = shards // 2
    groups = lax.axis_size("grp")
    me = lax.axis_index("seq")
    meet_all(shards, groups)
    cols = conv_part.shape[1]
    width = d_pre.shape[2]
    total = shards * rows
    latents = Latents(shape, total)
    positions = me * rows + lax.broadcasted_iota(jnp.int32, (rows, 1), 0)
    fc1_pair = PairSum(fc1_own, fc1_got, fc1_other, fc1_sum, pair_sems.at[0])
    map_pair = PairSum(map_own, map_got, map_other, map_sum, pair_sems.at[1])
    fc2_quarter = QuarterSum(shards, fc2_half, fc2_other, fc2_part, fc2_sum, fc2_sems)
    group = lax.axis_index("grp")
    small_copies = [
        grp_copy(
            small,
            small_in.at[step - 1],
            small_sems.at[0, step - 1],
            small_sems.at[1, step - 1],
            lax.rem(group + step, groups),
        )
        for step in range(1, groups)
    ]

    def partial(block):
        return dot_nt(d_pre[block], fc1[...])

    peers = [lax.rem(me + step, shards) for step in range(1, shards)]
    act_copies = []
    for n, peer in enumerate(peers):
        there = pl.ds(pl.multiple_of(peer * rows, 128), rows)
        act_copies.append(
            seq_copy(act_out.at[:, there], act_in.at[me], act_sems.at[0, n], act_sems.at[1, n], peer)
        )

    def fc1_grad():
        full = normed_full.wait()

        def tile(index):
            here = pl.ds(pl.multiple_of(index * 256, 256), 256)
            fc1_own[here, :] = dot_tn(
                full[:, :, here].reshape(total, 256), d_pre[...].reshape(total, width)
            ).astype(fc1_own.dtype)

        tile_loop(C // 256, tile)
        fc1_pair.begin()

    fc2_quarter.begin()
    map_own[...] = map_grad[...]
    map_pair.begin()

    def early(step):
        @pl.when(step == 1)
        def _():
            for copy in act_copies:
                copy.start()
            fc1_grad()

    def scatter_hook(step):
        @pl.when(step == 1)
        def _():
            fc2_quarter.spread()
            fc1_pair.across()
            map_pair.across()

    scatter_blocks(
        partial,
        to_y,
        from_y,
        to_z,
        from_z,
        acc,
        y_sems,
        z_sems,
        depth,
        None,
        scatter_hook,
        early,
    )
    normed, d_first, hidden = normed.wait(), d_first.wait(), hidden.wait()

    def norm_tile(index):
        start = pl.multiple_of(index * 16, 16)
        here = pl.ds(start, 16)
        held[pl.ds(EDGE + start, 16), :] = norm_back(
            acc[here, :], normed[here, :], inverse[here, :]
        ).astype(held.dtype)

    tile_loop(rows // 16, norm_tile)
    finish = exchange_edges(held, edge_sems, rows, shards)
    for copy in small_copies:
        copy.start()
    fc2_quarter.share()
    tile_loop(
        floats.shape[0] // 32,
        lambda i: floats.__setitem__(
            (pl.ds(i * 32, 32), slice(None)), hidden[pl.ds(i * 32, 32), :].astype(f32)
        ),
    )
    d_conv_params[...] = jnp.zeros_like(d_conv_params)
    masks = [latents.valid(positions, tap // 3 - 1, tap % 3 - 1) for tap in range(9)]

    def grad_tile(index):
        cols = pl.ds(pl.multiple_of(index * 256, 256), 256)
        d_conv = held[pl.ds(EDGE, rows), cols].astype(f32)
        d_conv_params[9:10, cols] = jnp.sum(d_conv, axis=0, keepdims=True)
        d_conv_params[10:11, cols] = jnp.sum(branch[:, cols].astype(f32), axis=0, keepdims=True)
        for tap in range(9):
            offset = EDGE + (tap // 3 - 1) * WMAX + tap % 3 - 1
            d_conv_params[tap : tap + 1, cols] = jnp.sum(
                d_conv * floats[offset : offset + rows, cols] * masks[tap],
                axis=0,
                keepdims=True,
            )

    tile_loop(C // 256, grad_tile)
    for goal in range(shards):
        conv_out[goal] = d_conv_params[:, goal * cols : (goal + 1) * cols]
    conv_in[me] = conv_out[me]
    conv_copies = []
    for step in range(1, shards):
        goal = lax.rem(me + step, shards)
        conv_copies.append(
            seq_copy(
                conv_out.at[goal],
                conv_in.at[me],
                conv_sems.at[0, step - 1],
                conv_sems.at[1, step - 1],
                goal,
            )
        )
        conv_copies[-1].start()
    finish()
    act_in[me] = act_out[:, pl.ds(pl.multiple_of(me * rows, 128), rows)]
    tile_loop(
        floats.shape[0] // 32,
        lambda i: floats.__setitem__(
            (pl.ds(i * 32, 32), slice(None)), held[pl.ds(i * 32, 32), :].astype(f32)
        ),
    )

    back_masks = []
    for tap in range(9):
        down_step, side_step = tap // 3 - 1, tap % 3 - 1
        back_masks.append(
            latents.valid(positions - down_step * WMAX - side_step, down_step, side_step)
        )

    def input_tile(index):
        cols = pl.ds(pl.multiple_of(index * 256, 256), 256)
        total = d_first[:, cols]
        for tap in range(9):
            offset = EDGE - (tap // 3 - 1) * WMAX - tap % 3 + 1
            total = total + (
                floats[offset : offset + rows, cols] * wide[tap : tap + 1, cols]
            ) * back_masks[tap]
        input_grad[:, cols] = total

    for copy in conv_copies:
        copy.wait()
    conv_total = conv_in[0]
    for device in range(1, shards):
        conv_total = conv_total + conv_in[device]
    tile_loop(C // 256, input_tile)
    fc1_pair.share()
    conv_part[...] = conv_total
    group_copies = []
    for step in range(1, groups):
        k = shards - 2 + step
        group_copies.append(
            grp_copy(
                conv_part,
                conv_group.at[step - 1],
                conv_sems.at[0, k],
                conv_sems.at[1, k],
                lax.rem(group + step, groups),
            )
        )
        group_copies[-1].start()
    fc2_quarter.share_core()
    for copy in act_copies:
        copy.wait()
    activations[...] = (second.wait()[...] + act_in[...].reshape(C, rows).astype(f32).T).astype(
        activations.dtype
    )
    map_pair.share()
    for copy in (*small_copies, *group_copies):
        copy.wait()
    small_total = small[...].astype(f32)
    for step in range(groups - 1):
        small_total = small_total + small_in[step].astype(f32)
    small_sum[...] = small_total
    conv_sum[...] = conv_part[...] + conv_group[0] + conv_group[1] + conv_group[2]
    fc2_quarter.finish()
    emit(fc2_sum)
    map_pair.finish()
    fc1_pair.finish()


class Late:
    def __init__(self, buffer, copy):
        self.buffer, self.copy = buffer, copy

    def wait(self):
        self.copy.wait()
        return self.buffer


def staged_body(body, n_in, n_out, late, staged):
    def run(*refs):
        ins, outs = list(refs[:n_in]), list(refs[n_in : n_in + n_out])
        rest = refs[n_in + n_out :]
        count = len(late) + len(staged)
        if not count:
            body(lambda *buffers: None, *refs)
            return
        kept, buffers, sems = rest[: -count - 1], rest[-count - 1 : -1], rest[-1]
        for n, k in enumerate(late):
            copy = pltpu.make_async_copy(ins[k], buffers[n], sems.at[n])
            copy.start()
            ins[k] = Late(buffers[n], copy)
        waiting = []
        for n, k in enumerate(staged, len(late)):
            waiting.append([buffers[n], pltpu.make_async_copy(buffers[n], outs[k], sems.at[n]), 0])
            outs[k] = buffers[n]

        def emit(*which):
            for entry in waiting:
                if not entry[2] and any(entry[0] is ref for ref in which):
                    entry[1].start()
                    entry[2] = 1

        body(emit, *ins, *outs, *kept)
        emit(*(entry[0] for entry in waiting))
        for entry in waiting:
            entry[1].wait()

    return run


def kernel_call(
    body, name, number, outs, scratch, operands, flops=0, far=(), scalars=(), late=(), staged=()
):
    vmem, anywhere, smem = (
        pl.BlockSpec(memory_space=space) for space in (pltpu.VMEM, pl.ANY, pltpu.SMEM)
    )
    in_specs = [
        anywhere if k in far or k in late else smem if k in scalars else vmem
        for k in range(len(operands))
    ]
    shapes = [jax.ShapeDtypeStruct(shape, dtype) for shape, dtype in outs]
    moved = sum(math.prod(s.shape) * s.dtype.itemsize for s in shapes) + sum(
        x.size * x.dtype.itemsize for x in operands
    )
    extra = [pltpu.VMEM(operands[k].shape, operands[k].dtype) for k in late]
    extra += [pltpu.VMEM(shapes[k].shape, shapes[k].dtype) for k in staged]
    if extra:
        extra.append(pltpu.SemaphoreType.DMA((len(extra),)))
    return pl.pallas_call(
        staged_body(body, len(operands), len(outs), late, staged),
        out_shape=shapes,
        in_specs=in_specs,
        out_specs=[anywhere if k in staged else vmem for k in range(len(shapes))],
        scratch_shapes=[*scratch, *extra],
        name=name,
        cost_estimate=pl.CostEstimate(flops=flops, bytes_accessed=moved, transcendentals=0),
        compiler_params=pltpu.CompilerParams(
            collective_id=number, has_side_effects=True, vmem_limit_bytes=VMEM_BYTES
        ),
    )(*operands)


def scatter_scratch(rows, depth):
    bf16 = jnp.bfloat16
    return [
        pltpu.VMEM((depth, rows, C), bf16),
        pltpu.VMEM((depth, rows, C), bf16),
        pltpu.VMEM((depth, rows, C), bf16),
        pltpu.VMEM((depth + 1, rows, C), bf16),
        pltpu.SemaphoreType.DMA((2, depth)),
        pltpu.SemaphoreType.DMA((2, 2, depth)),
    ]


def gather_scratch(depth):
    return pltpu.SemaphoreType.DMA((6, 2, depth + 1))


def total_scratch(shards):
    return [
        pltpu.VMEM((8, 128), jnp.float32),
        pltpu.VMEM((shards - 1, 8, 128), jnp.float32),
    ], pltpu.SemaphoreType.DMA((2, shards - 1))


def on_device_heads(
    hidden,
    latent_shape,
    cond_r,
    clip,
    cotangent,
    conv_weight,
    conv_bias,
    fc1_weight,
    fc1_bias,
    grn_gamma,
    grn_beta,
    fc2_weight,
    fc2_bias,
    time_weight,
    time_bias,
    map_weight,
    map_bias,
    query_weight,
    query_bias,
    key_weight,
    value_weight,
    value_bias,
    out_weight,
    out_bias,
):
    f32, bf16 = jnp.float32, jnp.bfloat16
    shards = lax.axis_size("seq")
    rows = hidden.shape[0]
    total = rows * shards
    cols = C // shards
    depth = shards // 2
    hidden_cols = FF // shards
    me = lax.axis_index("seq")
    shape = latent_shape[0]
    slot = lambda item: jnp.pad(item, (0, VEC_STEP - item.shape[0]))
    vec = jnp.concatenate(
        [
            fc1_bias,
            grn_gamma,
            grn_beta,
            *(slot(item) for item in (conv_bias, fc2_bias, query_bias, value_bias, out_bias)),
            slot(map_bias),
            jnp.pad(time_bias, (0, 2 * VEC_STEP - time_bias.shape[0])),
        ]
    ).astype(f32)[None]
    w_qkv = jnp.concatenate([query_weight.T, key_weight.T, value_weight.T], axis=0)
    ctx_rows = 256
    context_in = jax.nn.silu(clip.reshape(NLAT * NCTX, CLIP).astype(f32)).astype(bf16)
    context_in = jnp.pad(context_in, ((0, ctx_rows - NLAT * NCTX), (0, 0)))
    ctx_cols = (against(map_weight.T, context_in) + map_bias.astype(f32)[:, None]).astype(bf16)
    units = cols // 4
    vmem = pltpu.VMEM
    total_vmem, total_sems = total_scratch(shards)
    (
        normed_full,
        held,
        wide,
        normed_one,
        inverse_one,
        pre_act,
        root,
        ratio,
        denom,
        response,
        context,
        cot_full,
        shrink_parts,
        output_rows,
    ) = kernel_call(
        functools.partial(mixer_kernel, shards),
        "mixer",
        1,
        [
            ((shards, rows, C), bf16),
            ((rows + 2 * EDGE, C), bf16),
            ((32, C), f32),
            ((rows, C), f32),
            ((rows, 1), f32),
            ((shards, rows, hidden_cols), f32),
            ((8, hidden_cols), f32),
            ((8, hidden_cols), f32),
            ((8, 128), f32),
            ((shards, rows, hidden_cols), bf16),
            ((shards, cols, ctx_rows), bf16),
            ((shards, rows, C), bf16),
            ((shards, 4, units, hidden_cols), bf16),
            ((cols, C), bf16),
        ],
        [
            vmem((24, cols), f32),
            vmem((shards, 24, cols), f32),
            vmem((rows + 2 * EDGE, C), f32),
            vmem((rows, C), f32),
            vmem((shards, rows, hidden_cols), f32),
            vmem((8, hidden_cols), f32),
            *total_vmem,
            pltpu.SemaphoreType.DMA((2, 2)),
            pltpu.SemaphoreType.DMA((2, shards - 1)),
            gather_scratch(depth),
            total_sems,
            gather_scratch(depth),
            gather_scratch(depth),
            vmem((shards, 4, units, cols), bf16),
            pltpu.SemaphoreType.DMA((2,)),
            pltpu.SemaphoreType.DMA((2, shards + 2)),
            pltpu.SemaphoreType.DMA((2, shards + 2)),
        ],
        (
            shape,
            hidden,
            cond_r,
            time_weight,
            conv_weight,
            vec,
            fc1_weight,
            ctx_cols,
            cotangent,
            fc2_weight.T,
            out_weight,
        ),
        flops=2 * total * C * hidden_cols,
        far=(9, 10),
        scalars=(0,),
        late=(6, 8),
        staged=(0, 1, 2, 3, 5, 9, 10, 11, 12),
    )
    context = context.reshape(C, ctx_rows)
    shrink_rows = shrink_parts.reshape(C, hidden_cols)
    keys_all = total + ctx_rows
    (
        attn_blocks,
        first_sum,
        second_sum,
        normed_two,
        inverse_two,
        queries,
        keys,
        values,
    ) = kernel_call(
        functools.partial(mixed_in_kernel, shards),
        "mixed_in",
        2,
        [
            ((shards, rows, C), bf16),
            ((rows, C), f32),
            ((rows, C), f32),
            ((rows, C), f32),
            ((rows, 1), f32),
            ((shards, rows, cols), bf16),
            ((cols, keys_all), bf16),
            ((cols, keys_all), bf16),
        ],
        [pltpu.VMEM((rows, C), f32), *scatter_scratch(rows, depth), gather_scratch(depth)],
        (
            shape,
            response,
            shrink_rows,
            hidden,
            wide,
            w_qkv,
            vec,
            context,
        ),
        flops=2 * total * C * (hidden_cols + 3 * cols),
        scalars=(0,),
        late=(3, 5, 7),
        staged=(0, 1, 2, 3, 5, 6, 7),
    )

    tiles, tile_rows = 4, total // 4
    d_qkv, mixed_full, cot_cols = kernel_call(
        functools.partial(attend_kernel, shards),
        "attend",
        5,
        [
            ((3 * cols, keys_all), bf16),
            ((tiles, shards, cols, tile_rows), bf16),
            ((cols, total), bf16),
        ],
        [
            vmem((cols, keys_all), f32),
            vmem((cols, keys_all), f32),
            vmem((cols // HEAD_DIM, tile_rows, keys_all), f32),
            pltpu.SemaphoreType.DMA((tiles, 6, 2, depth + 1)),
        ],
        (
            shape,
            queries,
            keys,
            values,
            cot_full,
            output_rows,
        ),
        flops=12 * total * keys_all * 3 * 256,
        scalars=(0,),
    )
    (
        branch_blocks,
        d_first,
        d_pre,
        small,
        weight_sums,
        grad_map_w,
        act_cols,
        fc2_half,
    ) = kernel_call(
        functools.partial(attn_back_kernel, shards),
        "attn_back",
        3,
        [
            ((shards, rows, C), bf16),
            ((rows, C), f32),
            ((shards, rows, hidden_cols), bf16),
            ((SMALL_ROWS, 2 * cols), bf16),
            ((4 * cols, C), bf16),
            ((cols, CLIP), bf16),
            ((cols, total), bf16),
            ((shards, 2, units, hidden_cols), bf16),
        ],
        [
            vmem((8, C), f32),
            vmem((SMALL_ROWS, 2 * cols), f32),
            pltpu.VMEM((rows, C), f32),
            pltpu.VMEM((shards, rows, hidden_cols), f32),
            pltpu.VMEM((shards, rows, hidden_cols), bf16),
            pltpu.VMEM((8, hidden_cols), f32),
            *total_vmem,
            *scatter_scratch(rows, depth),
            gather_scratch(depth),
            total_sems,
            vmem((4 * cols, C), bf16),
            vmem((2 * cols, C), bf16),
            vmem((2 * cols, C), bf16),
            pltpu.SemaphoreType.DMA((2, 3)),
            vmem((shards, 8, 2 * cols), f32),
            pltpu.SemaphoreType.DMA((2, shards - 1)),
            vmem((shards, 4, units, hidden_cols), bf16),
            vmem((2, shards, units, hidden_cols), bf16),
            pltpu.SemaphoreType.DMA((2, 2)),
            vmem((shards, cols, ctx_rows), bf16),
            vmem((shards, cols, ctx_rows), bf16),
            pltpu.SemaphoreType.DMA((2, shards - 1)),
        ],
        (
            shape,
            cond_r,
            d_qkv,
            w_qkv,
            attn_blocks,
            context,
            mixed_full,
            cot_cols,
            out_weight.T,
            vec,
            cotangent,
            normed_two,
            inverse_two,
            first_sum,
            wide,
            shrink_rows,
            pre_act,
            root,
            ratio,
            denom,
            response,
            context_in,
        ),
        flops=2 * total * C * (hidden_cols + 6 * cols),
        scalars=(0,),
        late=(4, 5, 6, 7, 8, 10, 11, 13, 15, 16, 20, 21),
        staged=(0, 1, 2, 4, 6, 7),
    )
    groups = lax.axis_size("grp")
    branch_own = lax.dynamic_index_in_dim(branch_blocks, me, 0, keepdims=False)
    input_grad, fc1_sum, fc2_sum, map_sum, small, conv_small, activations = kernel_call(
        functools.partial(conv_back_kernel, shards),
        "conv_back",
        4,
        [
            ((rows, C), f32),
            ((C, hidden_cols), bf16),
            ((cols, FF), bf16),
            ((cols, CLIP), bf16),
            ((SMALL_ROWS, 2 * cols), f32),
            ((16, cols), f32),
            ((rows, C), bf16),
        ],
        [
            vmem((rows + 2 * EDGE, C), bf16),
            vmem((rows + 2 * EDGE, C), f32),
            vmem((rows, C), f32),
            *scatter_scratch(rows, depth),
            pltpu.SemaphoreType.DMA((2, 2)),
            vmem((16, C), f32),
            vmem((C, hidden_cols), bf16),
            vmem((C // 2, hidden_cols), bf16),
            vmem((C // 2, hidden_cols), bf16),
            vmem((shards, units, hidden_cols), bf16),
            vmem((shards, units, hidden_cols), bf16),
            vmem((cols, CLIP), bf16),
            vmem((cols // 2, CLIP), bf16),
            vmem((cols // 2, CLIP), bf16),
            pltpu.SemaphoreType.DMA((2, 2, 3)),
            pltpu.SemaphoreType.DMA((2, 3 + shards)),
            vmem((groups - 1, SMALL_ROWS, 2 * cols), bf16),
            pltpu.SemaphoreType.DMA((2, groups - 1)),
            vmem((shards, 16, cols), f32),
            vmem((shards, 16, cols), f32),
            vmem((16, cols), f32),
            vmem((groups - 1, 16, cols), f32),
            pltpu.SemaphoreType.DMA((2, shards + groups - 2)),
            vmem((shards, cols, rows), bf16),
            pltpu.SemaphoreType.DMA((2, shards - 1)),
        ],
        (
            shape,
            d_pre,
            fc1_weight,
            normed_one,
            inverse_one,
            d_first,
            held,
            wide,
            normed_full,
            branch_own,
            grad_map_w,
            act_cols,
            second_sum,
            fc2_half,
            small,
        ),
        flops=6 * total * C * hidden_cols,
        scalars=(0,),
        late=(3, 5, 6, 8, 12),
        staged=(1, 2),
    )
    two = lambda row: small[row : row + 2].reshape(hidden_cols)
    one = lambda row: small[row, :cols]
    part = lambda k: weight_sums[k * cols : (k + 1) * cols].astype(f32).T
    return (
        activations,
        input_grad,
        conv_small[:9],
        conv_small[9],
        fc1_sum.astype(f32),
        two(SMALL_FC1),
        two(SMALL_GAMMA),
        two(SMALL_BETA),
        fc2_sum.astype(f32).T,
        conv_small[10],
        small[:SMALL_FC1],
        small[SMALL_TIME],
        map_sum.astype(f32).T,
        one(SMALL_MAP),
        part(0),
        one(SMALL_QUERY),
        part(1),
        part(2),
        one(SMALL_VALUE),
        part(3),
        one(SMALL_OUT),
    )


def solution(mesh):
    in_specs = (
        P(("grp", "seq"), None),
        P("grp", None, None),
        P("grp", None),
        P("grp", None, None),
        P(("grp", "seq"), None),
        P(None, "seq"),
        P("seq"),
        P(None, "seq"),
        P("seq"),
        P("seq"),
        P("seq"),
        P(None, "seq"),
        P("seq"),
        P(None, "seq"),
        P("seq"),
        P(None, "seq"),
        P("seq"),
        P(None, "seq"),
        P("seq"),
        P(None, "seq"),
        P(None, "seq"),
        P("seq"),
        P(None, "seq"),
        P("seq"),
    )
    out_specs = (
        P(("grp", "seq"), None),
        P(("grp", "seq"), None),
        P(None, "seq"),
        P("seq"),
        P(None, "seq"),
        P("seq"),
        P("seq"),
        P("seq"),
        P(None, "seq"),
        P("seq"),
        P(None, "seq"),
        P("seq"),
        P(None, "seq"),
        P("seq"),
        P(None, "seq"),
        P("seq"),
        P(None, "seq"),
        P(None, "seq"),
        P("seq"),
        P(None, "seq"),
        P("seq"),
    )
    by_heads = mesh.shape["seq"] == 8 and mesh.shape["grp"] == 4
    return jax.shard_map(
        on_device_heads if by_heads else on_device, mesh=mesh, in_specs=in_specs, out_specs=out_specs, check_vma=False
    )
```

```python
import functools
import math

import jax
import jax.numpy as jnp
from jax import lax
from jax.experimental import pallas as pl
from jax.experimental.pallas import tpu as pltpu
from jax.sharding import PartitionSpec as P

C = 1536
HEADS = 24
HEAD_DIM = 64
FF = 6144
CLIP = 1280
NCTX = 77
NLAT = 3
WMAX = 64


EPS_NORM = 1e-06
SCORE_SCALE = 0.125
MASKED = -1e30
HIGHEST_PRECISION = lax.Precision.HIGHEST


def padded_2(block, sides, width):
    for axis, dim in sides:
        count = lax.axis_size(axis)
        forward = [(i, i + 1) for i in range(count - 1)]
        backward = [(target, source) for source, target in forward]
        low = lax.ppermute(
            lax.slice_in_dim(block, block.shape[dim] - width, None, axis=dim), axis, forward
        )
        high = lax.ppermute(lax.slice_in_dim(block, 0, width, axis=dim), axis, backward)
        block = jnp.concatenate([low, block, high], axis=dim)
    return block


def latent_grid(positions, shape_row):
    latent_count = shape_row.shape[0]
    heights = shape_row[:, 0]
    latent_width = shape_row[0, 1]
    pixel_counts = heights * latent_width
    end_points = jnp.cumsum(pixel_counts)
    start_points = end_points - pixel_counts
    segment = jnp.sum((positions[:, None] >= end_points[None, :]).astype(jnp.int32), axis=1)
    segment = jnp.minimum(segment, latent_count - 1)
    picked = (segment[:, None] == jnp.arange(latent_count, dtype=jnp.int32)[None, :]).astype(
        jnp.int32
    )
    first_pixel = jnp.sum(picked * start_points[None, :], axis=1)
    height = jnp.sum(picked * heights[None, :], axis=1)
    offset_in = positions - first_pixel
    row_index = jnp.floor_divide(offset_in, latent_width)
    column = offset_in - row_index * latent_width
    return (segment, row_index, column, height, latent_width)


def valid_tap(row_index, column, height, latent_width, down_step, side_step):
    upright = (row_index + down_step >= 0) & (row_index + down_step < height)
    across = (column + side_step >= 0) & (column + side_step < latent_width)
    return (upright & across).astype(jnp.float32)


def layer_stats(values_in):
    average = jnp.mean(values_in, axis=-1, keepdims=True)
    centred = values_in - average
    variance = jnp.mean(centred * centred, axis=-1, keepdims=True)
    inverse = lax.rsqrt(variance + EPS_NORM)
    return (centred * inverse, inverse)


def layer_back(gradient, normed, inverse):
    mean_grad = jnp.mean(gradient, axis=-1, keepdims=True)
    mean_mixed = jnp.mean(gradient * normed, axis=-1, keepdims=True)
    return inverse * (gradient - mean_grad - normed * mean_mixed)


def against(values_low, weight_low):
    return lax.dot_general(
        values_low, weight_low, (((1,), (1,)), ((), ())), preferred_element_type=jnp.float32
    )


def against_exact(values_in, weight_in):
    return lax.dot_general(
        values_in,
        weight_in,
        (((1,), (1,)), ((), ())),
        precision=HIGHEST_PRECISION,
        preferred_element_type=jnp.float32,
    )


def outer_sum(left_low, right_low):
    return lax.dot_general(
        left_low, right_low, (((0,), (0,)), ((), ())), preferred_element_type=jnp.float32
    )


def column_sum(picked, values_in):
    return lax.dot_general(
        picked,
        values_in,
        (((0,), (0,)), ((), ())),
        precision=HIGHEST_PRECISION,
        preferred_element_type=jnp.float32,
    )


def exact_gelu(values_in):
    return jax.nn.gelu(values_in, approximate=False)


def block_size(row_count, shard_rows):
    shard_total = row_count // shard_rows
    return math.gcd(shard_total, max(1, 1024 // shard_rows)) * shard_rows


def on_device(
    hidden,
    latent_shape,
    cond_r,
    clip,
    cotangent,
    conv_weight,
    conv_bias,
    fc1_weight,
    fc1_bias,
    grn_gamma,
    grn_beta,
    fc2_weight,
    fc2_bias,
    time_weight,
    time_bias,
    map_weight,
    map_bias,
    query_weight,
    query_bias,
    key_weight,
    value_weight,
    value_bias,
    out_weight,
    out_bias,
):
    tok_rows = hidden.shape[0]
    positions = lax.axis_index("seq") * tok_rows + jnp.arange(tok_rows, dtype=jnp.int32)
    shape_row = latent_shape[0]
    segment, row_index, column, height, latent_width = latent_grid(positions, shape_row)
    margin = WMAX + 1
    gathered = (
        lax.all_gather(conv_weight, "seq", axis=1, tiled=True),
        lax.all_gather(conv_bias, "seq", axis=0, tiled=True),
        lax.all_gather(fc1_weight, "seq", axis=1, tiled=True),
        lax.all_gather(fc1_bias, "seq", axis=0, tiled=True),
        lax.all_gather(grn_gamma, "seq", axis=0, tiled=True),
        lax.all_gather(grn_beta, "seq", axis=0, tiled=True),
        lax.all_gather(fc2_weight, "seq", axis=1, tiled=True),
        lax.all_gather(fc2_bias, "seq", axis=0, tiled=True),
        lax.all_gather(time_weight, "seq", axis=1, tiled=True),
        lax.all_gather(time_bias, "seq", axis=0, tiled=True),
        lax.all_gather(map_weight, "seq", axis=1, tiled=True),
        lax.all_gather(map_bias, "seq", axis=0, tiled=True),
        lax.all_gather(query_weight, "seq", axis=1, tiled=True),
        lax.all_gather(query_bias, "seq", axis=0, tiled=True),
        lax.all_gather(key_weight, "seq", axis=1, tiled=True),
        lax.all_gather(value_weight, "seq", axis=1, tiled=True),
        lax.all_gather(value_bias, "seq", axis=0, tiled=True),
        lax.all_gather(out_weight, "seq", axis=1, tiled=True),
        lax.all_gather(out_bias, "seq", axis=0, tiled=True),
    )
    (
        kernel_full,
        kernel_bias,
        expand_full,
        expand_bias,
        gamma_full,
        beta_full,
        shrink_full,
        shrink_bias,
        time_full,
        time_bias_full,
        mapper_full,
        mapper_bias,
        query_full,
        query_bias_full,
        key_full,
        value_full,
        value_bias_full,
        output_full,
        output_bias_full,
    ) = gathered
    padded = padded_2(hidden, (("seq", 0),), margin)
    conv_out = jnp.broadcast_to(kernel_bias.astype(jnp.float32)[None, :], (tok_rows, C))
    tap_list = []
    for down_step in (-1, 0, 1):
        for side_step in (-1, 0, 1):
            tap_number = 3 * (down_step + 1) + (side_step + 1)
            valid = valid_tap(row_index, column, height, latent_width, down_step, side_step)
            offset_rows = down_step * latent_width + side_step
            nearby = lax.dynamic_slice_in_dim(padded, margin + offset_rows, tok_rows, 0).astype(
                jnp.float32
            )
            conv_out = (
                conv_out
                + kernel_full[tap_number].astype(jnp.float32)[None, :] * nearby * valid[:, None]
            )
            tap_list.append((tap_number, down_step, side_step, offset_rows, valid))
    normed_one, inverse_one = layer_stats(conv_out)
    normed_low = normed_one.astype(jnp.bfloat16)
    pre_act = jnp.dot(
        normed_low, expand_full, preferred_element_type=jnp.float32
    ) + expand_bias.astype(jnp.float32)
    activated, gelu_pull = jax.vjp(exact_gelu, pre_act)
    picked = (segment[:, None] == jnp.arange(NLAT, dtype=jnp.int32)[None, :]).astype(jnp.float32)
    energy = lax.psum(column_sum(picked, activated * activated), "seq")
    root = jnp.sqrt(energy + 1.0)
    denom = jnp.mean(root, axis=-1, keepdims=True) + EPS_NORM
    ratio = root / denom
    ratio_rows = jnp.dot(picked, ratio, precision=HIGHEST_PRECISION)
    gamma_value = gamma_full.astype(jnp.float32)
    response = gamma_value * (activated * ratio_rows) + beta_full.astype(jnp.float32) + activated
    response_low = response.astype(jnp.bfloat16)
    branch = jnp.dot(
        response_low, shrink_full, preferred_element_type=jnp.float32
    ) + shrink_bias.astype(jnp.float32)
    first_sum = hidden.astype(jnp.float32) + branch
    modulation = jnp.dot(
        cond_r, time_full.astype(jnp.float32), precision=HIGHEST_PRECISION
    ) + time_bias_full.astype(jnp.float32)
    mod_rows = jnp.dot(picked, modulation, precision=HIGHEST_PRECISION)
    scale_rows = 1.0 + mod_rows[:, :C]
    second_sum = first_sum * scale_rows + mod_rows[:, C:]
    normed_two, inverse_two = layer_stats(second_sum)
    attn_in = normed_two.astype(jnp.bfloat16)
    context_in = jax.nn.silu(clip.reshape(NLAT * NCTX, CLIP).astype(jnp.float32)).astype(
        jnp.bfloat16
    )
    context = (
        jnp.dot(context_in, mapper_full, preferred_element_type=jnp.float32)
        + mapper_bias.astype(jnp.float32)
    ).astype(jnp.bfloat16)
    queries = (
        jnp.dot(attn_in, query_full, preferred_element_type=jnp.float32)
        + query_bias_full.astype(jnp.float32)
    ).astype(jnp.bfloat16)
    keys_low = jnp.dot(attn_in, key_full, preferred_element_type=jnp.float32).astype(jnp.bfloat16)
    values_low = (
        jnp.dot(attn_in, value_full, preferred_element_type=jnp.float32)
        + value_bias_full.astype(jnp.float32)
    ).astype(jnp.bfloat16)
    context_keys = jnp.dot(context, key_full, preferred_element_type=jnp.float32).astype(
        jnp.bfloat16
    )
    context_values = (
        jnp.dot(context, value_full, preferred_element_type=jnp.float32)
        + value_bias_full.astype(jnp.float32)
    ).astype(jnp.bfloat16)
    query_heads = queries.reshape(tok_rows, HEADS, HEAD_DIM)
    key_heads = keys_low.reshape(tok_rows, HEADS, HEAD_DIM)
    value_heads = values_low.reshape(tok_rows, HEADS, HEAD_DIM)
    ctx_key_heads = context_keys.reshape(NLAT * NCTX, HEADS, HEAD_DIM)
    ctx_value_heads = context_values.reshape(NLAT * NCTX, HEADS, HEAD_DIM)
    context_segment = jnp.arange(NLAT * NCTX, dtype=jnp.int32) // NCTX
    ctx_admit = segment[:, None] == context_segment[None, :]

    def segments_at(first_row, length):
        return latent_grid(first_row + jnp.arange(length, dtype=jnp.int32), shape_row)[0]

    ctx_scores = (
        jnp.einsum("qhd,khd->hqk", query_heads, ctx_key_heads, preferred_element_type=jnp.float32)
        * SCORE_SCALE
    )
    ctx_scores = jnp.where(ctx_admit[None], ctx_scores, MASKED)
    start_max = jnp.max(ctx_scores, axis=-1)
    ctx_expo = jnp.exp(ctx_scores - start_max[..., None])
    start_total = jnp.sum(ctx_expo, axis=-1)
    start_accum = jnp.einsum(
        "hqk,khd->qhd",
        ctx_expo.astype(jnp.bfloat16),
        ctx_value_heads,
        preferred_element_type=jnp.float32,
    )
    key_part = lax.all_gather(keys_low, "seq", axis=0, tiled=True)
    value_part = lax.all_gather(values_low, "seq", axis=0, tiled=True)
    block_rows = block_size(key_part.shape[0], tok_rows)
    block_count = key_part.shape[0] // block_rows
    key_stack = key_part.reshape(block_count, block_rows, HEADS, HEAD_DIM)
    value_stack = value_part.reshape(block_count, block_rows, HEADS, HEAD_DIM)

    def attend_visit(state_now, element):
        key_block, value_block, block_index = element
        key_segment = segments_at(block_index * block_rows, block_rows)
        admitted = segment[:, None] == key_segment[None, :]
        scores = (
            jnp.einsum("qhd,khd->hqk", query_heads, key_block, preferred_element_type=jnp.float32)
            * SCORE_SCALE
        )
        scores = jnp.where(admitted[None], scores, MASKED)
        old_max, old_total, old_accum = state_now
        new_max = jnp.maximum(old_max, jnp.max(scores, axis=-1))
        factor = jnp.exp(old_max - new_max)
        expo_block = jnp.exp(scores - new_max[..., None])
        new_total = old_total * factor + jnp.sum(expo_block, axis=-1)
        new_accum = old_accum * factor.T[:, :, None] + jnp.einsum(
            "hqk,khd->qhd",
            expo_block.astype(jnp.bfloat16),
            value_block,
            preferred_element_type=jnp.float32,
        )
        return ((new_max, new_total, new_accum), None)

    state_end, ignored = lax.scan(
        attend_visit,
        (start_max, start_total, start_accum),
        (key_stack, value_stack, jnp.arange(block_count, dtype=jnp.int32)),
    )
    run_max, run_total, accum = state_end
    mixed = accum / run_total.T[:, :, None]
    log_total = run_max + jnp.log(run_total)
    mixed_low = mixed.reshape(tok_rows, C).astype(jnp.bfloat16)
    activations = (
        second_sum
        + jnp.dot(mixed_low, output_full, preferred_element_type=jnp.float32)
        + output_bias_full.astype(jnp.float32)
    ).astype(jnp.bfloat16)
    cot_value = cotangent.astype(jnp.float32)
    grad_out_w = outer_sum(mixed_low, cotangent)
    grad_out_b = jnp.sum(cot_value, axis=0)
    d_mixed_low = against(cotangent, output_full).astype(jnp.bfloat16)
    dmix_heads = d_mixed_low.reshape(tok_rows, HEADS, HEAD_DIM)
    delta = jnp.sum(dmix_heads.astype(jnp.float32) * mixed, axis=-1).T
    ctx_probs = jnp.exp(ctx_scores - log_total[..., None])
    ctx_dprob = jnp.einsum(
        "qhd,khd->hqk", dmix_heads, ctx_value_heads, preferred_element_type=jnp.float32
    )
    ctx_dscore = (ctx_probs * (ctx_dprob - delta[..., None])).astype(jnp.bfloat16)
    dquery_start = (
        jnp.einsum("hqk,khd->qhd", ctx_dscore, ctx_key_heads, preferred_element_type=jnp.float32)
        * SCORE_SCALE
    )
    ctx_dkey_part = (
        jnp.einsum("hqk,qhd->khd", ctx_dscore, query_heads, preferred_element_type=jnp.float32)
        * SCORE_SCALE
    )
    ctx_dvalue_part = jnp.einsum(
        "hqk,qhd->khd",
        ctx_probs.astype(jnp.bfloat16),
        dmix_heads,
        preferred_element_type=jnp.float32,
    )
    key_part = lax.all_gather(keys_low, "seq", axis=0, tiled=True)
    value_part = lax.all_gather(values_low, "seq", axis=0, tiled=True)
    query_block_rows = block_size(key_part.shape[0], tok_rows)
    block_count = key_part.shape[0] // query_block_rows
    key_stack = key_part.reshape(block_count, query_block_rows, HEADS, HEAD_DIM)
    value_stack = value_part.reshape(block_count, query_block_rows, HEADS, HEAD_DIM)

    def query_visit(state_now, element):
        key_block, value_block, block_index = element
        key_segment = segments_at(block_index * query_block_rows, query_block_rows)
        admitted = segment[:, None] == key_segment[None, :]
        scores = (
            jnp.einsum("qhd,khd->hqk", query_heads, key_block, preferred_element_type=jnp.float32)
            * SCORE_SCALE
        )
        scores = jnp.where(admitted[None], scores, MASKED)
        probs = jnp.exp(scores - log_total[..., None])
        dprob = jnp.einsum(
            "qhd,khd->hqk", dmix_heads, value_block, preferred_element_type=jnp.float32
        )
        dscore = (probs * (dprob - delta[..., None])).astype(jnp.bfloat16)
        added = (
            jnp.einsum("hqk,khd->qhd", dscore, key_block, preferred_element_type=jnp.float32)
            * SCORE_SCALE
        )
        return (state_now + added, None)

    state_end, ignored = lax.scan(
        query_visit,
        dquery_start,
        (key_stack, value_stack, jnp.arange(block_count, dtype=jnp.int32)),
    )
    dquery = state_end
    lse_all, delta_all = (
        lax.all_gather(log_total.T, "seq", axis=0, tiled=True),
        lax.all_gather(delta.T, "seq", axis=0, tiled=True),
    )
    zero_heads = jnp.zeros((tok_rows, HEADS, HEAD_DIM), jnp.float32)
    query_part = lax.all_gather(queries, "seq", axis=0, tiled=True)
    dmix_part = lax.all_gather(d_mixed_low, "seq", axis=0, tiled=True)
    row_count = query_part.shape[0]
    key_block_rows = block_size(row_count, tok_rows)
    block_count = row_count // key_block_rows
    query_stack = query_part.reshape(block_count, key_block_rows, HEADS, HEAD_DIM)
    dmix_stack = dmix_part.reshape(block_count, key_block_rows, HEADS, HEAD_DIM)
    lse_stack = lse_all.reshape(block_count, key_block_rows, HEADS)
    delta_stack = delta_all.reshape(block_count, key_block_rows, HEADS)

    def key_visit(state_now, element):
        query_block, dmix_block, lse_block, delta_block, block_index = element
        query_segment = segments_at(block_index * key_block_rows, key_block_rows)
        admitted = segment[:, None] == query_segment[None, :]
        scores = (
            jnp.einsum("khd,qhd->hkq", key_heads, query_block, preferred_element_type=jnp.float32)
            * SCORE_SCALE
        )
        scores = jnp.where(admitted[None], scores, MASKED)
        probs = jnp.exp(scores - lse_block.T[:, None, :])
        dkey_now, dvalue_now = state_now
        dvalue_now = dvalue_now + jnp.einsum(
            "hkq,qhd->khd",
            probs.astype(jnp.bfloat16),
            dmix_block,
            preferred_element_type=jnp.float32,
        )
        dprob = jnp.einsum(
            "khd,qhd->hkq", value_heads, dmix_block, preferred_element_type=jnp.float32
        )
        dscore = (probs * (dprob - delta_block.T[:, None, :])).astype(jnp.bfloat16)
        dkey_now = (
            dkey_now
            + jnp.einsum("hkq,qhd->khd", dscore, query_block, preferred_element_type=jnp.float32)
            * SCORE_SCALE
        )
        return ((dkey_now, dvalue_now), None)

    state_end, ignored = lax.scan(
        key_visit,
        (zero_heads, zero_heads),
        (query_stack, dmix_stack, lse_stack, delta_stack, jnp.arange(block_count, dtype=jnp.int32)),
    )
    dkey, dvalue = state_end
    dquery_low = dquery.reshape(tok_rows, C).astype(jnp.bfloat16)
    dkey_low = dkey.reshape(tok_rows, C).astype(jnp.bfloat16)
    dvalue_low = dvalue.reshape(tok_rows, C).astype(jnp.bfloat16)
    ctx_dkey_flat = ctx_dkey_part.reshape(NLAT * NCTX, C)
    ctx_dvalue_flat = ctx_dvalue_part.reshape(NLAT * NCTX, C)
    context_value = context.astype(jnp.float32)
    d_attn_in = (
        against(dquery_low, query_full)
        + against(dkey_low, key_full)
        + against(dvalue_low, value_full)
    )
    grad_query_w = outer_sum(attn_in, dquery_low)
    grad_query_b = jnp.sum(dquery_low.astype(jnp.float32), axis=0)
    grad_key_w = outer_sum(attn_in, dkey_low) + column_sum(context_value, ctx_dkey_flat)
    grad_value_w = outer_sum(attn_in, dvalue_low) + column_sum(context_value, ctx_dvalue_flat)
    grad_value_b = jnp.sum(dvalue_low.astype(jnp.float32), axis=0) + jnp.sum(
        ctx_dvalue_flat, axis=0
    )
    d_context = against_exact(ctx_dkey_flat, key_full.astype(jnp.float32)) + against_exact(
        ctx_dvalue_flat, value_full.astype(jnp.float32)
    )
    grad_map_w = column_sum(context_in.astype(jnp.float32), d_context)
    grad_map_b = jnp.sum(d_context, axis=0)
    d_second = cot_value + layer_back(d_attn_in, normed_two, inverse_two)
    d_first = d_second * scale_rows
    d_mod_rows = jnp.concatenate([d_second * first_sum, d_second], axis=1)
    d_modulation = column_sum(picked, d_mod_rows)
    grad_time_w = lax.dot_general(
        cond_r,
        d_modulation,
        (((0,), (0,)), ((), ())),
        precision=HIGHEST_PRECISION,
        preferred_element_type=jnp.float32,
    )
    grad_time_b = jnp.sum(d_modulation, axis=0)
    d_branch_low = d_first.astype(jnp.bfloat16)
    grad_shrink_w = outer_sum(response_low, d_branch_low)
    grad_shrink_b = jnp.sum(d_branch_low.astype(jnp.float32), axis=0)
    d_response = against(d_branch_low, shrink_full)
    grad_gamma = jnp.sum(d_response * activated * ratio_rows, axis=0)
    grad_beta = jnp.sum(d_response, axis=0)
    d_ratio = lax.psum(column_sum(picked, d_response * gamma_value * activated), "seq")
    d_root = d_ratio / denom - jnp.sum(d_ratio * root, axis=-1, keepdims=True) / (
        FF * denom * denom
    )
    d_act = d_response * (gamma_value * ratio_rows + 1.0) + activated * jnp.dot(
        picked, d_root / root, precision=HIGHEST_PRECISION
    )
    d_pre_low = gelu_pull(d_act)[0].astype(jnp.bfloat16)
    grad_expand_w = outer_sum(normed_low, d_pre_low)
    grad_expand_b = jnp.sum(d_pre_low.astype(jnp.float32), axis=0)
    d_normed = against(d_pre_low, expand_full)
    d_conv_low = layer_back(d_normed, normed_one, inverse_one).astype(jnp.bfloat16)
    d_conv = d_conv_low.astype(jnp.float32)
    grad_kernel_b = jnp.sum(d_conv, axis=0)
    d_padded = padded_2(d_conv_low, (("seq", 0),), margin)
    kernel_rows = []
    input_grad = d_first
    for tap_number, down_step, side_step, offset_rows, valid in tap_list:
        nearby = lax.dynamic_slice_in_dim(padded, margin + offset_rows, tok_rows, 0).astype(
            jnp.float32
        )
        kernel_rows.append(jnp.sum(d_conv * nearby * valid[:, None], axis=0))
        source = positions - offset_rows
        src_segment, src_row, src_column, src_height, src_width = latent_grid(source, shape_row)
        src_valid = valid_tap(src_row, src_column, src_height, src_width, down_step, side_step)
        behind = lax.dynamic_slice_in_dim(d_padded, margin - offset_rows, tok_rows, 0).astype(
            jnp.float32
        )
        input_grad = (
            input_grad
            + kernel_full[tap_number].astype(jnp.float32)[None, :] * behind * src_valid[:, None]
        )
    grad_kernel_w = jnp.stack(kernel_rows, axis=0)
    gradients = (
        grad_kernel_w,
        grad_kernel_b,
        grad_expand_w,
        grad_expand_b,
        grad_gamma,
        grad_beta,
        grad_shrink_w,
        grad_shrink_b,
        grad_time_w,
        grad_time_b,
        grad_map_w,
        grad_map_b,
        grad_query_w,
        grad_query_b,
        grad_key_w,
        grad_value_w,
        grad_value_b,
        grad_out_w,
        grad_out_b,
    )
    shares = (
        lax.psum_scatter(gradients[0], "seq", scatter_dimension=1, tiled=True),
        lax.psum_scatter(gradients[1], "seq", scatter_dimension=0, tiled=True),
        lax.psum_scatter(gradients[2], "seq", scatter_dimension=1, tiled=True),
        lax.psum_scatter(gradients[3], "seq", scatter_dimension=0, tiled=True),
        lax.psum_scatter(gradients[4], "seq", scatter_dimension=0, tiled=True),
        lax.psum_scatter(gradients[5], "seq", scatter_dimension=0, tiled=True),
        lax.psum_scatter(gradients[6], "seq", scatter_dimension=1, tiled=True),
        lax.psum_scatter(gradients[7], "seq", scatter_dimension=0, tiled=True),
        lax.psum_scatter(gradients[8], "seq", scatter_dimension=1, tiled=True),
        lax.psum_scatter(gradients[9], "seq", scatter_dimension=0, tiled=True),
        lax.psum_scatter(gradients[10], "seq", scatter_dimension=1, tiled=True),
        lax.psum_scatter(gradients[11], "seq", scatter_dimension=0, tiled=True),
        lax.psum_scatter(gradients[12], "seq", scatter_dimension=1, tiled=True),
        lax.psum_scatter(gradients[13], "seq", scatter_dimension=0, tiled=True),
        lax.psum_scatter(gradients[14], "seq", scatter_dimension=1, tiled=True),
        lax.psum_scatter(gradients[15], "seq", scatter_dimension=1, tiled=True),
        lax.psum_scatter(gradients[16], "seq", scatter_dimension=0, tiled=True),
        lax.psum_scatter(gradients[17], "seq", scatter_dimension=1, tiled=True),
        lax.psum_scatter(gradients[18], "seq", scatter_dimension=0, tiled=True),
    )
    summed = (
        lax.psum(shares[0].astype(jnp.bfloat16), "grp").astype(jnp.float32),
        lax.psum(shares[1].astype(jnp.bfloat16), "grp").astype(jnp.float32),
        lax.psum(shares[2].astype(jnp.bfloat16), "grp").astype(jnp.float32),
        lax.psum(shares[3].astype(jnp.bfloat16), "grp").astype(jnp.float32),
        lax.psum(shares[4].astype(jnp.bfloat16), "grp").astype(jnp.float32),
        lax.psum(shares[5].astype(jnp.bfloat16), "grp").astype(jnp.float32),
        lax.psum(shares[6].astype(jnp.bfloat16), "grp").astype(jnp.float32),
        lax.psum(shares[7].astype(jnp.bfloat16), "grp").astype(jnp.float32),
        lax.psum(shares[8].astype(jnp.bfloat16), "grp").astype(jnp.float32),
        lax.psum(shares[9].astype(jnp.bfloat16), "grp").astype(jnp.float32),
        lax.psum(shares[10].astype(jnp.bfloat16), "grp").astype(jnp.float32),
        lax.psum(shares[11].astype(jnp.bfloat16), "grp").astype(jnp.float32),
        lax.psum(shares[12].astype(jnp.bfloat16), "grp").astype(jnp.float32),
        lax.psum(shares[13].astype(jnp.bfloat16), "grp").astype(jnp.float32),
        lax.psum(shares[14].astype(jnp.bfloat16), "grp").astype(jnp.float32),
        lax.psum(shares[15].astype(jnp.bfloat16), "grp").astype(jnp.float32),
        lax.psum(shares[16].astype(jnp.bfloat16), "grp").astype(jnp.float32),
        lax.psum(shares[17].astype(jnp.bfloat16), "grp").astype(jnp.float32),
        lax.psum(shares[18].astype(jnp.bfloat16), "grp").astype(jnp.float32),
    )
    return (
        activations,
        input_grad,
        summed[0],
        summed[1],
        summed[2],
        summed[3],
        summed[4],
        summed[5],
        summed[6],
        summed[7],
        summed[8],
        summed[9],
        summed[10],
        summed[11],
        summed[12],
        summed[13],
        summed[14],
        summed[15],
        summed[16],
        summed[17],
        summed[18],
    )


def mm(left, right):
    return jnp.dot(left, right, preferred_element_type=jnp.float32)


MESH_ID = pl.DeviceIdType.MESH


def dot_nt(left, right):
    return lax.dot_general(
        left, right, (((1,), (1,)), ((), ())), preferred_element_type=jnp.float32
    )


def place():
    me = lax.axis_index("seq")
    z, y = me // 2, lax.rem(me, 2)
    return me, z, y, me + 1 - 2 * y


def seq_copy(src, dst, send, recv, target):
    return pltpu.make_async_remote_copy(
        src_ref=src,
        dst_ref=dst,
        send_sem=send,
        recv_sem=recv,
        device_id={"seq": target},
        device_id_type=MESH_ID,
    )


def dot_tn(left, right):
    return lax.dot_general(
        left, right, (((0,), (0,)), ((), ())), preferred_element_type=jnp.float32
    )


def grp_copy(src, dst, send, recv, target):
    return pltpu.make_async_remote_copy(
        src_ref=src,
        dst_ref=dst,
        send_sem=send,
        recv_sem=recv,
        device_id={"grp": target},
        device_id_type=MESH_ID,
    )


def group_place():
    group = lax.axis_index("grp")
    core = lax.rem(group, 2)
    return group // 2, core, group + 1 - 2 * core, lax.rem(group + 2, 4)


def meet_all(shards, groups=0):
    me = lax.axis_index("seq")
    barrier = pltpu.get_barrier_semaphore()
    for step in range(1, groups):
        pl.semaphore_signal(
            barrier,
            inc=1,
            device_id={"grp": lax.rem(lax.axis_index("grp") + step, groups)},
            device_id_type=MESH_ID,
        )
    for step in range(1, shards):
        pl.semaphore_signal(
            barrier,
            inc=1,
            device_id={"seq": lax.rem(me + step, shards)},
            device_id_type=MESH_ID,
        )
    pl.semaphore_wait(barrier, shards - 1 + max(groups - 1, 0))


def tile_loop(count, body):
    def step(index, carry):
        body(index)
        return carry

    lax.fori_loop(0, count, step, 0)


def add_rows(target, target_row, left, left_row, right, count):
    def tile(index):
        low = index * 32
        here = pl.ds(pl.multiple_of(target_row + low, 32), 32)
        there = pl.ds(pl.multiple_of(left_row + low, 32), 32)
        value = left[there, :].astype(jnp.float32) + right[
            pl.ds(pl.multiple_of(low, 32), 32), :
        ].astype(jnp.float32)
        target[here, :] = value.astype(target.dtype)

    tile_loop(count // 32, tile)


class PairSum:
    def __init__(self, own, got, other, out, sems):
        x, core, self.core_peer, self.x_peer = group_place()
        self.half = own.shape[0] // 2
        self.own, self.got, self.other, self.out = own, got, other, out
        self.low = pl.multiple_of(core * self.half, self.half)
        mine = pl.ds(self.low, self.half)
        theirs = pl.ds(pl.multiple_of((1 - core) * self.half, self.half), self.half)
        pair = lambda k: (sems.at[0, k], sems.at[1, k])
        self.copies = (
            grp_copy(own.at[theirs], got, *pair(0), self.core_peer),
            grp_copy(own.at[mine], other, *pair(1), self.x_peer),
            grp_copy(out.at[mine], out.at[mine], *pair(2), self.core_peer),
        )

    def begin(self):
        self.copies[0].start()

    def across(self):
        self.copies[0].wait_recv()
        add_rows(self.own, self.low, self.own, self.low, self.got, self.half)
        self.copies[1].start()

    def share(self):
        self.copies[1].wait_recv()
        add_rows(self.out, self.low, self.own, self.low, self.other, self.half)
        self.copies[2].start()

    def finish(self):
        self.copies[2].wait_recv()
        for copy in self.copies:
            copy.wait_send()


class CoreHalf:
    def __init__(self, own, got, half, sems):
        _, core, core_peer, _ = group_place()
        self.own, self.got, self.half, self.core = own, got, half, core
        self.copies = [
            grp_copy(
                own.at[:, side * 2 + 1 - core],
                got.at[side],
                sems.at[0, side],
                sems.at[1, side],
                core_peer,
            )
            for side in (0, 1)
        ]

    def begin(self):
        for copy in self.copies:
            copy.start()

    def finish(self):
        for side, copy in enumerate(self.copies):
            copy.wait_recv()

            def tile(index, side=side):
                self.half[index, side] = (
                    self.own[index, side * 2 + self.core].astype(jnp.float32)
                    + self.got[side, index].astype(jnp.float32)
                ).astype(self.half.dtype)

            tile_loop(self.own.shape[0], tile)
        for copy in self.copies:
            copy.wait_send()


class QuarterSum:
    def __init__(self, shards, half, other, part, out, sems):
        x, core, core_peer, x_peer = group_place()
        me = lax.axis_index("seq")
        units, width = half.shape[2], half.shape[3]
        self.half, self.other, self.part, self.out = half, other, part, out
        self.x, self.me, self.shards = x, me, shards
        mine = x * 2 + core
        pair = lambda k: (sems.at[0, k], sems.at[1, k])

        def rows(quarter):
            return pl.ds(pl.multiple_of(quarter * units, units), units)

        self.block = (rows(mine), pl.ds(pl.multiple_of(me * width, 128), width))
        self.second = grp_copy(half.at[:, 1 - x], other, *pair(0), x_peer)
        self.third = []
        for step in range(1, shards):
            goal = lax.rem(me + step, shards)
            self.third.append(seq_copy(part.at[goal], out.at[self.block], *pair(step), goal))
        whole = out.at[rows(mine)]
        self.fourth = grp_copy(whole, whole, *pair(shards), x_peer)
        self.fifth = []
        for side in (0, 1):
            whole = out.at[rows(side * 2 + core)]
            self.fifth.append(grp_copy(whole, whole, *pair(shards + 1 + side), core_peer))

    def begin(self):
        self.second.start()

    def spread(self):
        self.second.wait_recv()

        def tile(index):
            self.part[index] = (
                self.half[index, self.x].astype(jnp.float32)
                + self.other[index].astype(jnp.float32)
            ).astype(self.part.dtype)

        tile_loop(self.shards, tile)
        for copy in self.third:
            copy.start()
        self.out[self.block] = self.part[self.me]

    def share(self):
        for copy in self.third:
            copy.wait_recv()
        self.fourth.start()

    def share_core(self):
        self.fourth.wait_recv()
        for copy in self.fifth:
            copy.start()

    def finish(self):
        for copy in self.fifth:
            copy.wait_recv()
        for copy in (self.second, *self.third, self.fourth, *self.fifth):
            copy.wait_send()


def in_line(direction, z, hops, depth):
    return z >= hops if direction == 0 else z + hops < depth


class Gather:
    def __init__(self, full, sems, depth, extra=0):
        self.full, self.depth, self.extra = full, depth, extra
        self.sems = [sems.at[k] for k in range(6)]
        self.me, self.z, self.y, self.other = place()
        self.rows = full.shape[1]

    def origin(self, direction, hops, far):
        column = 1 - self.y if far else self.y
        return (self.z - hops if direction == 0 else self.z + hops) * 2 + column

    def block(self, direction, hops, far=False):
        origin = self.origin(direction, hops, far)
        if not self.extra:
            return self.full.at[origin]
        return self.full.at[origin, pl.ds(0, self.rows - self.extra)]

    def pair(self, direction, hops):
        low = self.origin(direction, hops, False) - self.y
        return self.full.at[pl.ds(low, 2), pl.ds(self.rows - self.extra, self.extra)]

    def z_move(self, block, kind, direction, hops, arrival):
        send, recv = self.sems[kind], self.sems[kind + 1]
        target = self.me + 2 if direction == 0 else self.me - 2
        return seq_copy(
            block,
            block,
            send.at[direction, hops],
            recv.at[direction, hops if arrival else hops + 1],
            self.other if arrival else target,
        )

    def z_copy(self, direction, hops, arrival=False):
        return self.z_move(self.block(direction, hops), 0, direction, hops, arrival)

    def pair_copy(self, direction, hops, arrival=False):
        return self.z_move(self.pair(direction, hops), 4, direction, hops, arrival)

    def y_copy(self, direction, hops, arrival=False, own=False):
        if own:
            block = self.full.at[self.origin(direction, hops, arrival)]
        else:
            block = self.block(direction, hops, arrival)
        send, recv = self.sems[2], self.sems[3]
        return seq_copy(
            block, block, send.at[direction, hops], recv.at[direction, hops], self.other
        )

    def here(self, direction, hops):
        return in_line(direction, self.z, hops, self.depth)

    def onward(self, direction):
        return self.z < self.depth - 1 if direction == 0 else self.z > 0

    def start(self):
        for direction in (0, 1):

            @pl.when(self.onward(direction))
            def _():
                self.z_copy(direction, 0).start()

        self.y_copy(0, 0, own=True).start()

    def cross(self):
        self.y_copy(0, 0, True, own=True).wait_recv()
        if self.extra:
            for direction in (0, 1):

                @pl.when(self.onward(direction))
                def _():
                    self.pair_copy(direction, 0).start()

    def hop(self, hops):
        for direction in (0, 1):

            @pl.when(self.here(direction, hops))
            def _():
                self.z_copy(direction, hops, True).wait_recv()

                @pl.when(self.onward(direction))
                def _():
                    self.z_copy(direction, hops).start()

                self.y_copy(direction, hops).start()

        if self.extra:
            for direction in (0, 1):

                @pl.when(self.here(direction, hops))
                def _():
                    self.pair_copy(direction, hops, True).wait_recv()

                    @pl.when(self.onward(direction))
                    def _():
                        self.pair_copy(direction, hops).start()

    def near(self, hops, visit):
        for direction in (0, 1):

            @pl.when(self.here(direction, hops))
            def _():
                visit(self.origin(direction, hops, False))

    def far(self, hops, visit=None):
        for direction in (0, 1):

            @pl.when(self.here(direction, hops))
            def _():
                self.y_copy(direction, hops, True).wait_recv()
                if visit is not None:
                    visit(self.origin(direction, hops, True))

    def drain(self):
        self.y_copy(0, 0, own=True).wait_send()

        def step(hops, carry):
            for direction in (0, 1):
                here = self.here(direction, hops)

                @pl.when(here & self.onward(direction))
                def _():
                    self.z_copy(direction, hops).wait_send()
                    if self.extra:
                        self.pair_copy(direction, hops).wait_send()

                @pl.when(here & (hops > 0))
                def _():
                    self.y_copy(direction, hops).wait_send()

            return carry

        lax.fori_loop(0, self.depth, step, 0)

    def finish(self):
        def step(hops, carry):
            self.far(hops)
            return carry

        lax.fori_loop(1, self.depth, step, 0)
        self.drain()

    def run(self, visit, hook=None):
        self.start()
        visit(self.me)
        self.cross()
        visit(self.other)

        def step(hops, carry):
            @pl.when(hops < self.depth)
            def _():
                self.hop(hops)
                self.near(hops, visit)

            @pl.when(hops > 1)
            def _():
                self.far(hops - 1, visit)

            if hook is not None:
                hook(hops)
            return carry

        lax.fori_loop(1, self.depth + 1, step, 0)
        self.drain()


class LineGather:
    def __init__(self, full, sems, depth):
        self.full, self.sems, self.depth = full, sems, depth
        self.me, self.z, _, self.other = place()

    def copy(self, direction, hops, arrival=False):
        block = self.full.at[self.z - hops if direction == 0 else self.z + hops]
        target = self.me + 2 if direction == 0 else self.me - 2
        return seq_copy(
            block,
            block,
            self.sems.at[0, direction, hops],
            self.sems.at[1, direction, hops if arrival else hops + 1],
            self.other if arrival else target,
        )

    def hop(self, hops):
        for direction in (0, 1):

            @pl.when(in_line(direction, self.z, hops, self.depth))
            def _():
                if hops:
                    self.copy(direction, hops, True).wait_recv()

                @pl.when(in_line(1 - direction, self.z, 1, self.depth))
                def _():
                    self.copy(direction, hops).start()

    def drain(self):
        for hops in range(self.depth):
            for direction in (0, 1):
                here = in_line(direction, self.z, hops, self.depth)

                @pl.when(here & in_line(1 - direction, self.z, 1, self.depth))
                def _():
                    self.copy(direction, hops).wait_send()


class Reshard:
    def __init__(self, shards, part, out, local_sem, sems):
        x, core, core_peer, x_peer = group_place()
        me = lax.axis_index("seq")
        mine = x * 2 + core
        pair = lambda k: (sems.at[0, k], sems.at[1, k])
        self.local = pltpu.make_async_copy(part(me, mine), out.at[me, mine], local_sem)
        self.first = []
        for step in range(1, shards):
            goal = lax.rem(me + step, shards)
            self.first.append(seq_copy(part(goal, mine), out.at[me, mine], *pair(step - 1), goal))
        self.second = grp_copy(out.at[:, mine], out.at[:, mine], *pair(shards - 1), x_peer)
        self.third = []
        for side in (0, 1):
            whole = out.at[:, side * 2 + core]
            self.third.append(grp_copy(whole, whole, *pair(shards + side), core_peer))

    def begin_near(self):
        self.local.start()
        for copy in self.first[1::2]:
            copy.start()

    def begin_far(self):
        for copy in self.first[0::2]:
            copy.start()

    def share(self):
        self.local.wait()
        for copy in self.first:
            copy.wait_recv()
        self.second.start()

    def share_core(self):
        self.second.wait_recv()
        for copy in self.third:
            copy.start()

    def finish(self):
        for copy in self.third:
            copy.wait_recv()
        for copy in (*self.first, self.second, *self.third):
            copy.wait_send()


def side_by_side(target, row, parts, count):
    for pair in range(count // 2):
        value = jnp.concatenate([parts(2 * pair), parts(2 * pair + 1)], axis=1)
        rows, cols = value.shape
        target[row : row + rows, pair * cols : (pair + 1) * cols] = value


def scatter_blocks(
    partial, to_y, from_y, to_z, from_z, acc, y_sems, z_sems, depth, between=None, hook=None, early=None
):
    me, z, y, other = place()
    low = to_y.dtype

    def y_copy(goal):
        return seq_copy(
            to_y.at[goal], from_y.at[goal], y_sems.at[0, goal], y_sems.at[1, goal], other
        )

    def slot(direction, goal, at):
        return goal if direction == 0 else jnp.where(goal == at, depth, goal)

    def z_copy(direction, goal):
        return seq_copy(
            to_z.at[goal],
            from_z.at[slot(direction, goal, z - 1)],
            z_sems.at[0, direction, goal],
            z_sems.at[1, direction, goal],
            me + 2 if direction == 0 else me - 2,
        )

    def z_arrival(direction, goal):
        return seq_copy(
            to_z.at[goal],
            from_z.at[slot(direction, goal, z)],
            z_sems.at[0, direction, goal],
            z_sems.at[1, direction, goal],
            other,
        )

    def ahead(direction, hops):
        return in_line(1 - direction, z, hops, depth)

    def goal_of(direction, hops):
        return z + hops if direction == 0 else z - hops

    def over_y(step, carry):
        hops = depth - 1 - step
        for direction in (0, 1):
            here = ahead(direction, hops)
            if direction == 1:
                here = here & (hops > 0)

            @pl.when(here)
            def _():
                goal = goal_of(direction, hops)
                to_y[goal] = partial(goal * 2 + other - z * 2).astype(low)
                y_copy(goal).start()

        if early is not None:
            early(step)
        return carry

    lax.fori_loop(0, depth, over_y, 0)
    if between is not None:
        between()

    def along_z(step, carry):
        hops = depth - 1 - step
        for direction in (0, 1):

            @pl.when(ahead(direction, hops))
            def _():
                goal = goal_of(direction, hops)
                acc[...] = partial(goal * 2 + y)
                y_copy(goal).wait_recv()
                acc[...] += from_y[goal].astype(jnp.float32)

                @pl.when(in_line(direction, z, 1, depth))
                def _():
                    z_arrival(direction, goal).wait_recv()
                    acc[...] += from_z[slot(direction, goal, z)].astype(jnp.float32)

                to_z[goal] = acc[...].astype(low)
                z_copy(direction, goal).start()

        if hook is not None:
            hook(step)
        return carry

    lax.fori_loop(0, depth - 1, along_z, 0)
    acc[...] = partial(me)
    y_copy(z).wait_recv()
    acc[...] += from_y[z].astype(jnp.float32)
    for direction in (0, 1):

        @pl.when(in_line(direction, z, 1, depth))
        def _():
            z_arrival(direction, z).wait_recv()
            acc[...] += from_z[slot(direction, z, z)].astype(jnp.float32)

    def drain(goal, carry):
        y_copy(goal).wait_send()
        for direction in (0, 1):
            sent = goal > z if direction == 0 else goal < z

            @pl.when(sent)
            def _():
                z_copy(direction, goal).wait_send()

        return carry

    lax.fori_loop(0, depth, drain, 0)


def peer_total(mine, theirs, sems, shards, meanwhile=None):
    me = lax.axis_index("seq")
    copies = [
        seq_copy(
            mine,
            theirs.at[step - 1],
            sems.at[0, step - 1],
            sems.at[1, step - 1],
            lax.rem(me + step, shards),
        )
        for step in range(1, shards)
    ]
    for copy in copies:
        copy.start()
    if meanwhile is not None:
        meanwhile()
    for copy in copies:
        copy.wait()
    total = mine[...]
    for step in range(1, shards):
        total = total + theirs[step - 1]
    return total


EDGE = 80
VMEM_BYTES = 58 * 1024 * 1024
ROOT_HALF = math.sqrt(0.5)
DENSITY = 1.0 / math.sqrt(2.0 * math.pi)


def exchange_edges(held, sems, rows, shards):
    me = lax.axis_index("seq")

    def copy(kind):
        if kind == 0:
            source, target = pl.ds(EDGE + rows - WMAX, WMAX), pl.ds(EDGE - WMAX, WMAX)
        else:
            source, target = pl.ds(EDGE, WMAX), pl.ds(EDGE + rows, WMAX)
        return seq_copy(
            held.at[source],
            held.at[target],
            sems.at[0, kind],
            sems.at[1, kind],
            me + 1 if kind == 0 else me - 1,
        )

    first, last = me == 0, me == shards - 1
    zeros = jnp.zeros((EDGE, held.shape[1]), held.dtype)

    held[pl.ds(0, EDGE - WMAX), :] = zeros[: EDGE - WMAX]
    held[pl.ds(EDGE + rows + WMAX, EDGE - WMAX), :] = zeros[: EDGE - WMAX]

    @pl.when(first)
    def _():
        held[pl.ds(EDGE - WMAX, WMAX), :] = zeros[:WMAX]

    @pl.when(last)
    def _():
        held[pl.ds(EDGE + rows, WMAX), :] = zeros[:WMAX]

    @pl.when(jnp.logical_not(last))
    def _():
        copy(0).start()

    @pl.when(jnp.logical_not(first))
    def _():
        copy(1).start()

    def finish():
        @pl.when(jnp.logical_not(last))
        def _():
            copy(0).wait_send()
            copy(1).wait_recv()

        @pl.when(jnp.logical_not(first))
        def _():
            copy(1).wait_send()
            copy(0).wait_recv()

    return finish


def row_of(vector):
    return vector[...].astype(jnp.float32).reshape(1, vector.shape[0])


def column_of(vector):
    row = row_of(vector)
    fill = -row.shape[1] % 128
    row = jnp.concatenate([row, jnp.zeros((1, fill), jnp.float32)], axis=1)
    return jnp.broadcast_to(row, (8, row.shape[1])).T[: vector.shape[0], 0:1]


def stats_of(values_in):
    average = jnp.mean(values_in, axis=-1, keepdims=True)
    centred = values_in - average
    variance = jnp.mean(centred * centred, axis=-1, keepdims=True)
    inverse = lax.rsqrt(variance + EPS_NORM)
    return centred * inverse, inverse


class Latents:
    def __init__(self, shape, total):
        self.ends = []
        low = 0
        for latent in range(NLAT - 1):
            low = low + shape[latent, 0] * WMAX
            self.ends.append(low)
        self.total = total

    def segment(self, positions):
        out = jnp.zeros_like(positions)
        for end in self.ends:
            out = out + (positions >= end).astype(jnp.int32)
        return out

    def picks(self, start, count):
        segment = self.segment(start + lax.broadcasted_iota(jnp.int32, (count, 1), 0))
        return [(segment == latent).astype(jnp.float32) for latent in range(NLAT)]

    def valid(self, positions, down_step, side_step):
        segment = self.segment(positions)
        low, high = jnp.zeros_like(positions), jnp.full_like(positions, self.total)
        for latent, end in enumerate(self.ends):
            low = jnp.where(segment > latent, end, low)
            high = jnp.where(segment == latent, end, high)
        moved = positions + down_step * WMAX
        column = (positions & (WMAX - 1)) + side_step
        good = (moved >= low) & (moved < high) & (column >= 0) & (column < WMAX)
        return good.astype(jnp.float32)


def rows_of(picks, table):
    out = picks[0] * table[0:1]
    for latent in range(1, NLAT):
        out = out + picks[latent] * table[latent : latent + 1]
    return out


WIDE_SCALE, WIDE_SHIFT = 16, 24
SMALL_FC1, SMALL_GAMMA, SMALL_BETA, SMALL_TIME = 64, 66, 68, 70
SMALL_QUERY, SMALL_VALUE, SMALL_OUT, SMALL_MAP, SMALL_ROWS = 71, 72, 73, 74, 80


def mixer_kernel(
    shards,
    emit,
    shape,
    hidden,
    cond,
    time_weight,
    conv_weight,
    conv_bias,
    fc1_bias,
    gamma,
    beta,
    fc2_bias,
    time_bias,
    fc1,
    ctx_cols,
    cot,
    fc2,
    out_weight,
    full,
    held,
    wide,
    normed,
    inverse,
    pre,
    root_out,
    ratio_out,
    denom_out,
    response,
    ctx_full,
    d_mixed,
    cot_cols,
    fc2_rows,
    pack,
    packed,
    floats,
    conv,
    act,
    energy,
    mine,
    theirs,
    edge_sems,
    pack_sems,
    gather_sems,
    total_sems,
    ctx_sems,
    cot_sems,
    out_parts,
    out_rows,
    cot_line,
    to_other,
    other_sems,
    local_sems,
    fc2_sems,
    out_sems,
):
    f32 = jnp.float32
    rows = hidden.shape[0]
    depth = shards // 2
    me = lax.axis_index("seq")
    meet_all(shards, lax.axis_size("grp"))
    units, width = fc2_rows.shape[2:]
    out_units = out_parts.shape[3]

    def fc2_part(goal, quarter):
        here = pl.ds(pl.multiple_of(quarter * units, units), units)
        return fc2.at[here, pl.ds(pl.multiple_of(goal * width, 128), width)]

    def out_part(goal, quarter):
        return out_weight.at[pl.ds(goal // 2 * 2, 2), quarter]

    fc2_shard = Reshard(shards, fc2_part, fc2_rows, local_sems.at[0], fc2_sems)
    out_shard = Reshard(shards, out_part, out_parts, local_sems.at[1], out_sems)
    ctx_gather = Gather(ctx_full, ctx_sems, depth)
    _, z, y, other = place()
    cot_gather = LineGather(cot_line, cot_sems, depth)
    ctx_full[me] = ctx_cols[...]
    latents = Latents(shape, shards * rows)
    cols = pack.shape[1]
    fc1_bias, gamma, beta, time_bias = map(row_of, (fc1_bias, gamma, beta, time_bias))
    mod = (
        jnp.dot(
            cond[...],
            time_weight[...].astype(f32),
            precision=HIGHEST_PRECISION,
            preferred_element_type=f32,
        )
        + time_bias
    )
    pack[...] = jnp.zeros_like(pack)
    pack[0:9, :] = conv_weight[...].astype(f32)
    pack[9:10, :] = row_of(conv_bias)
    pack[10:11, :] = row_of(fc2_bias)
    pack[11 : 11 + NLAT, :] = mod[:, :cols]
    pack[11 + NLAT : 11 + 2 * NLAT, :] = mod[:, cols:]
    packed[me] = pack[...]
    pack_copies = [
        seq_copy(
            pack,
            packed.at[me],
            pack_sems.at[0, step - 1],
            pack_sems.at[1, step - 1],
            lax.rem(me + step, shards),
        )
        for step in range(1, shards)
    ]
    held[pl.ds(EDGE, rows), :] = hidden[...]
    finish = exchange_edges(held, edge_sems, rows, shards)
    for copy in pack_copies:
        copy.start()
    fc2_shard.begin_near()
    out_shard.begin_near()
    finish()
    fc2_shard.begin_far()
    out_shard.begin_far()
    ctx_gather.start()
    cot_line[z] = cot.wait()[...]
    cot_gather.hop(0)
    emit(held)
    tile_loop(
        floats.shape[0] // 32,
        lambda i: floats.__setitem__(
            (pl.ds(i * 32, 32), slice(None)), held[pl.ds(i * 32, 32), :].astype(f32)
        ),
    )
    for copy in pack_copies:
        copy.wait()
    wide[...] = jnp.zeros_like(wide)
    wide[0:16, :] = jnp.concatenate([packed[j, 0:16, :] for j in range(shards)], axis=1)
    for low, device in ((WIDE_SCALE, 0), (WIDE_SHIFT, shards // 2)):
        parts = []
        for j in range(device, device + shards // 2):
            parts.append(packed[j, 11 : 11 + NLAT, :])
            parts.append(packed[j, 11 + NLAT : 11 + 2 * NLAT, :])
        wide[low : low + NLAT, :] = jnp.concatenate(parts, axis=1)
    positions = me * rows + lax.broadcasted_iota(jnp.int32, (rows, 1), 0)
    masks = [latents.valid(positions, tap // 3 - 1, tap % 3 - 1) for tap in range(9)]

    def conv_tile(index):
        cols = pl.ds(pl.multiple_of(index * 256, 256), 256)
        total = jnp.broadcast_to(wide[9:10, cols], (rows, 256))
        for tap in range(9):
            offset = EDGE + (tap // 3 - 1) * WMAX + tap % 3 - 1
            total = total + (
                floats[offset : offset + rows, cols] * wide[tap : tap + 1, cols]
            ) * masks[tap]
        conv[:, cols] = total

    tile_loop(C // 256, conv_tile)

    def norm_tile(index):
        here = pl.ds(pl.multiple_of(index * 16, 16), 16)
        values, factor = stats_of(conv[here, :])
        normed[here, :] = values
        inverse[here, :] = factor
        full[me, here, :] = values.astype(full.dtype)

    tile_loop(rows // 16, norm_tile)
    energy[...] = jnp.zeros_like(energy)
    fc1 = fc1.wait()
    emit(wide, normed)

    def visit(block):
        pre[block] = (
            jnp.dot(full[block], fc1[...], preferred_element_type=f32) + fc1_bias
        )

        def tile(index):
            here = pl.ds(pl.multiple_of(index * 32, 32), 32)
            value = pre[block, here, :]
            value = value * (0.5 * (1.0 + lax.erf(value * ROOT_HALF)))
            act[block, here, :] = value
            square = value * value
            pick = latents.picks(block * rows + index * 32, 32)
            for latent in range(NLAT):
                energy[latent : latent + 1, :] += jnp.sum(
                    square * pick[latent], axis=0, keepdims=True
                )

        tile_loop(rows // 32, tile)

    def hook(hops):
        @pl.when(hops == 1)
        def _():
            ctx_gather.cross()
            ctx_gather.hop(1)

        @pl.when(hops == 2)
        def _():
            fc2_shard.share()
            out_shard.share()
            ctx_gather.hop(2)
            cot_gather.hop(1)

        @pl.when(hops == 3)
        def _():
            ctx_gather.hop(3)
            cot_gather.hop(2)

    Gather(full, gather_sems, depth, rows // 8).run(visit, hook)
    emit(full, pre)
    out_shard.share_core()
    fc2_shard.share_core()
    root = jnp.sqrt(energy[...] + 1.0)
    mine[...] = jnp.broadcast_to(jnp.sum(root, axis=1, keepdims=True), mine.shape)

    other_copies = [
        seq_copy(
            to_other.at[n],
            target.at[:, y],
            other_sems.at[0, n],
            other_sems.at[1, n],
            other,
        )
        for n, target in enumerate((d_mixed, cot_cols))
    ]
    wide_cols = 2 * cols

    def cot_part(block):
        rows_here = cot_line[block]
        pair = cot_line[block, :, pl.ds(pl.multiple_of(z * wide_cols, 128), wide_cols)]
        for side in (0, 1):
            taken = pair[:, side * cols : (side + 1) * cols]
            product = dot_nt(rows_here, out_rows[side]).astype(d_mixed.dtype)

            @pl.when(y == side)
            def _():
                d_mixed[block, side] = product
                cot_cols[block, side] = taken

            @pl.when(y != side)
            def _():
                to_other[0, block] = product
                to_other[1, block] = taken

    def meanwhile():
        cot_gather.hop(3)
        out_shard.finish()
        for quarter in range(4):
            for side in (0, 1):
                side_by_side(
                    out_rows.at[side],
                    quarter * out_units,
                    lambda j, quarter=quarter, side=side: out_parts[j, quarter, side],
                    shards,
                )
        tile_loop(depth, cot_part)
        for copy in other_copies:
            copy.start()

    denom = peer_total(mine, theirs, total_sems, shards, meanwhile) / FF + EPS_NORM
    ratio = root / denom[:, 0:1]
    root_out[...] = root
    denom_out[...] = denom
    ratio_out[...] = ratio
    scaled = ratio * gamma + 1.0

    def respond(index):
        block = index // (rows // 32)
        here = pl.ds(pl.multiple_of(lax.rem(index, rows // 32) * 32, 32), 32)
        response[block, here, :] = (
            act[block, here, :] * rows_of(latents.picks(index * 32, 32), scaled) + beta
        ).astype(response.dtype)

    tile_loop(shards * rows // 32, respond)
    emit(response)
    ctx_gather.finish()
    emit(ctx_full)
    fc2_shard.finish()
    emit(fc2_rows)
    cot_gather.drain()
    for copy in other_copies:
        copy.wait()


def mixed_in_kernel(
    shards,
    emit,
    shape,
    response,
    fc2,
    hidden,
    wide,
    w_qkv,
    q_bias,
    v_bias,
    context,
    full,
    first,
    second,
    normed,
    inverse,
    queries,
    keys,
    values,
    acc,
    to_y,
    from_y,
    to_z,
    from_z,
    y_sems,
    z_sems,
    gather_sems,
):
    f32 = jnp.float32
    rows = acc.shape[0]
    depth = shards // 2
    me = lax.axis_index("seq")
    meet_all(shards)
    latents = Latents(shape, shards * rows)
    cols = keys.shape[0]
    q_bias, v_bias = row_of(q_bias), column_of(v_bias)
    bias = wide[10:11, :]
    scale, shift = wide[WIDE_SCALE : WIDE_SCALE + 8, :], wide[WIDE_SHIFT : WIDE_SHIFT + 8, :]

    def partial(block):
        return dot_nt(response[block], fc2[...])

    scatter_blocks(partial, to_y, from_y, to_z, from_z, acc, y_sems, z_sems, depth)

    hidden = hidden.wait()

    def norm_tile(index):
        here = pl.ds(pl.multiple_of(index * 16, 16), 16)
        one = hidden[here, :].astype(f32) + acc[here, :] + bias
        pick = latents.picks(me * rows + index * 16, 16)
        two = one * (1.0 + rows_of(pick, scale)) + rows_of(pick, shift)
        first[here, :] = one
        second[here, :] = two
        value, factor = stats_of(two)
        normed[here, :] = value
        inverse[here, :] = factor
        full[me, here, :] = value.astype(full.dtype)

    tile_loop(rows // 16, norm_tile)
    emit(first, second, normed)
    w_qkv, context = w_qkv.wait(), context.wait()

    side = jnp.dot(w_qkv[cols:, :], context[...], preferred_element_type=f32)
    keys[:, shards * rows :] = side[:cols].astype(keys.dtype)
    values[:, shards * rows :] = (side[cols:] + v_bias).astype(values.dtype)

    def visit(block):
        value = full[block]
        query = dot_nt(value, w_qkv[:cols, :]) + q_bias
        queries[block] = query.astype(queries.dtype)
        here = pl.ds(pl.multiple_of(block * rows, 128), rows)
        side = dot_nt(w_qkv[cols:, :], value)
        keys[:, here] = side[:cols].astype(keys.dtype)
        values[:, here] = (side[cols:] + v_bias).astype(values.dtype)

    Gather(full, gather_sems, depth, rows // 8).run(visit)


def attend_kernel(
    shards,
    emit,
    shape,
    queries,
    keys,
    values,
    d_mixed_all,
    cot,
    d_qkv,
    mixed,
    cot_cols,
    dk_sum,
    dv_sum,
    probs_at,
    sems,
):
    f32, bf16 = jnp.float32, jnp.bfloat16
    cols = keys.shape[0]
    heads = cols // HEAD_DIM
    tiles, tile_rows = mixed.shape[0], mixed.shape[3]
    span = tile_rows // queries.shape[1]
    depth = shards // 2
    me = lax.axis_index("seq")
    meet_all(shards)
    latents = Latents(shape, tiles * tile_rows)
    place_at = lax.broadcasted_iota(jnp.int32, (1, keys.shape[1]), 1)
    token = place_at - tiles * tile_rows
    of_token = jnp.full_like(token, -1)
    for latent in range(NLAT):
        inside = (token >= latent * NCTX) & (token < (latent + 1) * NCTX)
        of_token = jnp.where(inside, latent, of_token)
    k_segment = jnp.where(token < 0, latents.segment(place_at), of_token)
    dk_sum[...] = jnp.zeros_like(dk_sum)
    dv_sum[...] = jnp.zeros_like(dv_sum)

    def gather_of(tile):
        return Gather(mixed.at[tile], sems.at[tile], depth)

    def step(tile, carry):
        blocks = pl.ds(tile * span, span)
        here = pl.ds(pl.multiple_of(tile * tile_rows, 128), tile_rows)
        query = queries[blocks].reshape(tile_rows, cols) * SCORE_SCALE
        cot_cols[:, here] = cot[blocks].reshape(tile_rows, cols).T
        d_mixed = d_mixed_all[blocks].reshape(tile_rows, cols)
        q_segment = latents.segment(
            tile * tile_rows + lax.broadcasted_iota(jnp.int32, (tile_rows, 1), 0)
        )
        bias = jnp.where(q_segment == k_segment, 0.0, MASKED)
        mixed_parts, d_query_parts = [], []
        for head in range(heads):
            own = slice(head * HEAD_DIM, (head + 1) * HEAD_DIM)
            scores = jnp.dot(query[:, own], keys[own, :], preferred_element_type=f32) + bias
            expo = jnp.exp(scores - jnp.max(scores, axis=-1, keepdims=True))
            probs_at[head] = expo * (1.0 / jnp.sum(expo, axis=-1, keepdims=True))
            mixed_parts.append(dot_nt(probs_at[head].astype(bf16), values[own, :]))
        mixed[tile, me] = jnp.concatenate(mixed_parts, axis=1).T.astype(bf16)
        gather_of(tile).start()
        for hops in range(1, depth):

            @pl.when(tile >= hops)
            def _():
                if hops == 1:
                    gather_of(tile - 1).cross()
                gather_of(tile - hops).hop(hops)

        for head in range(heads):
            own = slice(head * HEAD_DIM, (head + 1) * HEAD_DIM)
            dm_head = d_mixed[:, own]
            delta = jnp.sum(dm_head.astype(f32) * mixed_parts[head], axis=-1, keepdims=True)
            d_probs = jnp.dot(dm_head, values[own, :], preferred_element_type=f32)
            d_scores = (probs_at[head] * (d_probs - delta)).astype(bf16)
            d_query_parts.append(dot_nt(d_scores, keys[own, :]) * SCORE_SCALE)
            dk_sum[own, :] += dot_tn(query[:, own], d_scores)
            dv_sum[own, :] += dot_tn(dm_head, probs_at[head].astype(bf16))
        d_qkv[:cols, here] = jnp.concatenate(d_query_parts, axis=1).T.astype(bf16)
        return carry

    lax.fori_loop(0, tiles, step, 0)
    for late in range(1, depth):
        for hops in range(late, depth):
            if hops == 1:
                gather_of(tiles - 1).cross()
            gather_of(tiles - 1 + late - hops).hop(hops)
    d_qkv[:cols, tiles * tile_rows :] = jnp.zeros(
        (cols, d_qkv.shape[1] - tiles * tile_rows), bf16
    )
    d_qkv[cols : 2 * cols, :] = dk_sum[...].astype(bf16)
    d_qkv[2 * cols :, :] = dv_sum[...].astype(bf16)

    def close(tile, carry):
        gather_of(tile).finish()
        return carry

    lax.fori_loop(0, tiles, close, 0)


def norm_back(gradient, normed, inverse):
    mean_grad = jnp.mean(gradient, axis=-1, keepdims=True)
    mean_mixed = jnp.mean(gradient * normed, axis=-1, keepdims=True)
    return inverse * (gradient - mean_grad - normed * mean_mixed)


def attn_back_kernel(
    shards,
    emit,
    shape,
    cond,
    d_qkv,
    w_qkv,
    attn,
    context,
    mixed,
    cot_cols,
    out_weight,
    gamma,
    out_bias,
    cot,
    normed,
    inverse,
    first,
    wide,
    fc2,
    pre,
    root,
    ratio,
    denom,
    response,
    context_in,
    d_first,
    d_pre,
    small_out,
    weight_grads,
    map_grad,
    act_out,
    fc2_half,
    branch_sum,
    full,
    d_mod,
    small,
    acc,
    d_resp,
    act,
    sums,
    mine,
    theirs,
    to_y,
    from_y,
    to_z,
    from_z,
    y_sems,
    z_sems,
    gather_sems,
    total_sems,
    g_own,
    g_got,
    g_other,
    g_sems,
    mod_in,
    mod_sems,
    fc2_own,
    fc2_got,
    fc2_sems,
    ctx_out,
    ctx_in,
    ctx_sems,
):
    f32 = jnp.float32
    rows = acc.shape[0]
    depth = shards // 2
    me = lax.axis_index("seq")
    meet_all(shards, lax.axis_size("grp"))
    cols = ctx_out.shape[1]
    total = shards * rows
    latents = Latents(shape, total)
    gamma, out_bias = row_of(gamma), column_of(out_bias)
    width_one = gamma.shape[1]
    scale = wide[WIDE_SCALE : WIDE_SCALE + 8, :]
    later = (attn, context, mixed, cot_cols, out_weight)
    weight_sum = PairSum(g_own, g_got, g_other, weight_grads, g_sems)
    peers = [lax.rem(me + step, shards) for step in range(1, shards)]
    ctx_copies = [
        seq_copy(ctx_out.at[peer], ctx_in.at[me], ctx_sems.at[0, n], ctx_sems.at[1, n], peer)
        for n, peer in enumerate(peers)
    ]
    fc2_sum = CoreHalf(fc2_own, fc2_got, fc2_half, fc2_sems)

    def partial(block):
        here = pl.ds(pl.multiple_of(block * rows, 128), rows)
        return dot_tn(d_qkv[:, here], w_qkv[...])

    def between():
        low_type = ctx_out.dtype
        attn, context, mixed, cot_cols, out_weight = (item.wait() for item in later)
        for device in range(shards):
            ctx_out[device] = dot_tn(
                w_qkv[:, device * cols : (device + 1) * cols], d_qkv[:, total:]
            ).astype(low_type)
        g_own[: 3 * cols, :] = (
            jnp.dot(d_qkv[:, :total], attn[...].reshape(total, C), preferred_element_type=f32)
            + dot_nt(d_qkv[:, total:], context[...])
        ).astype(low_type)
        grad = None
        for tile in range(mixed.shape[0]):
            here = slice(tile * mixed.shape[3], (tile + 1) * mixed.shape[3])
            block = mixed[tile].reshape(C, mixed.shape[3])
            act_out[:, here] = (
                jnp.dot(out_weight[...], block, preferred_element_type=f32) + out_bias
            ).astype(low_type)
            part = dot_nt(cot_cols[:, here], block)
            grad = part if grad is None else grad + part
        g_own[3 * cols :, :] = grad.astype(low_type)
        weight_sum.begin()

    def scatter_hook(step):
        @pl.when(step == 1)
        def _():
            weight_sum.across()

    scatter_blocks(
        partial, to_y, from_y, to_z, from_z, acc, y_sems, z_sems, depth, between, scatter_hook
    )
    d_mod[...] = jnp.zeros_like(d_mod)
    branch_sum[...] = jnp.zeros_like(branch_sum)
    cot, normed, first = cot.wait(), normed.wait(), first.wait()

    def norm_tile(index):
        here = pl.ds(pl.multiple_of(index * 16, 16), 16)
        d_second = cot[here, :].astype(f32) + norm_back(
            acc[here, :], normed[here, :], inverse[here, :]
        )
        pick = latents.picks(me * rows + index * 16, 16)
        value = d_second * (1.0 + rows_of(pick, scale))
        d_first[here, :] = value
        value = value.astype(full.dtype)
        full[me, here, :] = value
        branch_sum[0:1, :] += jnp.sum(value.astype(f32), axis=0, keepdims=True)
        scaled = d_second * first[here, :]
        for latent in range(NLAT):
            chosen = pick[latent]
            d_mod[2 * latent : 2 * latent + 1, :] += jnp.sum(scaled * chosen, axis=0, keepdims=True)
            d_mod[2 * latent + 1 : 2 * latent + 2, :] += jnp.sum(
                d_second * chosen, axis=0, keepdims=True
            )

    tile_loop(rows // 16, norm_tile)
    sums[...] = jnp.zeros_like(sums)
    emit(d_first)
    fc2, pre = fc2.wait(), pre.wait()
    wide_mod = 2 * cols
    half = shards // 2

    def mod_part(device):
        low = pl.multiple_of(lax.rem(device, half) * wide_mod, 128)
        return d_mod.at[:, pl.ds(low, wide_mod)]

    mod_in[me] = mod_part(me)[...]
    mod_copies = [
        seq_copy(mod_part(peer), mod_in.at[me], mod_sems.at[0, k], mod_sems.at[1, k], peer)
        for k, peer in enumerate(peers)
    ]
    for copy in mod_copies:
        copy.start()

    def gather_hook(hops):
        @pl.when(hops == 2)
        def _():
            weight_sum.share()

    def visit(block):
        d_resp[block] = jnp.dot(full[block], fc2[...], preferred_element_type=f32)

        def tile(index):
            here = pl.ds(pl.multiple_of(index * 32, 32), 32)
            value = pre[block, here, :]
            phi = 0.5 * (1.0 + lax.erf(value * ROOT_HALF))
            pre[block, here, :] = phi + value * (DENSITY * jnp.exp(-0.5 * value * value))
            value = value * phi
            act[block, here, :] = value.astype(act.dtype)
            pull = d_resp[block, here, :]
            sums[NLAT : NLAT + 1, :] += jnp.sum(pull, axis=0, keepdims=True)
            pull = pull * value
            pick = latents.picks(block * rows + index * 32, 32)
            for latent in range(NLAT):
                sums[latent : latent + 1, :] += jnp.sum(
                    pull * pick[latent], axis=0, keepdims=True
                )

        tile_loop(rows // 32, tile)

    Gather(full, gather_sems, depth, rows // 8).run(visit, gather_hook)
    small[...] = jnp.zeros_like(small)
    wide_row = 2 * cols

    def keep(row, value):
        for part in range(value.shape[1] // wide_row):
            small[row + part : row + part + 1, :] = value[
                :, part * wide_row : (part + 1) * wide_row
            ]

    keep(SMALL_BETA, sums[NLAT : NLAT + 1, :])
    pulls = sums[...]
    keep(SMALL_GAMMA, jnp.sum(pulls[:NLAT] * ratio[:NLAT, :], axis=0, keepdims=True))
    d_ratio = pulls * gamma
    mine[...] = jnp.broadcast_to(jnp.sum(d_ratio * root[...], axis=1, keepdims=True), mine.shape)

    def meanwhile():
        for copy in ctx_copies:
            copy.start()
        ctx_in[me] = ctx_out[me]
        right = response.wait()[...].reshape(total, width_one)
        units = fc2_own.shape[2]
        for goal in range(0, shards, 4):
            here = slice(goal * 4 * units, (goal + 4) * 4 * units)
            part = dot_tn(full[:, :, here].reshape(total, 16 * units), right)
            fc2_own[goal : goal + 4] = part.reshape(4, 4, units, width_one).astype(fc2_own.dtype)
        fc2_sum.begin()

    pulled = peer_total(mine, theirs, total_sems, shards, meanwhile)[:, 0:1]
    below = denom[:, 0:1]
    d_root = d_ratio / below - pulled / (FF * below * below)
    back = d_root / root[...]
    scaled = ratio[...] * gamma + 1.0
    sums[0:1, :] = jnp.zeros((1, width_one), f32)

    def respond(index):
        block = index // (rows // 32)
        here = pl.ds(pl.multiple_of(lax.rem(index, rows // 32) * 32, 32), 32)
        pick = latents.picks(index * 32, 32)
        d_act = d_resp[block, here, :] * rows_of(pick, scaled) + act[block, here, :].astype(f32) * rows_of(
            pick, back
        )
        value = (d_act * pre[block, here, :]).astype(d_pre.dtype)
        d_pre[block, here, :] = value
        sums[0:1, :] += jnp.sum(value.astype(f32), axis=0, keepdims=True)

    tile_loop(shards * rows // 32, respond)
    emit(d_pre)
    for copy in mod_copies:
        copy.wait()
    mod_sum = mod_in[0]
    for device in range(1, shards):
        mod_sum = mod_sum + mod_in[device]
    keep(SMALL_FC1, sums[0:1, :])
    fc2_sum.finish()
    emit(fc2_half)
    chosen = [
        jnp.where(me < half, mod_sum[2 * n : 2 * n + 1], mod_sum[2 * n + 1 : 2 * n + 2])
        for n in range(NLAT)
    ]
    chosen = jnp.concatenate(chosen, axis=0)
    small[0:SMALL_FC1, :] = lax.dot_general(
        cond[...],
        chosen,
        (((0,), (0,)), ((), ())),
        precision=HIGHEST_PRECISION,
        preferred_element_type=f32,
    )
    keep(SMALL_TIME, jnp.sum(chosen, axis=0, keepdims=True))
    ones = lambda values: jnp.ones((8, values.shape[1]), values.dtype)
    for row, value in (
        (SMALL_QUERY, d_qkv[:cols, :]),
        (SMALL_VALUE, d_qkv[2 * cols :, :]),
        (SMALL_OUT, later[3].buffer[...]),
    ):
        small[row : row + 1, :cols] = dot_nt(ones(value), value)[0:1]
    for copy in ctx_copies:
        copy.wait()
    context_sum = ctx_in[0].astype(f32)
    for device in range(1, shards):
        context_sum = context_sum + ctx_in[device].astype(f32)
    at = lax.broadcasted_iota(jnp.int32, (1, context_sum.shape[1]), 1)
    context_sum = jnp.where(at < NLAT * NCTX, context_sum, 0.0)
    map_grad[...] = jnp.dot(
        context_sum.astype(map_grad.dtype), context_in.wait()[...], preferred_element_type=f32
    ).astype(map_grad.dtype)
    small[SMALL_MAP : SMALL_MAP + 1, :cols] = lax.dot_general(
        ones(context_sum),
        context_sum,
        (((1,), (1,)), ((), ())),
        precision=HIGHEST_PRECISION,
        preferred_element_type=f32,
    )[0:1]
    small_out[...] = small[...].astype(small_out.dtype)
    weight_sum.finish()


def conv_back_kernel(
    shards,
    emit,
    shape,
    d_pre,
    fc1,
    normed,
    inverse,
    d_first,
    hidden,
    wide,
    normed_full,
    branch,
    map_grad,
    act_out,
    second,
    fc2_half,
    small,
    input_grad,
    fc1_sum,
    fc2_sum,
    map_sum,
    small_sum,
    conv_sum,
    activations,
    held,
    floats,
    acc,
    to_y,
    from_y,
    to_z,
    from_z,
    y_sems,
    z_sems,
    edge_sems,
    d_conv_params,
    fc1_own,
    fc1_got,
    fc1_other,
    fc2_other,
    fc2_part,
    map_own,
    map_got,
    map_other,
    pair_sems,
    fc2_sems,
    small_in,
    small_sems,
    conv_out,
    conv_in,
    conv_part,
    conv_group,
    conv_sems,
    act_in,
    act_sems,
):
    f32 = jnp.float32
    rows = acc.shape[0]
    depth = shards // 2
    groups = lax.axis_size("grp")
    me = lax.axis_index("seq")
    meet_all(shards, groups)
    cols = conv_part.shape[1]
    width = d_pre.shape[2]
    total = shards * rows
    latents = Latents(shape, total)
    positions = me * rows + lax.broadcasted_iota(jnp.int32, (rows, 1), 0)
    fc1_pair = PairSum(fc1_own, fc1_got, fc1_other, fc1_sum, pair_sems.at[0])
    map_pair = PairSum(map_own, map_got, map_other, map_sum, pair_sems.at[1])
    fc2_quarter = QuarterSum(shards, fc2_half, fc2_other, fc2_part, fc2_sum, fc2_sems)
    group = lax.axis_index("grp")
    small_copies = [
        grp_copy(
            small,
            small_in.at[step - 1],
            small_sems.at[0, step - 1],
            small_sems.at[1, step - 1],
            lax.rem(group + step, groups),
        )
        for step in range(1, groups)
    ]

    def partial(block):
        return dot_nt(d_pre[block], fc1[...])

    peers = [lax.rem(me + step, shards) for step in range(1, shards)]
    act_copies = []
    for n, peer in enumerate(peers):
        there = pl.ds(pl.multiple_of(peer * rows, 128), rows)
        act_copies.append(
            seq_copy(act_out.at[:, there], act_in.at[me], act_sems.at[0, n], act_sems.at[1, n], peer)
        )

    def fc1_grad():
        full = normed_full.wait()

        def tile(index):
            here = pl.ds(pl.multiple_of(index * 256, 256), 256)
            fc1_own[here, :] = dot_tn(
                full[:, :, here].reshape(total, 256), d_pre[...].reshape(total, width)
            ).astype(fc1_own.dtype)

        tile_loop(C // 256, tile)
        fc1_pair.begin()

    fc2_quarter.begin()
    map_own[...] = map_grad[...]
    map_pair.begin()

    def early(step):
        @pl.when(step == 1)
        def _():
            for copy in act_copies:
                copy.start()
            fc1_grad()

    def scatter_hook(step):
        @pl.when(step == 1)
        def _():
            fc2_quarter.spread()
            fc1_pair.across()
            map_pair.across()

    scatter_blocks(
        partial,
        to_y,
        from_y,
        to_z,
        from_z,
        acc,
        y_sems,
        z_sems,
        depth,
        None,
        scatter_hook,
        early,
    )
    normed, d_first, hidden = normed.wait(), d_first.wait(), hidden.wait()

    def norm_tile(index):
        start = pl.multiple_of(index * 16, 16)
        here = pl.ds(start, 16)
        held[pl.ds(EDGE + start, 16), :] = norm_back(
            acc[here, :], normed[here, :], inverse[here, :]
        ).astype(held.dtype)

    tile_loop(rows // 16, norm_tile)
    finish = exchange_edges(held, edge_sems, rows, shards)
    for copy in small_copies:
        copy.start()
    fc2_quarter.share()
    tile_loop(
        floats.shape[0] // 32,
        lambda i: floats.__setitem__(
            (pl.ds(i * 32, 32), slice(None)), hidden[pl.ds(i * 32, 32), :].astype(f32)
        ),
    )
    d_conv_params[...] = jnp.zeros_like(d_conv_params)
    masks = [latents.valid(positions, tap // 3 - 1, tap % 3 - 1) for tap in range(9)]

    def grad_tile(index):
        cols = pl.ds(pl.multiple_of(index * 256, 256), 256)
        d_conv = held[pl.ds(EDGE, rows), cols].astype(f32)
        d_conv_params[9:10, cols] = jnp.sum(d_conv, axis=0, keepdims=True)
        d_conv_params[10:11, cols] = branch[0:1, cols]
        for tap in range(9):
            offset = EDGE + (tap // 3 - 1) * WMAX + tap % 3 - 1
            d_conv_params[tap : tap + 1, cols] = jnp.sum(
                d_conv * floats[offset : offset + rows, cols] * masks[tap],
                axis=0,
                keepdims=True,
            )

    tile_loop(C // 256, grad_tile)
    for goal in range(shards):
        conv_out[goal] = d_conv_params[:, goal * cols : (goal + 1) * cols]
    conv_in[me] = conv_out[me]
    conv_copies = []
    for step in range(1, shards):
        goal = lax.rem(me + step, shards)
        conv_copies.append(
            seq_copy(
                conv_out.at[goal],
                conv_in.at[me],
                conv_sems.at[0, step - 1],
                conv_sems.at[1, step - 1],
                goal,
            )
        )
        conv_copies[-1].start()
    finish()
    act_in[me] = act_out[:, pl.ds(pl.multiple_of(me * rows, 128), rows)]
    tile_loop(
        floats.shape[0] // 32,
        lambda i: floats.__setitem__(
            (pl.ds(i * 32, 32), slice(None)), held[pl.ds(i * 32, 32), :].astype(f32)
        ),
    )

    back_masks = []
    for tap in range(9):
        down_step, side_step = tap // 3 - 1, tap % 3 - 1
        back_masks.append(
            latents.valid(positions - down_step * WMAX - side_step, down_step, side_step)
        )

    def input_tile(index):
        cols = pl.ds(pl.multiple_of(index * 256, 256), 256)
        total = d_first[:, cols]
        for tap in range(9):
            offset = EDGE - (tap // 3 - 1) * WMAX - tap % 3 + 1
            total = total + (
                floats[offset : offset + rows, cols] * wide[tap : tap + 1, cols]
            ) * back_masks[tap]
        input_grad[:, cols] = total

    for copy in conv_copies:
        copy.wait()
    conv_total = conv_in[0]
    for device in range(1, shards):
        conv_total = conv_total + conv_in[device]
    tile_loop(C // 256, input_tile)
    fc1_pair.share()
    conv_part[...] = conv_total
    group_copies = []
    for step in range(1, groups):
        k = shards - 2 + step
        group_copies.append(
            grp_copy(
                conv_part,
                conv_group.at[step - 1],
                conv_sems.at[0, k],
                conv_sems.at[1, k],
                lax.rem(group + step, groups),
            )
        )
        group_copies[-1].start()
    fc2_quarter.share_core()
    for copy in act_copies:
        copy.wait()
    activations[...] = (second.wait()[...] + act_in[...].reshape(C, rows).astype(f32).T).astype(
        activations.dtype
    )
    map_pair.share()
    for copy in (*small_copies, *group_copies):
        copy.wait()
    small_total = small[...].astype(f32)
    for step in range(groups - 1):
        small_total = small_total + small_in[step].astype(f32)
    small_sum[...] = small_total
    conv_sum[...] = conv_part[...] + conv_group[0] + conv_group[1] + conv_group[2]
    fc2_quarter.finish()
    emit(fc2_sum)
    map_pair.finish()
    fc1_pair.finish()


class Late:
    def __init__(self, buffer, copy):
        self.buffer, self.copy = buffer, copy

    def wait(self):
        self.copy.wait()
        return self.buffer


def staged_body(body, n_in, n_out, late, staged):
    def run(*refs):
        ins, outs = list(refs[:n_in]), list(refs[n_in : n_in + n_out])
        rest = refs[n_in + n_out :]
        count = len(late) + len(staged)
        if not count:
            body(lambda *buffers: None, *refs)
            return
        kept, buffers, sems = rest[: -count - 1], rest[-count - 1 : -1], rest[-1]
        for n, k in enumerate(late):
            copy = pltpu.make_async_copy(ins[k], buffers[n], sems.at[n])
            copy.start()
            ins[k] = Late(buffers[n], copy)
        waiting = []
        for n, k in enumerate(staged, len(late)):
            waiting.append([buffers[n], pltpu.make_async_copy(buffers[n], outs[k], sems.at[n]), 0])
            outs[k] = buffers[n]

        def emit(*which):
            for entry in waiting:
                if not entry[2] and any(entry[0] is ref for ref in which):
                    entry[1].start()
                    entry[2] = 1

        body(emit, *ins, *outs, *kept)
        emit(*(entry[0] for entry in waiting))
        for entry in waiting:
            entry[1].wait()

    return run


def kernel_call(
    body, name, number, outs, scratch, operands, flops=0, far=(), scalars=(), late=(), staged=()
):
    vmem, anywhere, smem = (
        pl.BlockSpec(memory_space=space) for space in (pltpu.VMEM, pl.ANY, pltpu.SMEM)
    )
    in_specs = [
        anywhere if k in far or k in late else smem if k in scalars else vmem
        for k in range(len(operands))
    ]
    shapes = [jax.ShapeDtypeStruct(shape, dtype) for shape, dtype in outs]
    moved = sum(math.prod(s.shape) * s.dtype.itemsize for s in shapes) + sum(
        x.size * x.dtype.itemsize for x in operands
    )
    extra = [pltpu.VMEM(operands[k].shape, operands[k].dtype) for k in late]
    extra += [pltpu.VMEM(shapes[k].shape, shapes[k].dtype) for k in staged]
    if extra:
        extra.append(pltpu.SemaphoreType.DMA((len(extra),)))
    return pl.pallas_call(
        staged_body(body, len(operands), len(outs), late, staged),
        out_shape=shapes,
        in_specs=in_specs,
        out_specs=[anywhere if k in staged else vmem for k in range(len(shapes))],
        scratch_shapes=[*scratch, *extra],
        name=name,
        cost_estimate=pl.CostEstimate(flops=flops, bytes_accessed=moved, transcendentals=0),
        compiler_params=pltpu.CompilerParams(
            collective_id=number, has_side_effects=True, vmem_limit_bytes=VMEM_BYTES
        ),
    )(*operands)


def scatter_scratch(rows, depth):
    bf16 = jnp.bfloat16
    return [
        pltpu.VMEM((depth, rows, C), bf16),
        pltpu.VMEM((depth, rows, C), bf16),
        pltpu.VMEM((depth, rows, C), bf16),
        pltpu.VMEM((depth + 1, rows, C), bf16),
        pltpu.SemaphoreType.DMA((2, depth)),
        pltpu.SemaphoreType.DMA((2, 2, depth)),
    ]


def gather_scratch(depth):
    return pltpu.SemaphoreType.DMA((6, 2, depth + 1))


def total_scratch(shards):
    return [
        pltpu.VMEM((8, 128), jnp.float32),
        pltpu.VMEM((shards - 1, 8, 128), jnp.float32),
    ], pltpu.SemaphoreType.DMA((2, shards - 1))


def on_device_heads(
    hidden,
    latent_shape,
    cond_r,
    clip,
    cotangent,
    conv_weight,
    conv_bias,
    fc1_weight,
    fc1_bias,
    grn_gamma,
    grn_beta,
    fc2_weight,
    fc2_bias,
    time_weight,
    time_bias,
    map_weight,
    map_bias,
    query_weight,
    query_bias,
    key_weight,
    value_weight,
    value_bias,
    out_weight,
    out_bias,
):
    f32, bf16 = jnp.float32, jnp.bfloat16
    shards = lax.axis_size("seq")
    rows = hidden.shape[0]
    total = rows * shards
    cols = C // shards
    depth = shards // 2
    hidden_cols = FF // shards
    shape = latent_shape[0]
    w_qkv = jnp.concatenate([query_weight.T, key_weight.T, value_weight.T], axis=0)
    ctx_rows = 256
    context_in = jax.nn.silu(clip.reshape(NLAT * NCTX, CLIP).astype(f32)).astype(bf16)
    context_in = jnp.pad(context_in, ((0, ctx_rows - NLAT * NCTX), (0, 0)))
    ctx_cols = (against(map_weight.T, context_in) + map_bias.astype(f32)[:, None]).astype(bf16)
    units = cols // 4
    vmem = pltpu.VMEM
    total_vmem, total_sems = total_scratch(shards)
    (
        normed_full,
        held,
        wide,
        normed_one,
        inverse_one,
        pre_act,
        root,
        ratio,
        denom,
        response,
        context,
        d_mixed,
        cot_blocks,
        shrink_parts,
    ) = kernel_call(
        functools.partial(mixer_kernel, shards),
        "mixer",
        1,
        [
            ((shards, rows, C), bf16),
            ((rows + 2 * EDGE, C), bf16),
            ((32, C), f32),
            ((rows, C), f32),
            ((rows, 1), f32),
            ((shards, rows, hidden_cols), f32),
            ((8, hidden_cols), f32),
            ((8, hidden_cols), f32),
            ((8, 128), f32),
            ((shards, rows, hidden_cols), bf16),
            ((shards, cols, ctx_rows), bf16),
            ((depth, 2, rows, cols), bf16),
            ((depth, 2, rows, cols), bf16),
            ((shards, 4, units, hidden_cols), bf16),
        ],
        [
            vmem((24, cols), f32),
            vmem((shards, 24, cols), f32),
            vmem((rows + 2 * EDGE, C), f32),
            vmem((rows, C), f32),
            vmem((shards, rows, hidden_cols), f32),
            vmem((8, hidden_cols), f32),
            *total_vmem,
            pltpu.SemaphoreType.DMA((2, 2)),
            pltpu.SemaphoreType.DMA((2, shards - 1)),
            gather_scratch(depth),
            total_sems,
            gather_scratch(depth),
            pltpu.SemaphoreType.DMA((2, 2, depth + 1)),
            vmem((shards, 4, 2, units, cols), bf16),
            vmem((2, cols, C), bf16),
            vmem((depth, rows, C), bf16),
            vmem((2, depth, rows, cols), bf16),
            pltpu.SemaphoreType.DMA((2, 2)),
            pltpu.SemaphoreType.DMA((2,)),
            pltpu.SemaphoreType.DMA((2, shards + 2)),
            pltpu.SemaphoreType.DMA((2, shards + 2)),
        ],
        (
            shape,
            hidden,
            cond_r,
            time_weight,
            conv_weight,
            conv_bias,
            fc1_bias,
            grn_gamma,
            grn_beta,
            fc2_bias,
            time_bias,
            fc1_weight,
            ctx_cols,
            cotangent,
            fc2_weight.T,
            out_weight.reshape(shards, 4, units, cols),
        ),
        flops=2 * total * C * hidden_cols,
        far=(14, 15),
        scalars=(0,),
        late=(11, 13),
        staged=(0, 1, 2, 3, 5, 9, 10, 13),
    )
    context = context.reshape(C, ctx_rows)
    shrink_rows = shrink_parts.reshape(C, hidden_cols)
    keys_all = total + ctx_rows
    (
        attn_blocks,
        first_sum,
        second_sum,
        normed_two,
        inverse_two,
        queries,
        keys,
        values,
    ) = kernel_call(
        functools.partial(mixed_in_kernel, shards),
        "mixed_in",
        2,
        [
            ((shards, rows, C), bf16),
            ((rows, C), f32),
            ((rows, C), f32),
            ((rows, C), f32),
            ((rows, 1), f32),
            ((shards, rows, cols), bf16),
            ((cols, keys_all), bf16),
            ((cols, keys_all), bf16),
        ],
        [pltpu.VMEM((rows, C), f32), *scatter_scratch(rows, depth), gather_scratch(depth)],
        (
            shape,
            response,
            shrink_rows,
            hidden,
            wide,
            w_qkv,
            query_bias,
            value_bias,
            context,
        ),
        flops=2 * total * C * (hidden_cols + 3 * cols),
        scalars=(0,),
        late=(3, 5, 8),
        staged=(0, 1, 2, 3, 5, 6, 7),
    )

    tiles, tile_rows = 4, total // 4
    d_qkv, mixed_full, cot_cols = kernel_call(
        functools.partial(attend_kernel, shards),
        "attend",
        5,
        [
            ((3 * cols, keys_all), bf16),
            ((tiles, shards, cols, tile_rows), bf16),
            ((cols, total), bf16),
        ],
        [
            vmem((cols, keys_all), f32),
            vmem((cols, keys_all), f32),
            vmem((cols // HEAD_DIM, tile_rows, keys_all), f32),
            pltpu.SemaphoreType.DMA((tiles, 6, 2, depth + 1)),
        ],
        (
            shape,
            queries,
            keys,
            values,
            d_mixed.reshape(shards, rows, cols),
            cot_blocks.reshape(shards, rows, cols),
        ),
        flops=12 * total * keys_all * 3 * 256,
        scalars=(0,),
    )
    (
        d_first,
        d_pre,
        small,
        weight_sums,
        grad_map_w,
        act_cols,
        fc2_half,
        branch_sum,
    ) = kernel_call(
        functools.partial(attn_back_kernel, shards),
        "attn_back",
        3,
        [
            ((rows, C), f32),
            ((shards, rows, hidden_cols), bf16),
            ((SMALL_ROWS, 2 * cols), bf16),
            ((4 * cols, C), bf16),
            ((cols, CLIP), bf16),
            ((cols, total), bf16),
            ((shards, 2, units, hidden_cols), bf16),
            ((8, C), f32),
        ],
        [
            vmem((shards, rows, C), bf16),
            vmem((8, C), f32),
            vmem((SMALL_ROWS, 2 * cols), f32),
            pltpu.VMEM((rows, C), f32),
            pltpu.VMEM((shards, rows, hidden_cols), f32),
            pltpu.VMEM((shards, rows, hidden_cols), bf16),
            pltpu.VMEM((8, hidden_cols), f32),
            *total_vmem,
            *scatter_scratch(rows, depth),
            gather_scratch(depth),
            total_sems,
            vmem((4 * cols, C), bf16),
            vmem((2 * cols, C), bf16),
            vmem((2 * cols, C), bf16),
            pltpu.SemaphoreType.DMA((2, 3)),
            vmem((shards, 8, 2 * cols), f32),
            pltpu.SemaphoreType.DMA((2, shards - 1)),
            vmem((shards, 4, units, hidden_cols), bf16),
            vmem((2, shards, units, hidden_cols), bf16),
            pltpu.SemaphoreType.DMA((2, 2)),
            vmem((shards, cols, ctx_rows), bf16),
            vmem((shards, cols, ctx_rows), bf16),
            pltpu.SemaphoreType.DMA((2, shards - 1)),
        ],
        (
            shape,
            cond_r,
            d_qkv,
            w_qkv,
            attn_blocks,
            context,
            mixed_full,
            cot_cols,
            out_weight.T,
            grn_gamma,
            out_bias,
            cotangent,
            normed_two,
            inverse_two,
            first_sum,
            wide,
            shrink_rows,
            pre_act,
            root,
            ratio,
            denom,
            response,
            context_in,
        ),
        flops=2 * total * C * (hidden_cols + 6 * cols),
        scalars=(0,),
        late=(4, 5, 6, 7, 8, 11, 12, 14, 16, 17, 21, 22),
        staged=(0, 1, 3, 5, 6),
    )
    groups = lax.axis_size("grp")
    input_grad, fc1_sum, fc2_sum, map_sum, small, conv_small, activations = kernel_call(
        functools.partial(conv_back_kernel, shards),
        "conv_back",
        4,
        [
            ((rows, C), f32),
            ((C, hidden_cols), bf16),
            ((cols, FF), bf16),
            ((cols, CLIP), bf16),
            ((SMALL_ROWS, 2 * cols), f32),
            ((16, cols), f32),
            ((rows, C), bf16),
        ],
        [
            vmem((rows + 2 * EDGE, C), bf16),
            vmem((rows + 2 * EDGE, C), f32),
            vmem((rows, C), f32),
            *scatter_scratch(rows, depth),
            pltpu.SemaphoreType.DMA((2, 2)),
            vmem((16, C), f32),
            vmem((C, hidden_cols), bf16),
            vmem((C // 2, hidden_cols), bf16),
            vmem((C // 2, hidden_cols), bf16),
            vmem((shards, units, hidden_cols), bf16),
            vmem((shards, units, hidden_cols), bf16),
            vmem((cols, CLIP), bf16),
            vmem((cols // 2, CLIP), bf16),
            vmem((cols // 2, CLIP), bf16),
            pltpu.SemaphoreType.DMA((2, 2, 3)),
            pltpu.SemaphoreType.DMA((2, 3 + shards)),
            vmem((groups - 1, SMALL_ROWS, 2 * cols), bf16),
            pltpu.SemaphoreType.DMA((2, groups - 1)),
            vmem((shards, 16, cols), f32),
            vmem((shards, 16, cols), f32),
            vmem((16, cols), f32),
            vmem((groups - 1, 16, cols), f32),
            pltpu.SemaphoreType.DMA((2, shards + groups - 2)),
            vmem((shards, cols, rows), bf16),
            pltpu.SemaphoreType.DMA((2, shards - 1)),
        ],
        (
            shape,
            d_pre,
            fc1_weight,
            normed_one,
            inverse_one,
            d_first,
            held,
            wide,
            normed_full,
            branch_sum,
            grad_map_w,
            act_cols,
            second_sum,
            fc2_half,
            small,
        ),
        flops=6 * total * C * hidden_cols,
        scalars=(0,),
        late=(3, 5, 6, 8, 12),
        staged=(1, 2),
    )
    two = lambda row: small[row : row + 2].reshape(hidden_cols)
    one = lambda row: small[row, :cols]
    part = lambda k: weight_sums[k * cols : (k + 1) * cols].astype(f32).T
    return (
        activations,
        input_grad,
        conv_small[:9],
        conv_small[9],
        fc1_sum.astype(f32),
        two(SMALL_FC1),
        two(SMALL_GAMMA),
        two(SMALL_BETA),
        fc2_sum.astype(f32).T,
        conv_small[10],
        small[:SMALL_FC1],
        small[SMALL_TIME],
        map_sum.astype(f32).T,
        one(SMALL_MAP),
        part(0),
        one(SMALL_QUERY),
        part(1),
        part(2),
        one(SMALL_VALUE),
        part(3),
        one(SMALL_OUT),
    )


def solution(mesh):
    in_specs = (
        P(("grp", "seq"), None),
        P("grp", None, None),
        P("grp", None),
        P("grp", None, None),
        P(("grp", "seq"), None),
        P(None, "seq"),
        P("seq"),
        P(None, "seq"),
        P("seq"),
        P("seq"),
        P("seq"),
        P(None, "seq"),
        P("seq"),
        P(None, "seq"),
        P("seq"),
        P(None, "seq"),
        P("seq"),
        P(None, "seq"),
        P("seq"),
        P(None, "seq"),
        P(None, "seq"),
        P("seq"),
        P(None, "seq"),
        P("seq"),
    )
    out_specs = (
        P(("grp", "seq"), None),
        P(("grp", "seq"), None),
        P(None, "seq"),
        P("seq"),
        P(None, "seq"),
        P("seq"),
        P("seq"),
        P("seq"),
        P(None, "seq"),
        P("seq"),
        P(None, "seq"),
        P("seq"),
        P(None, "seq"),
        P("seq"),
        P(None, "seq"),
        P("seq"),
        P(None, "seq"),
        P(None, "seq"),
        P("seq"),
        P(None, "seq"),
        P("seq"),
    )
    by_heads = mesh.shape["seq"] == 8 and mesh.shape["grp"] == 4
    return jax.shard_map(
        on_device_heads if by_heads else on_device, mesh=mesh, in_specs=in_specs, out_specs=out_specs, check_vma=False
    )
```

```python
import functools
import math

import jax
import jax.numpy as jnp
from jax import lax
from jax.experimental import pallas as pl
from jax.experimental.pallas import tpu as pltpu
from jax.sharding import PartitionSpec as P

C = 1536
HEADS = 24
HEAD_DIM = 64
FF = 6144
CLIP = 1280
NCTX = 77
NLAT = 3
WMAX = 64


EPS_NORM = 1e-06
SCORE_SCALE = 0.125
MASKED = -1e30
HIGHEST_PRECISION = lax.Precision.HIGHEST


def padded_2(block, sides, width):
    for axis, dim in sides:
        count = lax.axis_size(axis)
        forward = [(i, i + 1) for i in range(count - 1)]
        backward = [(target, source) for source, target in forward]
        low = lax.ppermute(
            lax.slice_in_dim(block, block.shape[dim] - width, None, axis=dim), axis, forward
        )
        high = lax.ppermute(lax.slice_in_dim(block, 0, width, axis=dim), axis, backward)
        block = jnp.concatenate([low, block, high], axis=dim)
    return block


def latent_grid(positions, shape_row):
    latent_count = shape_row.shape[0]
    heights = shape_row[:, 0]
    latent_width = shape_row[0, 1]
    pixel_counts = heights * latent_width
    end_points = jnp.cumsum(pixel_counts)
    start_points = end_points - pixel_counts
    segment = jnp.sum((positions[:, None] >= end_points[None, :]).astype(jnp.int32), axis=1)
    segment = jnp.minimum(segment, latent_count - 1)
    picked = (segment[:, None] == jnp.arange(latent_count, dtype=jnp.int32)[None, :]).astype(
        jnp.int32
    )
    first_pixel = jnp.sum(picked * start_points[None, :], axis=1)
    height = jnp.sum(picked * heights[None, :], axis=1)
    offset_in = positions - first_pixel
    row_index = jnp.floor_divide(offset_in, latent_width)
    column = offset_in - row_index * latent_width
    return (segment, row_index, column, height, latent_width)


def valid_tap(row_index, column, height, latent_width, down_step, side_step):
    upright = (row_index + down_step >= 0) & (row_index + down_step < height)
    across = (column + side_step >= 0) & (column + side_step < latent_width)
    return (upright & across).astype(jnp.float32)


def layer_stats(values_in):
    average = jnp.mean(values_in, axis=-1, keepdims=True)
    centred = values_in - average
    variance = jnp.mean(centred * centred, axis=-1, keepdims=True)
    inverse = lax.rsqrt(variance + EPS_NORM)
    return (centred * inverse, inverse)


def layer_back(gradient, normed, inverse):
    mean_grad = jnp.mean(gradient, axis=-1, keepdims=True)
    mean_mixed = jnp.mean(gradient * normed, axis=-1, keepdims=True)
    return inverse * (gradient - mean_grad - normed * mean_mixed)


def against(values_low, weight_low):
    return lax.dot_general(
        values_low, weight_low, (((1,), (1,)), ((), ())), preferred_element_type=jnp.float32
    )


def against_exact(values_in, weight_in):
    return lax.dot_general(
        values_in,
        weight_in,
        (((1,), (1,)), ((), ())),
        precision=HIGHEST_PRECISION,
        preferred_element_type=jnp.float32,
    )


def outer_sum(left_low, right_low):
    return lax.dot_general(
        left_low, right_low, (((0,), (0,)), ((), ())), preferred_element_type=jnp.float32
    )


def column_sum(picked, values_in):
    return lax.dot_general(
        picked,
        values_in,
        (((0,), (0,)), ((), ())),
        precision=HIGHEST_PRECISION,
        preferred_element_type=jnp.float32,
    )


def exact_gelu(values_in):
    return jax.nn.gelu(values_in, approximate=False)


def block_size(row_count, shard_rows):
    shard_total = row_count // shard_rows
    return math.gcd(shard_total, max(1, 1024 // shard_rows)) * shard_rows


def on_device(
    hidden,
    latent_shape,
    cond_r,
    clip,
    cotangent,
    conv_weight,
    conv_bias,
    fc1_weight,
    fc1_bias,
    grn_gamma,
    grn_beta,
    fc2_weight,
    fc2_bias,
    time_weight,
    time_bias,
    map_weight,
    map_bias,
    query_weight,
    query_bias,
    key_weight,
    value_weight,
    value_bias,
    out_weight,
    out_bias,
):
    tok_rows = hidden.shape[0]
    positions = lax.axis_index("seq") * tok_rows + jnp.arange(tok_rows, dtype=jnp.int32)
    shape_row = latent_shape[0]
    segment, row_index, column, height, latent_width = latent_grid(positions, shape_row)
    margin = WMAX + 1
    gathered = (
        lax.all_gather(conv_weight, "seq", axis=1, tiled=True),
        lax.all_gather(conv_bias, "seq", axis=0, tiled=True),
        lax.all_gather(fc1_weight, "seq", axis=1, tiled=True),
        lax.all_gather(fc1_bias, "seq", axis=0, tiled=True),
        lax.all_gather(grn_gamma, "seq", axis=0, tiled=True),
        lax.all_gather(grn_beta, "seq", axis=0, tiled=True),
        lax.all_gather(fc2_weight, "seq", axis=1, tiled=True),
        lax.all_gather(fc2_bias, "seq", axis=0, tiled=True),
        lax.all_gather(time_weight, "seq", axis=1, tiled=True),
        lax.all_gather(time_bias, "seq", axis=0, tiled=True),
        lax.all_gather(map_weight, "seq", axis=1, tiled=True),
        lax.all_gather(map_bias, "seq", axis=0, tiled=True),
        lax.all_gather(query_weight, "seq", axis=1, tiled=True),
        lax.all_gather(query_bias, "seq", axis=0, tiled=True),
        lax.all_gather(key_weight, "seq", axis=1, tiled=True),
        lax.all_gather(value_weight, "seq", axis=1, tiled=True),
        lax.all_gather(value_bias, "seq", axis=0, tiled=True),
        lax.all_gather(out_weight, "seq", axis=1, tiled=True),
        lax.all_gather(out_bias, "seq", axis=0, tiled=True),
    )
    (
        kernel_full,
        kernel_bias,
        expand_full,
        expand_bias,
        gamma_full,
        beta_full,
        shrink_full,
        shrink_bias,
        time_full,
        time_bias_full,
        mapper_full,
        mapper_bias,
        query_full,
        query_bias_full,
        key_full,
        value_full,
        value_bias_full,
        output_full,
        output_bias_full,
    ) = gathered
    padded = padded_2(hidden, (("seq", 0),), margin)
    conv_out = jnp.broadcast_to(kernel_bias.astype(jnp.float32)[None, :], (tok_rows, C))
    tap_list = []
    for down_step in (-1, 0, 1):
        for side_step in (-1, 0, 1):
            tap_number = 3 * (down_step + 1) + (side_step + 1)
            valid = valid_tap(row_index, column, height, latent_width, down_step, side_step)
            offset_rows = down_step * latent_width + side_step
            nearby = lax.dynamic_slice_in_dim(padded, margin + offset_rows, tok_rows, 0).astype(
                jnp.float32
            )
            conv_out = (
                conv_out
                + kernel_full[tap_number].astype(jnp.float32)[None, :] * nearby * valid[:, None]
            )
            tap_list.append((tap_number, down_step, side_step, offset_rows, valid))
    normed_one, inverse_one = layer_stats(conv_out)
    normed_low = normed_one.astype(jnp.bfloat16)
    pre_act = jnp.dot(
        normed_low, expand_full, preferred_element_type=jnp.float32
    ) + expand_bias.astype(jnp.float32)
    activated, gelu_pull = jax.vjp(exact_gelu, pre_act)
    picked = (segment[:, None] == jnp.arange(NLAT, dtype=jnp.int32)[None, :]).astype(jnp.float32)
    energy = lax.psum(column_sum(picked, activated * activated), "seq")
    root = jnp.sqrt(energy + 1.0)
    denom = jnp.mean(root, axis=-1, keepdims=True) + EPS_NORM
    ratio = root / denom
    ratio_rows = jnp.dot(picked, ratio, precision=HIGHEST_PRECISION)
    gamma_value = gamma_full.astype(jnp.float32)
    response = gamma_value * (activated * ratio_rows) + beta_full.astype(jnp.float32) + activated
    response_low = response.astype(jnp.bfloat16)
    branch = jnp.dot(
        response_low, shrink_full, preferred_element_type=jnp.float32
    ) + shrink_bias.astype(jnp.float32)
    first_sum = hidden.astype(jnp.float32) + branch
    modulation = jnp.dot(
        cond_r, time_full.astype(jnp.float32), precision=HIGHEST_PRECISION
    ) + time_bias_full.astype(jnp.float32)
    mod_rows = jnp.dot(picked, modulation, precision=HIGHEST_PRECISION)
    scale_rows = 1.0 + mod_rows[:, :C]
    second_sum = first_sum * scale_rows + mod_rows[:, C:]
    normed_two, inverse_two = layer_stats(second_sum)
    attn_in = normed_two.astype(jnp.bfloat16)
    context_in = jax.nn.silu(clip.reshape(NLAT * NCTX, CLIP).astype(jnp.float32)).astype(
        jnp.bfloat16
    )
    context = (
        jnp.dot(context_in, mapper_full, preferred_element_type=jnp.float32)
        + mapper_bias.astype(jnp.float32)
    ).astype(jnp.bfloat16)
    queries = (
        jnp.dot(attn_in, query_full, preferred_element_type=jnp.float32)
        + query_bias_full.astype(jnp.float32)
    ).astype(jnp.bfloat16)
    keys_low = jnp.dot(attn_in, key_full, preferred_element_type=jnp.float32).astype(jnp.bfloat16)
    values_low = (
        jnp.dot(attn_in, value_full, preferred_element_type=jnp.float32)
        + value_bias_full.astype(jnp.float32)
    ).astype(jnp.bfloat16)
    context_keys = jnp.dot(context, key_full, preferred_element_type=jnp.float32).astype(
        jnp.bfloat16
    )
    context_values = (
        jnp.dot(context, value_full, preferred_element_type=jnp.float32)
        + value_bias_full.astype(jnp.float32)
    ).astype(jnp.bfloat16)
    query_heads = queries.reshape(tok_rows, HEADS, HEAD_DIM)
    key_heads = keys_low.reshape(tok_rows, HEADS, HEAD_DIM)
    value_heads = values_low.reshape(tok_rows, HEADS, HEAD_DIM)
    ctx_key_heads = context_keys.reshape(NLAT * NCTX, HEADS, HEAD_DIM)
    ctx_value_heads = context_values.reshape(NLAT * NCTX, HEADS, HEAD_DIM)
    context_segment = jnp.arange(NLAT * NCTX, dtype=jnp.int32) // NCTX
    ctx_admit = segment[:, None] == context_segment[None, :]

    def segments_at(first_row, length):
        return latent_grid(first_row + jnp.arange(length, dtype=jnp.int32), shape_row)[0]

    ctx_scores = (
        jnp.einsum("qhd,khd->hqk", query_heads, ctx_key_heads, preferred_element_type=jnp.float32)
        * SCORE_SCALE
    )
    ctx_scores = jnp.where(ctx_admit[None], ctx_scores, MASKED)
    start_max = jnp.max(ctx_scores, axis=-1)
    ctx_expo = jnp.exp(ctx_scores - start_max[..., None])
    start_total = jnp.sum(ctx_expo, axis=-1)
    start_accum = jnp.einsum(
        "hqk,khd->qhd",
        ctx_expo.astype(jnp.bfloat16),
        ctx_value_heads,
        preferred_element_type=jnp.float32,
    )
    key_part = lax.all_gather(keys_low, "seq", axis=0, tiled=True)
    value_part = lax.all_gather(values_low, "seq", axis=0, tiled=True)
    block_rows = block_size(key_part.shape[0], tok_rows)
    block_count = key_part.shape[0] // block_rows
    key_stack = key_part.reshape(block_count, block_rows, HEADS, HEAD_DIM)
    value_stack = value_part.reshape(block_count, block_rows, HEADS, HEAD_DIM)

    def attend_visit(state_now, element):
        key_block, value_block, block_index = element
        key_segment = segments_at(block_index * block_rows, block_rows)
        admitted = segment[:, None] == key_segment[None, :]
        scores = (
            jnp.einsum("qhd,khd->hqk", query_heads, key_block, preferred_element_type=jnp.float32)
            * SCORE_SCALE
        )
        scores = jnp.where(admitted[None], scores, MASKED)
        old_max, old_total, old_accum = state_now
        new_max = jnp.maximum(old_max, jnp.max(scores, axis=-1))
        factor = jnp.exp(old_max - new_max)
        expo_block = jnp.exp(scores - new_max[..., None])
        new_total = old_total * factor + jnp.sum(expo_block, axis=-1)
        new_accum = old_accum * factor.T[:, :, None] + jnp.einsum(
            "hqk,khd->qhd",
            expo_block.astype(jnp.bfloat16),
            value_block,
            preferred_element_type=jnp.float32,
        )
        return ((new_max, new_total, new_accum), None)

    state_end, ignored = lax.scan(
        attend_visit,
        (start_max, start_total, start_accum),
        (key_stack, value_stack, jnp.arange(block_count, dtype=jnp.int32)),
    )
    run_max, run_total, accum = state_end
    mixed = accum / run_total.T[:, :, None]
    log_total = run_max + jnp.log(run_total)
    mixed_low = mixed.reshape(tok_rows, C).astype(jnp.bfloat16)
    activations = (
        second_sum
        + jnp.dot(mixed_low, output_full, preferred_element_type=jnp.float32)
        + output_bias_full.astype(jnp.float32)
    ).astype(jnp.bfloat16)
    cot_value = cotangent.astype(jnp.float32)
    grad_out_w = outer_sum(mixed_low, cotangent)
    grad_out_b = jnp.sum(cot_value, axis=0)
    d_mixed_low = against(cotangent, output_full).astype(jnp.bfloat16)
    dmix_heads = d_mixed_low.reshape(tok_rows, HEADS, HEAD_DIM)
    delta = jnp.sum(dmix_heads.astype(jnp.float32) * mixed, axis=-1).T
    ctx_probs = jnp.exp(ctx_scores - log_total[..., None])
    ctx_dprob = jnp.einsum(
        "qhd,khd->hqk", dmix_heads, ctx_value_heads, preferred_element_type=jnp.float32
    )
    ctx_dscore = (ctx_probs * (ctx_dprob - delta[..., None])).astype(jnp.bfloat16)
    dquery_start = (
        jnp.einsum("hqk,khd->qhd", ctx_dscore, ctx_key_heads, preferred_element_type=jnp.float32)
        * SCORE_SCALE
    )
    ctx_dkey_part = (
        jnp.einsum("hqk,qhd->khd", ctx_dscore, query_heads, preferred_element_type=jnp.float32)
        * SCORE_SCALE
    )
    ctx_dvalue_part = jnp.einsum(
        "hqk,qhd->khd",
        ctx_probs.astype(jnp.bfloat16),
        dmix_heads,
        preferred_element_type=jnp.float32,
    )
    key_part = lax.all_gather(keys_low, "seq", axis=0, tiled=True)
    value_part = lax.all_gather(values_low, "seq", axis=0, tiled=True)
    query_block_rows = block_size(key_part.shape[0], tok_rows)
    block_count = key_part.shape[0] // query_block_rows
    key_stack = key_part.reshape(block_count, query_block_rows, HEADS, HEAD_DIM)
    value_stack = value_part.reshape(block_count, query_block_rows, HEADS, HEAD_DIM)

    def query_visit(state_now, element):
        key_block, value_block, block_index = element
        key_segment = segments_at(block_index * query_block_rows, query_block_rows)
        admitted = segment[:, None] == key_segment[None, :]
        scores = (
            jnp.einsum("qhd,khd->hqk", query_heads, key_block, preferred_element_type=jnp.float32)
            * SCORE_SCALE
        )
        scores = jnp.where(admitted[None], scores, MASKED)
        probs = jnp.exp(scores - log_total[..., None])
        dprob = jnp.einsum(
            "qhd,khd->hqk", dmix_heads, value_block, preferred_element_type=jnp.float32
        )
        dscore = (probs * (dprob - delta[..., None])).astype(jnp.bfloat16)
        added = (
            jnp.einsum("hqk,khd->qhd", dscore, key_block, preferred_element_type=jnp.float32)
            * SCORE_SCALE
        )
        return (state_now + added, None)

    state_end, ignored = lax.scan(
        query_visit,
        dquery_start,
        (key_stack, value_stack, jnp.arange(block_count, dtype=jnp.int32)),
    )
    dquery = state_end
    lse_all, delta_all = (
        lax.all_gather(log_total.T, "seq", axis=0, tiled=True),
        lax.all_gather(delta.T, "seq", axis=0, tiled=True),
    )
    zero_heads = jnp.zeros((tok_rows, HEADS, HEAD_DIM), jnp.float32)
    query_part = lax.all_gather(queries, "seq", axis=0, tiled=True)
    dmix_part = lax.all_gather(d_mixed_low, "seq", axis=0, tiled=True)
    row_count = query_part.shape[0]
    key_block_rows = block_size(row_count, tok_rows)
    block_count = row_count // key_block_rows
    query_stack = query_part.reshape(block_count, key_block_rows, HEADS, HEAD_DIM)
    dmix_stack = dmix_part.reshape(block_count, key_block_rows, HEADS, HEAD_DIM)
    lse_stack = lse_all.reshape(block_count, key_block_rows, HEADS)
    delta_stack = delta_all.reshape(block_count, key_block_rows, HEADS)

    def key_visit(state_now, element):
        query_block, dmix_block, lse_block, delta_block, block_index = element
        query_segment = segments_at(block_index * key_block_rows, key_block_rows)
        admitted = segment[:, None] == query_segment[None, :]
        scores = (
            jnp.einsum("khd,qhd->hkq", key_heads, query_block, preferred_element_type=jnp.float32)
            * SCORE_SCALE
        )
        scores = jnp.where(admitted[None], scores, MASKED)
        probs = jnp.exp(scores - lse_block.T[:, None, :])
        dkey_now, dvalue_now = state_now
        dvalue_now = dvalue_now + jnp.einsum(
            "hkq,qhd->khd",
            probs.astype(jnp.bfloat16),
            dmix_block,
            preferred_element_type=jnp.float32,
        )
        dprob = jnp.einsum(
            "khd,qhd->hkq", value_heads, dmix_block, preferred_element_type=jnp.float32
        )
        dscore = (probs * (dprob - delta_block.T[:, None, :])).astype(jnp.bfloat16)
        dkey_now = (
            dkey_now
            + jnp.einsum("hkq,qhd->khd", dscore, query_block, preferred_element_type=jnp.float32)
            * SCORE_SCALE
        )
        return ((dkey_now, dvalue_now), None)

    state_end, ignored = lax.scan(
        key_visit,
        (zero_heads, zero_heads),
        (query_stack, dmix_stack, lse_stack, delta_stack, jnp.arange(block_count, dtype=jnp.int32)),
    )
    dkey, dvalue = state_end
    dquery_low = dquery.reshape(tok_rows, C).astype(jnp.bfloat16)
    dkey_low = dkey.reshape(tok_rows, C).astype(jnp.bfloat16)
    dvalue_low = dvalue.reshape(tok_rows, C).astype(jnp.bfloat16)
    ctx_dkey_flat = ctx_dkey_part.reshape(NLAT * NCTX, C)
    ctx_dvalue_flat = ctx_dvalue_part.reshape(NLAT * NCTX, C)
    context_value = context.astype(jnp.float32)
    d_attn_in = (
        against(dquery_low, query_full)
        + against(dkey_low, key_full)
        + against(dvalue_low, value_full)
    )
    grad_query_w = outer_sum(attn_in, dquery_low)
    grad_query_b = jnp.sum(dquery_low.astype(jnp.float32), axis=0)
    grad_key_w = outer_sum(attn_in, dkey_low) + column_sum(context_value, ctx_dkey_flat)
    grad_value_w = outer_sum(attn_in, dvalue_low) + column_sum(context_value, ctx_dvalue_flat)
    grad_value_b = jnp.sum(dvalue_low.astype(jnp.float32), axis=0) + jnp.sum(
        ctx_dvalue_flat, axis=0
    )
    d_context = against_exact(ctx_dkey_flat, key_full.astype(jnp.float32)) + against_exact(
        ctx_dvalue_flat, value_full.astype(jnp.float32)
    )
    grad_map_w = column_sum(context_in.astype(jnp.float32), d_context)
    grad_map_b = jnp.sum(d_context, axis=0)
    d_second = cot_value + layer_back(d_attn_in, normed_two, inverse_two)
    d_first = d_second * scale_rows
    d_mod_rows = jnp.concatenate([d_second * first_sum, d_second], axis=1)
    d_modulation = column_sum(picked, d_mod_rows)
    grad_time_w = lax.dot_general(
        cond_r,
        d_modulation,
        (((0,), (0,)), ((), ())),
        precision=HIGHEST_PRECISION,
        preferred_element_type=jnp.float32,
    )
    grad_time_b = jnp.sum(d_modulation, axis=0)
    d_branch_low = d_first.astype(jnp.bfloat16)
    grad_shrink_w = outer_sum(response_low, d_branch_low)
    grad_shrink_b = jnp.sum(d_branch_low.astype(jnp.float32), axis=0)
    d_response = against(d_branch_low, shrink_full)
    grad_gamma = jnp.sum(d_response * activated * ratio_rows, axis=0)
    grad_beta = jnp.sum(d_response, axis=0)
    d_ratio = lax.psum(column_sum(picked, d_response * gamma_value * activated), "seq")
    d_root = d_ratio / denom - jnp.sum(d_ratio * root, axis=-1, keepdims=True) / (
        FF * denom * denom
    )
    d_act = d_response * (gamma_value * ratio_rows + 1.0) + activated * jnp.dot(
        picked, d_root / root, precision=HIGHEST_PRECISION
    )
    d_pre_low = gelu_pull(d_act)[0].astype(jnp.bfloat16)
    grad_expand_w = outer_sum(normed_low, d_pre_low)
    grad_expand_b = jnp.sum(d_pre_low.astype(jnp.float32), axis=0)
    d_normed = against(d_pre_low, expand_full)
    d_conv_low = layer_back(d_normed, normed_one, inverse_one).astype(jnp.bfloat16)
    d_conv = d_conv_low.astype(jnp.float32)
    grad_kernel_b = jnp.sum(d_conv, axis=0)
    d_padded = padded_2(d_conv_low, (("seq", 0),), margin)
    kernel_rows = []
    input_grad = d_first
    for tap_number, down_step, side_step, offset_rows, valid in tap_list:
        nearby = lax.dynamic_slice_in_dim(padded, margin + offset_rows, tok_rows, 0).astype(
            jnp.float32
        )
        kernel_rows.append(jnp.sum(d_conv * nearby * valid[:, None], axis=0))
        source = positions - offset_rows
        src_segment, src_row, src_column, src_height, src_width = latent_grid(source, shape_row)
        src_valid = valid_tap(src_row, src_column, src_height, src_width, down_step, side_step)
        behind = lax.dynamic_slice_in_dim(d_padded, margin - offset_rows, tok_rows, 0).astype(
            jnp.float32
        )
        input_grad = (
            input_grad
            + kernel_full[tap_number].astype(jnp.float32)[None, :] * behind * src_valid[:, None]
        )
    grad_kernel_w = jnp.stack(kernel_rows, axis=0)
    gradients = (
        grad_kernel_w,
        grad_kernel_b,
        grad_expand_w,
        grad_expand_b,
        grad_gamma,
        grad_beta,
        grad_shrink_w,
        grad_shrink_b,
        grad_time_w,
        grad_time_b,
        grad_map_w,
        grad_map_b,
        grad_query_w,
        grad_query_b,
        grad_key_w,
        grad_value_w,
        grad_value_b,
        grad_out_w,
        grad_out_b,
    )
    shares = (
        lax.psum_scatter(gradients[0], "seq", scatter_dimension=1, tiled=True),
        lax.psum_scatter(gradients[1], "seq", scatter_dimension=0, tiled=True),
        lax.psum_scatter(gradients[2], "seq", scatter_dimension=1, tiled=True),
        lax.psum_scatter(gradients[3], "seq", scatter_dimension=0, tiled=True),
        lax.psum_scatter(gradients[4], "seq", scatter_dimension=0, tiled=True),
        lax.psum_scatter(gradients[5], "seq", scatter_dimension=0, tiled=True),
        lax.psum_scatter(gradients[6], "seq", scatter_dimension=1, tiled=True),
        lax.psum_scatter(gradients[7], "seq", scatter_dimension=0, tiled=True),
        lax.psum_scatter(gradients[8], "seq", scatter_dimension=1, tiled=True),
        lax.psum_scatter(gradients[9], "seq", scatter_dimension=0, tiled=True),
        lax.psum_scatter(gradients[10], "seq", scatter_dimension=1, tiled=True),
        lax.psum_scatter(gradients[11], "seq", scatter_dimension=0, tiled=True),
        lax.psum_scatter(gradients[12], "seq", scatter_dimension=1, tiled=True),
        lax.psum_scatter(gradients[13], "seq", scatter_dimension=0, tiled=True),
        lax.psum_scatter(gradients[14], "seq", scatter_dimension=1, tiled=True),
        lax.psum_scatter(gradients[15], "seq", scatter_dimension=1, tiled=True),
        lax.psum_scatter(gradients[16], "seq", scatter_dimension=0, tiled=True),
        lax.psum_scatter(gradients[17], "seq", scatter_dimension=1, tiled=True),
        lax.psum_scatter(gradients[18], "seq", scatter_dimension=0, tiled=True),
    )
    summed = (
        lax.psum(shares[0].astype(jnp.bfloat16), "grp").astype(jnp.float32),
        lax.psum(shares[1].astype(jnp.bfloat16), "grp").astype(jnp.float32),
        lax.psum(shares[2].astype(jnp.bfloat16), "grp").astype(jnp.float32),
        lax.psum(shares[3].astype(jnp.bfloat16), "grp").astype(jnp.float32),
        lax.psum(shares[4].astype(jnp.bfloat16), "grp").astype(jnp.float32),
        lax.psum(shares[5].astype(jnp.bfloat16), "grp").astype(jnp.float32),
        lax.psum(shares[6].astype(jnp.bfloat16), "grp").astype(jnp.float32),
        lax.psum(shares[7].astype(jnp.bfloat16), "grp").astype(jnp.float32),
        lax.psum(shares[8].astype(jnp.bfloat16), "grp").astype(jnp.float32),
        lax.psum(shares[9].astype(jnp.bfloat16), "grp").astype(jnp.float32),
        lax.psum(shares[10].astype(jnp.bfloat16), "grp").astype(jnp.float32),
        lax.psum(shares[11].astype(jnp.bfloat16), "grp").astype(jnp.float32),
        lax.psum(shares[12].astype(jnp.bfloat16), "grp").astype(jnp.float32),
        lax.psum(shares[13].astype(jnp.bfloat16), "grp").astype(jnp.float32),
        lax.psum(shares[14].astype(jnp.bfloat16), "grp").astype(jnp.float32),
        lax.psum(shares[15].astype(jnp.bfloat16), "grp").astype(jnp.float32),
        lax.psum(shares[16].astype(jnp.bfloat16), "grp").astype(jnp.float32),
        lax.psum(shares[17].astype(jnp.bfloat16), "grp").astype(jnp.float32),
        lax.psum(shares[18].astype(jnp.bfloat16), "grp").astype(jnp.float32),
    )
    return (
        activations,
        input_grad,
        summed[0],
        summed[1],
        summed[2],
        summed[3],
        summed[4],
        summed[5],
        summed[6],
        summed[7],
        summed[8],
        summed[9],
        summed[10],
        summed[11],
        summed[12],
        summed[13],
        summed[14],
        summed[15],
        summed[16],
        summed[17],
        summed[18],
    )


def mm(left, right):
    return jnp.dot(left, right, preferred_element_type=jnp.float32)


MESH_ID = pl.DeviceIdType.MESH


def dot_nt(left, right):
    return lax.dot_general(
        left, right, (((1,), (1,)), ((), ())), preferred_element_type=jnp.float32
    )


def place():
    me = lax.axis_index("seq")
    z, y = me // 2, lax.rem(me, 2)
    return me, z, y, me + 1 - 2 * y


def seq_copy(src, dst, send, recv, target):
    return pltpu.make_async_remote_copy(
        src_ref=src,
        dst_ref=dst,
        send_sem=send,
        recv_sem=recv,
        device_id={"seq": target},
        device_id_type=MESH_ID,
    )


def dot_tn(left, right):
    return lax.dot_general(
        left, right, (((0,), (0,)), ((), ())), preferred_element_type=jnp.float32
    )


def grp_copy(src, dst, send, recv, target):
    return pltpu.make_async_remote_copy(
        src_ref=src,
        dst_ref=dst,
        send_sem=send,
        recv_sem=recv,
        device_id={"grp": target},
        device_id_type=MESH_ID,
    )


def group_place():
    group = lax.axis_index("grp")
    core = lax.rem(group, 2)
    return group // 2, core, group + 1 - 2 * core, lax.rem(group + 2, 4)


def meet_all(shards, groups=0):
    me = lax.axis_index("seq")
    barrier = pltpu.get_barrier_semaphore()
    for step in range(1, groups):
        pl.semaphore_signal(
            barrier,
            inc=1,
            device_id={"grp": lax.rem(lax.axis_index("grp") + step, groups)},
            device_id_type=MESH_ID,
        )
    for step in range(1, shards):
        pl.semaphore_signal(
            barrier,
            inc=1,
            device_id={"seq": lax.rem(me + step, shards)},
            device_id_type=MESH_ID,
        )
    pl.semaphore_wait(barrier, shards - 1 + max(groups - 1, 0))


def tile_loop(count, body):
    def step(index, carry):
        body(index)
        return carry

    lax.fori_loop(0, count, step, 0)


def add_rows(target, target_row, left, left_row, right, count):
    def tile(index):
        low = index * 32
        here = pl.ds(pl.multiple_of(target_row + low, 32), 32)
        there = pl.ds(pl.multiple_of(left_row + low, 32), 32)
        value = left[there, :].astype(jnp.float32) + right[
            pl.ds(pl.multiple_of(low, 32), 32), :
        ].astype(jnp.float32)
        target[here, :] = value.astype(target.dtype)

    tile_loop(count // 32, tile)


class PairSum:
    def __init__(self, own, got, other, out, sems):
        x, core, self.core_peer, self.x_peer = group_place()
        self.half = own.shape[0] // 2
        self.own, self.got, self.other, self.out = own, got, other, out
        self.low = pl.multiple_of(core * self.half, self.half)
        mine = pl.ds(self.low, self.half)
        theirs = pl.ds(pl.multiple_of((1 - core) * self.half, self.half), self.half)
        pair = lambda k: (sems.at[0, k], sems.at[1, k])
        self.copies = (
            grp_copy(own.at[theirs], got, *pair(0), self.core_peer),
            grp_copy(own.at[mine], other, *pair(1), self.x_peer),
            grp_copy(out.at[mine], out.at[mine], *pair(2), self.core_peer),
        )

    def begin(self):
        self.copies[0].start()

    def across(self):
        self.copies[0].wait_recv()
        add_rows(self.own, self.low, self.own, self.low, self.got, self.half)
        self.copies[1].start()

    def share(self):
        self.copies[1].wait_recv()
        add_rows(self.out, self.low, self.own, self.low, self.other, self.half)
        self.copies[2].start()

    def finish(self):
        self.copies[2].wait_recv()
        for copy in self.copies:
            copy.wait_send()


class CoreHalf:
    def __init__(self, own, got, half, sems):
        _, core, core_peer, _ = group_place()
        self.own, self.got, self.half, self.core = own, got, half, core
        self.copies = [
            grp_copy(
                own.at[:, side * 2 + 1 - core],
                got.at[side],
                sems.at[0, side],
                sems.at[1, side],
                core_peer,
            )
            for side in (0, 1)
        ]

    def begin(self):
        for copy in self.copies:
            copy.start()

    def finish(self):
        for side, copy in enumerate(self.copies):
            copy.wait_recv()

            def tile(index, side=side):
                self.half[index, side] = (
                    self.own[index, side * 2 + self.core].astype(jnp.float32)
                    + self.got[side, index].astype(jnp.float32)
                ).astype(self.half.dtype)

            tile_loop(self.own.shape[0], tile)
        for copy in self.copies:
            copy.wait_send()


class QuarterSum:
    def __init__(self, shards, half, other, part, out, sems):
        x, core, core_peer, x_peer = group_place()
        me = lax.axis_index("seq")
        units, width = half.shape[2], half.shape[3]
        self.half, self.other, self.part, self.out = half, other, part, out
        self.x, self.me, self.shards = x, me, shards
        mine = x * 2 + core
        pair = lambda k: (sems.at[0, k], sems.at[1, k])

        def rows(quarter):
            return pl.ds(pl.multiple_of(quarter * units, units), units)

        self.block = (rows(mine), pl.ds(pl.multiple_of(me * width, 128), width))
        self.second = grp_copy(half.at[:, 1 - x], other, *pair(0), x_peer)
        self.third = []
        for step in range(1, shards):
            goal = lax.rem(me + step, shards)
            self.third.append(seq_copy(part.at[goal], out.at[self.block], *pair(step), goal))
        whole = out.at[rows(mine)]
        self.fourth = grp_copy(whole, whole, *pair(shards), x_peer)
        self.fifth = []
        for side in (0, 1):
            whole = out.at[rows(side * 2 + core)]
            self.fifth.append(grp_copy(whole, whole, *pair(shards + 1 + side), core_peer))

    def begin(self):
        self.second.start()

    def spread(self):
        self.second.wait_recv()

        def tile(index):
            self.part[index] = (
                self.half[index, self.x].astype(jnp.float32)
                + self.other[index].astype(jnp.float32)
            ).astype(self.part.dtype)

        tile_loop(self.shards, tile)
        for copy in self.third:
            copy.start()
        self.out[self.block] = self.part[self.me]

    def share(self):
        for copy in self.third:
            copy.wait_recv()
        self.fourth.start()

    def share_core(self):
        self.fourth.wait_recv()
        for copy in self.fifth:
            copy.start()

    def finish(self):
        for copy in self.fifth:
            copy.wait_recv()
        for copy in (self.second, *self.third, self.fourth, *self.fifth):
            copy.wait_send()


def in_line(direction, z, hops, depth):
    return z >= hops if direction == 0 else z + hops < depth


class Gather:
    def __init__(self, full, sems, depth, extra=0):
        self.full, self.depth, self.extra = full, depth, extra
        self.sems = [sems.at[k] for k in range(6)]
        self.me, self.z, self.y, self.other = place()
        self.rows = full.shape[1]

    def origin(self, direction, hops, far):
        column = 1 - self.y if far else self.y
        return (self.z - hops if direction == 0 else self.z + hops) * 2 + column

    def block(self, direction, hops, far=False):
        origin = self.origin(direction, hops, far)
        if not self.extra:
            return self.full.at[origin]
        return self.full.at[origin, pl.ds(0, self.rows - self.extra)]

    def pair(self, direction, hops):
        low = self.origin(direction, hops, False) - self.y
        return self.full.at[pl.ds(low, 2), pl.ds(self.rows - self.extra, self.extra)]

    def z_move(self, block, kind, direction, hops, arrival):
        send, recv = self.sems[kind], self.sems[kind + 1]
        target = self.me + 2 if direction == 0 else self.me - 2
        return seq_copy(
            block,
            block,
            send.at[direction, hops],
            recv.at[direction, hops if arrival else hops + 1],
            self.other if arrival else target,
        )

    def z_copy(self, direction, hops, arrival=False):
        return self.z_move(self.block(direction, hops), 0, direction, hops, arrival)

    def pair_copy(self, direction, hops, arrival=False):
        return self.z_move(self.pair(direction, hops), 4, direction, hops, arrival)

    def y_copy(self, direction, hops, arrival=False, own=False):
        if own:
            block = self.full.at[self.origin(direction, hops, arrival)]
        else:
            block = self.block(direction, hops, arrival)
        send, recv = self.sems[2], self.sems[3]
        return seq_copy(
            block, block, send.at[direction, hops], recv.at[direction, hops], self.other
        )

    def here(self, direction, hops):
        return in_line(direction, self.z, hops, self.depth)

    def onward(self, direction):
        return self.z < self.depth - 1 if direction == 0 else self.z > 0

    def start(self):
        for direction in (0, 1):

            @pl.when(self.onward(direction))
            def _():
                self.z_copy(direction, 0).start()

        self.y_copy(0, 0, own=True).start()

    def cross(self):
        self.y_copy(0, 0, True, own=True).wait_recv()
        if self.extra:
            for direction in (0, 1):

                @pl.when(self.onward(direction))
                def _():
                    self.pair_copy(direction, 0).start()

    def hop(self, hops):
        for direction in (0, 1):

            @pl.when(self.here(direction, hops))
            def _():
                self.z_copy(direction, hops, True).wait_recv()

                @pl.when(self.onward(direction))
                def _():
                    self.z_copy(direction, hops).start()

                self.y_copy(direction, hops).start()

        if self.extra:
            for direction in (0, 1):

                @pl.when(self.here(direction, hops))
                def _():
                    self.pair_copy(direction, hops, True).wait_recv()

                    @pl.when(self.onward(direction))
                    def _():
                        self.pair_copy(direction, hops).start()

    def near(self, hops, visit):
        for direction in (0, 1):

            @pl.when(self.here(direction, hops))
            def _():
                visit(self.origin(direction, hops, False))

    def far(self, hops, visit=None):
        for direction in (0, 1):

            @pl.when(self.here(direction, hops))
            def _():
                self.y_copy(direction, hops, True).wait_recv()
                if visit is not None:
                    visit(self.origin(direction, hops, True))

    def drain(self):
        self.y_copy(0, 0, own=True).wait_send()

        def step(hops, carry):
            for direction in (0, 1):
                here = self.here(direction, hops)

                @pl.when(here & self.onward(direction))
                def _():
                    self.z_copy(direction, hops).wait_send()
                    if self.extra:
                        self.pair_copy(direction, hops).wait_send()

                @pl.when(here & (hops > 0))
                def _():
                    self.y_copy(direction, hops).wait_send()

            return carry

        lax.fori_loop(0, self.depth, step, 0)

    def finish(self):
        def step(hops, carry):
            self.far(hops)
            return carry

        lax.fori_loop(1, self.depth, step, 0)
        self.drain()

    def run(self, visit, hook=None):
        self.start()
        visit(self.me)
        self.cross()
        visit(self.other)

        def step(hops, carry):
            @pl.when(hops < self.depth)
            def _():
                self.hop(hops)
                self.near(hops, visit)

            @pl.when(hops > 1)
            def _():
                self.far(hops - 1, visit)

            if hook is not None:
                hook(hops)
            return carry

        lax.fori_loop(1, self.depth + 1, step, 0)
        self.drain()


class LineGather:
    def __init__(self, full, sems, depth):
        self.full, self.sems, self.depth = full, sems, depth
        self.me, self.z, _, self.other = place()

    def copy(self, direction, hops, arrival=False):
        block = self.full.at[self.z - hops if direction == 0 else self.z + hops]
        target = self.me + 2 if direction == 0 else self.me - 2
        return seq_copy(
            block,
            block,
            self.sems.at[0, direction, hops],
            self.sems.at[1, direction, hops if arrival else hops + 1],
            self.other if arrival else target,
        )

    def hop(self, hops):
        for direction in (0, 1):

            @pl.when(in_line(direction, self.z, hops, self.depth))
            def _():
                if hops:
                    self.copy(direction, hops, True).wait_recv()

                @pl.when(in_line(1 - direction, self.z, 1, self.depth))
                def _():
                    self.copy(direction, hops).start()

    def drain(self):
        for hops in range(self.depth):
            for direction in (0, 1):
                here = in_line(direction, self.z, hops, self.depth)

                @pl.when(here & in_line(1 - direction, self.z, 1, self.depth))
                def _():
                    self.copy(direction, hops).wait_send()


class Reshard:
    def __init__(self, shards, part, out, local_sem, sems):
        x, core, core_peer, x_peer = group_place()
        me = lax.axis_index("seq")
        mine = x * 2 + core
        pair = lambda k: (sems.at[0, k], sems.at[1, k])
        self.local = pltpu.make_async_copy(part(me, mine), out.at[me, mine], local_sem)
        self.first = []
        for step in range(1, shards):
            goal = lax.rem(me + step, shards)
            self.first.append(seq_copy(part(goal, mine), out.at[me, mine], *pair(step - 1), goal))
        self.second = grp_copy(out.at[:, mine], out.at[:, mine], *pair(shards - 1), x_peer)
        self.third = []
        for side in (0, 1):
            whole = out.at[:, side * 2 + core]
            self.third.append(grp_copy(whole, whole, *pair(shards + side), core_peer))

    def begin_near(self):
        self.local.start()
        for copy in self.first[1::2]:
            copy.start()

    def begin_far(self):
        for copy in self.first[0::2]:
            copy.start()

    def share(self):
        self.local.wait()
        for copy in self.first:
            copy.wait_recv()
        self.second.start()

    def share_core(self):
        self.second.wait_recv()
        for copy in self.third:
            copy.start()

    def finish(self):
        for copy in self.third:
            copy.wait_recv()
        for copy in (*self.first, self.second, *self.third):
            copy.wait_send()


def scatter_blocks(
    partial, to_y, from_y, to_z, from_z, acc, y_sems, z_sems, depth, between=None, hook=None, early=None
):
    me, z, y, other = place()
    low = to_y.dtype

    def y_copy(goal):
        return seq_copy(
            to_y.at[goal], from_y.at[goal], y_sems.at[0, goal], y_sems.at[1, goal], other
        )

    def slot(direction, goal, at):
        return goal if direction == 0 else jnp.where(goal == at, depth, goal)

    def z_copy(direction, goal):
        return seq_copy(
            to_z.at[goal],
            from_z.at[slot(direction, goal, z - 1)],
            z_sems.at[0, direction, goal],
            z_sems.at[1, direction, goal],
            me + 2 if direction == 0 else me - 2,
        )

    def z_arrival(direction, goal):
        return seq_copy(
            to_z.at[goal],
            from_z.at[slot(direction, goal, z)],
            z_sems.at[0, direction, goal],
            z_sems.at[1, direction, goal],
            other,
        )

    def ahead(direction, hops):
        return in_line(1 - direction, z, hops, depth)

    def goal_of(direction, hops):
        return z + hops if direction == 0 else z - hops

    def over_y(step, carry):
        hops = depth - 1 - step
        for direction in (0, 1):
            here = ahead(direction, hops)
            if direction == 1:
                here = here & (hops > 0)

            @pl.when(here)
            def _():
                goal = goal_of(direction, hops)
                to_y[goal] = partial(goal * 2 + other - z * 2).astype(low)
                y_copy(goal).start()

        if early is not None:
            early(step)
        return carry

    lax.fori_loop(0, depth, over_y, 0)
    if between is not None:
        between()

    def along_z(step, carry):
        hops = depth - 1 - step
        for direction in (0, 1):

            @pl.when(ahead(direction, hops))
            def _():
                goal = goal_of(direction, hops)
                acc[...] = partial(goal * 2 + y)
                y_copy(goal).wait_recv()
                acc[...] += from_y[goal].astype(jnp.float32)

                @pl.when(in_line(direction, z, 1, depth))
                def _():
                    z_arrival(direction, goal).wait_recv()
                    acc[...] += from_z[slot(direction, goal, z)].astype(jnp.float32)

                to_z[goal] = acc[...].astype(low)
                z_copy(direction, goal).start()

        if hook is not None:
            hook(step)
        return carry

    lax.fori_loop(0, depth - 1, along_z, 0)
    acc[...] = partial(me)
    y_copy(z).wait_recv()
    acc[...] += from_y[z].astype(jnp.float32)
    for direction in (0, 1):

        @pl.when(in_line(direction, z, 1, depth))
        def _():
            z_arrival(direction, z).wait_recv()
            acc[...] += from_z[slot(direction, z, z)].astype(jnp.float32)

    def drain(goal, carry):
        y_copy(goal).wait_send()
        for direction in (0, 1):
            sent = goal > z if direction == 0 else goal < z

            @pl.when(sent)
            def _():
                z_copy(direction, goal).wait_send()

        return carry

    lax.fori_loop(0, depth, drain, 0)


def peer_total(mine, theirs, sems, shards, meanwhile=None):
    me = lax.axis_index("seq")
    copies = [
        seq_copy(
            mine,
            theirs.at[step - 1],
            sems.at[0, step - 1],
            sems.at[1, step - 1],
            lax.rem(me + step, shards),
        )
        for step in range(1, shards)
    ]
    for copy in copies:
        copy.start()
    if meanwhile is not None:
        meanwhile()
    for copy in copies:
        copy.wait()
    total = mine[...]
    for step in range(1, shards):
        total = total + theirs[step - 1]
    return total


EDGE = 80
VMEM_BYTES = 58 * 1024 * 1024
ROOT_HALF = math.sqrt(0.5)
DENSITY = 1.0 / math.sqrt(2.0 * math.pi)


def exchange_edges(held, sems, rows, shards):
    me = lax.axis_index("seq")

    def copy(kind):
        if kind == 0:
            source, target = pl.ds(EDGE + rows - WMAX, WMAX), pl.ds(EDGE - WMAX, WMAX)
        else:
            source, target = pl.ds(EDGE, WMAX), pl.ds(EDGE + rows, WMAX)
        return seq_copy(
            held.at[source],
            held.at[target],
            sems.at[0, kind],
            sems.at[1, kind],
            me + 1 if kind == 0 else me - 1,
        )

    first, last = me == 0, me == shards - 1
    zeros = jnp.zeros((EDGE, held.shape[1]), held.dtype)

    held[pl.ds(0, EDGE - WMAX), :] = zeros[: EDGE - WMAX]
    held[pl.ds(EDGE + rows + WMAX, EDGE - WMAX), :] = zeros[: EDGE - WMAX]

    @pl.when(first)
    def _():
        held[pl.ds(EDGE - WMAX, WMAX), :] = zeros[:WMAX]

    @pl.when(last)
    def _():
        held[pl.ds(EDGE + rows, WMAX), :] = zeros[:WMAX]

    @pl.when(jnp.logical_not(last))
    def _():
        copy(0).start()

    @pl.when(jnp.logical_not(first))
    def _():
        copy(1).start()

    def finish():
        @pl.when(jnp.logical_not(last))
        def _():
            copy(0).wait_send()
            copy(1).wait_recv()

        @pl.when(jnp.logical_not(first))
        def _():
            copy(1).wait_send()
            copy(0).wait_recv()

    return finish


def row_of(vector):
    return vector[...].astype(jnp.float32).reshape(1, vector.shape[0])


def column_of(vector):
    row = row_of(vector)
    fill = -row.shape[1] % 128
    row = jnp.concatenate([row, jnp.zeros((1, fill), jnp.float32)], axis=1)
    return jnp.broadcast_to(row, (8, row.shape[1])).T[: vector.shape[0], 0:1]


def stats_of(values_in):
    average = jnp.mean(values_in, axis=-1, keepdims=True)
    centred = values_in - average
    variance = jnp.mean(centred * centred, axis=-1, keepdims=True)
    inverse = lax.rsqrt(variance + EPS_NORM)
    return centred * inverse, inverse


class Latents:
    def __init__(self, shape, total):
        self.ends = []
        low = 0
        for latent in range(NLAT - 1):
            low = low + shape[latent, 0] * WMAX
            self.ends.append(low)
        self.total = total

    def segment(self, positions):
        out = jnp.zeros_like(positions)
        for end in self.ends:
            out = out + (positions >= end).astype(jnp.int32)
        return out

    def picks(self, start, count):
        segment = self.segment(start + lax.broadcasted_iota(jnp.int32, (count, 1), 0))
        return [(segment == latent).astype(jnp.float32) for latent in range(NLAT)]

    def valid(self, positions, down_step, side_step):
        segment = self.segment(positions)
        low, high = jnp.zeros_like(positions), jnp.full_like(positions, self.total)
        for latent, end in enumerate(self.ends):
            low = jnp.where(segment > latent, end, low)
            high = jnp.where(segment == latent, end, high)
        moved = positions + down_step * WMAX
        column = (positions & (WMAX - 1)) + side_step
        good = (moved >= low) & (moved < high) & (column >= 0) & (column < WMAX)
        return good.astype(jnp.float32)


def rows_of(picks, table):
    out = picks[0] * table[0:1]
    for latent in range(1, NLAT):
        out = out + picks[latent] * table[latent : latent + 1]
    return out


WIDE_SCALE, WIDE_SHIFT = 16, 24
SMALL_FC1, SMALL_GAMMA, SMALL_BETA, SMALL_TIME = 64, 66, 68, 70
SMALL_QUERY, SMALL_VALUE, SMALL_OUT, SMALL_MAP, SMALL_ROWS = 71, 72, 73, 74, 80


def mixer_kernel(
    shards,
    emit,
    shape,
    hidden,
    cond,
    time_weight,
    conv_weight,
    conv_bias,
    fc1_bias,
    gamma,
    beta,
    fc2_bias,
    time_bias,
    fc1,
    ctx_cols,
    cot,
    fc2,
    out_weight,
    full,
    held,
    wide,
    normed,
    inverse,
    pre,
    root_out,
    ratio_out,
    denom_out,
    response,
    ctx_full,
    d_mixed,
    cot_cols,
    fc2_rows,
    pack,
    packed,
    floats,
    conv,
    act,
    energy,
    mine,
    theirs,
    edge_sems,
    pack_sems,
    gather_sems,
    total_sems,
    ctx_sems,
    cot_sems,
    out_parts,
    cot_line,
    to_other,
    other_sems,
    local_sems,
    fc2_sems,
    out_sems,
):
    f32 = jnp.float32
    rows = hidden.shape[0]
    depth = shards // 2
    me = lax.axis_index("seq")
    meet_all(shards, lax.axis_size("grp"))
    units, width = fc2_rows.shape[2:]
    out_units, wide_cols = out_parts.shape[2:]

    def fc2_part(goal, quarter):
        here = pl.ds(pl.multiple_of(quarter * units, units), units)
        return fc2.at[here, pl.ds(pl.multiple_of(goal * width, 128), width)]

    def out_part(goal, quarter):
        here = pl.ds(pl.multiple_of(quarter * out_units, out_units), out_units)
        return out_weight.at[here, pl.ds(pl.multiple_of(goal // 2 * wide_cols, 128), wide_cols)]

    fc2_shard = Reshard(shards, fc2_part, fc2_rows, local_sems.at[0], fc2_sems)
    out_shard = Reshard(shards, out_part, out_parts, local_sems.at[1], out_sems)
    ctx_gather = Gather(ctx_full, ctx_sems, depth)
    _, z, y, other = place()
    cot_gather = LineGather(cot_line, cot_sems, depth)
    ctx_full[me] = ctx_cols[...]
    latents = Latents(shape, shards * rows)
    cols = pack.shape[1]
    fc1_bias, gamma, beta, time_bias = map(row_of, (fc1_bias, gamma, beta, time_bias))
    mod = (
        jnp.dot(
            cond[...],
            time_weight[...].astype(f32),
            precision=HIGHEST_PRECISION,
            preferred_element_type=f32,
        )
        + time_bias
    )
    pack[...] = jnp.zeros_like(pack)
    pack[0:9, :] = conv_weight[...].astype(f32)
    pack[9:10, :] = row_of(conv_bias)
    pack[10:11, :] = row_of(fc2_bias)
    pack[11 : 11 + NLAT, :] = mod[:, :cols]
    pack[11 + NLAT : 11 + 2 * NLAT, :] = mod[:, cols:]
    packed[me] = pack[...]
    pack_copies = [
        seq_copy(
            pack,
            packed.at[me],
            pack_sems.at[0, step - 1],
            pack_sems.at[1, step - 1],
            lax.rem(me + step, shards),
        )
        for step in range(1, shards)
    ]
    held[pl.ds(EDGE, rows), :] = hidden[...]
    finish = exchange_edges(held, edge_sems, rows, shards)
    for copy in pack_copies:
        copy.start()
    fc2_shard.begin_near()
    out_shard.begin_near()
    finish()
    fc2_shard.begin_far()
    out_shard.begin_far()
    ctx_gather.start()
    cot_line[z] = cot.wait()[...]
    cot_gather.hop(0)
    emit(held)
    tile_loop(
        floats.shape[0] // 32,
        lambda i: floats.__setitem__(
            (pl.ds(i * 32, 32), slice(None)), held[pl.ds(i * 32, 32), :].astype(f32)
        ),
    )
    for copy in pack_copies:
        copy.wait()
    wide[...] = jnp.zeros_like(wide)
    wide[0:16, :] = jnp.concatenate([packed[j, 0:16, :] for j in range(shards)], axis=1)
    for low, device in ((WIDE_SCALE, 0), (WIDE_SHIFT, shards // 2)):
        parts = []
        for j in range(device, device + shards // 2):
            parts.append(packed[j, 11 : 11 + NLAT, :])
            parts.append(packed[j, 11 + NLAT : 11 + 2 * NLAT, :])
        wide[low : low + NLAT, :] = jnp.concatenate(parts, axis=1)
    positions = me * rows + lax.broadcasted_iota(jnp.int32, (rows, 1), 0)
    masks = [latents.valid(positions, tap // 3 - 1, tap % 3 - 1) for tap in range(9)]

    def conv_tile(index):
        cols = pl.ds(pl.multiple_of(index * 256, 256), 256)
        total = jnp.broadcast_to(wide[9:10, cols], (rows, 256))
        for tap in range(9):
            offset = EDGE + (tap // 3 - 1) * WMAX + tap % 3 - 1
            total = total + (
                floats[offset : offset + rows, cols] * wide[tap : tap + 1, cols]
            ) * masks[tap]
        conv[:, cols] = total

    tile_loop(C // 256, conv_tile)

    def norm_tile(index):
        here = pl.ds(pl.multiple_of(index * 16, 16), 16)
        values, factor = stats_of(conv[here, :])
        normed[here, :] = values
        inverse[here, :] = factor
        full[me, here, :] = values.astype(full.dtype)

    tile_loop(rows // 16, norm_tile)
    energy[...] = jnp.zeros_like(energy)
    fc1 = fc1.wait()
    emit(wide, normed)

    def visit(block):
        pre[block] = (
            jnp.dot(full[block], fc1[...], preferred_element_type=f32) + fc1_bias
        )

        def tile(index):
            here = pl.ds(pl.multiple_of(index * 32, 32), 32)
            value = pre[block, here, :]
            value = value * (0.5 * (1.0 + lax.erf(value * ROOT_HALF)))
            act[block, here, :] = value
            square = value * value
            pick = latents.picks(block * rows + index * 32, 32)
            for latent in range(NLAT):
                energy[latent : latent + 1, :] += jnp.sum(
                    square * pick[latent], axis=0, keepdims=True
                )

        tile_loop(rows // 32, tile)

    def hook(hops):
        @pl.when(hops == 1)
        def _():
            ctx_gather.cross()
            ctx_gather.hop(1)

        @pl.when(hops == 2)
        def _():
            fc2_shard.share()
            out_shard.share()
            ctx_gather.hop(2)
            cot_gather.hop(1)

        @pl.when(hops == 3)
        def _():
            ctx_gather.hop(3)
            cot_gather.hop(2)

    Gather(full, gather_sems, depth, rows // 8).run(visit, hook)
    emit(full, pre)
    out_shard.share_core()
    fc2_shard.share_core()
    root = jnp.sqrt(energy[...] + 1.0)
    mine[...] = jnp.broadcast_to(jnp.sum(root, axis=1, keepdims=True), mine.shape)

    other_copies = [
        seq_copy(
            to_other.at[n],
            target.at[:, y],
            other_sems.at[0, n],
            other_sems.at[1, n],
            other,
        )
        for n, target in enumerate((d_mixed, cot_cols))
    ]

    def cot_part(block):
        products = jnp.dot(
            cot_line[block], out_parts[...].reshape(C, wide_cols), preferred_element_type=f32
        ).astype(d_mixed.dtype)
        pair = cot_line[block, :, pl.ds(pl.multiple_of(z * wide_cols, 128), wide_cols)]
        for side in (0, 1):
            taken = pair[:, side * cols : (side + 1) * cols]
            product = products[:, side * cols : (side + 1) * cols]

            @pl.when(y == side)
            def _():
                d_mixed[block, side] = product
                cot_cols[block, side] = taken

            @pl.when(y != side)
            def _():
                to_other[0, block] = product
                to_other[1, block] = taken

    def meanwhile():
        cot_gather.hop(3)
        out_shard.finish()
        tile_loop(depth, cot_part)
        for copy in other_copies:
            copy.start()

    denom = peer_total(mine, theirs, total_sems, shards, meanwhile) / FF + EPS_NORM
    ratio = root / denom[:, 0:1]
    root_out[...] = root
    denom_out[...] = denom
    ratio_out[...] = ratio
    scaled = ratio * gamma + 1.0

    def respond(index):
        block = index // (rows // 32)
        here = pl.ds(pl.multiple_of(lax.rem(index, rows // 32) * 32, 32), 32)
        response[block, here, :] = (
            act[block, here, :] * rows_of(latents.picks(index * 32, 32), scaled) + beta
        ).astype(response.dtype)

    tile_loop(shards * rows // 32, respond)
    emit(response)
    ctx_gather.finish()
    emit(ctx_full)
    fc2_shard.finish()
    emit(fc2_rows)
    cot_gather.drain()
    for copy in other_copies:
        copy.wait()


def mixed_in_kernel(
    shards,
    emit,
    shape,
    response,
    fc2,
    hidden,
    wide,
    w_qkv,
    q_bias,
    v_bias,
    context,
    full,
    first,
    second,
    normed,
    inverse,
    queries,
    keys,
    values,
    acc,
    to_y,
    from_y,
    to_z,
    from_z,
    y_sems,
    z_sems,
    gather_sems,
):
    f32 = jnp.float32
    rows = acc.shape[0]
    depth = shards // 2
    me = lax.axis_index("seq")
    meet_all(shards)
    latents = Latents(shape, shards * rows)
    cols = keys.shape[0]
    q_bias, v_bias = row_of(q_bias), column_of(v_bias)
    bias = wide[10:11, :]
    scale, shift = wide[WIDE_SCALE : WIDE_SCALE + 8, :], wide[WIDE_SHIFT : WIDE_SHIFT + 8, :]

    def partial(block):
        return dot_nt(response[block], fc2[...])

    scatter_blocks(partial, to_y, from_y, to_z, from_z, acc, y_sems, z_sems, depth)

    hidden = hidden.wait()

    def norm_tile(index):
        here = pl.ds(pl.multiple_of(index * 16, 16), 16)
        one = hidden[here, :].astype(f32) + acc[here, :] + bias
        pick = latents.picks(me * rows + index * 16, 16)
        two = one * (1.0 + rows_of(pick, scale)) + rows_of(pick, shift)
        first[here, :] = one
        second[here, :] = two
        value, factor = stats_of(two)
        normed[here, :] = value
        inverse[here, :] = factor
        full[me, here, :] = value.astype(full.dtype)

    tile_loop(rows // 16, norm_tile)
    emit(first, second, normed)
    w_qkv, context = w_qkv.wait(), context.wait()

    side = jnp.dot(w_qkv[cols:, :], context[...], preferred_element_type=f32)
    keys[:, shards * rows :] = side[:cols].astype(keys.dtype)
    values[:, shards * rows :] = (side[cols:] + v_bias).astype(values.dtype)

    def visit(block):
        value = full[block]
        query = dot_nt(value, w_qkv[:cols, :]) + q_bias
        queries[block] = query.astype(queries.dtype)
        here = pl.ds(pl.multiple_of(block * rows, 128), rows)
        side = dot_nt(w_qkv[cols:, :], value)
        keys[:, here] = side[:cols].astype(keys.dtype)
        values[:, here] = (side[cols:] + v_bias).astype(values.dtype)

    Gather(full, gather_sems, depth, rows // 8).run(visit)


def attend_kernel(
    shards,
    emit,
    shape,
    queries,
    keys,
    values,
    d_mixed_all,
    cot,
    d_qkv,
    mixed,
    cot_cols,
    dk_sum,
    dv_sum,
    probs_at,
    sems,
):
    f32, bf16 = jnp.float32, jnp.bfloat16
    cols = keys.shape[0]
    heads = cols // HEAD_DIM
    tiles, tile_rows = mixed.shape[0], mixed.shape[3]
    span = tile_rows // queries.shape[1]
    depth = shards // 2
    me = lax.axis_index("seq")
    meet_all(shards)
    latents = Latents(shape, tiles * tile_rows)
    place_at = lax.broadcasted_iota(jnp.int32, (1, keys.shape[1]), 1)
    token = place_at - tiles * tile_rows
    of_token = jnp.full_like(token, -1)
    for latent in range(NLAT):
        inside = (token >= latent * NCTX) & (token < (latent + 1) * NCTX)
        of_token = jnp.where(inside, latent, of_token)
    k_segment = jnp.where(token < 0, latents.segment(place_at), of_token)
    dk_sum[...] = jnp.zeros_like(dk_sum)
    dv_sum[...] = jnp.zeros_like(dv_sum)

    def gather_of(tile):
        return Gather(mixed.at[tile], sems.at[tile], depth)

    def step(tile, carry):
        blocks = pl.ds(tile * span, span)
        here = pl.ds(pl.multiple_of(tile * tile_rows, 128), tile_rows)
        query = queries[blocks].reshape(tile_rows, cols) * SCORE_SCALE
        cot_cols[:, here] = cot[blocks].reshape(tile_rows, cols).T
        d_mixed = d_mixed_all[blocks].reshape(tile_rows, cols)
        q_segment = latents.segment(
            tile * tile_rows + lax.broadcasted_iota(jnp.int32, (tile_rows, 1), 0)
        )
        bias = jnp.where(q_segment == k_segment, 0.0, MASKED)
        mixed_parts, d_query_parts = [], []
        for head in range(heads):
            own = slice(head * HEAD_DIM, (head + 1) * HEAD_DIM)
            scores = jnp.dot(query[:, own], keys[own, :], preferred_element_type=f32) + bias
            expo = jnp.exp(scores - jnp.max(scores, axis=-1, keepdims=True))
            probs_at[head] = expo * (1.0 / jnp.sum(expo, axis=-1, keepdims=True))
            mixed_parts.append(dot_nt(probs_at[head].astype(bf16), values[own, :]))
        mixed[tile, me] = jnp.concatenate(mixed_parts, axis=1).T.astype(bf16)
        gather_of(tile).start()
        for hops in range(1, depth):

            @pl.when(tile >= hops)
            def _():
                if hops == 1:
                    gather_of(tile - 1).cross()
                gather_of(tile - hops).hop(hops)

        for head in range(heads):
            own = slice(head * HEAD_DIM, (head + 1) * HEAD_DIM)
            dm_head = d_mixed[:, own]
            delta = jnp.sum(dm_head.astype(f32) * mixed_parts[head], axis=-1, keepdims=True)
            d_probs = jnp.dot(dm_head, values[own, :], preferred_element_type=f32)
            d_scores = (probs_at[head] * (d_probs - delta)).astype(bf16)
            d_query_parts.append(dot_nt(d_scores, keys[own, :]) * SCORE_SCALE)
            dk_sum[own, :] += dot_tn(query[:, own], d_scores)
            dv_sum[own, :] += dot_tn(dm_head, probs_at[head].astype(bf16))
        d_qkv[:cols, here] = jnp.concatenate(d_query_parts, axis=1).T.astype(bf16)
        return carry

    lax.fori_loop(0, tiles, step, 0)
    for late in range(1, depth):
        for hops in range(late, depth):
            if hops == 1:
                gather_of(tiles - 1).cross()
            gather_of(tiles - 1 + late - hops).hop(hops)
    d_qkv[:cols, tiles * tile_rows :] = jnp.zeros(
        (cols, d_qkv.shape[1] - tiles * tile_rows), bf16
    )
    d_qkv[cols : 2 * cols, :] = dk_sum[...].astype(bf16)
    d_qkv[2 * cols :, :] = dv_sum[...].astype(bf16)

    def close(tile, carry):
        gather_of(tile).finish()
        return carry

    lax.fori_loop(0, tiles, close, 0)


def norm_back(gradient, normed, inverse):
    mean_grad = jnp.mean(gradient, axis=-1, keepdims=True)
    mean_mixed = jnp.mean(gradient * normed, axis=-1, keepdims=True)
    return inverse * (gradient - mean_grad - normed * mean_mixed)


def attn_back_kernel(
    shards,
    emit,
    shape,
    cond,
    d_qkv,
    w_qkv,
    attn,
    context,
    mixed,
    cot_cols,
    out_weight,
    gamma,
    out_bias,
    cot,
    normed,
    inverse,
    first,
    wide,
    fc2,
    pre,
    root,
    ratio,
    denom,
    response,
    context_in,
    d_first,
    d_pre,
    small_out,
    weight_grads,
    map_grad,
    act_out,
    fc2_half,
    branch_sum,
    full,
    d_mod,
    small,
    acc,
    d_resp,
    act,
    sums,
    mine,
    theirs,
    to_y,
    from_y,
    to_z,
    from_z,
    y_sems,
    z_sems,
    gather_sems,
    total_sems,
    g_own,
    g_got,
    g_other,
    g_sems,
    mod_in,
    mod_sems,
    fc2_own,
    fc2_got,
    fc2_sems,
    ctx_out,
    ctx_in,
    ctx_sems,
):
    f32 = jnp.float32
    rows = acc.shape[0]
    depth = shards // 2
    me = lax.axis_index("seq")
    meet_all(shards, lax.axis_size("grp"))
    cols = ctx_out.shape[1]
    total = shards * rows
    latents = Latents(shape, total)
    gamma, out_bias = row_of(gamma), column_of(out_bias)
    width_one = gamma.shape[1]
    scale = wide[WIDE_SCALE : WIDE_SCALE + 8, :]
    later = (attn, context, mixed, cot_cols, out_weight)
    weight_sum = PairSum(g_own, g_got, g_other, weight_grads, g_sems)
    peers = [lax.rem(me + step, shards) for step in range(1, shards)]
    ctx_copies = [
        seq_copy(ctx_out.at[peer], ctx_in.at[me], ctx_sems.at[0, n], ctx_sems.at[1, n], peer)
        for n, peer in enumerate(peers)
    ]
    fc2_sum = CoreHalf(fc2_own, fc2_got, fc2_half, fc2_sems)

    def partial(block):
        here = pl.ds(pl.multiple_of(block * rows, 128), rows)
        return dot_tn(d_qkv[:, here], w_qkv[...])

    def between():
        low_type = ctx_out.dtype
        attn, context, mixed, cot_cols, out_weight = (item.wait() for item in later)
        for device in range(shards):
            ctx_out[device] = dot_tn(
                w_qkv[:, device * cols : (device + 1) * cols], d_qkv[:, total:]
            ).astype(low_type)
        g_own[: 3 * cols, :] = (
            jnp.dot(d_qkv[:, :total], attn[...].reshape(total, C), preferred_element_type=f32)
            + dot_nt(d_qkv[:, total:], context[...])
        ).astype(low_type)
        grad = None
        for tile in range(mixed.shape[0]):
            here = slice(tile * mixed.shape[3], (tile + 1) * mixed.shape[3])
            block = mixed[tile].reshape(C, mixed.shape[3])
            act_out[:, here] = (
                jnp.dot(out_weight[...], block, preferred_element_type=f32) + out_bias
            ).astype(low_type)
            part = dot_nt(cot_cols[:, here], block)
            grad = part if grad is None else grad + part
        g_own[3 * cols :, :] = grad.astype(low_type)
        weight_sum.begin()

    def scatter_hook(step):
        @pl.when(step == 1)
        def _():
            weight_sum.across()

    scatter_blocks(
        partial, to_y, from_y, to_z, from_z, acc, y_sems, z_sems, depth, between, scatter_hook
    )
    d_mod[...] = jnp.zeros_like(d_mod)
    branch_sum[...] = jnp.zeros_like(branch_sum)
    cot, normed, first = cot.wait(), normed.wait(), first.wait()

    def norm_tile(index):
        here = pl.ds(pl.multiple_of(index * 16, 16), 16)
        d_second = cot[here, :].astype(f32) + norm_back(
            acc[here, :], normed[here, :], inverse[here, :]
        )
        pick = latents.picks(me * rows + index * 16, 16)
        value = d_second * (1.0 + rows_of(pick, scale))
        d_first[here, :] = value
        value = value.astype(full.dtype)
        full[me, here, :] = value
        branch_sum[0:1, :] += jnp.sum(value.astype(f32), axis=0, keepdims=True)
        scaled = d_second * first[here, :]
        for latent in range(NLAT):
            chosen = pick[latent]
            d_mod[2 * latent : 2 * latent + 1, :] += jnp.sum(scaled * chosen, axis=0, keepdims=True)
            d_mod[2 * latent + 1 : 2 * latent + 2, :] += jnp.sum(
                d_second * chosen, axis=0, keepdims=True
            )

    tile_loop(rows // 16, norm_tile)
    sums[...] = jnp.zeros_like(sums)
    emit(d_first)
    fc2, pre = fc2.wait(), pre.wait()
    wide_mod = 2 * cols
    half = shards // 2

    def mod_part(device):
        low = pl.multiple_of(lax.rem(device, half) * wide_mod, 128)
        return d_mod.at[:, pl.ds(low, wide_mod)]

    mod_in[me] = mod_part(me)[...]
    mod_copies = [
        seq_copy(mod_part(peer), mod_in.at[me], mod_sems.at[0, k], mod_sems.at[1, k], peer)
        for k, peer in enumerate(peers)
    ]
    for copy in mod_copies:
        copy.start()

    def gather_hook(hops):
        @pl.when(hops == 2)
        def _():
            weight_sum.share()

    def visit(block):
        d_resp[block] = jnp.dot(full[block], fc2[...], preferred_element_type=f32)

        def tile(index):
            here = pl.ds(pl.multiple_of(index * 32, 32), 32)
            value = pre[block, here, :]
            phi = 0.5 * (1.0 + lax.erf(value * ROOT_HALF))
            pre[block, here, :] = phi + value * (DENSITY * jnp.exp(-0.5 * value * value))
            value = value * phi
            act[block, here, :] = value.astype(act.dtype)
            pull = d_resp[block, here, :]
            sums[NLAT : NLAT + 1, :] += jnp.sum(pull, axis=0, keepdims=True)
            pull = pull * value
            pick = latents.picks(block * rows + index * 32, 32)
            for latent in range(NLAT):
                sums[latent : latent + 1, :] += jnp.sum(
                    pull * pick[latent], axis=0, keepdims=True
                )

        tile_loop(rows // 32, tile)

    Gather(full, gather_sems, depth, rows // 8).run(visit, gather_hook)
    small[...] = jnp.zeros_like(small)
    wide_row = 2 * cols

    def keep(row, value):
        for part in range(value.shape[1] // wide_row):
            small[row + part : row + part + 1, :] = value[
                :, part * wide_row : (part + 1) * wide_row
            ]

    keep(SMALL_BETA, sums[NLAT : NLAT + 1, :])
    pulls = sums[...]
    keep(SMALL_GAMMA, jnp.sum(pulls[:NLAT] * ratio[:NLAT, :], axis=0, keepdims=True))
    d_ratio = pulls * gamma
    mine[...] = jnp.broadcast_to(jnp.sum(d_ratio * root[...], axis=1, keepdims=True), mine.shape)

    def meanwhile():
        for copy in ctx_copies:
            copy.start()
        ctx_in[me] = ctx_out[me]
        right = response.wait()[...].reshape(total, width_one)
        units = fc2_own.shape[2]
        for goal in range(0, shards, 4):
            here = slice(goal * 4 * units, (goal + 4) * 4 * units)
            part = dot_tn(full[:, :, here].reshape(total, 16 * units), right)
            fc2_own[goal : goal + 4] = part.reshape(4, 4, units, width_one).astype(fc2_own.dtype)
        fc2_sum.begin()

    pulled = peer_total(mine, theirs, total_sems, shards, meanwhile)[:, 0:1]
    below = denom[:, 0:1]
    d_root = d_ratio / below - pulled / (FF * below * below)
    back = d_root / root[...]
    scaled = ratio[...] * gamma + 1.0
    sums[0:1, :] = jnp.zeros((1, width_one), f32)

    def respond(index):
        block = index // (rows // 32)
        here = pl.ds(pl.multiple_of(lax.rem(index, rows // 32) * 32, 32), 32)
        pick = latents.picks(index * 32, 32)
        d_act = d_resp[block, here, :] * rows_of(pick, scaled) + act[block, here, :].astype(f32) * rows_of(
            pick, back
        )
        value = (d_act * pre[block, here, :]).astype(d_pre.dtype)
        d_pre[block, here, :] = value
        sums[0:1, :] += jnp.sum(value.astype(f32), axis=0, keepdims=True)

    tile_loop(shards * rows // 32, respond)
    emit(d_pre)
    for copy in mod_copies:
        copy.wait()
    mod_sum = mod_in[0]
    for device in range(1, shards):
        mod_sum = mod_sum + mod_in[device]
    keep(SMALL_FC1, sums[0:1, :])
    fc2_sum.finish()
    emit(fc2_half)
    chosen = [
        jnp.where(me < half, mod_sum[2 * n : 2 * n + 1], mod_sum[2 * n + 1 : 2 * n + 2])
        for n in range(NLAT)
    ]
    chosen = jnp.concatenate(chosen, axis=0)
    small[0:SMALL_FC1, :] = lax.dot_general(
        cond[...],
        chosen,
        (((0,), (0,)), ((), ())),
        precision=HIGHEST_PRECISION,
        preferred_element_type=f32,
    )
    keep(SMALL_TIME, jnp.sum(chosen, axis=0, keepdims=True))
    ones = lambda values: jnp.ones((8, values.shape[1]), values.dtype)
    for row, value in (
        (SMALL_QUERY, d_qkv[:cols, :]),
        (SMALL_VALUE, d_qkv[2 * cols :, :]),
        (SMALL_OUT, later[3].buffer[...]),
    ):
        small[row : row + 1, :cols] = dot_nt(ones(value), value)[0:1]
    for copy in ctx_copies:
        copy.wait()
    context_sum = ctx_in[0].astype(f32)
    for device in range(1, shards):
        context_sum = context_sum + ctx_in[device].astype(f32)
    at = lax.broadcasted_iota(jnp.int32, (1, context_sum.shape[1]), 1)
    context_sum = jnp.where(at < NLAT * NCTX, context_sum, 0.0)
    map_grad[...] = jnp.dot(
        context_sum.astype(map_grad.dtype), context_in.wait()[...], preferred_element_type=f32
    ).astype(map_grad.dtype)
    small[SMALL_MAP : SMALL_MAP + 1, :cols] = lax.dot_general(
        ones(context_sum),
        context_sum,
        (((1,), (1,)), ((), ())),
        precision=HIGHEST_PRECISION,
        preferred_element_type=f32,
    )[0:1]
    small_out[...] = small[...].astype(small_out.dtype)
    weight_sum.finish()


def conv_back_kernel(
    shards,
    emit,
    shape,
    d_pre,
    fc1,
    normed,
    inverse,
    d_first,
    hidden,
    wide,
    normed_full,
    branch,
    map_grad,
    act_out,
    second,
    fc2_half,
    small,
    input_grad,
    fc1_sum,
    fc2_sum,
    map_sum,
    small_sum,
    conv_sum,
    activations,
    held,
    floats,
    acc,
    to_y,
    from_y,
    to_z,
    from_z,
    y_sems,
    z_sems,
    edge_sems,
    d_conv_params,
    fc1_own,
    fc1_got,
    fc1_other,
    fc2_other,
    fc2_part,
    map_own,
    map_got,
    map_other,
    pair_sems,
    fc2_sems,
    small_in,
    small_sems,
    conv_out,
    conv_in,
    conv_part,
    conv_group,
    conv_sems,
    act_in,
    act_sems,
):
    f32 = jnp.float32
    rows = acc.shape[0]
    depth = shards // 2
    groups = lax.axis_size("grp")
    me = lax.axis_index("seq")
    meet_all(shards, groups)
    cols = conv_part.shape[1]
    width = d_pre.shape[2]
    total = shards * rows
    latents = Latents(shape, total)
    positions = me * rows + lax.broadcasted_iota(jnp.int32, (rows, 1), 0)
    fc1_pair = PairSum(fc1_own, fc1_got, fc1_other, fc1_sum, pair_sems.at[0])
    map_pair = PairSum(map_own, map_got, map_other, map_sum, pair_sems.at[1])
    fc2_quarter = QuarterSum(shards, fc2_half, fc2_other, fc2_part, fc2_sum, fc2_sems)
    group = lax.axis_index("grp")
    small_copies = [
        grp_copy(
            small,
            small_in.at[step - 1],
            small_sems.at[0, step - 1],
            small_sems.at[1, step - 1],
            lax.rem(group + step, groups),
        )
        for step in range(1, groups)
    ]

    def partial(block):
        return dot_nt(d_pre[block], fc1[...])

    peers = [lax.rem(me + step, shards) for step in range(1, shards)]
    act_copies = []
    for n, peer in enumerate(peers):
        there = pl.ds(pl.multiple_of(peer * rows, 128), rows)
        act_copies.append(
            seq_copy(act_out.at[:, there], act_in.at[me], act_sems.at[0, n], act_sems.at[1, n], peer)
        )

    def fc1_grad():
        full = normed_full.wait()

        def tile(index):
            here = pl.ds(pl.multiple_of(index * 256, 256), 256)
            fc1_own[here, :] = dot_tn(
                full[:, :, here].reshape(total, 256), d_pre[...].reshape(total, width)
            ).astype(fc1_own.dtype)

        tile_loop(C // 256, tile)
        fc1_pair.begin()

    fc2_quarter.begin()
    map_own[...] = map_grad[...]
    map_pair.begin()

    def early(step):
        @pl.when(step == 1)
        def _():
            for copy in act_copies:
                copy.start()
            fc1_grad()

    def scatter_hook(step):
        @pl.when(step == 1)
        def _():
            fc2_quarter.spread()
            fc1_pair.across()
            map_pair.across()

    scatter_blocks(
        partial,
        to_y,
        from_y,
        to_z,
        from_z,
        acc,
        y_sems,
        z_sems,
        depth,
        None,
        scatter_hook,
        early,
    )
    normed, d_first, hidden = normed.wait(), d_first.wait(), hidden.wait()

    def norm_tile(index):
        start = pl.multiple_of(index * 16, 16)
        here = pl.ds(start, 16)
        held[pl.ds(EDGE + start, 16), :] = norm_back(
            acc[here, :], normed[here, :], inverse[here, :]
        ).astype(held.dtype)

    tile_loop(rows // 16, norm_tile)
    finish = exchange_edges(held, edge_sems, rows, shards)
    for copy in small_copies:
        copy.start()
    fc2_quarter.share()
    tile_loop(
        floats.shape[0] // 32,
        lambda i: floats.__setitem__(
            (pl.ds(i * 32, 32), slice(None)), hidden[pl.ds(i * 32, 32), :].astype(f32)
        ),
    )
    d_conv_params[...] = jnp.zeros_like(d_conv_params)
    masks = [latents.valid(positions, tap // 3 - 1, tap % 3 - 1) for tap in range(9)]

    def grad_tile(index):
        cols = pl.ds(pl.multiple_of(index * 256, 256), 256)
        d_conv = held[pl.ds(EDGE, rows), cols].astype(f32)
        d_conv_params[9:10, cols] = jnp.sum(d_conv, axis=0, keepdims=True)
        d_conv_params[10:11, cols] = branch[0:1, cols]
        for tap in range(9):
            offset = EDGE + (tap // 3 - 1) * WMAX + tap % 3 - 1
            d_conv_params[tap : tap + 1, cols] = jnp.sum(
                d_conv * floats[offset : offset + rows, cols] * masks[tap],
                axis=0,
                keepdims=True,
            )

    tile_loop(C // 256, grad_tile)
    for goal in range(shards):
        conv_out[goal] = d_conv_params[:, goal * cols : (goal + 1) * cols]
    conv_in[me] = conv_out[me]
    conv_copies = []
    for step in range(1, shards):
        goal = lax.rem(me + step, shards)
        conv_copies.append(
            seq_copy(
                conv_out.at[goal],
                conv_in.at[me],
                conv_sems.at[0, step - 1],
                conv_sems.at[1, step - 1],
                goal,
            )
        )
        conv_copies[-1].start()
    finish()
    act_in[me] = act_out[:, pl.ds(pl.multiple_of(me * rows, 128), rows)]
    tile_loop(
        floats.shape[0] // 32,
        lambda i: floats.__setitem__(
            (pl.ds(i * 32, 32), slice(None)), held[pl.ds(i * 32, 32), :].astype(f32)
        ),
    )

    back_masks = []
    for tap in range(9):
        down_step, side_step = tap // 3 - 1, tap % 3 - 1
        back_masks.append(
            latents.valid(positions - down_step * WMAX - side_step, down_step, side_step)
        )

    def input_tile(index):
        cols = pl.ds(pl.multiple_of(index * 256, 256), 256)
        total = d_first[:, cols]
        for tap in range(9):
            offset = EDGE - (tap // 3 - 1) * WMAX - tap % 3 + 1
            total = total + (
                floats[offset : offset + rows, cols] * wide[tap : tap + 1, cols]
            ) * back_masks[tap]
        input_grad[:, cols] = total

    for copy in conv_copies:
        copy.wait()
    conv_total = conv_in[0]
    for device in range(1, shards):
        conv_total = conv_total + conv_in[device]
    tile_loop(C // 256, input_tile)
    fc1_pair.share()
    conv_part[...] = conv_total
    group_copies = []
    for step in range(1, groups):
        k = shards - 2 + step
        group_copies.append(
            grp_copy(
                conv_part,
                conv_group.at[step - 1],
                conv_sems.at[0, k],
                conv_sems.at[1, k],
                lax.rem(group + step, groups),
            )
        )
        group_copies[-1].start()
    fc2_quarter.share_core()
    for copy in act_copies:
        copy.wait()
    activations[...] = (second.wait()[...] + act_in[...].reshape(C, rows).astype(f32).T).astype(
        activations.dtype
    )
    map_pair.share()
    for copy in (*small_copies, *group_copies):
        copy.wait()
    small_total = small[...].astype(f32)
    for step in range(groups - 1):
        small_total = small_total + small_in[step].astype(f32)
    small_sum[...] = small_total
    conv_sum[...] = conv_part[...] + conv_group[0] + conv_group[1] + conv_group[2]
    fc2_quarter.finish()
    emit(fc2_sum)
    map_pair.finish()
    fc1_pair.finish()


class Late:
    def __init__(self, buffer, copy):
        self.buffer, self.copy = buffer, copy

    def wait(self):
        self.copy.wait()
        return self.buffer


def staged_body(body, n_in, n_out, late, staged):
    def run(*refs):
        ins, outs = list(refs[:n_in]), list(refs[n_in : n_in + n_out])
        rest = refs[n_in + n_out :]
        count = len(late) + len(staged)
        if not count:
            body(lambda *buffers: None, *refs)
            return
        kept, buffers, sems = rest[: -count - 1], rest[-count - 1 : -1], rest[-1]
        for n, k in enumerate(late):
            copy = pltpu.make_async_copy(ins[k], buffers[n], sems.at[n])
            copy.start()
            ins[k] = Late(buffers[n], copy)
        waiting = []
        for n, k in enumerate(staged, len(late)):
            waiting.append([buffers[n], pltpu.make_async_copy(buffers[n], outs[k], sems.at[n]), 0])
            outs[k] = buffers[n]

        def emit(*which):
            for entry in waiting:
                if not entry[2] and any(entry[0] is ref for ref in which):
                    entry[1].start()
                    entry[2] = 1

        body(emit, *ins, *outs, *kept)
        emit(*(entry[0] for entry in waiting))
        for entry in waiting:
            entry[1].wait()

    return run


def kernel_call(
    body, name, number, outs, scratch, operands, flops=0, far=(), scalars=(), late=(), staged=()
):
    vmem, anywhere, smem = (
        pl.BlockSpec(memory_space=space) for space in (pltpu.VMEM, pl.ANY, pltpu.SMEM)
    )
    in_specs = [
        anywhere if k in far or k in late else smem if k in scalars else vmem
        for k in range(len(operands))
    ]
    shapes = [jax.ShapeDtypeStruct(shape, dtype) for shape, dtype in outs]
    moved = sum(math.prod(s.shape) * s.dtype.itemsize for s in shapes) + sum(
        x.size * x.dtype.itemsize for x in operands
    )
    extra = [pltpu.VMEM(operands[k].shape, operands[k].dtype) for k in late]
    extra += [pltpu.VMEM(shapes[k].shape, shapes[k].dtype) for k in staged]
    if extra:
        extra.append(pltpu.SemaphoreType.DMA((len(extra),)))
    return pl.pallas_call(
        staged_body(body, len(operands), len(outs), late, staged),
        out_shape=shapes,
        in_specs=in_specs,
        out_specs=[anywhere if k in staged else vmem for k in range(len(shapes))],
        scratch_shapes=[*scratch, *extra],
        name=name,
        cost_estimate=pl.CostEstimate(flops=flops, bytes_accessed=moved, transcendentals=0),
        compiler_params=pltpu.CompilerParams(
            collective_id=number, has_side_effects=True, vmem_limit_bytes=VMEM_BYTES
        ),
    )(*operands)


def scatter_scratch(rows, depth):
    bf16 = jnp.bfloat16
    return [
        pltpu.VMEM((depth, rows, C), bf16),
        pltpu.VMEM((depth, rows, C), bf16),
        pltpu.VMEM((depth, rows, C), bf16),
        pltpu.VMEM((depth + 1, rows, C), bf16),
        pltpu.SemaphoreType.DMA((2, depth)),
        pltpu.SemaphoreType.DMA((2, 2, depth)),
    ]


def gather_scratch(depth):
    return pltpu.SemaphoreType.DMA((6, 2, depth + 1))


def total_scratch(shards):
    return [
        pltpu.VMEM((8, 128), jnp.float32),
        pltpu.VMEM((shards - 1, 8, 128), jnp.float32),
    ], pltpu.SemaphoreType.DMA((2, shards - 1))


def on_device_heads(
    hidden,
    latent_shape,
    cond_r,
    clip,
    cotangent,
    conv_weight,
    conv_bias,
    fc1_weight,
    fc1_bias,
    grn_gamma,
    grn_beta,
    fc2_weight,
    fc2_bias,
    time_weight,
    time_bias,
    map_weight,
    map_bias,
    query_weight,
    query_bias,
    key_weight,
    value_weight,
    value_bias,
    out_weight,
    out_bias,
):
    f32, bf16 = jnp.float32, jnp.bfloat16
    shards = lax.axis_size("seq")
    rows = hidden.shape[0]
    total = rows * shards
    cols = C // shards
    depth = shards // 2
    hidden_cols = FF // shards
    shape = latent_shape[0]
    w_qkv = jnp.concatenate([query_weight.T, key_weight.T, value_weight.T], axis=0)
    ctx_rows = 256
    context_in = jax.nn.silu(clip.reshape(NLAT * NCTX, CLIP).astype(f32)).astype(bf16)
    context_in = jnp.pad(context_in, ((0, ctx_rows - NLAT * NCTX), (0, 0)))
    ctx_cols = (against(map_weight.T, context_in) + map_bias.astype(f32)[:, None]).astype(bf16)
    units = cols // 4
    vmem = pltpu.VMEM
    total_vmem, total_sems = total_scratch(shards)
    (
        normed_full,
        held,
        wide,
        normed_one,
        inverse_one,
        pre_act,
        root,
        ratio,
        denom,
        response,
        context,
        d_mixed,
        cot_blocks,
        shrink_parts,
    ) = kernel_call(
        functools.partial(mixer_kernel, shards),
        "mixer",
        1,
        [
            ((shards, rows, C), bf16),
            ((rows + 2 * EDGE, C), bf16),
            ((32, C), f32),
            ((rows, C), f32),
            ((rows, 1), f32),
            ((shards, rows, hidden_cols), f32),
            ((8, hidden_cols), f32),
            ((8, hidden_cols), f32),
            ((8, 128), f32),
            ((shards, rows, hidden_cols), bf16),
            ((shards, cols, ctx_rows), bf16),
            ((depth, 2, rows, cols), bf16),
            ((depth, 2, rows, cols), bf16),
            ((shards, 4, units, hidden_cols), bf16),
        ],
        [
            vmem((24, cols), f32),
            vmem((shards, 24, cols), f32),
            vmem((rows + 2 * EDGE, C), f32),
            vmem((rows, C), f32),
            vmem((shards, rows, hidden_cols), f32),
            vmem((8, hidden_cols), f32),
            *total_vmem,
            pltpu.SemaphoreType.DMA((2, 2)),
            pltpu.SemaphoreType.DMA((2, shards - 1)),
            gather_scratch(depth),
            total_sems,
            gather_scratch(depth),
            pltpu.SemaphoreType.DMA((2, 2, depth + 1)),
            vmem((shards, 4, units, 2 * cols), bf16),
            vmem((depth, rows, C), bf16),
            vmem((2, depth, rows, cols), bf16),
            pltpu.SemaphoreType.DMA((2, 2)),
            pltpu.SemaphoreType.DMA((2,)),
            pltpu.SemaphoreType.DMA((2, shards + 2)),
            pltpu.SemaphoreType.DMA((2, shards + 2)),
        ],
        (
            shape,
            hidden,
            cond_r,
            time_weight,
            conv_weight,
            conv_bias,
            fc1_bias,
            grn_gamma,
            grn_beta,
            fc2_bias,
            time_bias,
            fc1_weight,
            ctx_cols,
            cotangent,
            fc2_weight.T,
            out_weight.T,
        ),
        flops=2 * total * C * hidden_cols,
        far=(14, 15),
        scalars=(0,),
        late=(11, 13),
        staged=(0, 1, 2, 3, 5, 9, 10, 13),
    )
    context = context.reshape(C, ctx_rows)
    shrink_rows = shrink_parts.reshape(C, hidden_cols)
    keys_all = total + ctx_rows
    (
        attn_blocks,
        first_sum,
        second_sum,
        normed_two,
        inverse_two,
        queries,
        keys,
        values,
    ) = kernel_call(
        functools.partial(mixed_in_kernel, shards),
        "mixed_in",
        2,
        [
            ((shards, rows, C), bf16),
            ((rows, C), f32),
            ((rows, C), f32),
            ((rows, C), f32),
            ((rows, 1), f32),
            ((shards, rows, cols), bf16),
            ((cols, keys_all), bf16),
            ((cols, keys_all), bf16),
        ],
        [pltpu.VMEM((rows, C), f32), *scatter_scratch(rows, depth), gather_scratch(depth)],
        (
            shape,
            response,
            shrink_rows,
            hidden,
            wide,
            w_qkv,
            query_bias,
            value_bias,
            context,
        ),
        flops=2 * total * C * (hidden_cols + 3 * cols),
        scalars=(0,),
        late=(3, 5, 8),
        staged=(0, 1, 2, 3, 5, 6, 7),
    )

    tiles, tile_rows = 4, total // 4
    d_qkv, mixed_full, cot_cols = kernel_call(
        functools.partial(attend_kernel, shards),
        "attend",
        5,
        [
            ((3 * cols, keys_all), bf16),
            ((tiles, shards, cols, tile_rows), bf16),
            ((cols, total), bf16),
        ],
        [
            vmem((cols, keys_all), f32),
            vmem((cols, keys_all), f32),
            vmem((cols // HEAD_DIM, tile_rows, keys_all), f32),
            pltpu.SemaphoreType.DMA((tiles, 6, 2, depth + 1)),
        ],
        (
            shape,
            queries,
            keys,
            values,
            d_mixed.reshape(shards, rows, cols),
            cot_blocks.reshape(shards, rows, cols),
        ),
        flops=12 * total * keys_all * 3 * 256,
        scalars=(0,),
    )
    (
        d_first,
        d_pre,
        small,
        weight_sums,
        grad_map_w,
        act_cols,
        fc2_half,
        branch_sum,
    ) = kernel_call(
        functools.partial(attn_back_kernel, shards),
        "attn_back",
        3,
        [
            ((rows, C), f32),
            ((shards, rows, hidden_cols), bf16),
            ((SMALL_ROWS, 2 * cols), bf16),
            ((4 * cols, C), bf16),
            ((cols, CLIP), bf16),
            ((cols, total), bf16),
            ((shards, 2, units, hidden_cols), bf16),
            ((8, C), f32),
        ],
        [
            vmem((shards, rows, C), bf16),
            vmem((8, C), f32),
            vmem((SMALL_ROWS, 2 * cols), f32),
            pltpu.VMEM((rows, C), f32),
            pltpu.VMEM((shards, rows, hidden_cols), f32),
            pltpu.VMEM((shards, rows, hidden_cols), bf16),
            pltpu.VMEM((8, hidden_cols), f32),
            *total_vmem,
            *scatter_scratch(rows, depth),
            gather_scratch(depth),
            total_sems,
            vmem((4 * cols, C), bf16),
            vmem((2 * cols, C), bf16),
            vmem((2 * cols, C), bf16),
            pltpu.SemaphoreType.DMA((2, 3)),
            vmem((shards, 8, 2 * cols), f32),
            pltpu.SemaphoreType.DMA((2, shards - 1)),
            vmem((shards, 4, units, hidden_cols), bf16),
            vmem((2, shards, units, hidden_cols), bf16),
            pltpu.SemaphoreType.DMA((2, 2)),
            vmem((shards, cols, ctx_rows), bf16),
            vmem((shards, cols, ctx_rows), bf16),
            pltpu.SemaphoreType.DMA((2, shards - 1)),
        ],
        (
            shape,
            cond_r,
            d_qkv,
            w_qkv,
            attn_blocks,
            context,
            mixed_full,
            cot_cols,
            out_weight.T,
            grn_gamma,
            out_bias,
            cotangent,
            normed_two,
            inverse_two,
            first_sum,
            wide,
            shrink_rows,
            pre_act,
            root,
            ratio,
            denom,
            response,
            context_in,
        ),
        flops=2 * total * C * (hidden_cols + 6 * cols),
        scalars=(0,),
        late=(4, 5, 6, 7, 8, 11, 12, 14, 16, 17, 21, 22),
        staged=(0, 1, 3, 5, 6),
    )
    groups = lax.axis_size("grp")
    input_grad, fc1_sum, fc2_sum, map_sum, small, conv_small, activations = kernel_call(
        functools.partial(conv_back_kernel, shards),
        "conv_back",
        4,
        [
            ((rows, C), f32),
            ((C, hidden_cols), bf16),
            ((cols, FF), bf16),
            ((cols, CLIP), bf16),
            ((SMALL_ROWS, 2 * cols), f32),
            ((16, cols), f32),
            ((rows, C), bf16),
        ],
        [
            vmem((rows + 2 * EDGE, C), bf16),
            vmem((rows + 2 * EDGE, C), f32),
            vmem((rows, C), f32),
            *scatter_scratch(rows, depth),
            pltpu.SemaphoreType.DMA((2, 2)),
            vmem((16, C), f32),
            vmem((C, hidden_cols), bf16),
            vmem((C // 2, hidden_cols), bf16),
            vmem((C // 2, hidden_cols), bf16),
            vmem((shards, units, hidden_cols), bf16),
            vmem((shards, units, hidden_cols), bf16),
            vmem((cols, CLIP), bf16),
            vmem((cols // 2, CLIP), bf16),
            vmem((cols // 2, CLIP), bf16),
            pltpu.SemaphoreType.DMA((2, 2, 3)),
            pltpu.SemaphoreType.DMA((2, 3 + shards)),
            vmem((groups - 1, SMALL_ROWS, 2 * cols), bf16),
            pltpu.SemaphoreType.DMA((2, groups - 1)),
            vmem((shards, 16, cols), f32),
            vmem((shards, 16, cols), f32),
            vmem((16, cols), f32),
            vmem((groups - 1, 16, cols), f32),
            pltpu.SemaphoreType.DMA((2, shards + groups - 2)),
            vmem((shards, cols, rows), bf16),
            pltpu.SemaphoreType.DMA((2, shards - 1)),
        ],
        (
            shape,
            d_pre,
            fc1_weight,
            normed_one,
            inverse_one,
            d_first,
            held,
            wide,
            normed_full,
            branch_sum,
            grad_map_w,
            act_cols,
            second_sum,
            fc2_half,
            small,
        ),
        flops=6 * total * C * hidden_cols,
        scalars=(0,),
        late=(3, 5, 6, 8, 12),
        staged=(1, 2),
    )
    two = lambda row: small[row : row + 2].reshape(hidden_cols)
    one = lambda row: small[row, :cols]
    part = lambda k: weight_sums[k * cols : (k + 1) * cols].astype(f32).T
    return (
        activations,
        input_grad,
        conv_small[:9],
        conv_small[9],
        fc1_sum.astype(f32),
        two(SMALL_FC1),
        two(SMALL_GAMMA),
        two(SMALL_BETA),
        fc2_sum.astype(f32).T,
        conv_small[10],
        small[:SMALL_FC1],
        small[SMALL_TIME],
        map_sum.astype(f32).T,
        one(SMALL_MAP),
        part(0),
        one(SMALL_QUERY),
        part(1),
        part(2),
        one(SMALL_VALUE),
        part(3),
        one(SMALL_OUT),
    )


def solution(mesh):
    in_specs = (
        P(("grp", "seq"), None),
        P("grp", None, None),
        P("grp", None),
        P("grp", None, None),
        P(("grp", "seq"), None),
        P(None, "seq"),
        P("seq"),
        P(None, "seq"),
        P("seq"),
        P("seq"),
        P("seq"),
        P(None, "seq"),
        P("seq"),
        P(None, "seq"),
        P("seq"),
        P(None, "seq"),
        P("seq"),
        P(None, "seq"),
        P("seq"),
        P(None, "seq"),
        P(None, "seq"),
        P("seq"),
        P(None, "seq"),
        P("seq"),
    )
    out_specs = (
        P(("grp", "seq"), None),
        P(("grp", "seq"), None),
        P(None, "seq"),
        P("seq"),
        P(None, "seq"),
        P("seq"),
        P("seq"),
        P("seq"),
        P(None, "seq"),
        P("seq"),
        P(None, "seq"),
        P("seq"),
        P(None, "seq"),
        P("seq"),
        P(None, "seq"),
        P("seq"),
        P(None, "seq"),
        P(None, "seq"),
        P("seq"),
        P(None, "seq"),
        P("seq"),
    )
    by_heads = mesh.shape["seq"] == 8 and mesh.shape["grp"] == 4
    return jax.shard_map(
        on_device_heads if by_heads else on_device, mesh=mesh, in_specs=in_specs, out_specs=out_specs, check_vma=False
    )
```

```python
import functools
import math

import jax
import jax.numpy as jnp
from jax import lax
from jax.experimental import pallas as pl
from jax.experimental.pallas import tpu as pltpu
from jax.sharding import PartitionSpec as P

C = 1536
HEADS = 24
HEAD_DIM = 64
FF = 6144
CLIP = 1280
NCTX = 77
NLAT = 3
WMAX = 64


EPS_NORM = 1e-06
SCORE_SCALE = 0.125
MASKED = -1e30
HIGHEST_PRECISION = lax.Precision.HIGHEST


def padded_2(block, sides, width):
    for axis, dim in sides:
        count = lax.axis_size(axis)
        forward = [(i, i + 1) for i in range(count - 1)]
        backward = [(target, source) for source, target in forward]
        low = lax.ppermute(
            lax.slice_in_dim(block, block.shape[dim] - width, None, axis=dim), axis, forward
        )
        high = lax.ppermute(lax.slice_in_dim(block, 0, width, axis=dim), axis, backward)
        block = jnp.concatenate([low, block, high], axis=dim)
    return block


def latent_grid(positions, shape_row):
    latent_count = shape_row.shape[0]
    heights = shape_row[:, 0]
    latent_width = shape_row[0, 1]
    pixel_counts = heights * latent_width
    end_points = jnp.cumsum(pixel_counts)
    start_points = end_points - pixel_counts
    segment = jnp.sum((positions[:, None] >= end_points[None, :]).astype(jnp.int32), axis=1)
    segment = jnp.minimum(segment, latent_count - 1)
    picked = (segment[:, None] == jnp.arange(latent_count, dtype=jnp.int32)[None, :]).astype(
        jnp.int32
    )
    first_pixel = jnp.sum(picked * start_points[None, :], axis=1)
    height = jnp.sum(picked * heights[None, :], axis=1)
    offset_in = positions - first_pixel
    row_index = jnp.floor_divide(offset_in, latent_width)
    column = offset_in - row_index * latent_width
    return (segment, row_index, column, height, latent_width)


def valid_tap(row_index, column, height, latent_width, down_step, side_step):
    upright = (row_index + down_step >= 0) & (row_index + down_step < height)
    across = (column + side_step >= 0) & (column + side_step < latent_width)
    return (upright & across).astype(jnp.float32)


def layer_stats(values_in):
    average = jnp.mean(values_in, axis=-1, keepdims=True)
    centred = values_in - average
    variance = jnp.mean(centred * centred, axis=-1, keepdims=True)
    inverse = lax.rsqrt(variance + EPS_NORM)
    return (centred * inverse, inverse)


def layer_back(gradient, normed, inverse):
    mean_grad = jnp.mean(gradient, axis=-1, keepdims=True)
    mean_mixed = jnp.mean(gradient * normed, axis=-1, keepdims=True)
    return inverse * (gradient - mean_grad - normed * mean_mixed)


def against(values_low, weight_low):
    return lax.dot_general(
        values_low, weight_low, (((1,), (1,)), ((), ())), preferred_element_type=jnp.float32
    )


def against_exact(values_in, weight_in):
    return lax.dot_general(
        values_in,
        weight_in,
        (((1,), (1,)), ((), ())),
        precision=HIGHEST_PRECISION,
        preferred_element_type=jnp.float32,
    )


def outer_sum(left_low, right_low):
    return lax.dot_general(
        left_low, right_low, (((0,), (0,)), ((), ())), preferred_element_type=jnp.float32
    )


def column_sum(picked, values_in):
    return lax.dot_general(
        picked,
        values_in,
        (((0,), (0,)), ((), ())),
        precision=HIGHEST_PRECISION,
        preferred_element_type=jnp.float32,
    )


def exact_gelu(values_in):
    return jax.nn.gelu(values_in, approximate=False)


def block_size(row_count, shard_rows):
    shard_total = row_count // shard_rows
    return math.gcd(shard_total, max(1, 1024 // shard_rows)) * shard_rows


def on_device(
    hidden,
    latent_shape,
    cond_r,
    clip,
    cotangent,
    conv_weight,
    conv_bias,
    fc1_weight,
    fc1_bias,
    grn_gamma,
    grn_beta,
    fc2_weight,
    fc2_bias,
    time_weight,
    time_bias,
    map_weight,
    map_bias,
    query_weight,
    query_bias,
    key_weight,
    value_weight,
    value_bias,
    out_weight,
    out_bias,
):
    tok_rows = hidden.shape[0]
    positions = lax.axis_index("seq") * tok_rows + jnp.arange(tok_rows, dtype=jnp.int32)
    shape_row = latent_shape[0]
    segment, row_index, column, height, latent_width = latent_grid(positions, shape_row)
    margin = WMAX + 1
    gathered = (
        lax.all_gather(conv_weight, "seq", axis=1, tiled=True),
        lax.all_gather(conv_bias, "seq", axis=0, tiled=True),
        lax.all_gather(fc1_weight, "seq", axis=1, tiled=True),
        lax.all_gather(fc1_bias, "seq", axis=0, tiled=True),
        lax.all_gather(grn_gamma, "seq", axis=0, tiled=True),
        lax.all_gather(grn_beta, "seq", axis=0, tiled=True),
        lax.all_gather(fc2_weight, "seq", axis=1, tiled=True),
        lax.all_gather(fc2_bias, "seq", axis=0, tiled=True),
        lax.all_gather(time_weight, "seq", axis=1, tiled=True),
        lax.all_gather(time_bias, "seq", axis=0, tiled=True),
        lax.all_gather(map_weight, "seq", axis=1, tiled=True),
        lax.all_gather(map_bias, "seq", axis=0, tiled=True),
        lax.all_gather(query_weight, "seq", axis=1, tiled=True),
        lax.all_gather(query_bias, "seq", axis=0, tiled=True),
        lax.all_gather(key_weight, "seq", axis=1, tiled=True),
        lax.all_gather(value_weight, "seq", axis=1, tiled=True),
        lax.all_gather(value_bias, "seq", axis=0, tiled=True),
        lax.all_gather(out_weight, "seq", axis=1, tiled=True),
        lax.all_gather(out_bias, "seq", axis=0, tiled=True),
    )
    (
        kernel_full,
        kernel_bias,
        expand_full,
        expand_bias,
        gamma_full,
        beta_full,
        shrink_full,
        shrink_bias,
        time_full,
        time_bias_full,
        mapper_full,
        mapper_bias,
        query_full,
        query_bias_full,
        key_full,
        value_full,
        value_bias_full,
        output_full,
        output_bias_full,
    ) = gathered
    padded = padded_2(hidden, (("seq", 0),), margin)
    conv_out = jnp.broadcast_to(kernel_bias.astype(jnp.float32)[None, :], (tok_rows, C))
    tap_list = []
    for down_step in (-1, 0, 1):
        for side_step in (-1, 0, 1):
            tap_number = 3 * (down_step + 1) + (side_step + 1)
            valid = valid_tap(row_index, column, height, latent_width, down_step, side_step)
            offset_rows = down_step * latent_width + side_step
            nearby = lax.dynamic_slice_in_dim(padded, margin + offset_rows, tok_rows, 0).astype(
                jnp.float32
            )
            conv_out = (
                conv_out
                + kernel_full[tap_number].astype(jnp.float32)[None, :] * nearby * valid[:, None]
            )
            tap_list.append((tap_number, down_step, side_step, offset_rows, valid))
    normed_one, inverse_one = layer_stats(conv_out)
    normed_low = normed_one.astype(jnp.bfloat16)
    pre_act = jnp.dot(
        normed_low, expand_full, preferred_element_type=jnp.float32
    ) + expand_bias.astype(jnp.float32)
    activated, gelu_pull = jax.vjp(exact_gelu, pre_act)
    picked = (segment[:, None] == jnp.arange(NLAT, dtype=jnp.int32)[None, :]).astype(jnp.float32)
    energy = lax.psum(column_sum(picked, activated * activated), "seq")
    root = jnp.sqrt(energy + 1.0)
    denom = jnp.mean(root, axis=-1, keepdims=True) + EPS_NORM
    ratio = root / denom
    ratio_rows = jnp.dot(picked, ratio, precision=HIGHEST_PRECISION)
    gamma_value = gamma_full.astype(jnp.float32)
    response = gamma_value * (activated * ratio_rows) + beta_full.astype(jnp.float32) + activated
    response_low = response.astype(jnp.bfloat16)
    branch = jnp.dot(
        response_low, shrink_full, preferred_element_type=jnp.float32
    ) + shrink_bias.astype(jnp.float32)
    first_sum = hidden.astype(jnp.float32) + branch
    modulation = jnp.dot(
        cond_r, time_full.astype(jnp.float32), precision=HIGHEST_PRECISION
    ) + time_bias_full.astype(jnp.float32)
    mod_rows = jnp.dot(picked, modulation, precision=HIGHEST_PRECISION)
    scale_rows = 1.0 + mod_rows[:, :C]
    second_sum = first_sum * scale_rows + mod_rows[:, C:]
    normed_two, inverse_two = layer_stats(second_sum)
    attn_in = normed_two.astype(jnp.bfloat16)
    context_in = jax.nn.silu(clip.reshape(NLAT * NCTX, CLIP).astype(jnp.float32)).astype(
        jnp.bfloat16
    )
    context = (
        jnp.dot(context_in, mapper_full, preferred_element_type=jnp.float32)
        + mapper_bias.astype(jnp.float32)
    ).astype(jnp.bfloat16)
    queries = (
        jnp.dot(attn_in, query_full, preferred_element_type=jnp.float32)
        + query_bias_full.astype(jnp.float32)
    ).astype(jnp.bfloat16)
    keys_low = jnp.dot(attn_in, key_full, preferred_element_type=jnp.float32).astype(jnp.bfloat16)
    values_low = (
        jnp.dot(attn_in, value_full, preferred_element_type=jnp.float32)
        + value_bias_full.astype(jnp.float32)
    ).astype(jnp.bfloat16)
    context_keys = jnp.dot(context, key_full, preferred_element_type=jnp.float32).astype(
        jnp.bfloat16
    )
    context_values = (
        jnp.dot(context, value_full, preferred_element_type=jnp.float32)
        + value_bias_full.astype(jnp.float32)
    ).astype(jnp.bfloat16)
    query_heads = queries.reshape(tok_rows, HEADS, HEAD_DIM)
    key_heads = keys_low.reshape(tok_rows, HEADS, HEAD_DIM)
    value_heads = values_low.reshape(tok_rows, HEADS, HEAD_DIM)
    ctx_key_heads = context_keys.reshape(NLAT * NCTX, HEADS, HEAD_DIM)
    ctx_value_heads = context_values.reshape(NLAT * NCTX, HEADS, HEAD_DIM)
    context_segment = jnp.arange(NLAT * NCTX, dtype=jnp.int32) // NCTX
    ctx_admit = segment[:, None] == context_segment[None, :]

    def segments_at(first_row, length):
        return latent_grid(first_row + jnp.arange(length, dtype=jnp.int32), shape_row)[0]

    ctx_scores = (
        jnp.einsum("qhd,khd->hqk", query_heads, ctx_key_heads, preferred_element_type=jnp.float32)
        * SCORE_SCALE
    )
    ctx_scores = jnp.where(ctx_admit[None], ctx_scores, MASKED)
    start_max = jnp.max(ctx_scores, axis=-1)
    ctx_expo = jnp.exp(ctx_scores - start_max[..., None])
    start_total = jnp.sum(ctx_expo, axis=-1)
    start_accum = jnp.einsum(
        "hqk,khd->qhd",
        ctx_expo.astype(jnp.bfloat16),
        ctx_value_heads,
        preferred_element_type=jnp.float32,
    )
    key_part = lax.all_gather(keys_low, "seq", axis=0, tiled=True)
    value_part = lax.all_gather(values_low, "seq", axis=0, tiled=True)
    block_rows = block_size(key_part.shape[0], tok_rows)
    block_count = key_part.shape[0] // block_rows
    key_stack = key_part.reshape(block_count, block_rows, HEADS, HEAD_DIM)
    value_stack = value_part.reshape(block_count, block_rows, HEADS, HEAD_DIM)

    def attend_visit(state_now, element):
        key_block, value_block, block_index = element
        key_segment = segments_at(block_index * block_rows, block_rows)
        admitted = segment[:, None] == key_segment[None, :]
        scores = (
            jnp.einsum("qhd,khd->hqk", query_heads, key_block, preferred_element_type=jnp.float32)
            * SCORE_SCALE
        )
        scores = jnp.where(admitted[None], scores, MASKED)
        old_max, old_total, old_accum = state_now
        new_max = jnp.maximum(old_max, jnp.max(scores, axis=-1))
        factor = jnp.exp(old_max - new_max)
        expo_block = jnp.exp(scores - new_max[..., None])
        new_total = old_total * factor + jnp.sum(expo_block, axis=-1)
        new_accum = old_accum * factor.T[:, :, None] + jnp.einsum(
            "hqk,khd->qhd",
            expo_block.astype(jnp.bfloat16),
            value_block,
            preferred_element_type=jnp.float32,
        )
        return ((new_max, new_total, new_accum), None)

    state_end, ignored = lax.scan(
        attend_visit,
        (start_max, start_total, start_accum),
        (key_stack, value_stack, jnp.arange(block_count, dtype=jnp.int32)),
    )
    run_max, run_total, accum = state_end
    mixed = accum / run_total.T[:, :, None]
    log_total = run_max + jnp.log(run_total)
    mixed_low = mixed.reshape(tok_rows, C).astype(jnp.bfloat16)
    activations = (
        second_sum
        + jnp.dot(mixed_low, output_full, preferred_element_type=jnp.float32)
        + output_bias_full.astype(jnp.float32)
    ).astype(jnp.bfloat16)
    cot_value = cotangent.astype(jnp.float32)
    grad_out_w = outer_sum(mixed_low, cotangent)
    grad_out_b = jnp.sum(cot_value, axis=0)
    d_mixed_low = against(cotangent, output_full).astype(jnp.bfloat16)
    dmix_heads = d_mixed_low.reshape(tok_rows, HEADS, HEAD_DIM)
    delta = jnp.sum(dmix_heads.astype(jnp.float32) * mixed, axis=-1).T
    ctx_probs = jnp.exp(ctx_scores - log_total[..., None])
    ctx_dprob = jnp.einsum(
        "qhd,khd->hqk", dmix_heads, ctx_value_heads, preferred_element_type=jnp.float32
    )
    ctx_dscore = (ctx_probs * (ctx_dprob - delta[..., None])).astype(jnp.bfloat16)
    dquery_start = (
        jnp.einsum("hqk,khd->qhd", ctx_dscore, ctx_key_heads, preferred_element_type=jnp.float32)
        * SCORE_SCALE
    )
    ctx_dkey_part = (
        jnp.einsum("hqk,qhd->khd", ctx_dscore, query_heads, preferred_element_type=jnp.float32)
        * SCORE_SCALE
    )
    ctx_dvalue_part = jnp.einsum(
        "hqk,qhd->khd",
        ctx_probs.astype(jnp.bfloat16),
        dmix_heads,
        preferred_element_type=jnp.float32,
    )
    key_part = lax.all_gather(keys_low, "seq", axis=0, tiled=True)
    value_part = lax.all_gather(values_low, "seq", axis=0, tiled=True)
    query_block_rows = block_size(key_part.shape[0], tok_rows)
    block_count = key_part.shape[0] // query_block_rows
    key_stack = key_part.reshape(block_count, query_block_rows, HEADS, HEAD_DIM)
    value_stack = value_part.reshape(block_count, query_block_rows, HEADS, HEAD_DIM)

    def query_visit(state_now, element):
        key_block, value_block, block_index = element
        key_segment = segments_at(block_index * query_block_rows, query_block_rows)
        admitted = segment[:, None] == key_segment[None, :]
        scores = (
            jnp.einsum("qhd,khd->hqk", query_heads, key_block, preferred_element_type=jnp.float32)
            * SCORE_SCALE
        )
        scores = jnp.where(admitted[None], scores, MASKED)
        probs = jnp.exp(scores - log_total[..., None])
        dprob = jnp.einsum(
            "qhd,khd->hqk", dmix_heads, value_block, preferred_element_type=jnp.float32
        )
        dscore = (probs * (dprob - delta[..., None])).astype(jnp.bfloat16)
        added = (
            jnp.einsum("hqk,khd->qhd", dscore, key_block, preferred_element_type=jnp.float32)
            * SCORE_SCALE
        )
        return (state_now + added, None)

    state_end, ignored = lax.scan(
        query_visit,
        dquery_start,
        (key_stack, value_stack, jnp.arange(block_count, dtype=jnp.int32)),
    )
    dquery = state_end
    lse_all, delta_all = (
        lax.all_gather(log_total.T, "seq", axis=0, tiled=True),
        lax.all_gather(delta.T, "seq", axis=0, tiled=True),
    )
    zero_heads = jnp.zeros((tok_rows, HEADS, HEAD_DIM), jnp.float32)
    query_part = lax.all_gather(queries, "seq", axis=0, tiled=True)
    dmix_part = lax.all_gather(d_mixed_low, "seq", axis=0, tiled=True)
    row_count = query_part.shape[0]
    key_block_rows = block_size(row_count, tok_rows)
    block_count = row_count // key_block_rows
    query_stack = query_part.reshape(block_count, key_block_rows, HEADS, HEAD_DIM)
    dmix_stack = dmix_part.reshape(block_count, key_block_rows, HEADS, HEAD_DIM)
    lse_stack = lse_all.reshape(block_count, key_block_rows, HEADS)
    delta_stack = delta_all.reshape(block_count, key_block_rows, HEADS)

    def key_visit(state_now, element):
        query_block, dmix_block, lse_block, delta_block, block_index = element
        query_segment = segments_at(block_index * key_block_rows, key_block_rows)
        admitted = segment[:, None] == query_segment[None, :]
        scores = (
            jnp.einsum("khd,qhd->hkq", key_heads, query_block, preferred_element_type=jnp.float32)
            * SCORE_SCALE
        )
        scores = jnp.where(admitted[None], scores, MASKED)
        probs = jnp.exp(scores - lse_block.T[:, None, :])
        dkey_now, dvalue_now = state_now
        dvalue_now = dvalue_now + jnp.einsum(
            "hkq,qhd->khd",
            probs.astype(jnp.bfloat16),
            dmix_block,
            preferred_element_type=jnp.float32,
        )
        dprob = jnp.einsum(
            "khd,qhd->hkq", value_heads, dmix_block, preferred_element_type=jnp.float32
        )
        dscore = (probs * (dprob - delta_block.T[:, None, :])).astype(jnp.bfloat16)
        dkey_now = (
            dkey_now
            + jnp.einsum("hkq,qhd->khd", dscore, query_block, preferred_element_type=jnp.float32)
            * SCORE_SCALE
        )
        return ((dkey_now, dvalue_now), None)

    state_end, ignored = lax.scan(
        key_visit,
        (zero_heads, zero_heads),
        (query_stack, dmix_stack, lse_stack, delta_stack, jnp.arange(block_count, dtype=jnp.int32)),
    )
    dkey, dvalue = state_end
    dquery_low = dquery.reshape(tok_rows, C).astype(jnp.bfloat16)
    dkey_low = dkey.reshape(tok_rows, C).astype(jnp.bfloat16)
    dvalue_low = dvalue.reshape(tok_rows, C).astype(jnp.bfloat16)
    ctx_dkey_flat = ctx_dkey_part.reshape(NLAT * NCTX, C)
    ctx_dvalue_flat = ctx_dvalue_part.reshape(NLAT * NCTX, C)
    context_value = context.astype(jnp.float32)
    d_attn_in = (
        against(dquery_low, query_full)
        + against(dkey_low, key_full)
        + against(dvalue_low, value_full)
    )
    grad_query_w = outer_sum(attn_in, dquery_low)
    grad_query_b = jnp.sum(dquery_low.astype(jnp.float32), axis=0)
    grad_key_w = outer_sum(attn_in, dkey_low) + column_sum(context_value, ctx_dkey_flat)
    grad_value_w = outer_sum(attn_in, dvalue_low) + column_sum(context_value, ctx_dvalue_flat)
    grad_value_b = jnp.sum(dvalue_low.astype(jnp.float32), axis=0) + jnp.sum(
        ctx_dvalue_flat, axis=0
    )
    d_context = against_exact(ctx_dkey_flat, key_full.astype(jnp.float32)) + against_exact(
        ctx_dvalue_flat, value_full.astype(jnp.float32)
    )
    grad_map_w = column_sum(context_in.astype(jnp.float32), d_context)
    grad_map_b = jnp.sum(d_context, axis=0)
    d_second = cot_value + layer_back(d_attn_in, normed_two, inverse_two)
    d_first = d_second * scale_rows
    d_mod_rows = jnp.concatenate([d_second * first_sum, d_second], axis=1)
    d_modulation = column_sum(picked, d_mod_rows)
    grad_time_w = lax.dot_general(
        cond_r,
        d_modulation,
        (((0,), (0,)), ((), ())),
        precision=HIGHEST_PRECISION,
        preferred_element_type=jnp.float32,
    )
    grad_time_b = jnp.sum(d_modulation, axis=0)
    d_branch_low = d_first.astype(jnp.bfloat16)
    grad_shrink_w = outer_sum(response_low, d_branch_low)
    grad_shrink_b = jnp.sum(d_branch_low.astype(jnp.float32), axis=0)
    d_response = against(d_branch_low, shrink_full)
    grad_gamma = jnp.sum(d_response * activated * ratio_rows, axis=0)
    grad_beta = jnp.sum(d_response, axis=0)
    d_ratio = lax.psum(column_sum(picked, d_response * gamma_value * activated), "seq")
    d_root = d_ratio / denom - jnp.sum(d_ratio * root, axis=-1, keepdims=True) / (
        FF * denom * denom
    )
    d_act = d_response * (gamma_value * ratio_rows + 1.0) + activated * jnp.dot(
        picked, d_root / root, precision=HIGHEST_PRECISION
    )
    d_pre_low = gelu_pull(d_act)[0].astype(jnp.bfloat16)
    grad_expand_w = outer_sum(normed_low, d_pre_low)
    grad_expand_b = jnp.sum(d_pre_low.astype(jnp.float32), axis=0)
    d_normed = against(d_pre_low, expand_full)
    d_conv_low = layer_back(d_normed, normed_one, inverse_one).astype(jnp.bfloat16)
    d_conv = d_conv_low.astype(jnp.float32)
    grad_kernel_b = jnp.sum(d_conv, axis=0)
    d_padded = padded_2(d_conv_low, (("seq", 0),), margin)
    kernel_rows = []
    input_grad = d_first
    for tap_number, down_step, side_step, offset_rows, valid in tap_list:
        nearby = lax.dynamic_slice_in_dim(padded, margin + offset_rows, tok_rows, 0).astype(
            jnp.float32
        )
        kernel_rows.append(jnp.sum(d_conv * nearby * valid[:, None], axis=0))
        source = positions - offset_rows
        src_segment, src_row, src_column, src_height, src_width = latent_grid(source, shape_row)
        src_valid = valid_tap(src_row, src_column, src_height, src_width, down_step, side_step)
        behind = lax.dynamic_slice_in_dim(d_padded, margin - offset_rows, tok_rows, 0).astype(
            jnp.float32
        )
        input_grad = (
            input_grad
            + kernel_full[tap_number].astype(jnp.float32)[None, :] * behind * src_valid[:, None]
        )
    grad_kernel_w = jnp.stack(kernel_rows, axis=0)
    gradients = (
        grad_kernel_w,
        grad_kernel_b,
        grad_expand_w,
        grad_expand_b,
        grad_gamma,
        grad_beta,
        grad_shrink_w,
        grad_shrink_b,
        grad_time_w,
        grad_time_b,
        grad_map_w,
        grad_map_b,
        grad_query_w,
        grad_query_b,
        grad_key_w,
        grad_value_w,
        grad_value_b,
        grad_out_w,
        grad_out_b,
    )
    shares = (
        lax.psum_scatter(gradients[0], "seq", scatter_dimension=1, tiled=True),
        lax.psum_scatter(gradients[1], "seq", scatter_dimension=0, tiled=True),
        lax.psum_scatter(gradients[2], "seq", scatter_dimension=1, tiled=True),
        lax.psum_scatter(gradients[3], "seq", scatter_dimension=0, tiled=True),
        lax.psum_scatter(gradients[4], "seq", scatter_dimension=0, tiled=True),
        lax.psum_scatter(gradients[5], "seq", scatter_dimension=0, tiled=True),
        lax.psum_scatter(gradients[6], "seq", scatter_dimension=1, tiled=True),
        lax.psum_scatter(gradients[7], "seq", scatter_dimension=0, tiled=True),
        lax.psum_scatter(gradients[8], "seq", scatter_dimension=1, tiled=True),
        lax.psum_scatter(gradients[9], "seq", scatter_dimension=0, tiled=True),
        lax.psum_scatter(gradients[10], "seq", scatter_dimension=1, tiled=True),
        lax.psum_scatter(gradients[11], "seq", scatter_dimension=0, tiled=True),
        lax.psum_scatter(gradients[12], "seq", scatter_dimension=1, tiled=True),
        lax.psum_scatter(gradients[13], "seq", scatter_dimension=0, tiled=True),
        lax.psum_scatter(gradients[14], "seq", scatter_dimension=1, tiled=True),
        lax.psum_scatter(gradients[15], "seq", scatter_dimension=1, tiled=True),
        lax.psum_scatter(gradients[16], "seq", scatter_dimension=0, tiled=True),
        lax.psum_scatter(gradients[17], "seq", scatter_dimension=1, tiled=True),
        lax.psum_scatter(gradients[18], "seq", scatter_dimension=0, tiled=True),
    )
    summed = (
        lax.psum(shares[0].astype(jnp.bfloat16), "grp").astype(jnp.float32),
        lax.psum(shares[1].astype(jnp.bfloat16), "grp").astype(jnp.float32),
        lax.psum(shares[2].astype(jnp.bfloat16), "grp").astype(jnp.float32),
        lax.psum(shares[3].astype(jnp.bfloat16), "grp").astype(jnp.float32),
        lax.psum(shares[4].astype(jnp.bfloat16), "grp").astype(jnp.float32),
        lax.psum(shares[5].astype(jnp.bfloat16), "grp").astype(jnp.float32),
        lax.psum(shares[6].astype(jnp.bfloat16), "grp").astype(jnp.float32),
        lax.psum(shares[7].astype(jnp.bfloat16), "grp").astype(jnp.float32),
        lax.psum(shares[8].astype(jnp.bfloat16), "grp").astype(jnp.float32),
        lax.psum(shares[9].astype(jnp.bfloat16), "grp").astype(jnp.float32),
        lax.psum(shares[10].astype(jnp.bfloat16), "grp").astype(jnp.float32),
        lax.psum(shares[11].astype(jnp.bfloat16), "grp").astype(jnp.float32),
        lax.psum(shares[12].astype(jnp.bfloat16), "grp").astype(jnp.float32),
        lax.psum(shares[13].astype(jnp.bfloat16), "grp").astype(jnp.float32),
        lax.psum(shares[14].astype(jnp.bfloat16), "grp").astype(jnp.float32),
        lax.psum(shares[15].astype(jnp.bfloat16), "grp").astype(jnp.float32),
        lax.psum(shares[16].astype(jnp.bfloat16), "grp").astype(jnp.float32),
        lax.psum(shares[17].astype(jnp.bfloat16), "grp").astype(jnp.float32),
        lax.psum(shares[18].astype(jnp.bfloat16), "grp").astype(jnp.float32),
    )
    return (
        activations,
        input_grad,
        summed[0],
        summed[1],
        summed[2],
        summed[3],
        summed[4],
        summed[5],
        summed[6],
        summed[7],
        summed[8],
        summed[9],
        summed[10],
        summed[11],
        summed[12],
        summed[13],
        summed[14],
        summed[15],
        summed[16],
        summed[17],
        summed[18],
    )


def mm(left, right):
    return jnp.dot(left, right, preferred_element_type=jnp.float32)


MESH_ID = pl.DeviceIdType.MESH


def dot_nt(left, right):
    return lax.dot_general(
        left, right, (((1,), (1,)), ((), ())), preferred_element_type=jnp.float32
    )


def place():
    me = lax.axis_index("seq")
    z, y = me // 2, lax.rem(me, 2)
    return me, z, y, me + 1 - 2 * y


def seq_copy(src, dst, send, recv, target):
    return pltpu.make_async_remote_copy(
        src_ref=src,
        dst_ref=dst,
        send_sem=send,
        recv_sem=recv,
        device_id={"seq": target},
        device_id_type=MESH_ID,
    )


def dot_tn(left, right):
    return lax.dot_general(
        left, right, (((0,), (0,)), ((), ())), preferred_element_type=jnp.float32
    )


def grp_copy(src, dst, send, recv, target):
    return pltpu.make_async_remote_copy(
        src_ref=src,
        dst_ref=dst,
        send_sem=send,
        recv_sem=recv,
        device_id={"grp": target},
        device_id_type=MESH_ID,
    )


def group_place():
    group = lax.axis_index("grp")
    core = lax.rem(group, 2)
    return group // 2, core, group + 1 - 2 * core, lax.rem(group + 2, 4)


def meet_all(shards, groups=0):
    me = lax.axis_index("seq")
    barrier = pltpu.get_barrier_semaphore()
    for step in range(1, groups):
        pl.semaphore_signal(
            barrier,
            inc=1,
            device_id={"grp": lax.rem(lax.axis_index("grp") + step, groups)},
            device_id_type=MESH_ID,
        )
    for step in range(1, shards):
        pl.semaphore_signal(
            barrier,
            inc=1,
            device_id={"seq": lax.rem(me + step, shards)},
            device_id_type=MESH_ID,
        )
    pl.semaphore_wait(barrier, shards - 1 + max(groups - 1, 0))


def tile_loop(count, body):
    def step(index, carry):
        body(index)
        return carry

    lax.fori_loop(0, count, step, 0)


def add_rows(target, target_row, left, left_row, right, count):
    def tile(index):
        low = index * 32
        here = pl.ds(pl.multiple_of(target_row + low, 32), 32)
        there = pl.ds(pl.multiple_of(left_row + low, 32), 32)
        value = left[there, :].astype(jnp.float32) + right[
            pl.ds(pl.multiple_of(low, 32), 32), :
        ].astype(jnp.float32)
        target[here, :] = value.astype(target.dtype)

    tile_loop(count // 32, tile)


class PairSum:
    def __init__(self, own, got, other, out, sems):
        x, core, self.core_peer, self.x_peer = group_place()
        self.half = own.shape[0] // 2
        self.own, self.got, self.other, self.out = own, got, other, out
        self.low = pl.multiple_of(core * self.half, self.half)
        mine = pl.ds(self.low, self.half)
        theirs = pl.ds(pl.multiple_of((1 - core) * self.half, self.half), self.half)
        pair = lambda k: (sems.at[0, k], sems.at[1, k])
        self.copies = (
            grp_copy(own.at[theirs], got, *pair(0), self.core_peer),
            grp_copy(own.at[mine], other, *pair(1), self.x_peer),
            grp_copy(out.at[mine], out.at[mine], *pair(2), self.core_peer),
        )

    def begin(self):
        self.copies[0].start()

    def across(self):
        self.copies[0].wait_recv()
        add_rows(self.own, self.low, self.own, self.low, self.got, self.half)
        self.copies[1].start()

    def share(self):
        self.copies[1].wait_recv()
        add_rows(self.out, self.low, self.own, self.low, self.other, self.half)
        self.copies[2].start()

    def finish(self):
        self.copies[2].wait_recv()
        for copy in self.copies:
            copy.wait_send()


class CoreHalf:
    def __init__(self, own, got, half, sems):
        _, core, core_peer, _ = group_place()
        self.own, self.got, self.half, self.core = own, got, half, core
        self.copies = [
            grp_copy(
                own.at[:, side * 2 + 1 - core],
                got.at[side],
                sems.at[0, side],
                sems.at[1, side],
                core_peer,
            )
            for side in (0, 1)
        ]

    def begin(self):
        for copy in self.copies:
            copy.start()

    def finish(self):
        for side, copy in enumerate(self.copies):
            copy.wait_recv()

            def tile(index, side=side):
                self.half[index, side] = (
                    self.own[index, side * 2 + self.core].astype(jnp.float32)
                    + self.got[side, index].astype(jnp.float32)
                ).astype(self.half.dtype)

            tile_loop(self.own.shape[0], tile)
        for copy in self.copies:
            copy.wait_send()


class QuarterSum:
    def __init__(self, shards, half, other, part, out, sems):
        x, core, core_peer, x_peer = group_place()
        me = lax.axis_index("seq")
        units, width = half.shape[2], half.shape[3]
        self.half, self.other, self.part, self.out = half, other, part, out
        self.x, self.me, self.shards = x, me, shards
        mine = x * 2 + core
        pair = lambda k: (sems.at[0, k], sems.at[1, k])

        def rows(quarter):
            return pl.ds(pl.multiple_of(quarter * units, units), units)

        self.block = (rows(mine), pl.ds(pl.multiple_of(me * width, 128), width))
        self.second = grp_copy(half.at[:, 1 - x], other, *pair(0), x_peer)
        self.third = []
        for step in range(1, shards):
            goal = lax.rem(me + step, shards)
            self.third.append(seq_copy(part.at[goal], out.at[self.block], *pair(step), goal))
        whole = out.at[rows(mine)]
        self.fourth = grp_copy(whole, whole, *pair(shards), x_peer)
        self.fifth = []
        for side in (0, 1):
            whole = out.at[rows(side * 2 + core)]
            self.fifth.append(grp_copy(whole, whole, *pair(shards + 1 + side), core_peer))

    def begin(self):
        self.second.start()

    def spread(self):
        self.second.wait_recv()

        def tile(index):
            self.part[index] = (
                self.half[index, self.x].astype(jnp.float32)
                + self.other[index].astype(jnp.float32)
            ).astype(self.part.dtype)

        tile_loop(self.shards, tile)
        for copy in self.third:
            copy.start()
        self.out[self.block] = self.part[self.me]

    def share(self):
        for copy in self.third:
            copy.wait_recv()
        self.fourth.start()

    def share_core(self):
        self.fourth.wait_recv()
        for copy in self.fifth:
            copy.start()

    def finish(self):
        for copy in self.fifth:
            copy.wait_recv()
        for copy in (self.second, *self.third, self.fourth, *self.fifth):
            copy.wait_send()


def in_line(direction, z, hops, depth):
    return z >= hops if direction == 0 else z + hops < depth


class Gather:
    def __init__(self, full, sems, depth, extra=0):
        self.full, self.depth, self.extra = full, depth, extra
        self.sems = [sems.at[k] for k in range(6)]
        self.me, self.z, self.y, self.other = place()
        self.rows = full.shape[1]

    def origin(self, direction, hops, far):
        column = 1 - self.y if far else self.y
        return (self.z - hops if direction == 0 else self.z + hops) * 2 + column

    def block(self, direction, hops, far=False):
        origin = self.origin(direction, hops, far)
        if not self.extra:
            return self.full.at[origin]
        return self.full.at[origin, pl.ds(0, self.rows - self.extra)]

    def pair(self, direction, hops):
        low = self.origin(direction, hops, False) - self.y
        return self.full.at[pl.ds(low, 2), pl.ds(self.rows - self.extra, self.extra)]

    def z_move(self, block, kind, direction, hops, arrival):
        send, recv = self.sems[kind], self.sems[kind + 1]
        target = self.me + 2 if direction == 0 else self.me - 2
        return seq_copy(
            block,
            block,
            send.at[direction, hops],
            recv.at[direction, hops if arrival else hops + 1],
            self.other if arrival else target,
        )

    def z_copy(self, direction, hops, arrival=False):
        return self.z_move(self.block(direction, hops), 0, direction, hops, arrival)

    def pair_copy(self, direction, hops, arrival=False):
        return self.z_move(self.pair(direction, hops), 4, direction, hops, arrival)

    def y_copy(self, direction, hops, arrival=False, own=False):
        if own:
            block = self.full.at[self.origin(direction, hops, arrival)]
        else:
            block = self.block(direction, hops, arrival)
        send, recv = self.sems[2], self.sems[3]
        return seq_copy(
            block, block, send.at[direction, hops], recv.at[direction, hops], self.other
        )

    def here(self, direction, hops):
        return in_line(direction, self.z, hops, self.depth)

    def onward(self, direction):
        return self.z < self.depth - 1 if direction == 0 else self.z > 0

    def start(self):
        for direction in (0, 1):

            @pl.when(self.onward(direction))
            def _():
                self.z_copy(direction, 0).start()

        self.y_copy(0, 0, own=True).start()

    def cross(self):
        self.y_copy(0, 0, True, own=True).wait_recv()
        if self.extra:
            for direction in (0, 1):

                @pl.when(self.onward(direction))
                def _():
                    self.pair_copy(direction, 0).start()

    def hop(self, hops):
        for direction in (0, 1):

            @pl.when(self.here(direction, hops))
            def _():
                self.z_copy(direction, hops, True).wait_recv()

                @pl.when(self.onward(direction))
                def _():
                    self.z_copy(direction, hops).start()

                self.y_copy(direction, hops).start()

        if self.extra:
            for direction in (0, 1):

                @pl.when(self.here(direction, hops))
                def _():
                    self.pair_copy(direction, hops, True).wait_recv()

                    @pl.when(self.onward(direction))
                    def _():
                        self.pair_copy(direction, hops).start()

    def near(self, hops, visit):
        for direction in (0, 1):

            @pl.when(self.here(direction, hops))
            def _():
                visit(self.origin(direction, hops, False))

    def far(self, hops, visit=None):
        for direction in (0, 1):

            @pl.when(self.here(direction, hops))
            def _():
                self.y_copy(direction, hops, True).wait_recv()
                if visit is not None:
                    visit(self.origin(direction, hops, True))

    def drain(self):
        self.y_copy(0, 0, own=True).wait_send()

        def step(hops, carry):
            for direction in (0, 1):
                here = self.here(direction, hops)

                @pl.when(here & self.onward(direction))
                def _():
                    self.z_copy(direction, hops).wait_send()
                    if self.extra:
                        self.pair_copy(direction, hops).wait_send()

                @pl.when(here & (hops > 0))
                def _():
                    self.y_copy(direction, hops).wait_send()

            return carry

        lax.fori_loop(0, self.depth, step, 0)

    def finish(self):
        def step(hops, carry):
            self.far(hops)
            return carry

        lax.fori_loop(1, self.depth, step, 0)
        self.drain()

    def run(self, visit, hook=None):
        self.start()
        visit(self.me)
        self.cross()
        visit(self.other)

        def step(hops, carry):
            @pl.when(hops < self.depth)
            def _():
                self.hop(hops)
                self.near(hops, visit)

            @pl.when(hops > 1)
            def _():
                self.far(hops - 1, visit)

            if hook is not None:
                hook(hops)
            return carry

        lax.fori_loop(1, self.depth + 1, step, 0)
        self.drain()


class LineGather:
    def __init__(self, full, sems, depth):
        self.full, self.sems, self.depth = full, sems, depth
        self.me, self.z, _, self.other = place()

    def copy(self, direction, hops, arrival=False):
        block = self.full.at[self.z - hops if direction == 0 else self.z + hops]
        target = self.me + 2 if direction == 0 else self.me - 2
        return seq_copy(
            block,
            block,
            self.sems.at[0, direction, hops],
            self.sems.at[1, direction, hops if arrival else hops + 1],
            self.other if arrival else target,
        )

    def hop(self, hops):
        for direction in (0, 1):

            @pl.when(in_line(direction, self.z, hops, self.depth))
            def _():
                if hops:
                    self.copy(direction, hops, True).wait_recv()

                @pl.when(in_line(1 - direction, self.z, 1, self.depth))
                def _():
                    self.copy(direction, hops).start()

    def drain(self):
        for hops in range(self.depth):
            for direction in (0, 1):
                here = in_line(direction, self.z, hops, self.depth)

                @pl.when(here & in_line(1 - direction, self.z, 1, self.depth))
                def _():
                    self.copy(direction, hops).wait_send()


class Reshard:
    def __init__(self, shards, part, out, local_sem, sems):
        x, core, core_peer, x_peer = group_place()
        me = lax.axis_index("seq")
        mine = x * 2 + core
        pair = lambda k: (sems.at[0, k], sems.at[1, k])
        self.local = pltpu.make_async_copy(part(me, mine), out.at[me, mine], local_sem)
        self.first = []
        for step in range(1, shards):
            goal = lax.rem(me + step, shards)
            self.first.append(seq_copy(part(goal, mine), out.at[me, mine], *pair(step - 1), goal))
        self.second = grp_copy(out.at[:, mine], out.at[:, mine], *pair(shards - 1), x_peer)
        self.third = []
        for side in (0, 1):
            whole = out.at[:, side * 2 + core]
            self.third.append(grp_copy(whole, whole, *pair(shards + side), core_peer))

    def begin_near(self):
        self.local.start()
        for copy in self.first[1::2]:
            copy.start()

    def begin_far(self):
        for copy in self.first[0::2]:
            copy.start()

    def share(self):
        self.local.wait()
        for copy in self.first:
            copy.wait_recv()
        self.second.start()

    def share_core(self):
        self.second.wait_recv()
        for copy in self.third:
            copy.start()

    def finish(self):
        for copy in self.third:
            copy.wait_recv()
        for copy in (*self.first, self.second, *self.third):
            copy.wait_send()


def scatter_blocks(
    partial, to_y, from_y, to_z, from_z, acc, y_sems, z_sems, depth, between=None, hook=None, early=None
):
    me, z, y, other = place()
    low = to_y.dtype

    def y_copy(goal):
        return seq_copy(
            to_y.at[goal], from_y.at[goal], y_sems.at[0, goal], y_sems.at[1, goal], other
        )

    def slot(direction, goal, at):
        return goal if direction == 0 else jnp.where(goal == at, depth, goal)

    def z_copy(direction, goal):
        return seq_copy(
            to_z.at[goal],
            from_z.at[slot(direction, goal, z - 1)],
            z_sems.at[0, direction, goal],
            z_sems.at[1, direction, goal],
            me + 2 if direction == 0 else me - 2,
        )

    def z_arrival(direction, goal):
        return seq_copy(
            to_z.at[goal],
            from_z.at[slot(direction, goal, z)],
            z_sems.at[0, direction, goal],
            z_sems.at[1, direction, goal],
            other,
        )

    def ahead(direction, hops):
        return in_line(1 - direction, z, hops, depth)

    def goal_of(direction, hops):
        return z + hops if direction == 0 else z - hops

    def over_y(step, carry):
        hops = depth - 1 - step
        for direction in (0, 1):
            here = ahead(direction, hops)
            if direction == 1:
                here = here & (hops > 0)

            @pl.when(here)
            def _():
                goal = goal_of(direction, hops)
                to_y[goal] = partial(goal * 2 + other - z * 2).astype(low)
                y_copy(goal).start()

        if early is not None:
            early(step)
        return carry

    lax.fori_loop(0, depth, over_y, 0)
    if between is not None:
        between()

    def along_z(step, carry):
        hops = depth - 1 - step
        for direction in (0, 1):

            @pl.when(ahead(direction, hops))
            def _():
                goal = goal_of(direction, hops)
                acc[...] = partial(goal * 2 + y)
                y_copy(goal).wait_recv()
                acc[...] += from_y[goal].astype(jnp.float32)

                @pl.when(in_line(direction, z, 1, depth))
                def _():
                    z_arrival(direction, goal).wait_recv()
                    acc[...] += from_z[slot(direction, goal, z)].astype(jnp.float32)

                to_z[goal] = acc[...].astype(low)
                z_copy(direction, goal).start()

        if hook is not None:
            hook(step)
        return carry

    lax.fori_loop(0, depth - 1, along_z, 0)
    acc[...] = partial(me)
    y_copy(z).wait_recv()
    acc[...] += from_y[z].astype(jnp.float32)
    for direction in (0, 1):

        @pl.when(in_line(direction, z, 1, depth))
        def _():
            z_arrival(direction, z).wait_recv()
            acc[...] += from_z[slot(direction, z, z)].astype(jnp.float32)

    def drain(goal, carry):
        y_copy(goal).wait_send()
        for direction in (0, 1):
            sent = goal > z if direction == 0 else goal < z

            @pl.when(sent)
            def _():
                z_copy(direction, goal).wait_send()

        return carry

    lax.fori_loop(0, depth, drain, 0)


def peer_total(mine, theirs, sems, shards, meanwhile=None):
    me = lax.axis_index("seq")
    copies = [
        seq_copy(
            mine,
            theirs.at[step - 1],
            sems.at[0, step - 1],
            sems.at[1, step - 1],
            lax.rem(me + step, shards),
        )
        for step in range(1, shards)
    ]
    for copy in copies:
        copy.start()
    if meanwhile is not None:
        meanwhile()
    for copy in copies:
        copy.wait()
    total = mine[...]
    for step in range(1, shards):
        total = total + theirs[step - 1]
    return total


EDGE = 80
VMEM_BYTES = 58 * 1024 * 1024
ROOT_HALF = math.sqrt(0.5)
DENSITY = 1.0 / math.sqrt(2.0 * math.pi)


def exchange_edges(held, sems, rows, shards):
    me = lax.axis_index("seq")

    def copy(kind):
        if kind == 0:
            source, target = pl.ds(EDGE + rows - WMAX, WMAX), pl.ds(EDGE - WMAX, WMAX)
        else:
            source, target = pl.ds(EDGE, WMAX), pl.ds(EDGE + rows, WMAX)
        return seq_copy(
            held.at[source],
            held.at[target],
            sems.at[0, kind],
            sems.at[1, kind],
            me + 1 if kind == 0 else me - 1,
        )

    first, last = me == 0, me == shards - 1
    zeros = jnp.zeros((EDGE, held.shape[1]), held.dtype)

    held[pl.ds(0, EDGE - WMAX), :] = zeros[: EDGE - WMAX]
    held[pl.ds(EDGE + rows + WMAX, EDGE - WMAX), :] = zeros[: EDGE - WMAX]

    @pl.when(first)
    def _():
        held[pl.ds(EDGE - WMAX, WMAX), :] = zeros[:WMAX]

    @pl.when(last)
    def _():
        held[pl.ds(EDGE + rows, WMAX), :] = zeros[:WMAX]

    @pl.when(jnp.logical_not(last))
    def _():
        copy(0).start()

    @pl.when(jnp.logical_not(first))
    def _():
        copy(1).start()

    def finish():
        @pl.when(jnp.logical_not(last))
        def _():
            copy(0).wait_send()
            copy(1).wait_recv()

        @pl.when(jnp.logical_not(first))
        def _():
            copy(1).wait_send()
            copy(0).wait_recv()

    return finish


def row_of(vector):
    return vector[...].astype(jnp.float32).reshape(1, vector.shape[0])


def column_of(vector):
    row = row_of(vector)
    fill = -row.shape[1] % 128
    row = jnp.concatenate([row, jnp.zeros((1, fill), jnp.float32)], axis=1)
    return jnp.broadcast_to(row, (8, row.shape[1])).T[: vector.shape[0], 0:1]


def stats_of(values_in):
    average = jnp.mean(values_in, axis=-1, keepdims=True)
    centred = values_in - average
    variance = jnp.mean(centred * centred, axis=-1, keepdims=True)
    inverse = lax.rsqrt(variance + EPS_NORM)
    return centred * inverse, inverse


class Latents:
    def __init__(self, shape, total):
        self.ends = []
        low = 0
        for latent in range(NLAT - 1):
            low = low + shape[latent] * WMAX
            self.ends.append(low)
        self.total = total

    def segment(self, positions):
        out = jnp.zeros_like(positions)
        for end in self.ends:
            out = out + (positions >= end).astype(jnp.int32)
        return out

    def picks(self, start, count):
        segment = self.segment(start + lax.broadcasted_iota(jnp.int32, (count, 1), 0))
        return [(segment == latent).astype(jnp.float32) for latent in range(NLAT)]

    def valid(self, positions, down_step, side_step):
        segment = self.segment(positions)
        low, high = jnp.zeros_like(positions), jnp.full_like(positions, self.total)
        for latent, end in enumerate(self.ends):
            low = jnp.where(segment > latent, end, low)
            high = jnp.where(segment == latent, end, high)
        moved = positions + down_step * WMAX
        column = (positions & (WMAX - 1)) + side_step
        good = (moved >= low) & (moved < high) & (column >= 0) & (column < WMAX)
        return good.astype(jnp.float32)


def rows_of(picks, table):
    out = picks[0] * table[0:1]
    for latent in range(1, NLAT):
        out = out + picks[latent] * table[latent : latent + 1]
    return out


WIDE_SCALE, WIDE_SHIFT = 16, 24
SMALL_FC1, SMALL_GAMMA, SMALL_BETA, SMALL_TIME = 64, 66, 68, 70
SMALL_QUERY, SMALL_VALUE, SMALL_OUT, SMALL_MAP, SMALL_ROWS = 71, 72, 73, 74, 80


def mixer_kernel(
    shards,
    emit,
    shape,
    hidden,
    cond,
    time_weight,
    conv_weight,
    conv_bias,
    fc1_bias,
    gamma,
    beta,
    fc2_bias,
    time_bias,
    fc1,
    ctx_cols,
    cot,
    fc2,
    out_weight,
    full,
    held,
    wide,
    normed,
    inverse,
    pre,
    root_out,
    ratio_out,
    denom_out,
    response,
    ctx_full,
    d_mixed,
    cot_cols,
    fc2_rows,
    pack,
    packed,
    floats,
    conv,
    act,
    energy,
    mine,
    theirs,
    edge_sems,
    pack_sems,
    gather_sems,
    total_sems,
    ctx_sems,
    cot_sems,
    out_parts,
    cot_line,
    to_other,
    other_sems,
    local_sems,
    fc2_sems,
    out_sems,
):
    f32 = jnp.float32
    rows = hidden.shape[0]
    depth = shards // 2
    me = lax.axis_index("seq")
    meet_all(shards, lax.axis_size("grp"))
    units, width = fc2_rows.shape[2:]
    out_units, wide_cols = out_parts.shape[2:]

    def fc2_part(goal, quarter):
        here = pl.ds(pl.multiple_of(quarter * units, units), units)
        return fc2.at[here, pl.ds(pl.multiple_of(goal * width, 128), width)]

    def out_part(goal, quarter):
        here = pl.ds(pl.multiple_of(quarter * out_units, out_units), out_units)
        return out_weight.at[here, pl.ds(pl.multiple_of(goal // 2 * wide_cols, 128), wide_cols)]

    fc2_shard = Reshard(shards, fc2_part, fc2_rows, local_sems.at[0], fc2_sems)
    out_shard = Reshard(shards, out_part, out_parts, local_sems.at[1], out_sems)
    ctx_gather = Gather(ctx_full, ctx_sems, depth)
    _, z, y, other = place()
    cot_gather = LineGather(cot_line, cot_sems, depth)
    ctx_full[me] = ctx_cols[...]
    latents = Latents(shape, shards * rows)
    cols = pack.shape[1]
    fc1_bias, gamma, beta, time_bias = map(row_of, (fc1_bias, gamma, beta, time_bias))
    mod = (
        jnp.dot(
            cond[...],
            time_weight[...].astype(f32),
            precision=HIGHEST_PRECISION,
            preferred_element_type=f32,
        )
        + time_bias
    )
    pack[...] = jnp.zeros_like(pack)
    pack[0:9, :] = conv_weight[...].astype(f32)
    pack[9:10, :] = row_of(conv_bias)
    pack[10:11, :] = row_of(fc2_bias)
    pack[11 : 11 + NLAT, :] = mod[:, :cols]
    pack[11 + NLAT : 11 + 2 * NLAT, :] = mod[:, cols:]
    packed[me] = pack[...]
    pack_copies = [
        seq_copy(
            pack,
            packed.at[me],
            pack_sems.at[0, step - 1],
            pack_sems.at[1, step - 1],
            lax.rem(me + step, shards),
        )
        for step in range(1, shards)
    ]
    held[pl.ds(EDGE, rows), :] = hidden[...]
    finish = exchange_edges(held, edge_sems, rows, shards)
    for copy in pack_copies:
        copy.start()
    fc2_shard.begin_near()
    out_shard.begin_near()
    finish()
    fc2_shard.begin_far()
    out_shard.begin_far()
    ctx_gather.start()
    cot_line[z] = cot.wait()[...]
    cot_gather.hop(0)
    emit(held)
    tile_loop(
        floats.shape[0] // 32,
        lambda i: floats.__setitem__(
            (pl.ds(i * 32, 32), slice(None)), held[pl.ds(i * 32, 32), :].astype(f32)
        ),
    )
    for copy in pack_copies:
        copy.wait()
    wide[...] = jnp.zeros_like(wide)
    wide[0:16, :] = jnp.concatenate([packed[j, 0:16, :] for j in range(shards)], axis=1)
    for low, device in ((WIDE_SCALE, 0), (WIDE_SHIFT, shards // 2)):
        parts = []
        for j in range(device, device + shards // 2):
            parts.append(packed[j, 11 : 11 + NLAT, :])
            parts.append(packed[j, 11 + NLAT : 11 + 2 * NLAT, :])
        wide[low : low + NLAT, :] = jnp.concatenate(parts, axis=1)
    positions = me * rows + lax.broadcasted_iota(jnp.int32, (rows, 1), 0)
    masks = [latents.valid(positions, tap // 3 - 1, tap % 3 - 1) for tap in range(9)]

    def conv_tile(index):
        cols = pl.ds(pl.multiple_of(index * 256, 256), 256)
        total = jnp.broadcast_to(wide[9:10, cols], (rows, 256))
        for tap in range(9):
            offset = EDGE + (tap // 3 - 1) * WMAX + tap % 3 - 1
            total = total + (
                floats[offset : offset + rows, cols] * wide[tap : tap + 1, cols]
            ) * masks[tap]
        conv[:, cols] = total

    tile_loop(C // 256, conv_tile)

    def norm_tile(index):
        here = pl.ds(pl.multiple_of(index * 16, 16), 16)
        values, factor = stats_of(conv[here, :])
        normed[here, :] = values
        inverse[here, :] = factor
        full[me, here, :] = values.astype(full.dtype)

    tile_loop(rows // 16, norm_tile)
    energy[...] = jnp.zeros_like(energy)
    fc1 = fc1.wait()
    emit(wide, normed)

    def visit(block):
        pre[block] = (
            jnp.dot(full[block], fc1[...], preferred_element_type=f32) + fc1_bias
        )

        def tile(index):
            here = pl.ds(pl.multiple_of(index * 32, 32), 32)
            value = pre[block, here, :]
            value = value * (0.5 * (1.0 + lax.erf(value * ROOT_HALF)))
            act[block, here, :] = value
            square = value * value
            pick = latents.picks(block * rows + index * 32, 32)
            for latent in range(NLAT):
                energy[latent : latent + 1, :] += jnp.sum(
                    square * pick[latent], axis=0, keepdims=True
                )

        tile_loop(rows // 32, tile)

    def hook(hops):
        @pl.when(hops == 1)
        def _():
            ctx_gather.cross()
            ctx_gather.hop(1)

        @pl.when(hops == 2)
        def _():
            fc2_shard.share()
            out_shard.share()
            ctx_gather.hop(2)
            cot_gather.hop(1)

        @pl.when(hops == 3)
        def _():
            ctx_gather.hop(3)
            cot_gather.hop(2)

    Gather(full, gather_sems, depth, rows // 8).run(visit, hook)
    emit(full, pre)
    out_shard.share_core()
    fc2_shard.share_core()
    root = jnp.sqrt(energy[...] + 1.0)
    mine[...] = jnp.broadcast_to(jnp.sum(root, axis=1, keepdims=True), mine.shape)

    other_copies = [
        seq_copy(
            to_other.at[n],
            target.at[:, y],
            other_sems.at[0, n],
            other_sems.at[1, n],
            other,
        )
        for n, target in enumerate((d_mixed, cot_cols))
    ]

    def cot_part(block):
        products = jnp.dot(
            cot_line[block], out_parts[...].reshape(C, wide_cols), preferred_element_type=f32
        ).astype(d_mixed.dtype)
        pair = cot_line[block, :, pl.ds(pl.multiple_of(z * wide_cols, 128), wide_cols)]
        for side in (0, 1):
            taken = pair[:, side * cols : (side + 1) * cols]
            product = products[:, side * cols : (side + 1) * cols]

            @pl.when(y == side)
            def _():
                d_mixed[block, side] = product
                cot_cols[block, side] = taken

            @pl.when(y != side)
            def _():
                to_other[0, block] = product
                to_other[1, block] = taken

    def meanwhile():
        cot_gather.hop(3)
        out_shard.finish()
        tile_loop(depth, cot_part)
        for copy in other_copies:
            copy.start()

    denom = peer_total(mine, theirs, total_sems, shards, meanwhile) / FF + EPS_NORM
    ratio = root / denom[:, 0:1]
    root_out[...] = root
    denom_out[...] = denom
    ratio_out[...] = ratio
    scaled = ratio * gamma + 1.0

    def respond(index):
        block = index // (rows // 32)
        here = pl.ds(pl.multiple_of(lax.rem(index, rows // 32) * 32, 32), 32)
        response[block, here, :] = (
            act[block, here, :] * rows_of(latents.picks(index * 32, 32), scaled) + beta
        ).astype(response.dtype)

    tile_loop(shards * rows // 32, respond)
    emit(response)
    ctx_gather.finish()
    emit(ctx_full)
    fc2_shard.finish()
    emit(fc2_rows)
    cot_gather.drain()
    for copy in other_copies:
        copy.wait()


def mixed_in_kernel(
    shards,
    emit,
    shape,
    response,
    fc2,
    hidden,
    wide,
    w_qkv,
    q_bias,
    v_bias,
    context,
    full,
    first,
    second,
    normed,
    inverse,
    queries,
    keys,
    values,
    acc,
    to_y,
    from_y,
    to_z,
    from_z,
    y_sems,
    z_sems,
    gather_sems,
):
    f32 = jnp.float32
    rows = acc.shape[0]
    depth = shards // 2
    me = lax.axis_index("seq")
    meet_all(shards)
    latents = Latents(shape, shards * rows)
    cols = keys.shape[0]
    q_bias, v_bias = row_of(q_bias), column_of(v_bias)
    bias = wide[10:11, :]
    scale, shift = wide[WIDE_SCALE : WIDE_SCALE + 8, :], wide[WIDE_SHIFT : WIDE_SHIFT + 8, :]

    def partial(block):
        return dot_nt(response[block], fc2[...])

    scatter_blocks(partial, to_y, from_y, to_z, from_z, acc, y_sems, z_sems, depth)

    hidden = hidden.wait()

    def norm_tile(index):
        here = pl.ds(pl.multiple_of(index * 16, 16), 16)
        one = hidden[here, :].astype(f32) + acc[here, :] + bias
        pick = latents.picks(me * rows + index * 16, 16)
        two = one * (1.0 + rows_of(pick, scale)) + rows_of(pick, shift)
        first[here, :] = one
        second[here, :] = two
        value, factor = stats_of(two)
        normed[here, :] = value
        inverse[here, :] = factor
        full[me, here, :] = value.astype(full.dtype)

    tile_loop(rows // 16, norm_tile)
    emit(first, second, normed)
    w_qkv, context = w_qkv.wait(), context.wait()

    side = jnp.dot(w_qkv[cols:, :], context[...], preferred_element_type=f32)
    keys[:, shards * rows :] = side[:cols].astype(keys.dtype)
    values[:, shards * rows :] = (side[cols:] + v_bias).astype(values.dtype)

    def visit(block):
        value = full[block]
        query = dot_nt(value, w_qkv[:cols, :]) + q_bias
        queries[block] = query.astype(queries.dtype)
        here = pl.ds(pl.multiple_of(block * rows, 128), rows)
        side = dot_nt(w_qkv[cols:, :], value)
        keys[:, here] = side[:cols].astype(keys.dtype)
        values[:, here] = (side[cols:] + v_bias).astype(values.dtype)

    Gather(full, gather_sems, depth, rows // 8).run(visit)


def attend_kernel(
    shards,
    emit,
    shape,
    queries,
    keys,
    values,
    d_mixed_all,
    cot,
    d_qkv,
    mixed,
    cot_cols,
    dk_sum,
    dv_sum,
    probs_at,
    sems,
):
    f32, bf16 = jnp.float32, jnp.bfloat16
    cols = keys.shape[0]
    heads = cols // HEAD_DIM
    tiles, tile_rows = mixed.shape[0], mixed.shape[3]
    span = tile_rows // queries.shape[1]
    depth = shards // 2
    me = lax.axis_index("seq")
    meet_all(shards)
    latents = Latents(shape, tiles * tile_rows)
    place_at = lax.broadcasted_iota(jnp.int32, (1, keys.shape[1]), 1)
    token = place_at - tiles * tile_rows
    of_token = jnp.full_like(token, -1)
    for latent in range(NLAT):
        inside = (token >= latent * NCTX) & (token < (latent + 1) * NCTX)
        of_token = jnp.where(inside, latent, of_token)
    k_segment = jnp.where(token < 0, latents.segment(place_at), of_token)
    dk_sum[...] = jnp.zeros_like(dk_sum)
    dv_sum[...] = jnp.zeros_like(dv_sum)

    def gather_of(tile):
        return Gather(mixed.at[tile], sems.at[tile], depth)

    def step(tile, carry):
        blocks = pl.ds(tile * span, span)
        here = pl.ds(pl.multiple_of(tile * tile_rows, 128), tile_rows)
        query = queries[blocks].reshape(tile_rows, cols) * SCORE_SCALE
        cot_cols[:, here] = cot[blocks].reshape(tile_rows, cols).T
        d_mixed = d_mixed_all[blocks].reshape(tile_rows, cols)
        q_segment = latents.segment(
            tile * tile_rows + lax.broadcasted_iota(jnp.int32, (tile_rows, 1), 0)
        )
        bias = jnp.where(q_segment == k_segment, 0.0, MASKED)
        mixed_parts, d_query_parts = [], []
        for head in range(heads):
            own = slice(head * HEAD_DIM, (head + 1) * HEAD_DIM)
            scores = jnp.dot(query[:, own], keys[own, :], preferred_element_type=f32) + bias
            expo = jnp.exp(scores - jnp.max(scores, axis=-1, keepdims=True))
            probs_at[head] = expo * (1.0 / jnp.sum(expo, axis=-1, keepdims=True))
            mixed_parts.append(dot_nt(probs_at[head].astype(bf16), values[own, :]))
        mixed[tile, me] = jnp.concatenate(mixed_parts, axis=1).T.astype(bf16)
        gather_of(tile).start()
        for hops in range(1, depth):

            @pl.when(tile >= hops)
            def _():
                if hops == 1:
                    gather_of(tile - 1).cross()
                gather_of(tile - hops).hop(hops)

        for head in range(heads):
            own = slice(head * HEAD_DIM, (head + 1) * HEAD_DIM)
            dm_head = d_mixed[:, own]
            delta = jnp.sum(dm_head.astype(f32) * mixed_parts[head], axis=-1, keepdims=True)
            d_probs = jnp.dot(dm_head, values[own, :], preferred_element_type=f32)
            d_scores = (probs_at[head] * (d_probs - delta)).astype(bf16)
            d_query_parts.append(dot_nt(d_scores, keys[own, :]) * SCORE_SCALE)
            dk_sum[own, :] += dot_tn(query[:, own], d_scores)
            dv_sum[own, :] += dot_tn(dm_head, probs_at[head].astype(bf16))
        d_qkv[:cols, here] = jnp.concatenate(d_query_parts, axis=1).T.astype(bf16)
        return carry

    lax.fori_loop(0, tiles, step, 0)
    for late in range(1, depth):
        for hops in range(late, depth):
            if hops == 1:
                gather_of(tiles - 1).cross()
            gather_of(tiles - 1 + late - hops).hop(hops)
    d_qkv[:cols, tiles * tile_rows :] = jnp.zeros(
        (cols, d_qkv.shape[1] - tiles * tile_rows), bf16
    )
    d_qkv[cols : 2 * cols, :] = dk_sum[...].astype(bf16)
    d_qkv[2 * cols :, :] = dv_sum[...].astype(bf16)

    def close(tile, carry):
        gather_of(tile).finish()
        return carry

    lax.fori_loop(0, tiles, close, 0)


def norm_back(gradient, normed, inverse):
    mean_grad = jnp.mean(gradient, axis=-1, keepdims=True)
    mean_mixed = jnp.mean(gradient * normed, axis=-1, keepdims=True)
    return inverse * (gradient - mean_grad - normed * mean_mixed)


def attn_back_kernel(
    shards,
    emit,
    shape,
    cond,
    d_qkv,
    w_qkv,
    attn,
    context,
    mixed,
    cot_cols,
    out_weight,
    gamma,
    out_bias,
    cot,
    normed,
    inverse,
    first,
    wide,
    fc2,
    pre,
    root,
    ratio,
    denom,
    response,
    context_in,
    d_first,
    d_pre,
    small_out,
    weight_grads,
    map_grad,
    act_out,
    fc2_half,
    branch_sum,
    full,
    d_mod,
    small,
    acc,
    d_resp,
    act,
    sums,
    mine,
    theirs,
    to_y,
    from_y,
    to_z,
    from_z,
    y_sems,
    z_sems,
    gather_sems,
    total_sems,
    g_own,
    g_got,
    g_other,
    g_sems,
    mod_in,
    mod_sems,
    fc2_own,
    fc2_got,
    fc2_sems,
    ctx_out,
    ctx_in,
    ctx_sems,
):
    f32 = jnp.float32
    rows = acc.shape[0]
    depth = shards // 2
    me = lax.axis_index("seq")
    meet_all(shards, lax.axis_size("grp"))
    cols = ctx_out.shape[1]
    total = shards * rows
    latents = Latents(shape, total)
    gamma, out_bias = row_of(gamma), column_of(out_bias)
    width_one = gamma.shape[1]
    scale = wide[WIDE_SCALE : WIDE_SCALE + 8, :]
    later = (attn, context, mixed, cot_cols, out_weight)
    weight_sum = PairSum(g_own, g_got, g_other, weight_grads, g_sems)
    peers = [lax.rem(me + step, shards) for step in range(1, shards)]
    ctx_copies = [
        seq_copy(ctx_out.at[peer], ctx_in.at[me], ctx_sems.at[0, n], ctx_sems.at[1, n], peer)
        for n, peer in enumerate(peers)
    ]
    fc2_sum = CoreHalf(fc2_own, fc2_got, fc2_half, fc2_sems)

    def partial(block):
        here = pl.ds(pl.multiple_of(block * rows, 128), rows)
        return dot_tn(d_qkv[:, here], w_qkv[...])

    def between():
        low_type = ctx_out.dtype
        attn, context, mixed, cot_cols, out_weight = (item.wait() for item in later)
        for device in range(shards):
            ctx_out[device] = dot_tn(
                w_qkv[:, device * cols : (device + 1) * cols], d_qkv[:, total:]
            ).astype(low_type)
        g_own[: 3 * cols, :] = (
            jnp.dot(d_qkv[:, :total], attn[...].reshape(total, C), preferred_element_type=f32)
            + dot_nt(d_qkv[:, total:], context[...])
        ).astype(low_type)
        grad = None
        for tile in range(mixed.shape[0]):
            here = slice(tile * mixed.shape[3], (tile + 1) * mixed.shape[3])
            block = mixed[tile].reshape(C, mixed.shape[3])
            act_out[:, here] = (
                jnp.dot(out_weight[...], block, preferred_element_type=f32) + out_bias
            ).astype(low_type)
            part = dot_nt(cot_cols[:, here], block)
            grad = part if grad is None else grad + part
        g_own[3 * cols :, :] = grad.astype(low_type)
        weight_sum.begin()

    def scatter_hook(step):
        @pl.when(step == 1)
        def _():
            weight_sum.across()

    scatter_blocks(
        partial, to_y, from_y, to_z, from_z, acc, y_sems, z_sems, depth, between, scatter_hook
    )
    d_mod[...] = jnp.zeros_like(d_mod)
    branch_sum[...] = jnp.zeros_like(branch_sum)
    cot, normed, first = cot.wait(), normed.wait(), first.wait()

    def norm_tile(index):
        here = pl.ds(pl.multiple_of(index * 16, 16), 16)
        d_second = cot[here, :].astype(f32) + norm_back(
            acc[here, :], normed[here, :], inverse[here, :]
        )
        pick = latents.picks(me * rows + index * 16, 16)
        value = d_second * (1.0 + rows_of(pick, scale))
        d_first[here, :] = value
        value = value.astype(full.dtype)
        full[me, here, :] = value
        branch_sum[0:1, :] += jnp.sum(value.astype(f32), axis=0, keepdims=True)
        scaled = d_second * first[here, :]
        for latent in range(NLAT):
            chosen = pick[latent]
            d_mod[2 * latent : 2 * latent + 1, :] += jnp.sum(scaled * chosen, axis=0, keepdims=True)
            d_mod[2 * latent + 1 : 2 * latent + 2, :] += jnp.sum(
                d_second * chosen, axis=0, keepdims=True
            )

    tile_loop(rows // 16, norm_tile)
    sums[...] = jnp.zeros_like(sums)
    emit(d_first)
    fc2, pre = fc2.wait(), pre.wait()
    wide_mod = 2 * cols
    half = shards // 2

    def mod_part(device):
        low = pl.multiple_of(lax.rem(device, half) * wide_mod, 128)
        return d_mod.at[:, pl.ds(low, wide_mod)]

    mod_in[me] = mod_part(me)[...]
    mod_copies = [
        seq_copy(mod_part(peer), mod_in.at[me], mod_sems.at[0, k], mod_sems.at[1, k], peer)
        for k, peer in enumerate(peers)
    ]
    for copy in mod_copies:
        copy.start()

    def gather_hook(hops):
        @pl.when(hops == 2)
        def _():
            weight_sum.share()

    def visit(block):
        d_resp[block] = jnp.dot(full[block], fc2[...], preferred_element_type=f32)

        def tile(index):
            here = pl.ds(pl.multiple_of(index * 32, 32), 32)
            value = pre[block, here, :]
            phi = 0.5 * (1.0 + lax.erf(value * ROOT_HALF))
            pre[block, here, :] = phi + value * (DENSITY * jnp.exp(-0.5 * value * value))
            value = value * phi
            act[block, here, :] = value.astype(act.dtype)
            pull = d_resp[block, here, :]
            sums[NLAT : NLAT + 1, :] += jnp.sum(pull, axis=0, keepdims=True)
            pull = pull * value
            pick = latents.picks(block * rows + index * 32, 32)
            for latent in range(NLAT):
                sums[latent : latent + 1, :] += jnp.sum(
                    pull * pick[latent], axis=0, keepdims=True
                )

        tile_loop(rows // 32, tile)

    Gather(full, gather_sems, depth, rows // 8).run(visit, gather_hook)
    small[...] = jnp.zeros_like(small)
    wide_row = 2 * cols

    def keep(row, value):
        for part in range(value.shape[1] // wide_row):
            small[row + part : row + part + 1, :] = value[
                :, part * wide_row : (part + 1) * wide_row
            ]

    keep(SMALL_BETA, sums[NLAT : NLAT + 1, :])
    pulls = sums[...]
    keep(SMALL_GAMMA, jnp.sum(pulls[:NLAT] * ratio[:NLAT, :], axis=0, keepdims=True))
    d_ratio = pulls * gamma
    mine[...] = jnp.broadcast_to(jnp.sum(d_ratio * root[...], axis=1, keepdims=True), mine.shape)

    def meanwhile():
        for copy in ctx_copies:
            copy.start()
        ctx_in[me] = ctx_out[me]
        right = response.wait()[...].reshape(total, width_one)
        units = fc2_own.shape[2]
        for goal in range(0, shards, 4):
            here = slice(goal * 4 * units, (goal + 4) * 4 * units)
            part = dot_tn(full[:, :, here].reshape(total, 16 * units), right)
            fc2_own[goal : goal + 4] = part.reshape(4, 4, units, width_one).astype(fc2_own.dtype)
        fc2_sum.begin()

    pulled = peer_total(mine, theirs, total_sems, shards, meanwhile)[:, 0:1]
    below = denom[:, 0:1]
    d_root = d_ratio / below - pulled / (FF * below * below)
    back = d_root / root[...]
    scaled = ratio[...] * gamma + 1.0
    sums[0:1, :] = jnp.zeros((1, width_one), f32)

    def respond(index):
        block = index // (rows // 32)
        here = pl.ds(pl.multiple_of(lax.rem(index, rows // 32) * 32, 32), 32)
        pick = latents.picks(index * 32, 32)
        d_act = d_resp[block, here, :] * rows_of(pick, scaled) + act[block, here, :].astype(f32) * rows_of(
            pick, back
        )
        value = (d_act * pre[block, here, :]).astype(d_pre.dtype)
        d_pre[block, here, :] = value
        sums[0:1, :] += jnp.sum(value.astype(f32), axis=0, keepdims=True)

    tile_loop(shards * rows // 32, respond)
    emit(d_pre)
    for copy in mod_copies:
        copy.wait()
    mod_sum = mod_in[0]
    for device in range(1, shards):
        mod_sum = mod_sum + mod_in[device]
    keep(SMALL_FC1, sums[0:1, :])
    fc2_sum.finish()
    emit(fc2_half)
    chosen = [
        jnp.where(me < half, mod_sum[2 * n : 2 * n + 1], mod_sum[2 * n + 1 : 2 * n + 2])
        for n in range(NLAT)
    ]
    chosen = jnp.concatenate(chosen, axis=0)
    small[0:SMALL_FC1, :] = lax.dot_general(
        cond[...],
        chosen,
        (((0,), (0,)), ((), ())),
        precision=HIGHEST_PRECISION,
        preferred_element_type=f32,
    )
    keep(SMALL_TIME, jnp.sum(chosen, axis=0, keepdims=True))
    ones = lambda values: jnp.ones((8, values.shape[1]), values.dtype)
    for row, value in (
        (SMALL_QUERY, d_qkv[:cols, :]),
        (SMALL_VALUE, d_qkv[2 * cols :, :]),
        (SMALL_OUT, later[3].buffer[...]),
    ):
        small[row : row + 1, :cols] = dot_nt(ones(value), value)[0:1]
    for copy in ctx_copies:
        copy.wait()
    context_sum = ctx_in[0].astype(f32)
    for device in range(1, shards):
        context_sum = context_sum + ctx_in[device].astype(f32)
    at = lax.broadcasted_iota(jnp.int32, (1, context_sum.shape[1]), 1)
    context_sum = jnp.where(at < NLAT * NCTX, context_sum, 0.0)
    map_grad[...] = jnp.dot(
        context_sum.astype(map_grad.dtype), context_in.wait()[...], preferred_element_type=f32
    ).astype(map_grad.dtype)
    small[SMALL_MAP : SMALL_MAP + 1, :cols] = lax.dot_general(
        ones(context_sum),
        context_sum,
        (((1,), (1,)), ((), ())),
        precision=HIGHEST_PRECISION,
        preferred_element_type=f32,
    )[0:1]
    small_out[...] = small[...].astype(small_out.dtype)
    weight_sum.finish()


def conv_back_kernel(
    shards,
    emit,
    shape,
    d_pre,
    fc1,
    normed,
    inverse,
    d_first,
    hidden,
    wide,
    normed_full,
    branch,
    map_grad,
    act_out,
    second,
    fc2_half,
    small,
    input_grad,
    fc1_sum,
    fc2_sum,
    map_sum,
    small_sum,
    conv_sum,
    activations,
    held,
    floats,
    acc,
    to_y,
    from_y,
    to_z,
    from_z,
    y_sems,
    z_sems,
    edge_sems,
    d_conv_params,
    fc1_own,
    fc1_got,
    fc1_other,
    fc2_other,
    fc2_part,
    map_own,
    map_got,
    map_other,
    pair_sems,
    fc2_sems,
    small_in,
    small_sems,
    conv_out,
    conv_in,
    conv_part,
    conv_group,
    conv_sems,
    act_in,
    act_sems,
):
    f32 = jnp.float32
    rows = acc.shape[0]
    depth = shards // 2
    groups = lax.axis_size("grp")
    me = lax.axis_index("seq")
    meet_all(shards, groups)
    cols = conv_part.shape[1]
    width = d_pre.shape[2]
    total = shards * rows
    latents = Latents(shape, total)
    positions = me * rows + lax.broadcasted_iota(jnp.int32, (rows, 1), 0)
    fc1_pair = PairSum(fc1_own, fc1_got, fc1_other, fc1_sum, pair_sems.at[0])
    map_pair = PairSum(map_own, map_got, map_other, map_sum, pair_sems.at[1])
    fc2_quarter = QuarterSum(shards, fc2_half, fc2_other, fc2_part, fc2_sum, fc2_sems)
    group = lax.axis_index("grp")
    small_copies = [
        grp_copy(
            small,
            small_in.at[step - 1],
            small_sems.at[0, step - 1],
            small_sems.at[1, step - 1],
            lax.rem(group + step, groups),
        )
        for step in range(1, groups)
    ]

    def partial(block):
        return dot_nt(d_pre[block], fc1[...])

    peers = [lax.rem(me + step, shards) for step in range(1, shards)]
    act_copies = []
    for n, peer in enumerate(peers):
        there = pl.ds(pl.multiple_of(peer * rows, 128), rows)
        act_copies.append(
            seq_copy(act_out.at[:, there], act_in.at[me], act_sems.at[0, n], act_sems.at[1, n], peer)
        )

    def fc1_grad():
        full = normed_full.wait()

        def tile(index):
            here = pl.ds(pl.multiple_of(index * 256, 256), 256)
            fc1_own[here, :] = dot_tn(
                full[:, :, here].reshape(total, 256), d_pre[...].reshape(total, width)
            ).astype(fc1_own.dtype)

        tile_loop(C // 256, tile)
        fc1_pair.begin()

    fc2_quarter.begin()
    map_own[...] = map_grad[...]
    map_pair.begin()

    def early(step):
        @pl.when(step == 1)
        def _():
            for copy in act_copies:
                copy.start()
            fc1_grad()

    def scatter_hook(step):
        @pl.when(step == 1)
        def _():
            fc2_quarter.spread()
            fc1_pair.across()
            map_pair.across()

    scatter_blocks(
        partial,
        to_y,
        from_y,
        to_z,
        from_z,
        acc,
        y_sems,
        z_sems,
        depth,
        None,
        scatter_hook,
        early,
    )
    normed, d_first, hidden = normed.wait(), d_first.wait(), hidden.wait()

    def norm_tile(index):
        start = pl.multiple_of(index * 16, 16)
        here = pl.ds(start, 16)
        held[pl.ds(EDGE + start, 16), :] = norm_back(
            acc[here, :], normed[here, :], inverse[here, :]
        ).astype(held.dtype)

    tile_loop(rows // 16, norm_tile)
    finish = exchange_edges(held, edge_sems, rows, shards)
    for copy in small_copies:
        copy.start()
    fc2_quarter.share()
    tile_loop(
        floats.shape[0] // 32,
        lambda i: floats.__setitem__(
            (pl.ds(i * 32, 32), slice(None)), hidden[pl.ds(i * 32, 32), :].astype(f32)
        ),
    )
    d_conv_params[...] = jnp.zeros_like(d_conv_params)
    masks = [latents.valid(positions, tap // 3 - 1, tap % 3 - 1) for tap in range(9)]

    def grad_tile(index):
        cols = pl.ds(pl.multiple_of(index * 256, 256), 256)
        d_conv = held[pl.ds(EDGE, rows), cols].astype(f32)
        d_conv_params[9:10, cols] = jnp.sum(d_conv, axis=0, keepdims=True)
        d_conv_params[10:11, cols] = branch[0:1, cols]
        for tap in range(9):
            offset = EDGE + (tap // 3 - 1) * WMAX + tap % 3 - 1
            d_conv_params[tap : tap + 1, cols] = jnp.sum(
                d_conv * floats[offset : offset + rows, cols] * masks[tap],
                axis=0,
                keepdims=True,
            )

    tile_loop(C // 256, grad_tile)
    for goal in range(shards):
        conv_out[goal] = d_conv_params[:, goal * cols : (goal + 1) * cols]
    conv_in[me] = conv_out[me]
    conv_copies = []
    for step in range(1, shards):
        goal = lax.rem(me + step, shards)
        conv_copies.append(
            seq_copy(
                conv_out.at[goal],
                conv_in.at[me],
                conv_sems.at[0, step - 1],
                conv_sems.at[1, step - 1],
                goal,
            )
        )
        conv_copies[-1].start()
    finish()
    act_in[me] = act_out[:, pl.ds(pl.multiple_of(me * rows, 128), rows)]
    tile_loop(
        floats.shape[0] // 32,
        lambda i: floats.__setitem__(
            (pl.ds(i * 32, 32), slice(None)), held[pl.ds(i * 32, 32), :].astype(f32)
        ),
    )

    back_masks = []
    for tap in range(9):
        down_step, side_step = tap // 3 - 1, tap % 3 - 1
        back_masks.append(
            latents.valid(positions - down_step * WMAX - side_step, down_step, side_step)
        )

    def input_tile(index):
        cols = pl.ds(pl.multiple_of(index * 256, 256), 256)
        total = d_first[:, cols]
        for tap in range(9):
            offset = EDGE - (tap // 3 - 1) * WMAX - tap % 3 + 1
            total = total + (
                floats[offset : offset + rows, cols] * wide[tap : tap + 1, cols]
            ) * back_masks[tap]
        input_grad[:, cols] = total

    for copy in conv_copies:
        copy.wait()
    conv_total = conv_in[0]
    for device in range(1, shards):
        conv_total = conv_total + conv_in[device]
    tile_loop(C // 256, input_tile)
    fc1_pair.share()
    conv_part[...] = conv_total
    group_copies = []
    for step in range(1, groups):
        k = shards - 2 + step
        group_copies.append(
            grp_copy(
                conv_part,
                conv_group.at[step - 1],
                conv_sems.at[0, k],
                conv_sems.at[1, k],
                lax.rem(group + step, groups),
            )
        )
        group_copies[-1].start()
    fc2_quarter.share_core()
    for copy in act_copies:
        copy.wait()
    activations[...] = (second.wait()[...] + act_in[...].reshape(C, rows).astype(f32).T).astype(
        activations.dtype
    )
    map_pair.share()
    for copy in (*small_copies, *group_copies):
        copy.wait()
    small_total = small[...].astype(f32)
    for step in range(groups - 1):
        small_total = small_total + small_in[step].astype(f32)
    small_sum[...] = small_total
    conv_sum[...] = conv_part[...] + conv_group[0] + conv_group[1] + conv_group[2]
    fc2_quarter.finish()
    emit(fc2_sum)
    map_pair.finish()
    fc1_pair.finish()


class Late:
    def __init__(self, buffer, copy):
        self.buffer, self.copy = buffer, copy

    def wait(self):
        self.copy.wait()
        return self.buffer


def staged_body(body, n_in, n_out, late, staged):
    def run(*refs):
        ins, outs = list(refs[:n_in]), list(refs[n_in : n_in + n_out])
        rest = refs[n_in + n_out :]
        count = len(late) + len(staged)
        if not count:
            body(lambda *buffers: None, *refs)
            return
        kept, buffers, sems = rest[: -count - 1], rest[-count - 1 : -1], rest[-1]
        for n, k in enumerate(late):
            copy = pltpu.make_async_copy(ins[k], buffers[n], sems.at[n])
            copy.start()
            ins[k] = Late(buffers[n], copy)
        waiting = []
        for n, k in enumerate(staged, len(late)):
            waiting.append([buffers[n], pltpu.make_async_copy(buffers[n], outs[k], sems.at[n]), 0])
            outs[k] = buffers[n]

        def emit(*which):
            for entry in waiting:
                if not entry[2] and any(entry[0] is ref for ref in which):
                    entry[1].start()
                    entry[2] = 1

        body(emit, *ins, *outs, *kept)
        emit(*(entry[0] for entry in waiting))
        for entry in waiting:
            entry[1].wait()

    return run


def kernel_call(
    body, name, number, outs, scratch, operands, flops=0, far=(), scalars=(), late=(), staged=()
):
    vmem, anywhere, smem = (
        pl.BlockSpec(memory_space=space) for space in (pltpu.VMEM, pl.ANY, pltpu.SMEM)
    )
    in_specs = [
        anywhere if k in far or k in late else smem if k in scalars else vmem
        for k in range(len(operands))
    ]
    shapes = [jax.ShapeDtypeStruct(shape, dtype) for shape, dtype in outs]
    moved = sum(math.prod(s.shape) * s.dtype.itemsize for s in shapes) + sum(
        x.size * x.dtype.itemsize for x in operands
    )
    extra = [pltpu.VMEM(operands[k].shape, operands[k].dtype) for k in late]
    extra += [pltpu.VMEM(shapes[k].shape, shapes[k].dtype) for k in staged]
    if extra:
        extra.append(pltpu.SemaphoreType.DMA((len(extra),)))
    return pl.pallas_call(
        staged_body(body, len(operands), len(outs), late, staged),
        out_shape=shapes,
        in_specs=in_specs,
        out_specs=[anywhere if k in staged else vmem for k in range(len(shapes))],
        scratch_shapes=[*scratch, *extra],
        name=name,
        cost_estimate=pl.CostEstimate(flops=flops, bytes_accessed=moved, transcendentals=0),
        compiler_params=pltpu.CompilerParams(
            collective_id=number, has_side_effects=True, vmem_limit_bytes=VMEM_BYTES
        ),
    )(*operands)


def scatter_scratch(rows, depth):
    bf16 = jnp.bfloat16
    return [
        pltpu.VMEM((depth, rows, C), bf16),
        pltpu.VMEM((depth, rows, C), bf16),
        pltpu.VMEM((depth, rows, C), bf16),
        pltpu.VMEM((depth + 1, rows, C), bf16),
        pltpu.SemaphoreType.DMA((2, depth)),
        pltpu.SemaphoreType.DMA((2, 2, depth)),
    ]


def gather_scratch(depth):
    return pltpu.SemaphoreType.DMA((6, 2, depth + 1))


def total_scratch(shards):
    return [
        pltpu.VMEM((8, 128), jnp.float32),
        pltpu.VMEM((shards - 1, 8, 128), jnp.float32),
    ], pltpu.SemaphoreType.DMA((2, shards - 1))


def on_device_heads(
    hidden,
    latent_shape,
    cond_r,
    clip,
    cotangent,
    conv_weight,
    conv_bias,
    fc1_weight,
    fc1_bias,
    grn_gamma,
    grn_beta,
    fc2_weight,
    fc2_bias,
    time_weight,
    time_bias,
    map_weight,
    map_bias,
    query_weight,
    query_bias,
    key_weight,
    value_weight,
    value_bias,
    out_weight,
    out_bias,
):
    f32, bf16 = jnp.float32, jnp.bfloat16
    shards = lax.axis_size("seq")
    rows = hidden.shape[0]
    total = rows * shards
    cols = C // shards
    depth = shards // 2
    hidden_cols = FF // shards
    shape = latent_shape[0, :, 0]
    w_qkv = jnp.concatenate([query_weight.T, key_weight.T, value_weight.T], axis=0)
    ctx_rows = 256
    context_in = jnp.pad(
        clip.reshape(NLAT * NCTX, CLIP), ((0, ctx_rows - NLAT * NCTX), (0, 0))
    )
    context_in = jax.nn.silu(context_in.astype(f32)).astype(bf16)
    ctx_cols = (against(map_weight.T, context_in) + map_bias.astype(f32)[:, None]).astype(bf16)
    units = cols // 4
    vmem = pltpu.VMEM
    total_vmem, total_sems = total_scratch(shards)
    (
        normed_full,
        held,
        wide,
        normed_one,
        inverse_one,
        pre_act,
        root,
        ratio,
        denom,
        response,
        context,
        d_mixed,
        cot_blocks,
        shrink_parts,
    ) = kernel_call(
        functools.partial(mixer_kernel, shards),
        "mixer",
        1,
        [
            ((shards, rows, C), bf16),
            ((rows + 2 * EDGE, C), bf16),
            ((32, C), f32),
            ((rows, C), f32),
            ((rows, 1), f32),
            ((shards, rows, hidden_cols), f32),
            ((8, hidden_cols), f32),
            ((8, hidden_cols), f32),
            ((8, 128), f32),
            ((shards, rows, hidden_cols), bf16),
            ((shards, cols, ctx_rows), bf16),
            ((depth, 2, rows, cols), bf16),
            ((depth, 2, rows, cols), bf16),
            ((shards, 4, units, hidden_cols), bf16),
        ],
        [
            vmem((24, cols), f32),
            vmem((shards, 24, cols), f32),
            vmem((rows + 2 * EDGE, C), f32),
            vmem((rows, C), f32),
            vmem((shards, rows, hidden_cols), f32),
            vmem((8, hidden_cols), f32),
            *total_vmem,
            pltpu.SemaphoreType.DMA((2, 2)),
            pltpu.SemaphoreType.DMA((2, shards - 1)),
            gather_scratch(depth),
            total_sems,
            gather_scratch(depth),
            pltpu.SemaphoreType.DMA((2, 2, depth + 1)),
            vmem((shards, 4, units, 2 * cols), bf16),
            vmem((depth, rows, C), bf16),
            vmem((2, depth, rows, cols), bf16),
            pltpu.SemaphoreType.DMA((2, 2)),
            pltpu.SemaphoreType.DMA((2,)),
            pltpu.SemaphoreType.DMA((2, shards + 2)),
            pltpu.SemaphoreType.DMA((2, shards + 2)),
        ],
        (
            shape,
            hidden,
            cond_r,
            time_weight,
            conv_weight,
            conv_bias,
            fc1_bias,
            grn_gamma,
            grn_beta,
            fc2_bias,
            time_bias,
            fc1_weight,
            ctx_cols,
            cotangent,
            fc2_weight.T,
            out_weight.T,
        ),
        flops=2 * total * C * hidden_cols,
        far=(14, 15),
        scalars=(0,),
        late=(11, 13),
        staged=(0, 1, 2, 3, 5, 9, 10, 13),
    )
    context = context.reshape(C, ctx_rows)
    shrink_rows = shrink_parts.reshape(C, hidden_cols)
    keys_all = total + ctx_rows
    (
        attn_blocks,
        first_sum,
        second_sum,
        normed_two,
        inverse_two,
        queries,
        keys,
        values,
    ) = kernel_call(
        functools.partial(mixed_in_kernel, shards),
        "mixed_in",
        2,
        [
            ((shards, rows, C), bf16),
            ((rows, C), f32),
            ((rows, C), f32),
            ((rows, C), f32),
            ((rows, 1), f32),
            ((shards, rows, cols), bf16),
            ((cols, keys_all), bf16),
            ((cols, keys_all), bf16),
        ],
        [pltpu.VMEM((rows, C), f32), *scatter_scratch(rows, depth), gather_scratch(depth)],
        (
            shape,
            response,
            shrink_rows,
            hidden,
            wide,
            w_qkv,
            query_bias,
            value_bias,
            context,
        ),
        flops=2 * total * C * (hidden_cols + 3 * cols),
        scalars=(0,),
        late=(3, 5, 8),
        staged=(0, 1, 2, 3, 5, 6, 7),
    )

    tiles, tile_rows = 4, total // 4
    d_qkv, mixed_full, cot_cols = kernel_call(
        functools.partial(attend_kernel, shards),
        "attend",
        5,
        [
            ((3 * cols, keys_all), bf16),
            ((tiles, shards, cols, tile_rows), bf16),
            ((cols, total), bf16),
        ],
        [
            vmem((cols, keys_all), f32),
            vmem((cols, keys_all), f32),
            vmem((cols // HEAD_DIM, tile_rows, keys_all), f32),
            pltpu.SemaphoreType.DMA((tiles, 6, 2, depth + 1)),
        ],
        (
            shape,
            queries,
            keys,
            values,
            d_mixed.reshape(shards, rows, cols),
            cot_blocks.reshape(shards, rows, cols),
        ),
        flops=12 * total * keys_all * 3 * 256,
        scalars=(0,),
    )
    (
        d_first,
        d_pre,
        small,
        weight_sums,
        grad_map_w,
        act_cols,
        fc2_half,
        branch_sum,
    ) = kernel_call(
        functools.partial(attn_back_kernel, shards),
        "attn_back",
        3,
        [
            ((rows, C), f32),
            ((shards, rows, hidden_cols), bf16),
            ((SMALL_ROWS, 2 * cols), bf16),
            ((4 * cols, C), bf16),
            ((cols, CLIP), bf16),
            ((cols, total), bf16),
            ((shards, 2, units, hidden_cols), bf16),
            ((8, C), f32),
        ],
        [
            vmem((shards, rows, C), bf16),
            vmem((8, C), f32),
            vmem((SMALL_ROWS, 2 * cols), f32),
            pltpu.VMEM((rows, C), f32),
            pltpu.VMEM((shards, rows, hidden_cols), f32),
            pltpu.VMEM((shards, rows, hidden_cols), bf16),
            pltpu.VMEM((8, hidden_cols), f32),
            *total_vmem,
            *scatter_scratch(rows, depth),
            gather_scratch(depth),
            total_sems,
            vmem((4 * cols, C), bf16),
            vmem((2 * cols, C), bf16),
            vmem((2 * cols, C), bf16),
            pltpu.SemaphoreType.DMA((2, 3)),
            vmem((shards, 8, 2 * cols), f32),
            pltpu.SemaphoreType.DMA((2, shards - 1)),
            vmem((shards, 4, units, hidden_cols), bf16),
            vmem((2, shards, units, hidden_cols), bf16),
            pltpu.SemaphoreType.DMA((2, 2)),
            vmem((shards, cols, ctx_rows), bf16),
            vmem((shards, cols, ctx_rows), bf16),
            pltpu.SemaphoreType.DMA((2, shards - 1)),
        ],
        (
            shape,
            cond_r,
            d_qkv,
            w_qkv,
            attn_blocks,
            context,
            mixed_full,
            cot_cols,
            out_weight.T,
            grn_gamma,
            out_bias,
            cotangent,
            normed_two,
            inverse_two,
            first_sum,
            wide,
            shrink_rows,
            pre_act,
            root,
            ratio,
            denom,
            response,
            context_in,
        ),
        flops=2 * total * C * (hidden_cols + 6 * cols),
        scalars=(0,),
        late=(4, 5, 6, 7, 8, 11, 12, 14, 16, 17, 21, 22),
        staged=(0, 1, 3, 5, 6),
    )
    groups = lax.axis_size("grp")
    input_grad, fc1_sum, fc2_sum, map_sum, small, conv_small, activations = kernel_call(
        functools.partial(conv_back_kernel, shards),
        "conv_back",
        4,
        [
            ((rows, C), f32),
            ((C, hidden_cols), bf16),
            ((cols, FF), bf16),
            ((cols, CLIP), bf16),
            ((SMALL_ROWS, 2 * cols), f32),
            ((16, cols), f32),
            ((rows, C), bf16),
        ],
        [
            vmem((rows + 2 * EDGE, C), bf16),
            vmem((rows + 2 * EDGE, C), f32),
            vmem((rows, C), f32),
            *scatter_scratch(rows, depth),
            pltpu.SemaphoreType.DMA((2, 2)),
            vmem((16, C), f32),
            vmem((C, hidden_cols), bf16),
            vmem((C // 2, hidden_cols), bf16),
            vmem((C // 2, hidden_cols), bf16),
            vmem((shards, units, hidden_cols), bf16),
            vmem((shards, units, hidden_cols), bf16),
            vmem((cols, CLIP), bf16),
            vmem((cols // 2, CLIP), bf16),
            vmem((cols // 2, CLIP), bf16),
            pltpu.SemaphoreType.DMA((2, 2, 3)),
            pltpu.SemaphoreType.DMA((2, 3 + shards)),
            vmem((groups - 1, SMALL_ROWS, 2 * cols), bf16),
            pltpu.SemaphoreType.DMA((2, groups - 1)),
            vmem((shards, 16, cols), f32),
            vmem((shards, 16, cols), f32),
            vmem((16, cols), f32),
            vmem((groups - 1, 16, cols), f32),
            pltpu.SemaphoreType.DMA((2, shards + groups - 2)),
            vmem((shards, cols, rows), bf16),
            pltpu.SemaphoreType.DMA((2, shards - 1)),
        ],
        (
            shape,
            d_pre,
            fc1_weight,
            normed_one,
            inverse_one,
            d_first,
            held,
            wide,
            normed_full,
            branch_sum,
            grad_map_w,
            act_cols,
            second_sum,
            fc2_half,
            small,
        ),
        flops=6 * total * C * hidden_cols,
        scalars=(0,),
        late=(3, 5, 6, 8, 12),
        staged=(1, 2),
    )
    two = lambda row: small[row : row + 2].reshape(hidden_cols)
    one = lambda row: small[row, :cols]
    part = lambda k: weight_sums[k * cols : (k + 1) * cols].astype(f32).T
    return (
        activations,
        input_grad,
        conv_small[:9],
        conv_small[9],
        fc1_sum.astype(f32),
        two(SMALL_FC1),
        two(SMALL_GAMMA),
        two(SMALL_BETA),
        fc2_sum.astype(f32).T,
        conv_small[10],
        small[:SMALL_FC1],
        small[SMALL_TIME],
        map_sum.astype(f32).T,
        one(SMALL_MAP),
        part(0),
        one(SMALL_QUERY),
        part(1),
        part(2),
        one(SMALL_VALUE),
        part(3),
        one(SMALL_OUT),
    )


def solution(mesh):
    in_specs = (
        P(("grp", "seq"), None),
        P("grp", None, None),
        P("grp", None),
        P("grp", None, None),
        P(("grp", "seq"), None),
        P(None, "seq"),
        P("seq"),
        P(None, "seq"),
        P("seq"),
        P("seq"),
        P("seq"),
        P(None, "seq"),
        P("seq"),
        P(None, "seq"),
        P("seq"),
        P(None, "seq"),
        P("seq"),
        P(None, "seq"),
        P("seq"),
        P(None, "seq"),
        P(None, "seq"),
        P("seq"),
        P(None, "seq"),
        P("seq"),
    )
    out_specs = (
        P(("grp", "seq"), None),
        P(("grp", "seq"), None),
        P(None, "seq"),
        P("seq"),
        P(None, "seq"),
        P("seq"),
        P("seq"),
        P("seq"),
        P(None, "seq"),
        P("seq"),
        P(None, "seq"),
        P("seq"),
        P(None, "seq"),
        P("seq"),
        P(None, "seq"),
        P("seq"),
        P(None, "seq"),
        P(None, "seq"),
        P("seq"),
        P(None, "seq"),
        P("seq"),
    )
    by_heads = mesh.shape["seq"] == 8 and mesh.shape["grp"] == 4
    return jax.shard_map(
        on_device_heads if by_heads else on_device, mesh=mesh, in_specs=in_specs, out_specs=out_specs, check_vma=False
    )
```
